32 devices in a mesh: dp: 8 (over z, x), tensor: 4 (over y, core).
Axes of the slice: x: 2, y: 2, z: 4, core: 2. Of those that a mesh axis runs over, the one named last changes fastest.
Arguments:
- tokens: bfloat16 [4096, 2048], P(('dp', 'tensor')), may hold values from -6 to 6
- cotangent: bfloat16 [4096, 2048], P(('dp', 'tensor')), may hold values from -6 to 6
- segment_ids: int32 [4096], P('dp'), may hold values from 0 to 4095, as said below
- gains: float32 [2, 4352], replicated, may hold values from 0.5 to 1.5
- gain_first: float32 [2, 4352], replicated, may hold values from -512 to 512
- gain_second: float32 [2, 4352], replicated, may hold values from 16384 to 131072
- query_weight: float32 [2, 2048, 2048], P(None, 'dp', 'tensor'), may hold values from -0.125 to 0.125
- query_first: float32 [2, 2048, 2048], P(None, 'dp', 'tensor'), may hold values from -32 to 32
- query_second: float32 [2, 2048, 2048], P(None, 'dp', 'tensor'), may hold values from 106.496 to 409.6
- keyvalue_weight: float32 [2, 2, 2048, 1024], P(None, None, 'dp', 'tensor'), may hold values from -0.125 to 0.125
- keyvalue_first: float32 [2, 2, 2048, 1024], P(None, None, 'dp', 'tensor'), may hold values from -48 to 48
- keyvalue_second: float32 [2, 2, 2048, 1024], P(None, None, 'dp', 'tensor'), may hold values from 311.296 to 1228.8
- output_weight: float32 [2, 2048, 2048], P(None, 'dp', 'tensor'), may hold values from -1.5 to 1.5
- output_first: float32 [2, 2048, 2048], P(None, 'dp', 'tensor'), may hold values from -4 to 4
- output_second: float32 [2, 2048, 2048], P(None, 'dp', 'tensor'), may hold values from 2.16 to 8.64
- mlp_weight: float32 [2, 3, 2048, 6144], P(None, None, 'dp', 'tensor'), may hold values from -0.125 to 0.125
- mlp_first: float32 [2, 3, 2048, 6144], P(None, None, 'dp', 'tensor'), may hold values from -16 to 16
- mlp_second: float32 [2, 3, 2048, 6144], P(None, None, 'dp', 'tensor'), may hold values from 34.4064 to 139.264
Outputs:
- block_output: float32 [4096, 2048], P(('dp', 'tensor'))
- input_grad: float32 [4096, 2048], P(('dp', 'tensor'))
- gain_first_new: float32 [2, 4352], replicated
- gain_second_new: float32 [2, 4352], replicated
- gains_new: float32 [2, 4352], replicated
- head_gain_grads: float32 [2, 256], replicated
- query_first_new: float32 [2, 2048, 2048], P(None, 'dp', 'tensor')
- query_second_new: float32 [2, 2048, 2048], P(None, 'dp', 'tensor')
- query_new: float32 [2, 2048, 2048], P(None, 'dp', 'tensor')
- keyvalue_first_new: float32 [2, 2, 2048, 1024], P(None, None, 'dp', 'tensor')
- keyvalue_second_new: float32 [2, 2, 2048, 1024], P(None, None, 'dp', 'tensor')
- keyvalue_new: float32 [2, 2, 2048, 1024], P(None, None, 'dp', 'tensor')
- output_first_new: float32 [2, 2048, 2048], P(None, 'dp', 'tensor')
- output_second_new: float32 [2, 2048, 2048], P(None, 'dp', 'tensor')
- output_new: float32 [2, 2048, 2048], P(None, 'dp', 'tensor')
- mlp_first_new: float32 [2, 3, 2048, 6144], P(None, None, 'dp', 'tensor')
- mlp_second_new: float32 [2, 3, 2048, 6144], P(None, None, 'dp', 'tensor')
- mlp_new: float32 [2, 3, 2048, 6144], P(None, None, 'dp', 'tensor')
The draws below stay inside these ranges and needn't reach their ends.
Inputs may be any that keep to these rules, and one draw needn't show every extreme that they name: `segment_ids`: each id is the global index of the first token of its sequence, so ids never fall. Every group of 512 tokens held by one index of dp begins a sequence, and no sequence crosses a group's end. In every group one sequence holds more than three quarters of the group's tokens, and in one group a single sequence holds all 512.
All inputs are finite; a program needn't handle non-finite values.
Results may differ from the reference program's by a relative error of at most 0.04.
Values may be sent and summed in bfloat16 or wider, within the bound.
A program may use at most 320 MiB of HBM per device.

```python
import math
import jax
import jax.numpy as jnp
from jax import lax

D = 2048
HQ = 16
HK = 8
HD = 128
FF = 6144
TOK_DEV = 512
LAYERS = 2
STEP = 10
TOKENS = 4096
QW = 2048
KW = 1024
GW = 4352


def draw_segment_ids(key, part):
    key = jax.random.fold_in(key, 11)
    groups = TOKENS // TOK_DEV
    spare = TOK_DEV // 4
    first_key, second_key, third_key, fourth_key = jax.random.split(key, 4)
    group_index = jnp.arange(groups, dtype=jnp.int32)[:, None]
    longest = jax.random.randint(first_key, (groups, 1), TOK_DEV - spare + 1, TOK_DEV + 1)
    chosen = jax.random.randint(second_key, (), 0, groups - 1)
    longest = jnp.where(group_index == chosen, TOK_DEV, longest).astype(jnp.int32)
    offset = jax.random.randint(third_key, (groups, 1), 0, TOK_DEV - longest + 1).astype(jnp.int32)
    place = jnp.arange(TOK_DEV, dtype=jnp.int32)[None, :]
    inside = (place >= offset) & (place < offset + longest)
    cuts = jax.random.randint(fourth_key, (groups, TOK_DEV), 0, 8) == 0
    final = (group_index == groups - 1) & (place == TOK_DEV - 1)
    flags = (place == offset) | (place == offset + longest) | cuts & jnp.logical_not(inside) | final | (place == 0)
    starts = lax.cummax(jnp.where(flags, place, 0), axis=1)
    ids = group_index * TOK_DEV + starts
    return ids.reshape(TOKENS).astype(jnp.int32)


def levels(stream_key, shape, pieces, least, top_value):
    def one(dim, parts):
        steps = jax.random.uniform(jax.random.fold_in(jax.random.fold_in(stream_key, 6), dim), (parts,), jnp.float32, least / len(pieces), top_value / len(pieces))
        return jnp.repeat(jnp.exp(steps), shape[dim] // parts).reshape((-1,) + (1,) * (len(shape) - dim - 1))

    factor_of = one(*pieces[0])
    for cut in pieces[1:]:
        factor_of = factor_of * one(*cut)
    return factor_of


def noise(own_key, extent, spread, bound, cuts=(), kind=jnp.bfloat16):
    level = levels(own_key, extent, cuts, -0.22, 0.18) if cuts else 1.0
    drawn = jax.random.normal(own_key, extent, jnp.float32) * spread * level
    return jnp.minimum(jnp.maximum(drawn, -bound), bound).astype(kind)


def setup_inputs(seed: int = 0) -> dict:
    key_of = jax.random.split(jax.random.key(seed), 19)
    return {
        "tokens": noise(key_of[0], (TOKENS, D), 1.0, 6.0, ((0, 32),)),
        "cotangent": noise(key_of[1], (TOKENS, D), 1.0, 6.0, ((0, 32),)),
        "segment_ids": draw_segment_ids(jax.random.fold_in(key_of[18], 71), 0),
        "gains": jnp.clip(1.0 + 0.1 * jax.random.normal(key_of[3], (LAYERS, GW), jnp.float32), 0.5, 1.5),
        "gain_first": noise(key_of[4], (LAYERS, GW), (1.5 * TOKENS ** 0.5), 512.0, (), jnp.float32),
        "gain_second": jnp.clip(jnp.exp(jax.random.uniform(key_of[5], (LAYERS, GW), jnp.float32, math.log(16384.0), math.log(131072.0))), 16384.0, 131072.0),
        "query_weight": noise(key_of[6], (LAYERS, D, QW), D ** -0.5, 0.125, ((1, 8), (2, 4)), jnp.float32),
        "query_first": noise(key_of[7], (LAYERS, D, QW), (0.078 * TOKENS ** 0.5), 32.0, ((1, 8), (2, 4)), jnp.float32),
        "query_second": jnp.clip(jnp.exp(math.log(409.6) - 1.34707364 * jax.random.uniform(key_of[8], (LAYERS, D, QW), jnp.float32) ** levels(key_of[8], (LAYERS, D, QW), ((1, 8), (2, 4)), -0.2, 0.2)), 106.496, 409.6),
        "keyvalue_weight": noise(key_of[9], (LAYERS, 2, D, KW), D ** -0.5, 0.125, ((2, 8), (3, 4)), jnp.float32),
        "keyvalue_first": noise(key_of[10], (LAYERS, 2, D, KW), (0.13 * TOKENS ** 0.5), 48.0, ((2, 8), (3, 4)), jnp.float32),
        "keyvalue_second": jnp.clip(jnp.exp(math.log(1228.8) - 1.3730492 * jax.random.uniform(key_of[11], (LAYERS, 2, D, KW), jnp.float32) ** levels(key_of[11], (LAYERS, 2, D, KW), ((2, 8), (3, 4)), -0.2, 0.2)), 311.296, 1228.8),
        "output_weight": noise(key_of[12], (LAYERS, D, QW), (D * 4 // TOK_DEV) ** -0.5, 1.5, ((1, 8), (2, 4)), jnp.float32),
        "output_first": noise(key_of[13], (LAYERS, D, QW), (0.25 * (TOKENS / TOK_DEV) ** 0.5), 4.0, ((1, 8), (2, 4)), jnp.float32),
        "output_second": jnp.clip(jnp.exp(math.log(8.64) - 1.3862944 * jax.random.uniform(key_of[14], (LAYERS, D, QW), jnp.float32) ** levels(key_of[14], (LAYERS, D, QW), ((1, 8), (2, 4)), -0.2, 0.2)), 2.16, 8.64),
        "mlp_weight": noise(key_of[15], (LAYERS, 3, D, FF), D ** -0.5, 0.125, ((2, 8), (3, 4)), jnp.float32),
        "mlp_first": noise(key_of[16], (LAYERS, 3, D, FF), (0.044 * TOKENS ** 0.5), 16.0, ((2, 8), (3, 4)), jnp.float32),
        "mlp_second": jnp.clip(jnp.exp(math.log(139.264) - 1.3981289 * jax.random.uniform(key_of[17], (LAYERS, 3, D, FF), jnp.float32) ** levels(key_of[17], (LAYERS, 3, D, FF), ((2, 8), (3, 4)), -0.2, 0.2)), 34.4064, 139.264),
    }


EPSILON = 1e-06
THETA = 1000000.0
BETA_ONE = 0.9
BETA_TWO = 0.95
ADAM_EPS = 1e-08
DECAY = 0.1
RATE = 0.05
GAIN_RATE = 0.8
HIGHEST = lax.Precision.HIGHEST

@jax.custom_vjp
def low(v):
    return lax.optimization_barrier(v.astype(jnp.bfloat16)).astype(jnp.float32)

@jax.custom_vjp
def low_back(v):
    return v

def low_keep(v):
    return (low(v), None)

def low_pass(kept, grad):
    return (grad,)

def back_keep(v):
    return (v, None)

def back_low(kept, grad):
    return (low(grad),)
low.defvjp(low_keep, low_pass)
low_back.defvjp(back_keep, back_low)

def product_of(left, right):
    return jnp.dot(left, right, precision=HIGHEST, preferred_element_type=jnp.float32)

def rms_norm(values, gain):
    return values * lax.rsqrt(lax.optimization_barrier(jnp.mean(values * values, axis=-1, keepdims=True)) + EPSILON) * gain

def rope_tables(positions, head_size):
    half = head_size // 2
    frequency = jnp.power(THETA, -2.0 * jnp.arange(half, dtype=jnp.float32) / head_size)
    angle = positions.astype(jnp.float32)[:, None] * frequency[None, :]
    return (jnp.cos(angle)[:, None, :], jnp.sin(angle)[:, None, :])

def rotate(values, cosine, sine):
    half = values.shape[-1] // 2
    first = values[..., :half]
    second = values[..., half:]
    return jnp.concatenate([first * cosine - second * sine, second * cosine + first * sine], axis=-1)

def head_prep(raw, gain, cosine, sine):
    heads = raw.reshape(raw.shape[0], -1, gain.shape[0])
    return rotate(rms_norm(heads, gain), cosine, sine)

def attend_group(inputs):
    query, keys, values, segments = inputs
    count = segments.shape[0]
    index = jnp.arange(count, dtype=jnp.int32)
    mask = (segments[:, None] == segments[None, :]) & (index[None, :] <= index[:, None])
    scale = query.shape[-1] ** (-0.5)
    scores = low_back(jnp.einsum('qjgd,kjd->jgqk', query, keys, precision=HIGHEST) * scale)
    scores = jnp.where(mask, scores, -1e+30)
    probs = low(jax.nn.softmax(scores, axis=-1))
    return jnp.einsum('jgqk,kjd->qjgd', probs, values, precision=HIGHEST)

def block(hidden, gain, query_w, keyvalue_w, output_w, mlp_w, cosine, sine, segments):
    groups = TOKENS // TOK_DEV
    normed = low(rms_norm(hidden, gain[:D]))
    query_raw = low_back(product_of(normed, low(query_w)))
    key_raw = low_back(product_of(normed, low(keyvalue_w[0])))
    values = low(low_back(product_of(normed, low(keyvalue_w[1]))))
    query = low(head_prep(query_raw, gain[2 * D:2 * D + HD], cosine, sine))
    keys = low(head_prep(key_raw, gain[2 * D + HD:], cosine, sine))
    attended = lax.map(jax.checkpoint(attend_group), (query.reshape(groups, TOK_DEV, HK, HQ // HK, HD), keys.reshape(groups, TOK_DEV, HK, HD), values.reshape(groups, TOK_DEV, HK, HD), segments))
    attended = low(low_back(attended.reshape(TOKENS, QW)))
    middle = hidden + low_back(product_of(attended, low(output_w).T))
    normed_mlp = low(rms_norm(middle, gain[D:2 * D]))
    gate = low_back(product_of(normed_mlp, low(mlp_w[0])))
    up = low_back(product_of(normed_mlp, low(mlp_w[1])))
    act = low(jax.nn.silu(gate) * up)
    return middle + low_back(product_of(act, low(mlp_w[2]).T))

def adamw(weight, first, second, grad, rate, decay):
    first_new = BETA_ONE * first + (1.0 - BETA_ONE) * grad
    second_new = BETA_TWO * second + (1.0 - BETA_TWO) * grad * grad
    first_hat = first_new / (1.0 - BETA_ONE ** STEP)
    second_hat = second_new / (1.0 - BETA_TWO ** STEP)
    weight_new = weight - rate * (first_hat / (jnp.sqrt(second_hat) + ADAM_EPS) + decay * weight)
    return (first_new, second_new, weight_new)

def reference(tokens, cotangent, segment_ids, gains, gain_first, gain_second, query_weight, query_first, query_second, keyvalue_weight, keyvalue_first, keyvalue_second, output_weight, output_first, output_second, mlp_weight, mlp_first, mlp_second):
    groups = TOKENS // TOK_DEV
    segments = segment_ids.reshape(groups, TOK_DEV)
    index = jnp.arange(TOKENS, dtype=jnp.int32)
    positions = index - segment_ids
    cosine, sine = rope_tables(positions, HD)

    def forward(hidden, gain_all, query_all, keyvalue_all, output_all, mlp_all):
        for layer in range(LAYERS):
            hidden = block(hidden, gain_all[layer], query_all[layer], keyvalue_all[layer], output_all[layer], mlp_all[layer], cosine, sine, segments)
        return hidden
    output, pullback = jax.vjp(forward, tokens.astype(jnp.float32), gains, query_weight, keyvalue_weight, output_weight, mlp_weight)
    input_grad, gain_grad, query_grad, keyvalue_grad, output_grad, mlp_grad = pullback(cotangent.astype(jnp.float32))
    head_gain_grads = gain_grad[:, 2 * D:]
    gain_first_new, gain_second_new, gains_new = adamw(gains, gain_first, gain_second, gain_grad, GAIN_RATE, 0.0)
    query_first_new, query_second_new, query_new = adamw(query_weight, query_first, query_second, query_grad, RATE, DECAY)
    keyvalue_first_new, keyvalue_second_new, keyvalue_new = adamw(keyvalue_weight, keyvalue_first, keyvalue_second, keyvalue_grad, RATE, DECAY)
    output_first_new, output_second_new, output_new = adamw(output_weight, output_first, output_second, output_grad, RATE * math.sqrt(TOK_DEV // 4), DECAY)
    mlp_first_new, mlp_second_new, mlp_new = adamw(mlp_weight, mlp_first, mlp_second, mlp_grad, RATE, DECAY)
    return (output, input_grad, gain_first_new, gain_second_new, gains_new, head_gain_grads, query_first_new, query_second_new, query_new, keyvalue_first_new, keyvalue_second_new, keyvalue_new, output_first_new, output_second_new, output_new, mlp_first_new, mlp_second_new, mlp_new)
```

```python
from functools import partial
import math

import jax
import jax.numpy as jnp
from jax import lax
from jax.experimental import pallas as pl
from jax.experimental.pallas import tpu as pltpu
from jax.sharding import PartitionSpec as P

HD = 128
STEP = 10
EPSILON = 1e-06
THETA = 1000000.0
BETA_ONE = 0.9
BETA_TWO = 0.95
ADAM_EPS = 1e-08
DECAY = 0.1
RATE = 0.05
GAIN_RATE = 0.8
OUTPUT_FACTOR = math.sqrt(128)

BF16 = jnp.bfloat16
F32 = jnp.float32
MESH = pl.DeviceIdType.MESH
CHUNK = 32


def places(dp_size):
    spread = dp_size // 4
    me = lax.axis_index("dp")
    z = me // spread
    return spread, me, lax.rem(me, spread), lax.rem(z, 2), z // 2


def flip_lo(dp_size):
    spread = dp_size // 4
    return [(i, i + spread * (1 - 2 * ((i // spread) % 2))) for i in range(dp_size)]


def flip_hi(dp_size):
    spread = dp_size // 4
    return [(i, i + 2 * spread * (1 - 2 * (i // (2 * spread)))) for i in range(dp_size)]


def shift_r(dp_size, step):
    spread = dp_size // 4
    return [(i, (i // spread) * spread + (i % spread + step) % spread) for i in range(dp_size)]


def near(spread):
    dp = lax.axis_index("dp")
    tensor = lax.axis_index("tensor")
    core = lax.rem(tensor, 2)
    y = tensor // 2
    low = lax.rem(dp // spread, 2)
    core_id = {"dp": dp, "tensor": y * 2 + 1 - core}
    y_id = {"dp": dp, "tensor": (1 - y) * 2 + core}
    z_id = {"dp": dp + spread * (1 - 2 * low), "tensor": tensor}
    return core, y, low, core_id, y_id, z_id


def greet(ids):
    barrier = pltpu.get_barrier_semaphore()
    for one in ids:
        pl.semaphore_signal(barrier, inc=1, device_id=one, device_id_type=MESH)
    pl.semaphore_wait(barrier, len(ids))


def gather_rows(joined, send, recv, spread):
    core, y, low, core_id, y_id, z_id = near(spread)

    def block(l, yy, c):
        return joined.at[l * 4 + yy * 2 + c]

    def move(slot, ref, to):
        return pltpu.make_async_remote_copy(
            src_ref=ref, dst_ref=ref, send_sem=send.at[slot], recv_sem=recv.at[slot],
            device_id=to, device_id_type=MESH,
        )

    own = block(low, y, core)
    from_z = block(1 - low, y, core)
    from_y = block(low, 1 - y, core)
    diag = block(1 - low, 1 - y, core)
    to_z = move(0, own, z_id)
    to_y = move(1, own, y_id)
    to_core = move(3, own, core_id)
    to_z.start()
    to_y.start()
    to_core.start()
    to_z.wait_recv()
    on_y = move(2, from_z, y_id)
    on_y.start()
    core_z = move(4, from_z, core_id)
    core_z.start()
    to_y.wait_recv()
    core_y = move(5, from_y, core_id)
    core_y.start()
    on_y.wait_recv()
    core_d = move(6, diag, core_id)
    core_d.start()
    for one in (to_core, core_z, core_y, core_d):
        one.wait_recv()
    for one in (to_z, to_y, to_core, on_y, core_z, core_y, core_d):
        one.wait_send()


def reduce_rows(part, core_in, y_in, z_in, sums, send, recv, spread, finish):
    core, y, low, core_id, y_id, z_id = near(spread)
    rows = part.shape[1]
    order = ((1 - low, 1 - y), (low, 1 - y), (1 - low, y), (low, y))

    def move(slot, src, dst, to):
        return pltpu.make_async_remote_copy(
            src_ref=src, dst_ref=dst, send_sem=send.at[slot], recv_sem=recv.at[slot],
            device_id=to, device_id_type=MESH,
        )

    across = [
        move(k, part.at[l * 4 + yy * 2 + 1 - core], core_in.at[k], core_id)
        for k, (l, yy) in enumerate(order)
    ]
    for one in across:
        one.start()
    diag = move(4, sums.at[0], y_in.at[0], y_id)
    to_y = move(5, sums.at[1], y_in.at[1], y_id)
    to_z = move(6, sums.at[2], z_in, z_id)

    def mine(k):
        l, yy = order[k]
        return l * 4 + yy * 2 + core

    def add(k, extra):
        def step(i, carry):
            at = pl.ds(pl.multiple_of(i * CHUNK, CHUNK), CHUNK)
            total = part[mine(k), at, :].astype(F32) + core_in[k, at, :].astype(F32)
            if extra is not None:
                total = total + extra[at, :].astype(F32)
            sums[k, at, :] = total.astype(BF16)
            return carry

        lax.fori_loop(0, rows // CHUNK, step, 0)

    across[0].wait_recv()
    add(0, None)
    diag.start()
    across[1].wait_recv()
    add(1, None)
    to_y.start()
    across[2].wait_recv()
    diag.wait_recv()
    add(2, y_in.at[0])
    to_z.start()
    across[3].wait_recv()
    to_y.wait_recv()
    to_z.wait_recv()

    def last(i, carry):
        at = pl.ds(pl.multiple_of(i * CHUNK, CHUNK), CHUNK)
        total = part[mine(3), at, :].astype(F32) + core_in[3, at, :].astype(F32)
        total = total + y_in[1, at, :].astype(F32) + z_in[at, :].astype(F32)
        finish(at, total)
        return carry

    lax.fori_loop(0, rows // CHUNK, last, 0)
    for one in (*across, diag, to_y, to_z):
        one.wait_send()


def scale_of(v):
    return lax.rsqrt(jnp.mean(v * v, axis=-1, keepdims=True) + EPSILON)


def own_block(spread):
    core, y, low, *_ = near(spread)
    return low * 4 + y * 2 + core


def start_kernel(spread, tokens, grad, gain, joined, joined_grad, send, recv):
    core, y, low, core_id, y_id, z_id = near(spread)
    mine = own_block(spread)
    rows = tokens.shape[0]

    def step(i, carry):
        at = pl.ds(pl.multiple_of(i * CHUNK, CHUNK), CHUNK)
        v = tokens[at, :].astype(F32)
        joined[mine, at, :] = (v * scale_of(v) * gain[...]).astype(BF16)
        joined_grad[mine, at, :] = grad[at, :]
        return carry

    lax.fori_loop(0, rows // CHUNK, step, 0)
    greet((core_id, y_id, z_id))
    gather_rows(joined, send.at[0], recv.at[0], spread)
    gather_rows(joined_grad, send.at[1], recv.at[1], spread)


def forward_kernel(spread, gather, part, hidden, gain, *rest):
    if gather:
        result, joined, core_in, y_in, z_in, sums, send, recv, gsend, grecv = rest
    else:
        result, core_in, y_in, z_in, sums, send, recv = rest
    core, y, low, core_id, y_id, z_id = near(spread)
    greet((core_id, y_id, z_id))

    def finish(at, total):
        v = hidden[at, :] + total
        result[at, :] = v
        if gather:
            joined[own_block(spread), at, :] = (v * scale_of(v) * gain[...]).astype(BF16)

    reduce_rows(part, core_in, y_in, z_in, sums, send, recv, spread, finish)
    if gather:
        gather_rows(joined, gsend, grecv, spread)


def backward_kernel(spread, gather, part, grad, value, gain, *rest):
    if gather:
        result, d_gain, joined, core_in, y_in, z_in, sums, send, recv, gsend, grecv = rest
    else:
        result, d_gain, core_in, y_in, z_in, sums, send, recv = rest
    core, y, low, core_id, y_id, z_id = near(spread)
    greet((core_id, y_id, z_id))
    d_gain[...] = jnp.zeros_like(d_gain)

    def finish(at, total):
        v = value[at, :]
        scale = scale_of(v)
        normed = v * scale
        d_gain[...] += jnp.sum(total * normed, axis=0, keepdims=True)
        d_normed = total * gain[...]
        inner = jnp.mean(d_normed * normed, axis=-1, keepdims=True)
        g = grad[at, :] + scale * (d_normed - normed * inner)
        result[at, :] = g
        if gather:
            joined[own_block(spread), at, :] = g.astype(BF16)

    reduce_rows(part, core_in, y_in, z_in, sums, send, recv, spread, finish)
    if gather:
        gather_rows(joined, gsend, grecv, spread)


def sds(shape, dtype):
    return jax.ShapeDtypeStruct(shape, dtype)


VM = pl.BlockSpec(memory_space=pltpu.VMEM)


def reduce_scratch(rows, width):
    return [
        pltpu.VMEM((4, rows, width), BF16),
        pltpu.VMEM((2, rows, width), BF16),
        pltpu.VMEM((rows, width), BF16),
        pltpu.VMEM((3, rows, width), BF16),
        pltpu.SemaphoreType.DMA((7,)),
        pltpu.SemaphoreType.DMA((7,)),
    ]


def params(collective_id):
    return pltpu.CompilerParams(
        collective_id=collective_id, has_side_effects=True, vmem_limit_bytes=48 * 1024 * 1024
    )


def cost(flops, moved):
    return pl.CostEstimate(flops=flops, bytes_accessed=moved, transcendentals=0)


LINK_COST = 100 * 1024 * 1024


def start_exchange(tokens, grad, gain, spread):
    rows, width = tokens.shape
    return pl.pallas_call(
        partial(start_kernel, spread),
        out_shape=[sds((8, rows, width), BF16), sds((8, rows, width), BF16)],
        in_specs=[VM] * 3,
        out_specs=[VM] * 2,
        scratch_shapes=[pltpu.SemaphoreType.DMA((2, 7)), pltpu.SemaphoreType.DMA((2, 7))],
        compiler_params=params(1),
        cost_estimate=cost(0, LINK_COST),
        name="start_exchange",
    )(tokens, grad, gain)


def forward_exchange(part, hidden, gain, spread, gather):
    rows, width = hidden.shape
    outs = [sds((rows, width), F32)]
    scratch = reduce_scratch(rows, width)
    if gather:
        outs.append(sds((8, rows, width), BF16))
        scratch += [pltpu.SemaphoreType.DMA((7,)), pltpu.SemaphoreType.DMA((7,))]
    return pl.pallas_call(
        partial(forward_kernel, spread, gather),
        out_shape=outs,
        in_specs=[VM] * 3,
        out_specs=[VM] * len(outs),
        scratch_shapes=scratch,
        compiler_params=params(2 if gather else 3),
        cost_estimate=cost(0, LINK_COST),
        name="forward_exchange" if gather else "forward_collect",
    )(part.reshape(8, rows, width), hidden, gain)


def backward_exchange(part, grad, value, gain, spread, gather):
    rows, width = grad.shape
    outs = [sds((rows, width), F32), sds((1, width), F32)]
    scratch = reduce_scratch(rows, width)
    if gather:
        outs.append(sds((8, rows, width), BF16))
        scratch += [pltpu.SemaphoreType.DMA((7,)), pltpu.SemaphoreType.DMA((7,))]
    return pl.pallas_call(
        partial(backward_kernel, spread, gather),
        out_shape=outs,
        in_specs=[VM] * 4,
        out_specs=[VM] * len(outs),
        scratch_shapes=scratch,
        compiler_params=params(4 if gather else 5),
        cost_estimate=cost(0, LINK_COST),
        name="backward_exchange" if gather else "backward_collect",
    )(part.reshape(8, rows, width), grad, value, gain)


def assemble_kernel(*refs):
    count = (len(refs) - 3) // 1
    places_ref, pieces, out, sems = refs[0], refs[1:-2], refs[-2], refs[-1]
    rows = pieces[0].shape[0]
    copies = []
    for k, piece in enumerate(pieces):
        at = pl.ds(pl.multiple_of(places_ref[k] * rows, rows), rows)
        copies.append(pltpu.make_async_copy(piece, out.at[at], sems.at[k]))
    for one in copies:
        one.start()
    for one in copies:
        one.wait()


def assemble(pieces, sources):
    rows, width = pieces[0].shape
    count = len(pieces)
    return pl.pallas_call(
        assemble_kernel,
        out_shape=sds((rows * count, width), BF16),
        in_specs=[pl.BlockSpec(memory_space=pltpu.SMEM)] + [pl.BlockSpec(memory_space=pl.ANY)] * count,
        out_specs=pl.BlockSpec(memory_space=pl.ANY),
        scratch_shapes=[pltpu.SemaphoreType.DMA((count,))],
        cost_estimate=cost(0, 2 * rows * count * width * 2),
        name="assemble",
    )(jnp.stack(sources), *pieces)


def gather_weights(pair, dp_size):
    spread, me, r, low, high = places(dp_size)
    keep = jnp.where(low == 0, pair[0], pair[1])
    give = jnp.where(low == 0, pair[1], pair[0])
    got = lax.ppermute(give, "dp", flip_lo(dp_size))
    other_low = me + spread * (1 - 2 * low)
    pieces = [keep, got]
    sources = [me, other_low]
    hop = 2 * spread * (1 - 2 * high)
    pieces = pieces + [lax.ppermute(one, "dp", flip_hi(dp_size)) for one in pieces]
    sources = sources + [one + hop for one in sources]
    quad, quad_sources = pieces, sources
    for step in range(1, spread):
        pieces = pieces + [lax.ppermute(one, "dp", shift_r(dp_size, step)) for one in quad]
        delta = lax.rem(r + spread - step, spread) - r
        sources = sources + [one + delta for one in quad_sources]
    return assemble(pieces, sources)


def scatter_grads(grad, dp_size):
    spread, me, r, low, high = places(dp_size)
    rows = grad.shape[0] // dp_size
    width = grad.shape[1]
    blocks = grad.reshape(4, spread, rows, width)
    total = lax.dynamic_index_in_dim(blocks, r, axis=1, keepdims=False)
    for step in range(1, spread):
        give = lax.dynamic_index_in_dim(blocks, lax.rem(r + step, spread), axis=1, keepdims=False)
        got = lax.ppermute(give, "dp", shift_r(dp_size, step))
        total = total.astype(F32) + got.astype(F32)
    total = total.astype(BF16).reshape(2, 2, rows, width)
    give = lax.dynamic_index_in_dim(total, 1 - high, axis=0, keepdims=False)
    keep = lax.dynamic_index_in_dim(total, high, axis=0, keepdims=False)
    got = lax.ppermute(give, "dp", flip_hi(dp_size))
    total = (keep.astype(F32) + got.astype(F32)).astype(BF16)
    keep = lax.dynamic_index_in_dim(total, low, axis=0, keepdims=False)
    give = lax.dynamic_index_in_dim(total, 1 - low, axis=0, keepdims=False)
    got = lax.ppermute(give, "dp", flip_lo(dp_size))
    return jnp.where(low == 0, keep, got), jnp.where(low == 0, got, keep)


def halves(weight):
    weight = weight.astype(BF16)
    half = weight.shape[-1] // 2
    return weight[..., :half], weight[..., half:]


def fetch(masters, layer, dp_size):
    query_all, keyvalue_all, output_all, mlp_all = masters
    q, o = halves(query_all[layer]), halves(output_all[layer])
    k, v = halves(keyvalue_all[layer, 0]), halves(keyvalue_all[layer, 1])
    g, u, d = (halves(mlp_all[layer, i]) for i in range(3))

    def bundle(*arrays):
        return tuple(jnp.concatenate([one[i] for one in arrays], axis=1) for i in range(2))

    return (
        gather_weights(bundle(q, k, v), dp_size),
        gather_weights(o, dp_size),
        gather_weights(bundle(g, u), dp_size),
        gather_weights(d, dp_size),
    )


def rms_norm(values, gain):
    return values * lax.rsqrt(jnp.mean(values * values, axis=-1, keepdims=True) + EPSILON) * gain


def rope_tables(positions, head_size):
    half = head_size // 2
    frequency = jnp.power(THETA, -2.0 * jnp.arange(half, dtype=F32) / head_size)
    angle = positions.astype(F32)[:, None] * frequency[None, :]
    return (jnp.cos(angle)[:, None, :], jnp.sin(angle)[:, None, :])


def rotate(values, cosine, sine):
    half = values.shape[-1] // 2
    first = values[..., :half]
    second = values[..., half:]
    return jnp.concatenate(
        [first * cosine - second * sine, second * cosine + first * sine], axis=-1
    )


def head_prep(raw, gain, cosine, sine):
    heads = raw.reshape(raw.shape[0], -1, gain.shape[0])
    return rotate(rms_norm(heads, gain), cosine, sine)


def silu_product(gate, up):
    return jax.nn.silu(gate) * up


def attend(query, keys, values, mask):
    scale = query.shape[-1] ** (-0.5)
    scores = jnp.einsum("bqgd,bkd->bgqk", query, keys, preferred_element_type=F32) * scale
    scores = jnp.where(mask, scores, -1e30)
    top = jnp.max(scores, axis=-1, keepdims=True)
    weights = jnp.exp(scores - top)
    total = jnp.sum(weights, axis=-1, keepdims=True)
    probs = (weights / total).astype(BF16)
    result = jnp.einsum("bgqk,bkd->bqgd", probs, values, preferred_element_type=F32)
    return (result.astype(BF16), top + jnp.log(total))


def attend_back(query, keys, values, logsum, d_out, mask):
    scale = query.shape[-1] ** (-0.5)
    scores = jnp.einsum("bqgd,bkd->bgqk", query, keys, preferred_element_type=F32) * scale
    scores = jnp.where(mask, scores, -1e30)
    probs = jnp.exp(scores - logsum)
    d_probs = jnp.einsum("bqgd,bkd->bgqk", d_out, values, preferred_element_type=F32)
    delta = jnp.sum(d_probs * probs, axis=-1, keepdims=True)
    d_scores = (probs * (d_probs - delta)).astype(BF16)
    d_query = jnp.einsum("bgqk,bkd->bqgd", d_scores, keys, preferred_element_type=F32) * scale
    d_keys = jnp.einsum("bgqk,bqgd->bkd", d_scores, query, preferred_element_type=F32) * scale
    d_values = jnp.einsum("bgqk,bqgd->bkd", probs.astype(BF16), d_out, preferred_element_type=F32)
    return (d_query, d_keys, d_values)


def dot(a, b):
    return jnp.dot(a, b, preferred_element_type=F32)


def back_dot(a, b):
    return lax.dot_general(a, b, (((1,), (1,)), ((), ())), preferred_element_type=F32)


def weight_dot(a, b):
    return lax.dot_general(a, b, (((0,), (0,)), ((), ())), preferred_element_type=F32).astype(BF16)


def adamw(weight, first, second, grad, rate, decay):
    first_new = BETA_ONE * first + (1.0 - BETA_ONE) * grad
    second_new = BETA_TWO * second + (1.0 - BETA_TWO) * grad * grad
    first_hat = first_new / (1.0 - BETA_ONE**STEP)
    second_hat = second_new / (1.0 - BETA_TWO**STEP)
    weight_new = weight - rate * (first_hat / (jnp.sqrt(second_hat) + ADAM_EPS) + decay * weight)
    return (first_new, second_new, weight_new)


def body(
    tokens, cotangent, segment_ids, gains, gain_first, gain_second,
    query_weight, query_first, query_second,
    keyvalue_weight, keyvalue_first, keyvalue_second,
    output_weight, output_first, output_second,
    mlp_weight, mlp_first, mlp_second,
):
    dp_size = lax.axis_size("dp")
    spread, me, r, low, high = places(dp_size)
    layers = gains.shape[0]
    local_rows, width = tokens.shape
    group = segment_ids.shape[0]
    rows = 8 * local_rows
    index = jnp.arange(group, dtype=jnp.int32)
    other = lax.ppermute(segment_ids, "dp", flip_lo(dp_size))
    segments = jnp.stack([jnp.where(low == 0, segment_ids, other), jnp.where(low == 0, other, segment_ids)])
    positions = (index[None, :] - (segments - segments[:, :1])).reshape(rows)
    mask = (segments[:, :, None] == segments[:, None, :]) & (index[None, None, :] <= index[None, :, None])
    mask = mask[:, None]
    cosine, sine = rope_tables(positions, HD)
    masters = (query_weight, keyvalue_weight, output_weight, mlp_weight)

    def gain_row(layer, part):
        return gains[layer, part * width : (part + 1) * width].reshape(1, width)

    prepare = partial(head_prep, cosine=cosine, sine=sine)
    weights = [fetch(masters, layer, dp_size) for layer in range(layers)]
    hidden = tokens.astype(F32)
    joined, joined_grad = start_exchange(tokens, cotangent, gain_row(0, 0), spread)
    joined = joined.reshape(rows, width)
    saved = []
    for layer in range(layers):
        qkv_w, output_w, gateup_w, down_w = weights[layer]
        q_size = output_w.shape[1]
        kv_size = (qkv_w.shape[1] - q_size) // 2
        raw = dot(joined, qkv_w)
        values = raw[:, q_size + kv_size :].astype(BF16)
        gain_q = gains[layer, 2 * width : 2 * width + HD]
        gain_k = gains[layer, 2 * width + HD :]
        query, query_back = jax.vjp(prepare, raw[:, :q_size], gain_q)
        keys, key_back = jax.vjp(prepare, raw[:, q_size : q_size + kv_size], gain_k)
        query = query.astype(BF16).reshape(2, group, -1, HD)
        keys = keys.astype(BF16).reshape(2, group, HD)
        values = values.reshape(2, group, HD)
        attended, logsum = attend(query, keys, values, mask)
        attended = attended.reshape(rows, -1)
        part = back_dot(attended, output_w).astype(BF16)
        middle, joined_mlp = forward_exchange(part, hidden, gain_row(layer, 1), spread, True)
        joined_mlp = joined_mlp.reshape(rows, width)
        gateup = dot(joined_mlp, gateup_w)
        ff = down_w.shape[1]
        product, product_back = jax.vjp(silu_product, gateup[:, :ff], gateup[:, ff:])
        product = product.astype(BF16)
        part = back_dot(product, down_w).astype(BF16)
        record = (
            hidden, joined, query_back, key_back, query, keys, values, logsum, attended,
            middle, joined_mlp, product_back, product,
        )
        saved.append(record)
        if layer + 1 < layers:
            hidden, joined = forward_exchange(part, middle, gain_row(layer + 1, 0), spread, True)
            joined = joined.reshape(rows, width)
        else:
            (hidden,) = forward_exchange(part, middle, gain_row(layer, 0), spread, False)

    block_output = hidden
    grad = cotangent.astype(F32)
    grad_rows = joined_grad.reshape(rows, width)
    reduced = [None] * layers
    gain_grads = [None] * layers
    for layer in reversed(range(layers)):
        qkv_w, output_w, gateup_w, down_w = weights[layer]
        (
            hidden, joined, query_back, key_back, query, keys, values, logsum, attended,
            middle, joined_mlp, product_back, product,
        ) = saved[layer]
        d_product = dot(grad_rows, down_w)
        d_gate, d_up = product_back(d_product)
        d_gateup = jnp.concatenate([d_gate.astype(BF16), d_up.astype(BF16)], axis=1)
        part = back_dot(d_gateup, gateup_w).astype(BF16)
        grad_down = scatter_grads(weight_dot(grad_rows, product), dp_size)
        grad_gateup = scatter_grads(weight_dot(joined_mlp, d_gateup), dp_size)
        grad, d_gain_mlp, grad_rows = backward_exchange(
            part, grad, middle, gain_row(layer, 1), spread, True
        )
        grad_rows = grad_rows.reshape(rows, width)
        d_attended = dot(grad_rows, output_w).astype(BF16)
        grad_output = scatter_grads(weight_dot(grad_rows, attended), dp_size)
        d_query, d_keys, d_values = attend_back(
            query, keys, values, logsum, d_attended.reshape(query.shape), mask
        )
        d_query_raw, d_gain_query = query_back(d_query.reshape(rows, -1, HD))
        d_key_raw, d_gain_key = key_back(d_keys.reshape(rows, -1, HD))
        d_raw = jnp.concatenate(
            [d_query_raw.astype(BF16), d_key_raw.astype(BF16), d_values.reshape(rows, -1).astype(BF16)],
            axis=1,
        )
        part = back_dot(d_raw, qkv_w).astype(BF16)
        grad_qkv = scatter_grads(weight_dot(joined, d_raw), dp_size)
        if layer > 0:
            grad, d_gain_attn, grad_rows = backward_exchange(
                part, grad, hidden, gain_row(layer, 0), spread, True
            )
            grad_rows = grad_rows.reshape(rows, width)
        else:
            grad, d_gain_attn = backward_exchange(
                part, grad, hidden, gain_row(layer, 0), spread, False
            )
        gain_grads[layer] = jnp.concatenate(
            [d_gain_attn[0], d_gain_mlp[0], d_gain_query, d_gain_key]
        )
        q_size = output_w.shape[1]
        kv_size = (qkv_w.shape[1] - q_size) // 2
        ff = down_w.shape[1]

        def columns(pair, start, size):
            return jnp.concatenate([one[:, start : start + size] for one in pair], axis=1).astype(F32)

        reduced[layer] = (
            columns(grad_qkv, 0, q_size),
            jnp.stack([columns(grad_qkv, q_size, kv_size), columns(grad_qkv, q_size + kv_size, kv_size)]),
            columns(grad_output, 0, q_size),
            jnp.stack([columns(grad_gateup, 0, ff), columns(grad_gateup, ff, ff), columns(grad_down, 0, ff)]),
        )
    stacked = [jnp.stack([entry[i] for entry in reduced]) for i in range(4)]
    gain_total = lax.psum(jnp.stack(gain_grads), ("dp", "tensor"))
    head_gain_grads = gain_total[:, 2 * width :]
    gain_new = adamw(gains, gain_first, gain_second, gain_total, GAIN_RATE, 0.0)
    query_new = adamw(query_weight, query_first, query_second, stacked[0], RATE, DECAY)
    keyvalue_new = adamw(keyvalue_weight, keyvalue_first, keyvalue_second, stacked[1], RATE, DECAY)
    output_new = adamw(output_weight, output_first, output_second, stacked[2], RATE * OUTPUT_FACTOR, DECAY)
    mlp_new = adamw(mlp_weight, mlp_first, mlp_second, stacked[3], RATE, DECAY)
    return (block_output, grad, *gain_new, head_gain_grads, *query_new, *keyvalue_new, *output_new, *mlp_new)


def solution(mesh):
    token = P(("dp", "tensor"), None)
    flat = P(None, "dp", "tensor")
    deep = P(None, None, "dp", "tensor")
    placed = (token, token, P("dp"), P(), P(), P(), *[flat] * 3, *[deep] * 3, *[flat] * 3, *[deep] * 3)
    outs = (token, token, P(), P(), P(), P(), *[flat] * 3, *[deep] * 3, *[flat] * 3, *[deep] * 3)
    return jax.shard_map(body, mesh=mesh, in_specs=placed, out_specs=outs, check_vma=False)
```

```python
from functools import partial
import math
from types import SimpleNamespace

import jax
import jax.numpy as jnp
from jax import lax
from jax.experimental import pallas as pl
from jax.experimental.pallas import tpu as pltpu
from jax.sharding import PartitionSpec as P

HD = 128
STEP = 10
EPSILON = 1e-06
THETA = 1000000.0
BETA_ONE = 0.9
BETA_TWO = 0.95
ADAM_EPS = 1e-08
DECAY = 0.1
RATE = 0.05
GAIN_RATE = 0.8
OUTPUT_FACTOR = math.sqrt(128)

BF16 = jnp.bfloat16
F32 = jnp.float32
MESH = pl.DeviceIdType.MESH
CHUNK = 32
VMEM_LIMIT = 60 * 1024 * 1024


class Place:
    def __init__(self, spread):
        self.spread = spread
        self.dp = lax.axis_index("dp")
        self.tensor = lax.axis_index("tensor")
        self.core = lax.rem(self.tensor, 2)
        self.y = self.tensor // 2
        self.z = self.dp // spread
        self.r = lax.rem(self.dp, spread)
        self.low = lax.rem(self.z, 2)
        self.core_id = {"dp": self.dp, "tensor": self.y * 2 + 1 - self.core}
        self.y_id = {"dp": self.dp, "tensor": (1 - self.y) * 2 + self.core}
        self.low_id = {"dp": self.dp + spread * (1 - 2 * self.low), "tensor": self.tensor}
        self.own_pair = self.low * 2 + self.y
        self.pairs = (
            (1 - self.low) * 2 + 1 - self.y,
            self.low * 2 + 1 - self.y,
            (1 - self.low) * 2 + self.y,
            self.own_pair,
        )

    def z_dp(self, step):
        return lax.rem(self.z + 4 + step, 4) * self.spread + self.r

    def z_id(self, step):
        return {"dp": self.z_dp(step), "tensor": self.tensor}

    def r_dp(self, step):
        return self.z * self.spread + lax.rem(self.r + self.spread + step, self.spread)

    def r_id(self, step):
        return {"dp": self.r_dp(step), "tensor": self.tensor}

    def greet(self):
        ids = [self.core_id, self.y_id]
        ids += [self.z_id(k) for k in range(1, 4)]
        ids += [self.r_id(k) for k in range(1, self.spread)]
        barrier = pltpu.get_barrier_semaphore()
        for one in ids:
            pl.semaphore_signal(barrier, inc=1, device_id=one, device_id_type=MESH)
        pl.semaphore_wait(barrier, len(ids))


class Links:
    def __init__(self, send, recv):
        self.send, self.recv, self.count = send, recv, 0
        self.local = []

    def remote(self, src, dst, to):
        slot = self.count
        self.count += 1
        return pltpu.make_async_remote_copy(
            src_ref=src, dst_ref=dst, send_sem=self.send.at[slot], recv_sem=self.recv.at[slot],
            device_id=to, device_id_type=MESH,
        )

    def copy(self, src, dst):
        slot = self.count
        self.count += 1
        return pltpu.make_async_copy(src, dst, self.send.at[slot])


def tile(start, size):
    return pl.ds(pl.multiple_of(start, size), size)


class Spread:
    def __init__(self, links, place, joined):
        rows = joined.shape[0] // 8

        def block(pair, core):
            return joined.at[tile((pair * 2 + core) * rows, rows)]

        c = place.core
        diag, y, z, own = place.pairs
        own, from_z, from_y, from_d = (block(p, c) for p in (own, z, y, diag))
        self.to_z = links.remote(own, own, place.low_id)
        self.to_y = links.remote(own, own, place.y_id)
        self.to_core = links.remote(own, own, place.core_id)
        self.on_y = links.remote(from_z, from_z, place.y_id)
        self.core_z = links.remote(from_z, from_z, place.core_id)
        self.core_y = links.remote(from_y, from_y, place.core_id)
        self.core_d = links.remote(from_d, from_d, place.core_id)

    def start(self):
        self.to_z.start()
        self.to_y.start()
        self.to_core.start()

    def own_ready(self):
        self.to_core.wait_recv()

    def pass_z(self):
        self.to_z.wait_recv()
        self.on_y.start()
        self.core_z.start()

    def pass_y(self):
        self.to_y.wait_recv()
        self.core_y.start()

    def z_ready(self):
        self.core_z.wait_recv()

    def y_ready(self):
        self.core_y.wait_recv()

    def pass_d(self):
        self.on_y.wait_recv()
        self.core_d.start()

    def d_ready(self):
        self.core_d.wait_recv()

    def drain(self):
        for one in (self.to_z, self.to_y, self.to_core, self.on_y, self.core_z, self.core_y, self.core_d):
            one.wait_send()


def consume(gathered, place, work, pump=lambda: None):
    diag, y, z, own = place.pairs
    gathered.own_ready()
    work(own)
    gathered.pass_z()
    gathered.pass_y()
    pump()
    gathered.z_ready()
    work(z)
    gathered.y_ready()
    work(y)
    gathered.pass_d()
    pump()
    gathered.d_ready()
    work(diag)
    gathered.drain()


def collect(links, place, ns, work, finish, before, pump=lambda: None):
    part, core_in, y_in, z_in, sums = ns.part, ns.core_in, ns.y_in, ns.z_in, ns.sums
    rows = part.shape[0] // 8
    core = place.core

    def block(pair, c):
        return tile((pair * 2 + c) * rows, rows)

    across = [
        links.remote(part.at[block(p, 1 - core)], core_in.at[k], place.core_id)
        for k, p in enumerate(place.pairs)
    ]
    diag = links.remote(sums.at[0], y_in.at[0], place.y_id)
    to_y = links.remote(sums.at[1], y_in.at[1], place.y_id)
    to_z = links.remote(sums.at[2], z_in, place.low_id)

    def term(k, i):
        start = (place.pairs[k] * 2 + core) * rows + i * CHUNK
        at = tile(i * CHUNK, CHUNK)
        return part[tile(start, CHUNK), :].astype(F32) + core_in[k, at, :].astype(F32)

    def add(k, extra):
        def step(i, carry):
            at = tile(i * CHUNK, CHUNK)
            total = term(k, i)
            if extra is not None:
                total = total + extra[at, :].astype(F32)
            sums[k, at, :] = total.astype(BF16)
            return carry

        lax.fori_loop(0, rows // CHUNK, step, 0)

    work(place.pairs[0])
    across[0].start()
    work(place.pairs[1])
    across[1].start()
    across[0].wait_recv()
    add(0, None)
    diag.start()
    before()
    work(place.pairs[2])
    across[2].start()
    across[1].wait_recv()
    add(1, None)
    to_y.start()
    work(place.pairs[3])
    across[3].start()
    across[2].wait_recv()
    pump()
    diag.wait_recv()
    add(2, y_in.at[0])
    to_z.start()
    across[3].wait_recv()
    pump()
    to_y.wait_recv()
    to_z.wait_recv()

    def last(i, carry):
        at = tile(i * CHUNK, CHUNK)
        total = term(3, i) + y_in[1, at, :].astype(F32) + z_in[at, :].astype(F32)
        finish(at, total)
        return carry

    lax.fori_loop(0, rows // CHUNK, last, 0)
    for one in (*across, diag, to_y, to_z):
        one.wait_send()


class Gather:
    def __init__(self, links, place, own, land, save):
        rows = own.shape[1]
        self.place, self.own, self.land, self.rows = place, own, land, rows
        spread = place.spread

        def at(dp):
            return land.at[tile(dp * rows, rows)]

        mine = at(place.dp)
        self.out = [
            links.remote(own.at[lax.rem(place.low + k, 2)], mine, place.z_id(k)) for k in range(1, 4)
        ]
        self.side = [links.remote(own.at[place.low], mine, place.r_id(s)) for s in range(1, spread)]
        self.on = [
            [
                links.remote(at(place.z_dp(-k)), at(place.z_dp(-k)), place.r_id(s))
                for s in range(1, spread)
            ]
            for k in range(1, 4)
        ]
        self.save = None if save is None else links.copy(land, save)

    def start(self):
        for one in self.out + self.side:
            one.start()
        step = 32 if self.rows % 32 == 0 else self.rows

        def copy(i, carry):
            self.land[tile(self.place.dp * self.rows + i * step, step), :] = self.own[
                self.place.low, tile(i * step, step), :
            ]
            return carry

        lax.fori_loop(0, self.rows // step, copy, 0)

    def forward(self, k):
        self.out[k].wait_recv()
        for one in self.on[k]:
            one.start()

    def finish(self):
        for one in self.side:
            one.wait_recv()
        for group in self.on:
            for one in group:
                one.wait_recv()
        if self.save is not None:
            self.save.start()

    def drain(self):
        for one in self.out + self.side:
            one.wait_send()
        for group in self.on:
            for one in group:
                one.wait_send()
        if self.save is not None:
            self.save.wait()


class Pump:
    def __init__(self):
        self.steps = []

    def add(self, *steps):
        self.steps += steps

    def __call__(self):
        if self.steps:
            self.steps.pop(0)()

    def rest(self):
        while self.steps:
            self()


def forwards(*gathers):
    return [partial(one.forward, k) for one in gathers for k in range(3)]


def scale_of(v):
    return lax.rsqrt(jnp.mean(v * v, axis=-1, keepdims=True) + EPSILON)


def mm(a, b):
    return jnp.dot(a, b, preferred_element_type=F32)


def mm_nt(a, b):
    return lax.dot_general(a, b, (((1,), (1,)), ((), ())), preferred_element_type=F32)


def project_heads(ns, pair):
    span = ns.joined.shape[0] // 4
    rows = tile(pair * span, span)
    raw = mm(ns.joined[rows, :], ns.wqkv[...])
    ns.raw[rows, :] = raw
    cosine, sine = ns.cosine[rows, :], ns.sine[rows, :]
    q_size, kv_size = ns.q.shape[1], ns.k.shape[1]

    def heads(out, start, size, gain):
        for h in range(size // HD):
            v = raw[:, start + h * HD : start + (h + 1) * HD]
            v = v * scale_of(v) * gain[...]
            turned = v * cosine + pltpu.roll(v, HD // 2, axis=1) * sine
            out[rows, h * HD : (h + 1) * HD] = turned.astype(BF16)

    heads(ns.q, 0, q_size, ns.gain_q)
    heads(ns.k, q_size, kv_size, ns.gain_k)
    ns.v[rows, :] = raw[:, q_size + kv_size :].astype(BF16)


def attend(ns):
    group = ns.bias.shape[1]
    span = ns.joined.shape[0] // 4
    q_heads = ns.q.shape[1] // HD
    share = q_heads // (ns.k.shape[1] // HD)
    scale = HD**-0.5

    def one_group(b, carry):
        for e in range(q_heads):
            kv = slice((e // share) * HD, (e // share + 1) * HD)
            for half in range(group // span):
                rows = tile(b * group + half * span, span)
                seen = (half + 1) * span
                keys = ns.k[tile(b * group, group), kv][:seen]
                values = ns.v[tile(b * group, group), kv][:seen]
                s = mm_nt(ns.q[rows, e * HD : (e + 1) * HD], keys) * scale
                s = s + ns.bias[b, half * span : (half + 1) * span, :seen].astype(F32)
                p = jnp.exp(s - jnp.max(s, axis=-1, keepdims=True))
                p = p / jnp.sum(p, axis=-1, keepdims=True)
                ns.att[rows, e * HD : (e + 1) * HD] = mm(p.astype(BF16), values).astype(BF16)
        return carry

    lax.fori_loop(0, 2, one_group, 0)


def project_out(ns, source, weight, pair, width=512):
    span = ns.part.shape[0] // 4
    rows = tile(pair * span, span)

    def step(j, carry):
        at = tile(j * width, width)
        ns.part[rows, at] = mm_nt(source[rows, :], weight[at, :]).astype(BF16)
        return carry

    lax.fori_loop(0, ns.part.shape[1] // width, step, 0)


def gate_up(ns, pair, slot, width=256):
    span = ns.joined.shape[0] // 4
    rows = tile(pair * span, span)
    ff = ns.product.shape[1]

    def step(j, carry):
        here, there = tile(j * width, width), tile(ff + j * width, width)
        x = ns.joined[rows, :]
        gate = mm(x, ns.wgu[:, here])
        up = mm(x, ns.wgu[:, there])
        ns.gu_stage[slot, :, here] = gate
        ns.gu_stage[slot, :, there] = up
        ns.product[rows, here] = (gate / (1.0 + jnp.exp(-gate)) * up).astype(BF16)
        return carry

    lax.fori_loop(0, ff // width, step, 0)


def forward_layer_kernel(first, last, spread, ns):
    place = Place(spread)
    links = Links(ns.send, ns.recv)
    pump = Pump()
    local = ns.hidden.shape[0]
    own_rows = (place.own_pair * 2 + place.core) * local
    span = 2 * local

    if first:
        get_qkv = Gather(links, place, ns.own_qkv, ns.wqkv, ns.save_wqkv)
        get_o = Gather(links, place, ns.own_o, ns.wo, ns.save_wo)
    get_gu = Gather(links, place, ns.own_gu, ns.wgu, ns.save_wgu)
    get_down = Gather(links, place, ns.own_down, ns.wdown, ns.save_wdown)
    if not last:
        next_qkv = Gather(links, place, ns.own_next_qkv, ns.wnext_qkv, ns.save_wnext_qkv)
        next_o = Gather(links, place, ns.own_next_o, ns.wnext_o, ns.save_wnext_o)

    if first:
        def norm(i, carry):
            v = ns.hidden[tile(i * CHUNK, CHUNK), :].astype(F32)
            ns.joined[tile(own_rows + i * CHUNK, CHUNK), :] = (v * scale_of(v) * ns.gain_attn[...]).astype(BF16)
            return carry

        lax.fori_loop(0, local // CHUNK, norm, 0)
    else:
        loads = [
            links.copy(ns.joined_in, ns.joined),
            links.copy(ns.wqkv_in, ns.wqkv),
            links.copy(ns.wo_in, ns.wo),
        ]
        for one in loads:
            one.start()
    place.greet()
    if first:
        get_qkv.start()
        gathered = Spread(links, place, ns.joined)
        gathered.start()
        get_o.start()
        for step in forwards(get_qkv, get_o):
            step()
        get_gu.start()
        get_down.start()
        get_qkv.finish()
        get_o.finish()
        consume(gathered, place, partial(project_heads, ns))
        save_a = links.copy(ns.joined, ns.save_a)
        save_a.start()
    else:
        get_gu.start()
        get_down.start()
        for one in loads:
            one.wait()

        def every(i, carry):
            project_heads(ns, i)
            return carry

        lax.fori_loop(0, 4, every, 0)

    pump.add(*forwards(get_gu, get_down))
    attend(ns)
    pump()

    def middle(at, total):
        v = ns.hidden[at, :].astype(F32) + total
        ns.mid[at, :] = v
        ns.joined[tile(own_rows + at.start, CHUNK), :] = (v * scale_of(v) * ns.gain_mlp[...]).astype(BF16)

    def before_middle():
        if first:
            save_a.wait()

    collect(
        links, place, ns, partial(project_out, ns, ns.att, ns.wo), middle, before_middle, pump
    )
    gathered = Spread(links, place, ns.joined)
    gathered.start()
    pump.rest()
    get_gu.finish()
    get_down.finish()
    if last:
        def put(i, carry):
            at = tile(i * CHUNK, CHUNK)
            ns.joined_grad[tile(own_rows + i * CHUNK, CHUNK), :] = ns.cotangent[at, :]
            return carry

        lax.fori_loop(0, local // CHUNK, put, 0)
        spread_grad = Spread(links, place, ns.joined_grad)
    else:
        next_qkv.start()
        next_o.start()
        pump.add(*forwards(next_qkv, next_o))

    saves = []

    def gate_up_pair(pair):
        slot = len(saves) % 2
        if len(saves) >= 2:
            saves[-2].wait()
        gate_up(ns, pair, slot)
        save = links.copy(ns.gu_stage.at[slot], ns.save_gateup.at[tile(pair * span, span)])
        save.start()
        saves.append(save)

    consume(gathered, place, gate_up_pair)
    save_b = links.copy(ns.joined, ns.save_b)
    save_b.start()
    if last:
        spread_grad.start()

    def result(at, total):
        v = ns.mid[at, :] + total
        ns.out[at, :] = v
        if not last:
            ns.joined[tile(own_rows + at.start, CHUNK), :] = (v * scale_of(v) * ns.gain_next[...]).astype(BF16)

    if last:
        pump.add(spread_grad.pass_z, spread_grad.pass_y)
    collect(
        links, place, ns, partial(project_out, ns, ns.product, ns.wdown), result, save_b.wait, pump
    )
    pump.rest()
    if last:
        spread_grad.own_ready()
        spread_grad.z_ready()
        spread_grad.y_ready()
        spread_grad.pass_d()
        spread_grad.d_ready()
        spread_grad.drain()
        final = links.copy(ns.joined_grad, ns.save_next)
    else:
        gathered = Spread(links, place, ns.joined)
        gathered.start()
        next_qkv.finish()
        next_o.finish()
        gathered.own_ready()
        gathered.pass_z()
        gathered.pass_y()
        gathered.z_ready()
        gathered.y_ready()
        gathered.pass_d()
        gathered.d_ready()
        gathered.drain()
        final = links.copy(ns.joined, ns.save_next)
    final.start()
    for save in saves[-2:]:
        save.wait()
    if first:
        get_qkv.drain()
        get_o.drain()
    get_gu.drain()
    get_down.drain()
    if not last:
        next_qkv.drain()
        next_o.drain()
    final.wait()
    assert links.count <= ns.send.shape[0]


def call(kernel, ins, outs, scratch, collective_id, name):
    names = [*ins, *outs, *scratch]

    def run(*refs):
        kernel(SimpleNamespace(**dict(zip(names, refs))))

    def space(in_vmem):
        return pl.BlockSpec(memory_space=pltpu.VMEM if in_vmem else pl.ANY)

    results = pl.pallas_call(
        run,
        out_shape=[jax.ShapeDtypeStruct(shape, dtype) for shape, dtype, _ in outs.values()],
        in_specs=[space(v) for _, v in ins.values()],
        out_specs=[space(v) for _, _, v in outs.values()],
        scratch_shapes=list(scratch.values()),
        compiler_params=pltpu.CompilerParams(
            collective_id=collective_id, has_side_effects=True, vmem_limit_bytes=VMEM_LIMIT
        ),
        cost_estimate=pl.CostEstimate(
            flops=13 * 10**9, bytes_accessed=10**8, transcendentals=10**6
        ),
        name=name,
    )(*[array for array, _ in ins.values()])
    return dict(zip(outs, results))


def exchange_scratch(rows, width):
    return {
        "joined": pltpu.VMEM((8 * rows, width), BF16),
        "part": pltpu.VMEM((8 * rows, width), BF16),
        "core_in": pltpu.VMEM((4, rows, width), BF16),
        "y_in": pltpu.VMEM((2, rows, width), BF16),
        "z_in": pltpu.VMEM((rows, width), BF16),
        "sums": pltpu.VMEM((3, rows, width), BF16),
    }


def forward_layer(layer, hidden, carry, pieces, next_pieces, tables, gains, cotangent, spread):
    rows, width = hidden.shape
    own_qkv, own_o, own_gu, own_down = pieces
    first, last = layer == 0, next_pieces is None
    total = 8 * rows
    d_rows = own_gu.shape[1] * 4 * spread
    qkv, o, gu, ff = own_qkv.shape[2], own_o.shape[2], own_gu.shape[2], own_down.shape[2]
    kv = (qkv - o) // 2
    cosine, sine, bias = tables

    def row(start, size):
        return gains[:, start : start + size]

    ins = {"hidden": (hidden, True)}
    if first:
        ins["gain_attn"] = (row(0, width)[layer : layer + 1], True)
        ins["own_qkv"] = (own_qkv, True)
        ins["own_o"] = (own_o, True)
    else:
        ins["joined_in"] = (carry[0], False)
        ins["wqkv_in"] = (carry[1], False)
        ins["wo_in"] = (carry[2], False)
    ins["own_gu"] = (own_gu, True)
    ins["own_down"] = (own_down, True)
    if last:
        ins["cotangent"] = (cotangent, True)
    else:
        ins["own_next_qkv"] = (next_pieces[0], True)
        ins["own_next_o"] = (next_pieces[1], True)
        ins["gain_next"] = (row(0, width)[layer + 1 : layer + 2], True)
    ins["gain_mlp"] = (row(width, width)[layer : layer + 1], True)
    ins["gain_q"] = (row(2 * width, HD)[layer : layer + 1], True)
    ins["gain_k"] = (row(2 * width + HD, HD)[layer : layer + 1], True)
    ins["cosine"], ins["sine"], ins["bias"] = (cosine, True), (sine, True), (bias, True)
    outs = {
        "out": ((rows, width), F32, True),
        "mid": ((rows, width), F32, True),
        "raw": ((total, qkv), F32, True),
        "q": ((total, o), BF16, True),
        "k": ((total, kv), BF16, True),
        "v": ((total, kv), BF16, True),
        "att": ((total, o), BF16, True),
        "product": ((total, ff), BF16, True),
        "save_gateup": ((total, gu), F32, False),
        "save_b": ((total, width), BF16, False),
        "save_next": ((total, width), BF16, False),
        "save_wgu": ((d_rows, gu), BF16, False),
        "save_wdown": ((d_rows, ff), BF16, False),
    }
    if first:
        outs["save_a"] = ((total, width), BF16, False)
        outs["save_wqkv"] = ((d_rows, qkv), BF16, False)
        outs["save_wo"] = ((d_rows, o), BF16, False)
    if not last:
        outs["save_wnext_qkv"] = ((d_rows, qkv), BF16, False)
        outs["save_wnext_o"] = ((d_rows, o), BF16, False)
    scratch = exchange_scratch(rows, width)
    scratch["gu_stage"] = pltpu.VMEM((2, 2 * rows, gu), F32)
    scratch["wqkv"] = pltpu.VMEM((d_rows, qkv), BF16)
    scratch["wo"] = pltpu.VMEM((d_rows, o), BF16)
    scratch["wgu"] = pltpu.VMEM((d_rows, gu), BF16)
    scratch["wdown"] = pltpu.VMEM((d_rows, ff), BF16)
    if not last:
        scratch["wnext_qkv"] = pltpu.VMEM((d_rows, qkv), BF16)
        scratch["wnext_o"] = pltpu.VMEM((d_rows, o), BF16)
    else:
        scratch["joined_grad"] = pltpu.VMEM((total, width), BF16)
    count = 64 + 32 * spread
    scratch["send"] = pltpu.SemaphoreType.DMA((count,))
    scratch["recv"] = pltpu.SemaphoreType.DMA((count,))
    kernel = partial(forward_layer_kernel, first, last, spread)
    return call(kernel, ins, outs, scratch, 1 + int(last) + 2 * int(not first), "forward_layer")


def places(dp_size):
    spread = dp_size // 4
    me = lax.axis_index("dp")
    z = me // spread
    return spread, me, lax.rem(me, spread), lax.rem(z, 2), z // 2


def flip_lo(dp_size):
    spread = dp_size // 4
    return [(i, i + spread * (1 - 2 * ((i // spread) % 2))) for i in range(dp_size)]


def flip_hi(dp_size):
    spread = dp_size // 4
    return [(i, i + 2 * spread * (1 - 2 * (i // (2 * spread)))) for i in range(dp_size)]


def shift_r(dp_size, step):
    spread = dp_size // 4
    return [(i, (i // spread) * spread + (i % spread + step) % spread) for i in range(dp_size)]


def near(spread):
    dp = lax.axis_index("dp")
    tensor = lax.axis_index("tensor")
    core = lax.rem(tensor, 2)
    y = tensor // 2
    low = lax.rem(dp // spread, 2)
    core_id = {"dp": dp, "tensor": y * 2 + 1 - core}
    y_id = {"dp": dp, "tensor": (1 - y) * 2 + core}
    z_id = {"dp": dp + spread * (1 - 2 * low), "tensor": tensor}
    return core, y, low, core_id, y_id, z_id


def greet(ids):
    barrier = pltpu.get_barrier_semaphore()
    for one in ids:
        pl.semaphore_signal(barrier, inc=1, device_id=one, device_id_type=MESH)
    pl.semaphore_wait(barrier, len(ids))


def gather_rows(joined, send, recv, spread):
    core, y, low, core_id, y_id, z_id = near(spread)

    def block(l, yy, c):
        return joined.at[l * 4 + yy * 2 + c]

    def move(slot, ref, to):
        return pltpu.make_async_remote_copy(
            src_ref=ref, dst_ref=ref, send_sem=send.at[slot], recv_sem=recv.at[slot],
            device_id=to, device_id_type=MESH,
        )

    own = block(low, y, core)
    from_z = block(1 - low, y, core)
    from_y = block(low, 1 - y, core)
    diag = block(1 - low, 1 - y, core)
    to_z = move(0, own, z_id)
    to_y = move(1, own, y_id)
    to_core = move(3, own, core_id)
    to_z.start()
    to_y.start()
    to_core.start()
    to_z.wait_recv()
    on_y = move(2, from_z, y_id)
    on_y.start()
    core_z = move(4, from_z, core_id)
    core_z.start()
    to_y.wait_recv()
    core_y = move(5, from_y, core_id)
    core_y.start()
    on_y.wait_recv()
    core_d = move(6, diag, core_id)
    core_d.start()
    for one in (to_core, core_z, core_y, core_d):
        one.wait_recv()
    for one in (to_z, to_y, to_core, on_y, core_z, core_y, core_d):
        one.wait_send()


def reduce_rows(part, core_in, y_in, z_in, sums, send, recv, spread, finish):
    core, y, low, core_id, y_id, z_id = near(spread)
    rows = part.shape[1]
    order = ((1 - low, 1 - y), (low, 1 - y), (1 - low, y), (low, y))

    def move(slot, src, dst, to):
        return pltpu.make_async_remote_copy(
            src_ref=src, dst_ref=dst, send_sem=send.at[slot], recv_sem=recv.at[slot],
            device_id=to, device_id_type=MESH,
        )

    across = [
        move(k, part.at[l * 4 + yy * 2 + 1 - core], core_in.at[k], core_id)
        for k, (l, yy) in enumerate(order)
    ]
    for one in across:
        one.start()
    diag = move(4, sums.at[0], y_in.at[0], y_id)
    to_y = move(5, sums.at[1], y_in.at[1], y_id)
    to_z = move(6, sums.at[2], z_in, z_id)

    def mine(k):
        l, yy = order[k]
        return l * 4 + yy * 2 + core

    def add(k, extra):
        def step(i, carry):
            at = pl.ds(pl.multiple_of(i * CHUNK, CHUNK), CHUNK)
            total = part[mine(k), at, :].astype(F32) + core_in[k, at, :].astype(F32)
            if extra is not None:
                total = total + extra[at, :].astype(F32)
            sums[k, at, :] = total.astype(BF16)
            return carry

        lax.fori_loop(0, rows // CHUNK, step, 0)

    across[0].wait_recv()
    add(0, None)
    diag.start()
    across[1].wait_recv()
    add(1, None)
    to_y.start()
    across[2].wait_recv()
    diag.wait_recv()
    add(2, y_in.at[0])
    to_z.start()
    across[3].wait_recv()
    to_y.wait_recv()
    to_z.wait_recv()

    def last(i, carry):
        at = pl.ds(pl.multiple_of(i * CHUNK, CHUNK), CHUNK)
        total = part[mine(3), at, :].astype(F32) + core_in[3, at, :].astype(F32)
        total = total + y_in[1, at, :].astype(F32) + z_in[at, :].astype(F32)
        finish(at, total)
        return carry

    lax.fori_loop(0, rows // CHUNK, last, 0)
    for one in (*across, diag, to_y, to_z):
        one.wait_send()


def own_block(spread):
    core, y, low, *_ = near(spread)
    return low * 4 + y * 2 + core


def backward_kernel(spread, gather, part, grad, value, gain, *rest):
    if gather:
        result, d_gain, joined, core_in, y_in, z_in, sums, send, recv, gsend, grecv = rest
    else:
        result, d_gain, core_in, y_in, z_in, sums, send, recv = rest
    core, y, low, core_id, y_id, z_id = near(spread)
    greet((core_id, y_id, z_id))
    d_gain[...] = jnp.zeros_like(d_gain)

    def finish(at, total):
        v = value[at, :]
        scale = scale_of(v)
        normed = v * scale
        d_gain[...] += jnp.sum(total * normed, axis=0, keepdims=True)
        d_normed = total * gain[...]
        inner = jnp.mean(d_normed * normed, axis=-1, keepdims=True)
        g = grad[at, :] + scale * (d_normed - normed * inner)
        result[at, :] = g
        if gather:
            joined[own_block(spread), at, :] = g.astype(BF16)

    reduce_rows(part, core_in, y_in, z_in, sums, send, recv, spread, finish)
    if gather:
        gather_rows(joined, gsend, grecv, spread)


def sds(shape, dtype):
    return jax.ShapeDtypeStruct(shape, dtype)


VM = pl.BlockSpec(memory_space=pltpu.VMEM)


def reduce_scratch(rows, width):
    return [
        pltpu.VMEM((4, rows, width), BF16),
        pltpu.VMEM((2, rows, width), BF16),
        pltpu.VMEM((rows, width), BF16),
        pltpu.VMEM((3, rows, width), BF16),
        pltpu.SemaphoreType.DMA((7,)),
        pltpu.SemaphoreType.DMA((7,)),
    ]


def params(collective_id):
    return pltpu.CompilerParams(
        collective_id=collective_id, has_side_effects=True, vmem_limit_bytes=48 * 1024 * 1024
    )


def cost(flops, moved):
    return pl.CostEstimate(flops=flops, bytes_accessed=moved, transcendentals=0)


LINK_COST = 100 * 1024 * 1024


def backward_exchange(part, grad, value, gain, spread, gather):
    rows, width = grad.shape
    outs = [sds((rows, width), F32), sds((1, width), F32)]
    scratch = reduce_scratch(rows, width)
    if gather:
        outs.append(sds((8, rows, width), BF16))
        scratch += [pltpu.SemaphoreType.DMA((7,)), pltpu.SemaphoreType.DMA((7,))]
    return pl.pallas_call(
        partial(backward_kernel, spread, gather),
        out_shape=outs,
        in_specs=[VM] * 4,
        out_specs=[VM] * len(outs),
        scratch_shapes=scratch,
        compiler_params=params(6 if gather else 7),
        cost_estimate=cost(0, LINK_COST),
        name="backward_exchange" if gather else "backward_collect",
    )(part.reshape(8, rows, width), grad, value, gain)


def scatter_grads(grad, dp_size):
    spread, me, r, low, high = places(dp_size)
    rows = grad.shape[0] // dp_size
    width = grad.shape[1]
    blocks = grad.reshape(4, spread, rows, width)
    total = lax.dynamic_index_in_dim(blocks, r, axis=1, keepdims=False)
    for step in range(1, spread):
        give = lax.dynamic_index_in_dim(blocks, lax.rem(r + step, spread), axis=1, keepdims=False)
        got = lax.ppermute(give, "dp", shift_r(dp_size, step))
        total = total.astype(F32) + got.astype(F32)
    total = total.astype(BF16).reshape(2, 2, rows, width)
    give = lax.dynamic_index_in_dim(total, 1 - high, axis=0, keepdims=False)
    keep = lax.dynamic_index_in_dim(total, high, axis=0, keepdims=False)
    got = lax.ppermute(give, "dp", flip_hi(dp_size))
    total = (keep.astype(F32) + got.astype(F32)).astype(BF16)
    keep = lax.dynamic_index_in_dim(total, low, axis=0, keepdims=False)
    give = lax.dynamic_index_in_dim(total, 1 - low, axis=0, keepdims=False)
    got = lax.ppermute(give, "dp", flip_lo(dp_size))
    return jnp.where(low == 0, keep, got), jnp.where(low == 0, got, keep)


def halves(weight):
    weight = weight.astype(BF16)
    half = weight.shape[-1] // 2
    return weight[..., :half], weight[..., half:]


def rms_norm(values, gain):
    return values * lax.rsqrt(jnp.mean(values * values, axis=-1, keepdims=True) + EPSILON) * gain


def rope_tables(positions, head_size):
    half = head_size // 2
    frequency = jnp.power(THETA, -2.0 * jnp.arange(half, dtype=F32) / head_size)
    angle = positions.astype(F32)[:, None] * frequency[None, :]
    return (jnp.cos(angle)[:, None, :], jnp.sin(angle)[:, None, :])


def rotate(values, cosine, sine):
    half = values.shape[-1] // 2
    first = values[..., :half]
    second = values[..., half:]
    return jnp.concatenate(
        [first * cosine - second * sine, second * cosine + first * sine], axis=-1
    )


def head_prep(raw, gain, cosine, sine):
    heads = raw.reshape(raw.shape[0], -1, gain.shape[0])
    return rotate(rms_norm(heads, gain), cosine, sine)


def silu_product(gate, up):
    return jax.nn.silu(gate) * up


def attend_back(query, keys, values, d_out, mask):
    scale = query.shape[-1] ** (-0.5)
    scores = jnp.einsum("bqgd,bkd->bgqk", query, keys, preferred_element_type=F32) * scale
    scores = jnp.where(mask, scores, -1e30)
    probs = jax.nn.softmax(scores, axis=-1)
    d_probs = jnp.einsum("bqgd,bkd->bgqk", d_out, values, preferred_element_type=F32)
    delta = jnp.sum(d_probs * probs, axis=-1, keepdims=True)
    d_scores = (probs * (d_probs - delta)).astype(BF16)
    d_query = jnp.einsum("bgqk,bkd->bqgd", d_scores, keys, preferred_element_type=F32) * scale
    d_keys = jnp.einsum("bgqk,bqgd->bkd", d_scores, query, preferred_element_type=F32) * scale
    d_values = jnp.einsum("bgqk,bqgd->bkd", probs.astype(BF16), d_out, preferred_element_type=F32)
    return (d_query, d_keys, d_values)


def dot(a, b):
    return jnp.dot(a, b, preferred_element_type=F32)


def back_dot(a, b):
    return lax.dot_general(a, b, (((1,), (1,)), ((), ())), preferred_element_type=F32)


def weight_dot(a, b):
    return lax.dot_general(a, b, (((0,), (0,)), ((), ())), preferred_element_type=F32).astype(BF16)


def adamw(weight, first, second, grad, rate, decay):
    first_new = BETA_ONE * first + (1.0 - BETA_ONE) * grad
    second_new = BETA_TWO * second + (1.0 - BETA_TWO) * grad * grad
    first_hat = first_new / (1.0 - BETA_ONE**STEP)
    second_hat = second_new / (1.0 - BETA_TWO**STEP)
    weight_new = weight - rate * (first_hat / (jnp.sqrt(second_hat) + ADAM_EPS) + decay * weight)
    return (first_new, second_new, weight_new)


def own_pieces(masters, layer):
    query_all, keyvalue_all, output_all, mlp_all = masters

    def both(*arrays):
        pairs = [halves(one) for one in arrays]
        return jnp.stack([jnp.concatenate([one[i] for one in pairs], axis=1) for i in range(2)])

    return (
        both(query_all[layer], keyvalue_all[layer, 0], keyvalue_all[layer, 1]),
        both(output_all[layer]),
        both(mlp_all[layer, 0], mlp_all[layer, 1]),
        both(mlp_all[layer, 2]),
    )


def body(
    tokens, cotangent, segment_ids, gains, gain_first, gain_second,
    query_weight, query_first, query_second,
    keyvalue_weight, keyvalue_first, keyvalue_second,
    output_weight, output_first, output_second,
    mlp_weight, mlp_first, mlp_second,
):
    dp_size = lax.axis_size("dp")
    spread, me, r, low, high = places(dp_size)
    layers = gains.shape[0]
    local_rows, width = tokens.shape
    group = segment_ids.shape[0]
    rows = 8 * local_rows
    index = jnp.arange(group, dtype=jnp.int32)
    other = lax.ppermute(segment_ids, "dp", flip_lo(dp_size))
    segments = jnp.stack([jnp.where(low == 0, segment_ids, other), jnp.where(low == 0, other, segment_ids)])
    positions = (index[None, :] - (segments - segments[:, :1])).reshape(rows)
    mask = (segments[:, :, None] == segments[:, None, :]) & (index[None, None, :] <= index[None, :, None])
    bias = jnp.where(mask, 0.0, -1e30).astype(BF16)
    mask = mask[:, None]
    cosine, sine = rope_tables(positions, HD)
    tables = (
        jnp.concatenate([cosine[:, 0], cosine[:, 0]], axis=1),
        jnp.concatenate([-sine[:, 0], sine[:, 0]], axis=1),
        bias,
    )
    masters = (query_weight, keyvalue_weight, output_weight, mlp_weight)

    def gain_row(layer, part):
        return gains[layer, part * width : (part + 1) * width].reshape(1, width)

    prepare = partial(head_prep, cosine=cosine, sine=sine)
    pieces = [own_pieces(masters, layer) for layer in range(layers)]
    hidden, carry = tokens, None
    saved = []
    for layer in range(layers):
        after = pieces[layer + 1] if layer + 1 < layers else None
        kept = forward_layer(layer, hidden, carry, pieces[layer], after, tables, gains, cotangent, spread)
        if layer == 0:
            carry = (kept["save_a"], kept["save_wqkv"], kept["save_wo"])
        kept["hidden"], kept["a"], kept["wqkv"], kept["wo"] = hidden, *carry
        saved.append(kept)
        hidden = kept["out"]
        if after is not None:
            carry = (kept["save_next"], kept["save_wnext_qkv"], kept["save_wnext_o"])

    block_output = hidden
    grad = cotangent.astype(F32)
    grad_rows = saved[-1]["save_next"]
    reduced = [None] * layers
    gain_grads = [None] * layers
    for layer in reversed(range(layers)):
        kept = saved[layer]
        qkv_w, output_w, gateup_w, down_w = kept["wqkv"], kept["wo"], kept["save_wgu"], kept["save_wdown"]
        q_size, ff = output_w.shape[1], down_w.shape[1]
        kv_size = (qkv_w.shape[1] - q_size) // 2
        query = kept["q"].reshape(2, group, -1, HD)
        keys = kept["k"].reshape(2, group, HD)
        values = kept["v"].reshape(2, group, HD)
        gateup = kept["save_gateup"]
        _, product_back = jax.vjp(silu_product, gateup[:, :ff], gateup[:, ff:])
        raw = kept["raw"]
        gain_q = gains[layer, 2 * width : 2 * width + HD]
        gain_k = gains[layer, 2 * width + HD :]
        _, query_back = jax.vjp(prepare, raw[:, :q_size], gain_q)
        _, key_back = jax.vjp(prepare, raw[:, q_size : q_size + kv_size], gain_k)
        d_product = dot(grad_rows, down_w)
        d_gate, d_up = product_back(d_product)
        d_gateup = jnp.concatenate([d_gate.astype(BF16), d_up.astype(BF16)], axis=1)
        part = back_dot(d_gateup, gateup_w).astype(BF16)
        grad_down = scatter_grads(weight_dot(grad_rows, kept["product"]), dp_size)
        grad_gateup = scatter_grads(weight_dot(kept["save_b"], d_gateup), dp_size)
        grad, d_gain_mlp, grad_rows = backward_exchange(
            part, grad, kept["mid"], gain_row(layer, 1), spread, True
        )
        grad_rows = grad_rows.reshape(rows, width)
        d_attended = dot(grad_rows, output_w).astype(BF16)
        grad_output = scatter_grads(weight_dot(grad_rows, kept["att"]), dp_size)
        d_query, d_keys, d_values = attend_back(
            query, keys, values, d_attended.reshape(query.shape), mask
        )
        d_query_raw, d_gain_query = query_back(d_query.reshape(rows, -1, HD))
        d_key_raw, d_gain_key = key_back(d_keys.reshape(rows, -1, HD))
        d_raw = jnp.concatenate(
            [d_query_raw.astype(BF16), d_key_raw.astype(BF16), d_values.reshape(rows, -1).astype(BF16)],
            axis=1,
        )
        part = back_dot(d_raw, qkv_w).astype(BF16)
        grad_qkv = scatter_grads(weight_dot(kept["a"], d_raw), dp_size)
        value = kept["hidden"].astype(F32)
        if layer > 0:
            grad, d_gain_attn, grad_rows = backward_exchange(
                part, grad, value, gain_row(layer, 0), spread, True
            )
            grad_rows = grad_rows.reshape(rows, width)
        else:
            grad, d_gain_attn = backward_exchange(
                part, grad, value, gain_row(layer, 0), spread, False
            )
        gain_grads[layer] = jnp.concatenate(
            [d_gain_attn[0], d_gain_mlp[0], d_gain_query, d_gain_key]
        )

        def columns(pair, start, size):
            return jnp.concatenate([one[:, start : start + size] for one in pair], axis=1).astype(F32)

        reduced[layer] = (
            columns(grad_qkv, 0, q_size),
            jnp.stack([columns(grad_qkv, q_size, kv_size), columns(grad_qkv, q_size + kv_size, kv_size)]),
            columns(grad_output, 0, q_size),
            jnp.stack([columns(grad_gateup, 0, ff), columns(grad_gateup, ff, ff), columns(grad_down, 0, ff)]),
        )
    stacked = [jnp.stack([entry[i] for entry in reduced]) for i in range(4)]
    gain_total = lax.psum(jnp.stack(gain_grads), ("dp", "tensor"))
    head_gain_grads = gain_total[:, 2 * width :]
    gain_new = adamw(gains, gain_first, gain_second, gain_total, GAIN_RATE, 0.0)
    query_new = adamw(query_weight, query_first, query_second, stacked[0], RATE, DECAY)
    keyvalue_new = adamw(keyvalue_weight, keyvalue_first, keyvalue_second, stacked[1], RATE, DECAY)
    output_new = adamw(output_weight, output_first, output_second, stacked[2], RATE * OUTPUT_FACTOR, DECAY)
    mlp_new = adamw(mlp_weight, mlp_first, mlp_second, stacked[3], RATE, DECAY)
    return (block_output, grad, *gain_new, head_gain_grads, *query_new, *keyvalue_new, *output_new, *mlp_new)


def solution(mesh):
    token = P(("dp", "tensor"), None)
    flat = P(None, "dp", "tensor")
    deep = P(None, None, "dp", "tensor")
    placed = (token, token, P("dp"), P(), P(), P(), *[flat] * 3, *[deep] * 3, *[flat] * 3, *[deep] * 3)
    outs = (token, token, P(), P(), P(), P(), *[flat] * 3, *[deep] * 3, *[flat] * 3, *[deep] * 3)
    return jax.shard_map(body, mesh=mesh, in_specs=placed, out_specs=outs, check_vma=False)
```

```python
from functools import partial
import math
from types import SimpleNamespace

import jax
import jax.numpy as jnp
from jax import lax
from jax.experimental import pallas as pl
from jax.experimental.pallas import tpu as pltpu
from jax.sharding import PartitionSpec as P

HD = 128
STEP = 10
EPSILON = 1e-06
THETA = 1000000.0
BETA_ONE = 0.9
BETA_TWO = 0.95
ADAM_EPS = 1e-08
DECAY = 0.1
RATE = 0.05
GAIN_RATE = 0.8
OUTPUT_FACTOR = math.sqrt(128)

BF16 = jnp.bfloat16
F32 = jnp.float32
MESH = pl.DeviceIdType.MESH
CHUNK = 32
VMEM_LIMIT = 60 * 1024 * 1024


class Place:
    def __init__(self, spread):
        self.spread = spread
        self.dp = lax.axis_index("dp")
        self.tensor = lax.axis_index("tensor")
        self.core = lax.rem(self.tensor, 2)
        self.y = self.tensor // 2
        self.z = self.dp // spread
        self.r = lax.rem(self.dp, spread)
        self.low = lax.rem(self.z, 2)
        self.core_id = {"dp": self.dp, "tensor": self.y * 2 + 1 - self.core}
        self.y_id = {"dp": self.dp, "tensor": (1 - self.y) * 2 + self.core}
        self.low_id = {"dp": self.dp + spread * (1 - 2 * self.low), "tensor": self.tensor}
        self.own_pair = self.low * 2 + self.y
        self.pairs = (
            (1 - self.low) * 2 + 1 - self.y,
            self.low * 2 + 1 - self.y,
            (1 - self.low) * 2 + self.y,
            self.own_pair,
        )

    def z_dp(self, step):
        return lax.rem(self.z + 4 + step, 4) * self.spread + self.r

    def z_id(self, step):
        return {"dp": self.z_dp(step), "tensor": self.tensor}

    def r_dp(self, step):
        return self.z * self.spread + lax.rem(self.r + self.spread + step, self.spread)

    def r_id(self, step):
        return {"dp": self.r_dp(step), "tensor": self.tensor}

    def greet(self):
        ids = [self.core_id, self.y_id]
        ids += [self.z_id(k) for k in range(1, 4)]
        ids += [self.r_id(k) for k in range(1, self.spread)]
        barrier = pltpu.get_barrier_semaphore()
        for one in ids:
            pl.semaphore_signal(barrier, inc=1, device_id=one, device_id_type=MESH)
        pl.semaphore_wait(barrier, len(ids))


class Links:
    def __init__(self, send, recv):
        self.send, self.recv, self.count = send, recv, 0
        self.local = []

    def remote(self, src, dst, to):
        slot = self.count
        self.count += 1
        return pltpu.make_async_remote_copy(
            src_ref=src, dst_ref=dst, send_sem=self.send.at[slot], recv_sem=self.recv.at[slot],
            device_id=to, device_id_type=MESH,
        )

    def copy(self, src, dst):
        slot = self.count
        self.count += 1
        return pltpu.make_async_copy(src, dst, self.send.at[slot])


def tile(start, size):
    return pl.ds(pl.multiple_of(start, size), size)


class Spread:
    def __init__(self, links, place, joined):
        rows = joined.shape[0] // 8

        def block(pair, core):
            return joined.at[tile((pair * 2 + core) * rows, rows)]

        c = place.core
        diag, y, z, own = place.pairs
        own, from_z, from_y, from_d = (block(p, c) for p in (own, z, y, diag))
        self.to_z = links.remote(own, own, place.low_id)
        self.to_y = links.remote(own, own, place.y_id)
        self.to_core = links.remote(own, own, place.core_id)
        self.on_y = links.remote(from_z, from_z, place.y_id)
        self.core_z = links.remote(from_z, from_z, place.core_id)
        self.core_y = links.remote(from_y, from_y, place.core_id)
        self.core_d = links.remote(from_d, from_d, place.core_id)

    def start(self):
        self.to_z.start()
        self.to_y.start()
        self.to_core.start()

    def own_ready(self):
        self.to_core.wait_recv()

    def pass_z(self):
        self.to_z.wait_recv()
        self.on_y.start()
        self.core_z.start()

    def pass_y(self):
        self.to_y.wait_recv()
        self.core_y.start()

    def z_ready(self):
        self.core_z.wait_recv()

    def y_ready(self):
        self.core_y.wait_recv()

    def pass_d(self):
        self.on_y.wait_recv()
        self.core_d.start()

    def d_ready(self):
        self.core_d.wait_recv()

    def drain(self):
        for one in (self.to_z, self.to_y, self.to_core, self.on_y, self.core_z, self.core_y, self.core_d):
            one.wait_send()


def consume(gathered, place, work, pump=lambda: None):
    diag, y, z, own = place.pairs
    gathered.own_ready()
    work(own)
    gathered.pass_z()
    gathered.pass_y()
    pump()
    gathered.z_ready()
    work(z)
    gathered.y_ready()
    work(y)
    gathered.pass_d()
    pump()
    gathered.d_ready()
    work(diag)
    gathered.drain()


def collect(links, place, ns, work, finish, before, pump=lambda: None):
    part, core_in, y_in, z_in, sums = ns.part, ns.core_in, ns.y_in, ns.z_in, ns.sums
    rows = part.shape[0] // 8
    core = place.core

    def block(pair, c):
        return tile((pair * 2 + c) * rows, rows)

    across = [
        links.remote(part.at[block(p, 1 - core)], core_in.at[k], place.core_id)
        for k, p in enumerate(place.pairs)
    ]
    diag = links.remote(sums.at[0], y_in.at[0], place.y_id)
    to_y = links.remote(sums.at[1], y_in.at[1], place.y_id)
    to_z = links.remote(sums.at[2], z_in, place.low_id)

    def term(k, i):
        start = (place.pairs[k] * 2 + core) * rows + i * CHUNK
        at = tile(i * CHUNK, CHUNK)
        return part[tile(start, CHUNK), :].astype(F32) + core_in[k, at, :].astype(F32)

    def add(k, extra):
        def step(i, carry):
            at = tile(i * CHUNK, CHUNK)
            total = term(k, i)
            if extra is not None:
                total = total + extra[at, :].astype(F32)
            sums[k, at, :] = total.astype(BF16)
            return carry

        lax.fori_loop(0, rows // CHUNK, step, 0)

    work(place.pairs[0])
    across[0].start()
    work(place.pairs[1])
    across[1].start()
    across[0].wait_recv()
    add(0, None)
    diag.start()
    before()
    work(place.pairs[2])
    across[2].start()
    across[1].wait_recv()
    add(1, None)
    to_y.start()
    work(place.pairs[3])
    across[3].start()
    across[2].wait_recv()
    pump()
    diag.wait_recv()
    add(2, y_in.at[0])
    to_z.start()
    across[3].wait_recv()
    pump()
    to_y.wait_recv()
    to_z.wait_recv()

    def last(i, carry):
        at = tile(i * CHUNK, CHUNK)
        total = term(3, i) + y_in[1, at, :].astype(F32) + z_in[at, :].astype(F32)
        finish(at, total)
        return carry

    lax.fori_loop(0, rows // CHUNK, last, 0)
    for one in (*across, diag, to_y, to_z):
        one.wait_send()


class Gather:
    def __init__(self, links, place, own, land, save):
        rows = own.shape[1]
        self.place, self.own, self.land, self.rows = place, own, land, rows
        spread = place.spread

        def at(dp):
            return land.at[tile(dp * rows, rows)]

        mine = at(place.dp)
        self.out = [
            links.remote(own.at[lax.rem(place.low + k, 2)], mine, place.z_id(k)) for k in range(1, 4)
        ]
        self.side = [links.remote(own.at[place.low], mine, place.r_id(s)) for s in range(1, spread)]
        self.on = [
            [
                links.remote(at(place.z_dp(-k)), at(place.z_dp(-k)), place.r_id(s))
                for s in range(1, spread)
            ]
            for k in range(1, 4)
        ]
        self.save = None if save is None else links.copy(land, save)

    def start(self):
        for one in self.out + self.side:
            one.start()
        step = 32 if self.rows % 32 == 0 else self.rows

        def copy(i, carry):
            self.land[tile(self.place.dp * self.rows + i * step, step), :] = self.own[
                self.place.low, tile(i * step, step), :
            ]
            return carry

        lax.fori_loop(0, self.rows // step, copy, 0)

    def forward(self, k):
        self.out[k].wait_recv()
        for one in self.on[k]:
            one.start()

    def finish(self):
        for one in self.side:
            one.wait_recv()
        for group in self.on:
            for one in group:
                one.wait_recv()
        if self.save is not None:
            self.save.start()

    def drain(self):
        for one in self.out + self.side:
            one.wait_send()
        for group in self.on:
            for one in group:
                one.wait_send()
        if self.save is not None:
            self.save.wait()


class Pump:
    def __init__(self):
        self.steps = []

    def add(self, *steps):
        self.steps += steps

    def __call__(self, count=1):
        for _ in range(count):
            if self.steps:
                self.steps.pop(0)()

    def rest(self):
        while self.steps:
            self()


def forwards(*gathers):
    return [partial(one.forward, k) for one in gathers for k in range(3)]


def scale_of(v):
    return lax.rsqrt(jnp.mean(v * v, axis=-1, keepdims=True) + EPSILON)


def mm(a, b):
    return jnp.dot(a, b, preferred_element_type=F32)


def mm_nt(a, b):
    return lax.dot_general(a, b, (((1,), (1,)), ((), ())), preferred_element_type=F32)


def project_heads(ns, pair):
    span = ns.joined.shape[0] // 4
    rows = tile(pair * span, span)
    raw = mm(ns.joined[rows, :], ns.wqkv[...])
    ns.raw[rows, :] = raw
    cosine, sine = ns.cosine[rows, :], ns.sine[rows, :]
    q_size, kv_size = ns.q.shape[1], ns.k.shape[1]

    def heads(out, start, size, gain):
        for h in range(size // HD):
            v = raw[:, start + h * HD : start + (h + 1) * HD]
            v = v * scale_of(v) * gain[...]
            turned = v * cosine + pltpu.roll(v, HD // 2, axis=1) * sine
            out[rows, h * HD : (h + 1) * HD] = turned.astype(BF16)

    heads(ns.q, 0, q_size, ns.gain_q)
    heads(ns.k, q_size, kv_size, ns.gain_k)
    ns.v[rows, :] = raw[:, q_size + kv_size :].astype(BF16)


def attend(ns):
    group = ns.bias.shape[1]
    span = ns.joined.shape[0] // 4
    q_heads = ns.q.shape[1] // HD
    share = q_heads // (ns.k.shape[1] // HD)
    scale = HD**-0.5

    def one_group(b, carry):
        for e in range(q_heads):
            kv = slice((e // share) * HD, (e // share + 1) * HD)
            for half in range(group // span):
                rows = tile(b * group + half * span, span)
                seen = (half + 1) * span
                keys = ns.k[tile(b * group, group), kv][:seen]
                values = ns.v[tile(b * group, group), kv][:seen]
                s = mm_nt(ns.q[rows, e * HD : (e + 1) * HD], keys) * scale
                s = s + ns.bias[b, half * span : (half + 1) * span, :seen].astype(F32)
                p = jnp.exp(s - jnp.max(s, axis=-1, keepdims=True))
                p = p / jnp.sum(p, axis=-1, keepdims=True)
                ns.att[rows, e * HD : (e + 1) * HD] = mm(p.astype(BF16), values).astype(BF16)
        return carry

    lax.fori_loop(0, 2, one_group, 0)


def project_out(ns, source, weight, pair, width=512):
    span = ns.part.shape[0] // 4
    rows = tile(pair * span, span)

    def step(j, carry):
        at = tile(j * width, width)
        ns.part[rows, at] = mm_nt(source[rows, :], weight[at, :]).astype(BF16)
        return carry

    lax.fori_loop(0, ns.part.shape[1] // width, step, 0)


def gate_up(ns, pair, slot, width=256):
    span = ns.joined.shape[0] // 4
    rows = tile(pair * span, span)
    ff = ns.product.shape[1]

    def step(j, carry):
        here, there = tile(j * width, width), tile(ff + j * width, width)
        x = ns.joined[rows, :]
        gate = mm(x, ns.wgu[:, here])
        up = mm(x, ns.wgu[:, there])
        ns.gu_stage[slot, :, here] = gate.astype(BF16)
        ns.gu_stage[slot, :, there] = up.astype(BF16)
        ns.product[rows, here] = (gate / (1.0 + jnp.exp(-gate)) * up).astype(BF16)
        return carry

    lax.fori_loop(0, ff // width, step, 0)


def forward_layer_kernel(first, last, spread, ns):
    place = Place(spread)
    links = Links(ns.send, ns.recv)
    pump = Pump()
    local = ns.hidden.shape[0]
    own_rows = (place.own_pair * 2 + place.core) * local
    span = 2 * local

    if first:
        get_qkv = Gather(links, place, ns.own_qkv, ns.wqkv, ns.save_wqkv)
        get_o = Gather(links, place, ns.own_o, ns.wo, ns.save_wo)
    get_gu = Gather(links, place, ns.own_gu, ns.wgu, ns.save_wgu)
    get_down = Gather(links, place, ns.own_down, ns.wdown, ns.save_wdown)
    if not last:
        next_qkv = Gather(links, place, ns.own_next_qkv, ns.wnext_qkv, ns.save_wnext_qkv)
        next_o = Gather(links, place, ns.own_next_o, ns.wnext_o, ns.save_wnext_o)

    if first:
        def norm(i, carry):
            v = ns.hidden[tile(i * CHUNK, CHUNK), :].astype(F32)
            ns.joined[tile(own_rows + i * CHUNK, CHUNK), :] = (v * scale_of(v) * ns.gain_attn[...]).astype(BF16)
            return carry

        lax.fori_loop(0, local // CHUNK, norm, 0)
    else:
        loads = [
            links.copy(ns.joined_in, ns.joined),
            links.copy(ns.wqkv_in, ns.wqkv),
            links.copy(ns.wo_in, ns.wo),
        ]
        for one in loads:
            one.start()
    place.greet()
    if first:
        get_qkv.start()
        gathered = Spread(links, place, ns.joined)
        gathered.start()
        get_o.start()
        for step in forwards(get_qkv, get_o):
            step()
        get_gu.start()
        get_down.start()
        get_qkv.finish()
        get_o.finish()
        consume(gathered, place, partial(project_heads, ns))
        save_a = links.copy(ns.joined, ns.save_a)
        save_a.start()
    else:
        get_gu.start()
        get_down.start()
        for one in loads:
            one.wait()

        def every(i, carry):
            project_heads(ns, i)
            return carry

        lax.fori_loop(0, 4, every, 0)

    pump.add(*forwards(get_gu, get_down))
    attend(ns)
    pump()

    def middle(at, total):
        v = ns.hidden[at, :].astype(F32) + total
        ns.mid[at, :] = v
        ns.joined[tile(own_rows + at.start, CHUNK), :] = (v * scale_of(v) * ns.gain_mlp[...]).astype(BF16)

    def before_middle():
        if first:
            save_a.wait()

    collect(
        links, place, ns, partial(project_out, ns, ns.att, ns.wo), middle, before_middle, pump
    )
    gathered = Spread(links, place, ns.joined)
    gathered.start()
    pump.rest()
    get_gu.finish()
    get_down.finish()
    if last:
        def put(i, carry):
            at = tile(i * CHUNK, CHUNK)
            ns.joined_grad[tile(own_rows + i * CHUNK, CHUNK), :] = ns.cotangent[at, :]
            return carry

        lax.fori_loop(0, local // CHUNK, put, 0)
        spread_grad = Spread(links, place, ns.joined_grad)
    else:
        next_qkv.start()
        next_o.start()
        pump.add(*forwards(next_qkv, next_o))

    saves = []

    def gate_up_pair(pair):
        slot = len(saves) % 2
        if len(saves) >= 2:
            saves[-2].wait()
        gate_up(ns, pair, slot)
        save = links.copy(ns.gu_stage.at[slot], ns.save_gateup.at[tile(pair * span, span)])
        save.start()
        saves.append(save)

    consume(gathered, place, gate_up_pair)
    save_b = links.copy(ns.joined, ns.save_b)
    save_b.start()
    if last:
        spread_grad.start()

    def result(at, total):
        v = ns.mid[at, :] + total
        ns.out[at, :] = v
        if not last:
            ns.joined[tile(own_rows + at.start, CHUNK), :] = (v * scale_of(v) * ns.gain_next[...]).astype(BF16)

    if last:
        pump.add(spread_grad.pass_z, spread_grad.pass_y)
    collect(
        links, place, ns, partial(project_out, ns, ns.product, ns.wdown), result, save_b.wait, pump
    )
    pump.rest()
    if last:
        spread_grad.own_ready()
        spread_grad.z_ready()
        spread_grad.y_ready()
        spread_grad.pass_d()
        spread_grad.d_ready()
        spread_grad.drain()
        final = links.copy(ns.joined_grad, ns.save_next)
    else:
        gathered = Spread(links, place, ns.joined)
        gathered.start()
        next_qkv.finish()
        next_o.finish()
        gathered.own_ready()
        gathered.pass_z()
        gathered.pass_y()
        gathered.z_ready()
        gathered.y_ready()
        gathered.pass_d()
        gathered.d_ready()
        gathered.drain()
        final = links.copy(ns.joined, ns.save_next)
    final.start()
    for save in saves[-2:]:
        save.wait()
    if first:
        get_qkv.drain()
        get_o.drain()
    get_gu.drain()
    get_down.drain()
    if not last:
        next_qkv.drain()
        next_o.drain()
    final.wait()
    assert links.count <= ns.send.shape[0]


def call(kernel, ins, outs, scratch, collective_id, name):
    names = [*ins, *outs, *scratch]

    def run(*refs):
        kernel(SimpleNamespace(**dict(zip(names, refs))))

    def space(in_vmem):
        return pl.BlockSpec(memory_space=pltpu.VMEM if in_vmem else pl.ANY)

    results = pl.pallas_call(
        run,
        out_shape=[jax.ShapeDtypeStruct(shape, dtype) for shape, dtype, _ in outs.values()],
        in_specs=[space(v) for _, v in ins.values()],
        out_specs=[space(v) for _, _, v in outs.values()],
        scratch_shapes=list(scratch.values()),
        compiler_params=pltpu.CompilerParams(
            collective_id=collective_id, has_side_effects=True, vmem_limit_bytes=VMEM_LIMIT
        ),
        cost_estimate=pl.CostEstimate(
            flops=13 * 10**9, bytes_accessed=10**8, transcendentals=10**6
        ),
        name=name,
    )(*[array for array, _ in ins.values()])
    return dict(zip(outs, results))


def exchange_scratch(rows, width):
    return {
        "joined": pltpu.VMEM((8 * rows, width), BF16),
        "part": pltpu.VMEM((8 * rows, width), BF16),
        "core_in": pltpu.VMEM((4, rows, width), BF16),
        "y_in": pltpu.VMEM((2, rows, width), BF16),
        "z_in": pltpu.VMEM((rows, width), BF16),
        "sums": pltpu.VMEM((3, rows, width), BF16),
    }


def forward_layer(layer, hidden, carry, pieces, next_pieces, tables, gains, cotangent, spread):
    rows, width = hidden.shape
    own_qkv, own_o, own_gu, own_down = pieces
    first, last = layer == 0, next_pieces is None
    total = 8 * rows
    d_rows = own_gu.shape[1] * 4 * spread
    qkv, o, gu, ff = own_qkv.shape[2], own_o.shape[2], own_gu.shape[2], own_down.shape[2]
    kv = (qkv - o) // 2
    cosine, sine, bias = tables

    def row(start, size):
        return gains[:, start : start + size]

    ins = {"hidden": (hidden, True)}
    if first:
        ins["gain_attn"] = (row(0, width)[layer : layer + 1], True)
        ins["own_qkv"] = (own_qkv, True)
        ins["own_o"] = (own_o, True)
    else:
        ins["joined_in"] = (carry[0], False)
        ins["wqkv_in"] = (carry[1], False)
        ins["wo_in"] = (carry[2], False)
    ins["own_gu"] = (own_gu, True)
    ins["own_down"] = (own_down, True)
    if last:
        ins["cotangent"] = (cotangent, True)
    else:
        ins["own_next_qkv"] = (next_pieces[0], True)
        ins["own_next_o"] = (next_pieces[1], True)
        ins["gain_next"] = (row(0, width)[layer + 1 : layer + 2], True)
    ins["gain_mlp"] = (row(width, width)[layer : layer + 1], True)
    ins["gain_q"] = (row(2 * width, HD)[layer : layer + 1], True)
    ins["gain_k"] = (row(2 * width + HD, HD)[layer : layer + 1], True)
    ins["cosine"], ins["sine"], ins["bias"] = (cosine, True), (sine, True), (bias, True)
    outs = {
        "out": ((rows, width), F32, True),
        "mid": ((rows, width), F32, True),
        "raw": ((total, qkv), F32, True),
        "q": ((total, o), BF16, True),
        "k": ((total, kv), BF16, True),
        "v": ((total, kv), BF16, True),
        "att": ((total, o), BF16, True),
        "product": ((total, ff), BF16, True),
        "save_gateup": ((total, gu), BF16, False),
        "save_b": ((total, width), BF16, False),
        "save_next": ((total, width), BF16, False),
        "save_wgu": ((d_rows, gu), BF16, False),
        "save_wdown": ((d_rows, ff), BF16, False),
    }
    if first:
        outs["save_a"] = ((total, width), BF16, False)
        outs["save_wqkv"] = ((d_rows, qkv), BF16, False)
        outs["save_wo"] = ((d_rows, o), BF16, False)
    if not last:
        outs["save_wnext_qkv"] = ((d_rows, qkv), BF16, False)
        outs["save_wnext_o"] = ((d_rows, o), BF16, False)
    scratch = exchange_scratch(rows, width)
    scratch["gu_stage"] = pltpu.VMEM((2, 2 * rows, gu), BF16)
    scratch["wqkv"] = pltpu.VMEM((d_rows, qkv), BF16)
    scratch["wo"] = pltpu.VMEM((d_rows, o), BF16)
    scratch["wgu"] = pltpu.VMEM((d_rows, gu), BF16)
    scratch["wdown"] = pltpu.VMEM((d_rows, ff), BF16)
    if not last:
        scratch["wnext_qkv"] = pltpu.VMEM((d_rows, qkv), BF16)
        scratch["wnext_o"] = pltpu.VMEM((d_rows, o), BF16)
    else:
        scratch["joined_grad"] = pltpu.VMEM((total, width), BF16)
    count = 64 + 32 * spread
    scratch["send"] = pltpu.SemaphoreType.DMA((count,))
    scratch["recv"] = pltpu.SemaphoreType.DMA((count,))
    kernel = partial(forward_layer_kernel, first, last, spread)
    return call(kernel, ins, outs, scratch, 1 + int(last) + 2 * int(not first), "forward_layer")


def mm_tn(a, b):
    return lax.dot_general(a, b, (((0,), (0,)), ((), ())), preferred_element_type=F32)


class Reduce:
    def __init__(self, links, place, blocks, x_in, z_in, out):
        self.place, self.blocks, self.x_in, self.z_in, self.out = place, blocks, x_in, z_in, out
        spread = place.spread
        rows = out.shape[1]
        self.rows = rows

        def block(q, r):
            return blocks.at[q, tile(r * rows, rows)]

        self.x_out = [
            [
                links.remote(
                    block(q, lax.rem(place.r + s, spread)), x_in.at[s - 1, q], place.r_id(s)
                )
                for s in range(1, spread)
            ]
            for q in range(4)
        ]
        self.z_out = [
            links.remote(block(q, place.r), z_in.at[q - 1], place.z_id(q)) for q in range(1, 4)
        ]

    def compute(self, q, left, right):
        part = self.blocks.shape[1]
        step = min(256, part)
        start = lax.rem(self.place.z + q, 4) * part

        def one(i, carry):
            product = mm_tn(left[:, tile(start + i * step, step)], right())
            self.blocks[q, tile(i * step, step), :] = product.astype(BF16)
            return carry

        lax.fori_loop(0, part // step, one, 0)
        for one_copy in self.x_out[q]:
            one_copy.start()

    def pass_on(self, q):
        for one in self.x_out[q]:
            one.wait_recv()
        step = min(64, self.rows)
        start = self.place.r * self.rows

        def add(i, carry):
            at = tile(start + i * step, step)
            total = self.blocks[q, at, :].astype(F32)
            for s in range(self.place.spread - 1):
                total = total + self.x_in[s, q, tile(i * step, step), :].astype(F32)
            self.blocks[q, at, :] = total.astype(BF16)
            return carry

        lax.fori_loop(0, self.rows // step, add, 0)
        if q:
            self.z_out[q - 1].start()

    def finish(self):
        for one in self.z_out:
            one.wait_recv()
        step = min(64, self.rows)
        low = self.place.low
        start = self.place.r * self.rows

        def add(i, carry):
            at = tile(i * step, step)
            near = self.blocks[0, tile(start + i * step, step), :].astype(F32)
            self.out[low, at, :] = (near + self.z_in[1, at, :].astype(F32)).astype(BF16)
            far = self.z_in[0, at, :].astype(F32) + self.z_in[2, at, :].astype(F32)
            self.out[1 - low, at, :] = far.astype(BF16)
            return carry

        lax.fori_loop(0, self.rows // step, add, 0)

    def drain(self):
        for group in self.x_out:
            for one in group:
                one.wait_send()
        for one in self.z_out:
            one.wait_send()


ORDER = (2, 1, 3, 0)


def gate_up_back(ns, pair, slot, width=256):
    span = ns.joined.shape[0] // 4
    rows = tile(pair * span, span)
    ff = ns.product.shape[1]

    def step(j, carry):
        here, there = tile(j * width, width), tile(ff + j * width, width)
        d_act = mm(ns.joined[rows, :], ns.wdown[:, here])
        gate = ns.stage[slot, :, here].astype(F32)
        up = ns.stage[slot, :, there].astype(F32)
        gated = 1.0 / (1.0 + jnp.exp(-gate))
        ns.d_gateup[rows, here] = (d_act * up * gated * (1.0 + gate * (1.0 - gated))).astype(BF16)
        ns.d_gateup[rows, there] = (d_act * gate * gated).astype(BF16)
        return carry

    lax.fori_loop(0, ff // width, step, 0)


def head_back(ns, rows, d_out, raw, gain, d_gain, d_raw_columns):
    d_turned = d_out * ns.cosine[rows, :] + pltpu.roll(d_out * ns.sine[rows, :], HD // 2, axis=1)
    scale = scale_of(raw)
    normed = raw * scale
    d_gain[...] += jnp.sum(d_turned * normed, axis=0, keepdims=True)
    d_normed = d_turned * gain[...]
    inner = jnp.mean(d_normed * normed, axis=-1, keepdims=True)
    ns.d_raw[rows, d_raw_columns] = (scale * (d_normed - normed * inner)).astype(BF16)


def attend_back(ns):
    group = ns.bias.shape[1]
    span = ns.joined.shape[0] // 4
    q_size, kv_size = ns.q.shape[1], ns.k.shape[1]
    share = q_size // kv_size
    scale = HD**-0.5

    def one_group(b, carry):
        whole = tile(b * group, group)
        for kv in range(kv_size // HD):
            columns = slice(kv * HD, (kv + 1) * HD)
            ns.d_keys[...] = jnp.zeros_like(ns.d_keys)
            ns.d_values[...] = jnp.zeros_like(ns.d_values)
            for e in range(kv * share, (kv + 1) * share):
                mine = slice(e * HD, (e + 1) * HD)
                for half in range(group // span):
                    rows = tile(b * group + half * span, span)
                    seen = (half + 1) * span
                    keys = ns.k[whole, columns][:seen]
                    values = ns.v[whole, columns][:seen]
                    query = ns.q[rows, mine]
                    d_out = ns.d_att[rows, mine]
                    s = mm_nt(query, keys) * scale
                    s = s + ns.bias[b, half * span : (half + 1) * span, :seen].astype(F32)
                    p = jnp.exp(s - jnp.max(s, axis=-1, keepdims=True))
                    p = p / jnp.sum(p, axis=-1, keepdims=True)
                    d_p = mm_nt(d_out, values)
                    delta = jnp.sum(d_p * p, axis=-1, keepdims=True)
                    d_s = (p * (d_p - delta)).astype(BF16)
                    ns.d_values[:seen, :] += mm_tn(p.astype(BF16), d_out)
                    ns.d_keys[:seen, :] += mm_tn(d_s, query)
                    d_query = mm(d_s, keys) * scale
                    head_back(ns, rows, d_query, ns.raw[rows, mine], ns.gain_q, ns.d_gain_q, mine)
            key_columns = slice(q_size + kv * HD, q_size + (kv + 1) * HD)
            d_keys = ns.d_keys[...] * scale
            head_back(ns, whole, d_keys, ns.raw[whole, key_columns], ns.gain_k, ns.d_gain_k, key_columns)
            value_columns = slice(q_size + kv_size + kv * HD, q_size + kv_size + (kv + 1) * HD)
            ns.d_raw[whole, value_columns] = ns.d_values[...].astype(BF16)
        return carry

    lax.fori_loop(0, 2, one_group, 0)


def backward_layer_kernel(first, spread, ns):
    place = Place(spread)
    links = Links(ns.send, ns.recv)
    pump = Pump()
    local = ns.grad.shape[0]
    own_rows = (place.own_pair * 2 + place.core) * local
    span = 2 * local
    width = ns.grad.shape[1]
    qkv, o, ff = ns.wqkv_in.shape[1], ns.wo_in.shape[1], ns.wdown_in.shape[1]

    def loads(*pairs):
        copies = [links.copy(src, dst) for src, dst in pairs]
        for one in copies:
            one.start()
        return copies

    def wait(copies):
        for one in copies:
            one.wait()

    red_down = Reduce(links, place, ns.blocks.at[0], ns.x_in.at[0], ns.z_in_w.at[0], ns.g_down)
    red_gate = Reduce(links, place, ns.blocks.at[1], ns.x_in.at[1], ns.z_in_w.at[1], ns.g_gate)
    red_up = Reduce(links, place, ns.blocks.at[0], ns.x_in.at[2], ns.z_in_w.at[2], ns.g_up)
    red_o = Reduce(links, place, ns.blocks_o, ns.x_in_o, ns.z_in_o, ns.g_o)
    red_qkv = Reduce(links, place, ns.blocks_qkv, ns.x_in_qkv, ns.z_in_qkv, ns.g_qkv)
    gathered = Spread(links, place, ns.joined)

    def back_norm(value, grad, gain, d_gain, out, gather):
        def finish(at, total):
            v = value[at, :].astype(F32)
            scale = scale_of(v)
            normed = v * scale
            d_gain[...] += jnp.sum(total * normed, axis=0, keepdims=True)
            d_normed = total * gain[...]
            inner = jnp.mean(d_normed * normed, axis=-1, keepdims=True)
            g = grad[at, :].astype(F32) + scale * (d_normed - normed * inner)
            out[at, :] = g
            if gather:
                ns.joined[tile(own_rows + at.start, CHUNK), :] = g.astype(BF16)

        return finish

    for one in (ns.d_gain_attn, ns.d_gain_mlp, ns.d_gain_q, ns.d_gain_k):
        one[...] = jnp.zeros_like(one)

    def mlp_scope(wgu, wdown, b, d_gateup, product, stage):
        ns.wdown, ns.d_gateup, ns.product, ns.stage = wdown, d_gateup, product, stage
        first_loads = loads((ns.joined_in, ns.joined), (ns.product_in, product))
        down_load = loads((ns.wdown_in, wdown))
        gateup_loads = [
            links.copy(ns.gateup_in.at[tile(p * span, span)], stage.at[i % 2]) for i, p in enumerate(place.pairs)
        ]
        for one in gateup_loads[:2]:
            one.start()
        up_load = loads((ns.wgu_in, wgu))
        b_load = loads((ns.b_in, b))
        place.greet()
        wait(first_loads)
        for q in ORDER:
            red_down.compute(q, ns.joined, lambda: product[...])
        wait(down_load)
        for i, pair in enumerate(place.pairs):
            gateup_loads[i].wait()
            gate_up_back(ns, pair, i % 2)
            if i + 2 < 4:
                gateup_loads[i + 2].start()
        wait(up_load)
        wait(b_load)
        gate = lambda: d_gateup[:, :ff]
        up = lambda: d_gateup[:, ff:]

        def drain_down():
            red_down.finish()
            red_down.drain()

        pump.add(*[partial(red_gate.compute, q, b, gate) for q in ORDER])
        pump.add(*[partial(red_down.pass_on, q) for q in ORDER])
        pump.add(drain_down)
        pump.add(*[partial(red_up.compute, q, b, up) for q in ORDER])
        pump.add(*[partial(red_gate.pass_on, q) for q in ORDER])

        collect(
            links, place, ns, partial(project_out, ns, d_gateup, wgu),
            back_norm(ns.mid, ns.grad, ns.gain_mlp, ns.d_gain_mlp, ns.grad_mid, True),
            lambda: None, lambda: pump(5),
        )
        gathered.start()
        pump.rest()

    rows_all = ns.wgu_in.shape[0]
    total = 8 * local
    pl.run_scoped(
        mlp_scope,
        pltpu.VMEM((rows_all, 2 * ff), BF16),
        pltpu.VMEM((rows_all, ff), BF16),
        pltpu.VMEM((total, width), BF16),
        pltpu.VMEM((total, 2 * ff), BF16),
        pltpu.VMEM((total, ff), BF16),
        pltpu.VMEM((2, span, 2 * ff), BF16),
    )

    def attention_scope(
        cosine, sine, bias, hidden, wqkv, wo, a, q, k, v, raw, att, d_att, d_raw, d_keys, d_values
    ):
        ns.cosine, ns.sine, ns.bias, ns.hidden = cosine, sine, bias, hidden
        ns.wqkv, ns.wo, ns.q, ns.k, ns.v, ns.raw, ns.att = wqkv, wo, q, k, v, raw, att
        ns.d_att, ns.d_raw, ns.d_keys, ns.d_values = d_att, d_raw, d_keys, d_values
        wait_for = loads(
            (ns.wo_in, wo), (ns.att_in, att), (ns.q_in, q), (ns.k_in, k), (ns.v_in, v), (ns.raw_in, raw),
            (ns.wqkv_in, wqkv), (ns.a_in, a), (ns.cosine_in, cosine), (ns.sine_in, sine), (ns.bias_in, bias),
            (ns.hidden_in, hidden),
        )
        wait(wait_for)

        def d_attended(pair):
            rows = tile(pair * span, span)
            d_att[rows, :] = mm(ns.joined[rows, :], wo[...]).astype(BF16)

        consume(gathered, place, d_attended)
        for q_part in ORDER:
            red_o.compute(q_part, ns.joined, lambda: att[...])
        attend_back(ns)
        for q_part in ORDER:
            red_qkv.compute(q_part, a, lambda: d_raw[...])
        pump.add(*[partial(red_up.pass_on, q) for q in ORDER])
        pump.add(*[partial(red_o.pass_on, q) for q in ORDER])
        pump.add(*[partial(red_qkv.pass_on, q) for q in ORDER])
        collect(
            links, place, ns, partial(project_out, ns, d_raw, wqkv),
            back_norm(hidden, ns.grad_mid, ns.gain_attn, ns.d_gain_attn, ns.out, not first),
            lambda: None, lambda: pump(4),
        )

    pl.run_scoped(
        attention_scope,
        pltpu.VMEM(ns.cosine_in.shape, F32),
        pltpu.VMEM(ns.sine_in.shape, F32),
        pltpu.VMEM(ns.bias_in.shape, BF16),
        pltpu.VMEM(ns.hidden_in.shape, ns.hidden_in.dtype),
        pltpu.VMEM((rows_all, qkv), BF16),
        pltpu.VMEM((rows_all, o), BF16),
        pltpu.VMEM((total, width), BF16),
        pltpu.VMEM(ns.q_in.shape, BF16),
        pltpu.VMEM(ns.k_in.shape, BF16),
        pltpu.VMEM(ns.v_in.shape, BF16),
        pltpu.VMEM(ns.raw_in.shape, F32),
        pltpu.VMEM(ns.att_in.shape, BF16),
        pltpu.VMEM((total, o), BF16),
        pltpu.VMEM((total, qkv), BF16),
        pltpu.VMEM((ns.bias_in.shape[1], HD), F32),
        pltpu.VMEM((ns.bias_in.shape[1], HD), F32),
    )
    if not first:
        gathered = Spread(links, place, ns.joined)
        gathered.start()
        pump(2)
        gathered.own_ready()
        gathered.pass_z()
        gathered.pass_y()
        gathered.z_ready()
        gathered.y_ready()
        gathered.pass_d()
        gathered.d_ready()
        gathered.drain()
        final = links.copy(ns.joined, ns.save_next)
        final.start()
    pump.rest()
    for one in (red_gate, red_up, red_o, red_qkv):
        one.finish()
        one.drain()
    if not first:
        final.wait()
    assert links.count <= ns.send.shape[0]


def backward_layer(layer, grad, grad_rows, kept, tables, gains, spread):
    rows, width = grad.shape
    first = layer == 0
    total = 8 * rows
    cosine, sine, bias = tables
    d_rows, ff = kept["save_wdown"].shape
    o, qkv = kept["wo"].shape[1], kept["wqkv"].shape[1]
    part = d_rows // 4
    block = part // spread

    def row(start, size):
        return gains[layer : layer + 1, start : start + size]

    ins = {
        "grad": (grad, True),
        "joined_in": (grad_rows, False),
        "mid": (kept["mid"], True),
        "hidden_in": (kept["hidden"], False),
        "product_in": (kept["product"], False),
        "gateup_in": (kept["save_gateup"], False),
        "b_in": (kept["save_b"], False),
        "a_in": (kept["a"], False),
        "wdown_in": (kept["save_wdown"], False),
        "wgu_in": (kept["save_wgu"], False),
        "wqkv_in": (kept["wqkv"], False),
        "wo_in": (kept["wo"], False),
        "q_in": (kept["q"], False),
        "k_in": (kept["k"], False),
        "v_in": (kept["v"], False),
        "raw_in": (kept["raw"], False),
        "att_in": (kept["att"], False),
        "gain_attn": (row(0, width), True),
        "gain_mlp": (row(width, width), True),
        "gain_q": (row(2 * width, HD), True),
        "gain_k": (row(2 * width + HD, HD), True),
        "cosine_in": (cosine, False),
        "sine_in": (sine, False),
        "bias_in": (bias, False),
    }
    outs = {
        "out": ((rows, width), F32, True),
        "d_gain_attn": ((1, width), F32, True),
        "d_gain_mlp": ((1, width), F32, True),
        "d_gain_q": ((1, HD), F32, True),
        "d_gain_k": ((1, HD), F32, True),
        "g_down": ((2, block, ff), BF16, True),
        "g_gate": ((2, block, ff), BF16, True),
        "g_up": ((2, block, ff), BF16, True),
        "g_o": ((2, block, o), BF16, True),
        "g_qkv": ((2, block, qkv), BF16, True),
    }
    if not first:
        outs["save_next"] = ((total, width), BF16, False)
    scratch = exchange_scratch(rows, width)
    side = spread - 1
    scratch["grad_mid"] = pltpu.VMEM((rows, width), F32)
    scratch["blocks"] = pltpu.VMEM((2, 4, part, ff), BF16)
    scratch["blocks_o"] = pltpu.VMEM((4, part, o), BF16)
    scratch["blocks_qkv"] = pltpu.VMEM((4, part, qkv), BF16)
    scratch["x_in"] = pltpu.VMEM((3, side, 4, block, ff), BF16)
    scratch["x_in_o"] = pltpu.VMEM((side, 4, block, o), BF16)
    scratch["x_in_qkv"] = pltpu.VMEM((side, 4, block, qkv), BF16)
    scratch["z_in_w"] = pltpu.VMEM((3, 3, block, ff), BF16)
    scratch["z_in_o"] = pltpu.VMEM((3, block, o), BF16)
    scratch["z_in_qkv"] = pltpu.VMEM((3, block, qkv), BF16)
    count = 96 + 24 * spread
    scratch["send"] = pltpu.SemaphoreType.DMA((count,))
    scratch["recv"] = pltpu.SemaphoreType.DMA((count,))
    kernel = partial(backward_layer_kernel, first, spread)
    return call(kernel, ins, outs, scratch, 6 if first else 5, "backward_layer")


def places(dp_size):
    spread = dp_size // 4
    me = lax.axis_index("dp")
    z = me // spread
    return spread, me, lax.rem(me, spread), lax.rem(z, 2), z // 2


def flip_lo(dp_size):
    spread = dp_size // 4
    return [(i, i + spread * (1 - 2 * ((i // spread) % 2))) for i in range(dp_size)]


def flip_hi(dp_size):
    spread = dp_size // 4
    return [(i, i + 2 * spread * (1 - 2 * (i // (2 * spread)))) for i in range(dp_size)]


def shift_r(dp_size, step):
    spread = dp_size // 4
    return [(i, (i // spread) * spread + (i % spread + step) % spread) for i in range(dp_size)]


def halves(weight):
    weight = weight.astype(BF16)
    half = weight.shape[-1] // 2
    return weight[..., :half], weight[..., half:]


def rope_tables(positions, head_size):
    half = head_size // 2
    frequency = jnp.power(THETA, -2.0 * jnp.arange(half, dtype=F32) / head_size)
    angle = positions.astype(F32)[:, None] * frequency[None, :]
    return (jnp.cos(angle)[:, None, :], jnp.sin(angle)[:, None, :])


def adamw(weight, first, second, grad, rate, decay):
    first_new = BETA_ONE * first + (1.0 - BETA_ONE) * grad
    second_new = BETA_TWO * second + (1.0 - BETA_TWO) * grad * grad
    first_hat = first_new / (1.0 - BETA_ONE**STEP)
    second_hat = second_new / (1.0 - BETA_TWO**STEP)
    weight_new = weight - rate * (first_hat / (jnp.sqrt(second_hat) + ADAM_EPS) + decay * weight)
    return (first_new, second_new, weight_new)


def own_pieces(masters, layer):
    query_all, keyvalue_all, output_all, mlp_all = masters

    def both(*arrays):
        pairs = [halves(one) for one in arrays]
        return jnp.stack([jnp.concatenate([one[i] for one in pairs], axis=1) for i in range(2)])

    return (
        both(query_all[layer], keyvalue_all[layer, 0], keyvalue_all[layer, 1]),
        both(output_all[layer]),
        both(mlp_all[layer, 0], mlp_all[layer, 1]),
        both(mlp_all[layer, 2]),
    )


def body(
    tokens, cotangent, segment_ids, gains, gain_first, gain_second,
    query_weight, query_first, query_second,
    keyvalue_weight, keyvalue_first, keyvalue_second,
    output_weight, output_first, output_second,
    mlp_weight, mlp_first, mlp_second,
):
    dp_size = lax.axis_size("dp")
    spread, me, r, low, high = places(dp_size)
    layers = gains.shape[0]
    local_rows, width = tokens.shape
    group = segment_ids.shape[0]
    rows = 8 * local_rows
    index = jnp.arange(group, dtype=jnp.int32)
    other = lax.ppermute(segment_ids, "dp", flip_lo(dp_size))
    segments = jnp.stack([jnp.where(low == 0, segment_ids, other), jnp.where(low == 0, other, segment_ids)])
    positions = (index[None, :] - (segments - segments[:, :1])).reshape(rows)
    mask = (segments[:, :, None] == segments[:, None, :]) & (index[None, None, :] <= index[None, :, None])
    bias = jnp.where(mask, 0.0, -1e30).astype(BF16)
    cosine, sine = rope_tables(positions, HD)
    tables = (
        jnp.concatenate([cosine[:, 0], cosine[:, 0]], axis=1),
        jnp.concatenate([-sine[:, 0], sine[:, 0]], axis=1),
        bias,
    )
    masters = (query_weight, keyvalue_weight, output_weight, mlp_weight)

    pieces = [own_pieces(masters, layer) for layer in range(layers)]
    hidden, carry = tokens, None
    saved = []
    for layer in range(layers):
        after = pieces[layer + 1] if layer + 1 < layers else None
        kept = forward_layer(layer, hidden, carry, pieces[layer], after, tables, gains, cotangent, spread)
        if layer == 0:
            carry = (kept["save_a"], kept["save_wqkv"], kept["save_wo"])
        kept["hidden"], kept["a"], kept["wqkv"], kept["wo"] = hidden, *carry
        saved.append(kept)
        hidden = kept["out"]
        if after is not None:
            carry = (kept["save_next"], kept["save_wnext_qkv"], kept["save_wnext_o"])

    block_output = hidden
    grad = cotangent
    grad_rows = saved[-1]["save_next"]
    reduced = [None] * layers
    gain_grads = [None] * layers
    for layer in reversed(range(layers)):
        kept = saved[layer]
        done = backward_layer(layer, grad, grad_rows, kept, tables, gains, spread)
        grad, grad_rows = done["out"], done.get("save_next")
        gain_grads[layer] = jnp.concatenate(
            [done[name] for name in ("d_gain_attn", "d_gain_mlp", "d_gain_q", "d_gain_k")], axis=1
        )[0]
        q_size = kept["wo"].shape[1]
        kv_size = (kept["wqkv"].shape[1] - q_size) // 2

        def columns(pair, start, size):
            return jnp.concatenate([one[:, start : start + size] for one in pair], axis=1).astype(F32)

        grad_qkv = done["g_qkv"]
        reduced[layer] = (
            columns(grad_qkv, 0, q_size),
            jnp.stack([columns(grad_qkv, q_size, kv_size), columns(grad_qkv, q_size + kv_size, kv_size)]),
            columns(done["g_o"], 0, q_size),
            jnp.stack([columns(done[name], 0, done[name].shape[2]) for name in ("g_gate", "g_up", "g_down")]),
        )
    stacked = [jnp.stack([entry[i] for entry in reduced]) for i in range(4)]
    gain_total = lax.psum(jnp.stack(gain_grads), ("dp", "tensor"))
    head_gain_grads = gain_total[:, 2 * width :]
    gain_new = adamw(gains, gain_first, gain_second, gain_total, GAIN_RATE, 0.0)
    query_new = adamw(query_weight, query_first, query_second, stacked[0], RATE, DECAY)
    keyvalue_new = adamw(keyvalue_weight, keyvalue_first, keyvalue_second, stacked[1], RATE, DECAY)
    output_new = adamw(output_weight, output_first, output_second, stacked[2], RATE * OUTPUT_FACTOR, DECAY)
    mlp_new = adamw(mlp_weight, mlp_first, mlp_second, stacked[3], RATE, DECAY)
    return (block_output, grad, *gain_new, head_gain_grads, *query_new, *keyvalue_new, *output_new, *mlp_new)


def solution(mesh):
    token = P(("dp", "tensor"), None)
    flat = P(None, "dp", "tensor")
    deep = P(None, None, "dp", "tensor")
    placed = (token, token, P("dp"), P(), P(), P(), *[flat] * 3, *[deep] * 3, *[flat] * 3, *[deep] * 3)
    outs = (token, token, P(), P(), P(), P(), *[flat] * 3, *[deep] * 3, *[flat] * 3, *[deep] * 3)
    return jax.shard_map(body, mesh=mesh, in_specs=placed, out_specs=outs, check_vma=False)
```

```python
from functools import partial
import math
from types import SimpleNamespace

import jax
import jax.numpy as jnp
from jax import lax
from jax.experimental import pallas as pl
from jax.experimental.pallas import tpu as pltpu
from jax.sharding import PartitionSpec as P

HD = 128
STEP = 10
EPSILON = 1e-06
THETA = 1000000.0
BETA_ONE = 0.9
BETA_TWO = 0.95
ADAM_EPS = 1e-08
DECAY = 0.1
RATE = 0.05
GAIN_RATE = 0.8
OUTPUT_FACTOR = math.sqrt(128)

BF16 = jnp.bfloat16
F32 = jnp.float32
MESH = pl.DeviceIdType.MESH
CHUNK = 32
VMEM_LIMIT = 60 * 1024 * 1024


class Place:
    def __init__(self, spread):
        self.spread = spread
        self.dp = lax.axis_index("dp")
        self.tensor = lax.axis_index("tensor")
        self.core = lax.rem(self.tensor, 2)
        self.y = self.tensor // 2
        self.z = self.dp // spread
        self.r = lax.rem(self.dp, spread)
        self.low = lax.rem(self.z, 2)
        self.core_id = {"dp": self.dp, "tensor": self.y * 2 + 1 - self.core}
        self.y_id = {"dp": self.dp, "tensor": (1 - self.y) * 2 + self.core}
        self.low_id = {"dp": self.dp + spread * (1 - 2 * self.low), "tensor": self.tensor}
        self.own_pair = self.low * 2 + self.y
        self.pairs = (
            (1 - self.low) * 2 + 1 - self.y,
            self.low * 2 + 1 - self.y,
            (1 - self.low) * 2 + self.y,
            self.own_pair,
        )

    def z_dp(self, step):
        return lax.rem(self.z + 4 + step, 4) * self.spread + self.r

    def z_id(self, step):
        return {"dp": self.z_dp(step), "tensor": self.tensor}

    def r_dp(self, step):
        return self.z * self.spread + lax.rem(self.r + self.spread + step, self.spread)

    def r_id(self, step):
        return {"dp": self.r_dp(step), "tensor": self.tensor}

    def greet(self):
        ids = [self.core_id, self.y_id]
        ids += [self.z_id(k) for k in range(1, 4)]
        ids += [self.r_id(k) for k in range(1, self.spread)]
        barrier = pltpu.get_barrier_semaphore()
        for one in ids:
            pl.semaphore_signal(barrier, inc=1, device_id=one, device_id_type=MESH)
        pl.semaphore_wait(barrier, len(ids))


class Links:
    def __init__(self, send, recv):
        self.send, self.recv, self.count = send, recv, 0
        self.local = []

    def remote(self, src, dst, to):
        slot = self.count
        self.count += 1
        return pltpu.make_async_remote_copy(
            src_ref=src, dst_ref=dst, send_sem=self.send.at[slot], recv_sem=self.recv.at[slot],
            device_id=to, device_id_type=MESH,
        )

    def copy(self, src, dst):
        slot = self.count
        self.count += 1
        return pltpu.make_async_copy(src, dst, self.send.at[slot])


def tile(start, size):
    return pl.ds(pl.multiple_of(start, size), size)


class Spread:
    def __init__(self, links, place, joined):
        rows = joined.shape[0] // 8

        def block(pair, core):
            return joined.at[tile((pair * 2 + core) * rows, rows)]

        c = place.core
        diag, y, z, own = place.pairs
        own, from_z, from_y, from_d = (block(p, c) for p in (own, z, y, diag))
        self.to_z = links.remote(own, own, place.low_id)
        self.to_y = links.remote(own, own, place.y_id)
        self.to_core = links.remote(own, own, place.core_id)
        self.on_y = links.remote(from_z, from_z, place.y_id)
        self.core_z = links.remote(from_z, from_z, place.core_id)
        self.core_y = links.remote(from_y, from_y, place.core_id)
        self.core_d = links.remote(from_d, from_d, place.core_id)

    def start(self):
        self.to_z.start()
        self.to_y.start()
        self.to_core.start()

    def own_ready(self):
        self.to_core.wait_recv()

    def pass_z(self):
        self.to_z.wait_recv()
        self.on_y.start()
        self.core_z.start()

    def pass_y(self):
        self.to_y.wait_recv()
        self.core_y.start()

    def z_ready(self):
        self.core_z.wait_recv()

    def y_ready(self):
        self.core_y.wait_recv()

    def pass_d(self):
        self.on_y.wait_recv()
        self.core_d.start()

    def d_ready(self):
        self.core_d.wait_recv()

    def drain(self):
        for one in (self.to_z, self.to_y, self.to_core, self.on_y, self.core_z, self.core_y, self.core_d):
            one.wait_send()


def collect(links, place, ns, work, finish, before=(), sent=(), late=()):
    part, core_in, y_in, z_in, sums = ns.part, ns.core_in, ns.y_in, ns.z_in, ns.sums
    rows = part.shape[0] // 8
    core = place.core

    def block(pair, c):
        return tile((pair * 2 + c) * rows, rows)

    across = [
        links.remote(part.at[block(p, 1 - core)], core_in.at[k], place.core_id)
        for k, p in enumerate(place.pairs)
    ]
    diag = links.remote(sums.at[0], y_in.at[0], place.y_id)
    to_y = links.remote(sums.at[1], y_in.at[1], place.y_id)
    to_z = links.remote(sums.at[2], z_in, place.low_id)

    def term(k, i):
        start = (place.pairs[k] * 2 + core) * rows + i * CHUNK
        at = tile(i * CHUNK, CHUNK)
        return part[tile(start, CHUNK), :].astype(F32) + core_in[k, at, :].astype(F32)

    def add(k, extra):
        def step(i, carry):
            at = tile(i * CHUNK, CHUNK)
            total = term(k, i)
            if extra is not None:
                total = total + extra[at, :].astype(F32)
            sums[k, at, :] = total.astype(BF16)
            return carry

        lax.fori_loop(0, rows // CHUNK, step, 0)

    work(place.pairs[0])
    across[0].start()
    work(place.pairs[1])
    across[1].start()
    across[0].wait_recv()
    add(0, None)
    diag.start()
    run(before)
    work(place.pairs[2])
    across[2].start()
    across[1].wait_recv()
    add(1, None)
    to_y.start()
    work(place.pairs[3])
    across[3].start()
    run(sent)
    across[2].wait_recv()
    diag.wait_recv()
    add(2, y_in.at[0])
    to_z.start()
    run(late)
    across[3].wait_recv()
    to_y.wait_recv()
    to_z.wait_recv()

    def last(i, carry):
        at = tile(i * CHUNK, CHUNK)
        total = term(3, i) + y_in[1, at, :].astype(F32) + z_in[at, :].astype(F32)
        finish(at, total)
        return carry

    lax.fori_loop(0, rows // CHUNK, last, 0)
    for one in (*across, diag, to_y, to_z):
        one.wait_send()


class Gather:
    def __init__(self, links, place, sources, own, stage, land, save):
        rows = own.shape[1]
        self.place, self.own, self.land, self.rows, self.stage = place, own, land, rows, stage
        self.starts, self.loads = [], []
        start = 0
        for one in sources:
            size = one.shape[1]
            self.starts.append((start, size // 2))
            self.loads.append(links.copy(one, stage.at[:, start : start + size]))
            start += size
        spread = place.spread

        def at(dp):
            return land.at[tile(dp * rows, rows)]

        mine = at(place.dp)
        self.out = [
            links.remote(own.at[lax.rem(place.low + k, 2)], mine, place.z_id(k)) for k in range(1, 4)
        ]
        self.side = [links.remote(own.at[place.low], mine, place.r_id(s)) for s in range(1, spread)]
        self.on = [
            [
                links.remote(at(place.z_dp(-k)), at(place.z_dp(-k)), place.r_id(s))
                for s in range(1, spread)
            ]
            for k in range(1, 4)
        ]
        self.save = links.copy(land, save)

    def load(self):
        for one in self.loads:
            one.start()

    def cast(self):
        for one in self.loads:
            one.wait()
        step = min(64, self.rows)

        def round_rows(i, carry):
            at = tile(i * step, step)
            for low in range(2):
                to = 0
                for start, half in self.starts:
                    piece = self.stage[at, start + low * half : start + (low + 1) * half]
                    self.own[low, at, to : to + half] = piece.astype(BF16)
                    to += half
            return carry

        lax.fori_loop(0, self.rows // step, round_rows, 0)

    def start(self):
        for one in self.out + self.side:
            one.start()
        step = min(64, self.rows)

        def copy(i, carry):
            self.land[tile(self.place.dp * self.rows + i * step, step), :] = self.own[
                self.place.low, tile(i * step, step), :
            ]
            return carry

        lax.fori_loop(0, self.rows // step, copy, 0)

    def forward(self):
        for k in range(3):
            self.out[k].wait_recv()
            for one in self.on[k]:
                one.start()

    def finish(self):
        for one in self.side:
            one.wait_recv()
        for group in self.on:
            for one in group:
                one.wait_recv()
        self.save.start()

    def drain(self):
        for one in self.out + self.side:
            one.wait_send()
        for group in self.on:
            for one in group:
                one.wait_send()
        self.save.wait()


class Weights:
    def __init__(self, gathers):
        self.gathers, self.at = gathers, 0
        for one in gathers[:2]:
            one.load()

    def next(self):
        if self.at < len(self.gathers):
            one = self.gathers[self.at]
            one.cast()
            if self.at + 2 < len(self.gathers):
                self.gathers[self.at + 2].load()
            one.start()
            self.at += 1


def run(steps):
    for one in steps:
        one()


def scale_of(v):
    return lax.rsqrt(jnp.mean(v * v, axis=-1, keepdims=True) + EPSILON)


def mm(a, b):
    return jnp.dot(a, b, preferred_element_type=F32)


def mm_nt(a, b):
    return lax.dot_general(a, b, (((1,), (1,)), ((), ())), preferred_element_type=F32)


def project_heads(ns, pair):
    span = ns.joined.shape[0] // 4
    rows = tile(pair * span, span)
    raw = mm(ns.joined[rows, :], ns.wqkv[...])
    ns.raw[rows, :] = raw
    cosine, sine = ns.cosine[rows, :], ns.sine[rows, :]
    q_size, kv_size = ns.q.shape[1], ns.k.shape[1]

    def heads(out, start, size, gain):
        for h in range(size // HD):
            v = raw[:, start + h * HD : start + (h + 1) * HD]
            v = v * scale_of(v) * gain[...]
            turned = v * cosine + pltpu.roll(v, HD // 2, axis=1) * sine
            out[rows, h * HD : (h + 1) * HD] = turned.astype(BF16)

    heads(ns.q, 0, q_size, ns.gain_q)
    heads(ns.k, q_size, kv_size, ns.gain_k)
    ns.v[rows, :] = raw[:, q_size + kv_size :].astype(BF16)


def attend(ns):
    group = ns.bias.shape[1]
    span = ns.joined.shape[0] // 4
    q_heads = ns.q.shape[1] // HD
    share = q_heads // (ns.k.shape[1] // HD)
    scale = HD**-0.5

    def one_group(b, carry):
        for e in range(q_heads):
            kv = slice((e // share) * HD, (e // share + 1) * HD)
            for half in range(group // span):
                rows = tile(b * group + half * span, span)
                seen = (half + 1) * span
                keys = ns.k[tile(b * group, group), kv][:seen]
                values = ns.v[tile(b * group, group), kv][:seen]
                s = mm_nt(ns.q[rows, e * HD : (e + 1) * HD], keys) * scale
                s = s + ns.bias[b, half * span : (half + 1) * span, :seen].astype(F32)
                p = jnp.exp(s - jnp.max(s, axis=-1, keepdims=True))
                p = p / jnp.sum(p, axis=-1, keepdims=True)
                ns.att[rows, e * HD : (e + 1) * HD] = mm(p.astype(BF16), values).astype(BF16)
        return carry

    lax.fori_loop(0, 2, one_group, 0)


def project_out(ns, source, weight, pair, width=512):
    span = ns.part.shape[0] // 4
    rows = tile(pair * span, span)

    def step(j, carry):
        at = tile(j * width, width)
        ns.part[rows, at] = mm_nt(source[rows, :], weight[at, :]).astype(BF16)
        return carry

    lax.fori_loop(0, ns.part.shape[1] // width, step, 0)


def gate_up(ns, pair, slot, width=256):
    span = ns.joined.shape[0] // 4
    rows = tile(pair * span, span)
    ff = ns.product.shape[1]

    def step(j, carry):
        here, there = tile(j * width, width), tile(ff + j * width, width)
        x = ns.joined[rows, :]
        gate = mm(x, ns.wgate[:, here])
        up = mm(x, ns.wup[:, here])
        ns.gu_stage[slot, :, here] = gate.astype(BF16)
        ns.gu_stage[slot, :, there] = up.astype(BF16)
        ns.product[rows, here] = (gate / (1.0 + jnp.exp(-gate)) * up).astype(BF16)
        return carry

    lax.fori_loop(0, ff // width, step, 0)


def forward_layer_kernel(layer, last, spread, ns):
    first = layer == 0
    place = Place(spread)
    links = Links(ns.send, ns.recv)
    local = ns.hidden.shape[0]
    own_rows = (place.own_pair * 2 + place.core) * local
    span = 2 * local
    gathers = []

    def gather(own, land, save, *sources):
        stage = ns.stage.at[len(gathers) % 2]
        gathers.append(Gather(links, place, sources, own, stage, land, save))
        return gathers[-1]

    def attention_weights(at):
        kv = ns.keyvalue_weight
        return (ns.query_weight.at[at], kv.at[at, 0], kv.at[at, 1]), ns.output_weight.at[at]

    mlp = ns.mlp_weight
    if first:
        qkv_source, o_source = attention_weights(layer)
        get_qkv = gather(ns.own_qkv, ns.wqkv, ns.save_wqkv, *qkv_source)
        get_o = gather(ns.own_o, ns.wo, ns.save_wo, o_source)
        get_gate = gather(ns.own_gate, ns.wgate, ns.save_wgate, mlp.at[layer, 0])
    get_up = gather(ns.own_up, ns.wup, ns.save_wup, mlp.at[layer, 1])
    get_down = gather(ns.own_down, ns.wdown, ns.save_wdown, mlp.at[layer, 2])
    if not last:
        qkv_source, o_source = attention_weights(layer + 1)
        next_qkv = gather(ns.own_next_qkv, ns.wnext_qkv, ns.save_wnext_qkv, *qkv_source)
        next_o = gather(ns.own_next_o, ns.wnext_o, ns.save_wnext_o, o_source)
        next_gate = gather(ns.own_next_gate, ns.wnext_gate, ns.save_wnext_gate, mlp.at[layer + 1, 0])
    weights = Weights(gathers)
    if first:
        tokens_in = Spread(links, place, ns.joined)
    mlp_in = Spread(links, place, ns.joined)
    layer_out = Spread(links, place, ns.joined_grad if last else ns.joined)
    diag, y, z, own = place.pairs
    heads = partial(project_heads, ns)

    if first:
        def norm(i, carry):
            v = ns.hidden[tile(i * CHUNK, CHUNK), :].astype(F32)
            ns.joined[tile(own_rows + i * CHUNK, CHUNK), :] = (v * scale_of(v) * ns.gain_attn[...]).astype(BF16)
            return carry

        lax.fori_loop(0, local // CHUNK, norm, 0)
        place.greet()
        tokens_in.start()
        weights.next()
        weights.next()
        tokens_in.pass_z()
        tokens_in.pass_y()
        get_qkv.forward()
        tokens_in.pass_d()
        get_o.forward()
        weights.next()
        tokens_in.own_ready()
        tokens_in.z_ready()
        tokens_in.y_ready()
        get_qkv.finish()
        heads(own)
        heads(z)
        heads(y)
        tokens_in.d_ready()
        heads(diag)
        tokens_in.drain()
        save_a = links.copy(ns.joined, ns.save_a)
        save_a.start()
        get_o.finish()
    else:
        loads = [
            links.copy(ns.joined_in, ns.joined),
            links.copy(ns.wqkv_in, ns.wqkv),
            links.copy(ns.wo_in, ns.wo),
        ]
        gate_load = links.copy(ns.wgate_in, ns.wgate)
        for one in loads:
            one.start()
        gate_load.start()
        place.greet()
        weights.next()
        for one in loads:
            one.wait()

        def every(i, carry):
            heads(i)
            return carry

        lax.fori_loop(0, 4, every, 0)
        gate_load.wait()

    attend(ns)

    def middle(at, total):
        v = ns.hidden[at, :].astype(F32) + total
        ns.mid[at, :] = v
        ns.joined[tile(own_rows + at.start, CHUNK), :] = (v * scale_of(v) * ns.gain_mlp[...]).astype(BF16)

    collect(
        links, place, ns, partial(project_out, ns, ns.att, ns.wo), middle,
        before=[save_a.wait] if first else [],
        sent=[weights.next, (get_gate if first else get_up).forward],
    )
    mlp_in.start()
    if first:
        weights.next()
    mlp_in.pass_z()
    (get_up if first else get_down).forward()
    mlp_in.pass_y()
    mlp_in.own_ready()
    if first:
        get_gate.finish()
    get_up.finish()
    saves = []

    def gate_up_pair(pair):
        slot = len(saves) % 2
        if len(saves) >= 2:
            saves[-2].wait()
        gate_up(ns, pair, slot)
        save = links.copy(ns.gu_stage.at[slot], ns.save_gateup.at[tile(pair * span, span)])
        save.start()
        saves.append(save)

    gate_up_pair(own)
    mlp_in.z_ready()
    gate_up_pair(z)
    mlp_in.pass_d()
    mlp_in.y_ready()
    gate_up_pair(y)
    if last:
        def put(i, carry):
            at = tile(i * CHUNK, CHUNK)
            ns.joined_grad[tile(own_rows + i * CHUNK, CHUNK), :] = ns.cotangent[at, :]
            return carry

        lax.fori_loop(0, local // CHUNK, put, 0)
        layer_out.start()
    else:
        weights.next()
        weights.next()
    if first:
        get_down.forward()
    mlp_in.d_ready()
    gate_up_pair(diag)
    mlp_in.drain()
    save_b = links.copy(ns.joined, ns.save_b)
    save_b.start()
    get_down.finish()

    def result(at, total):
        v = ns.mid[at, :] + total
        ns.out[at, :] = v
        if not last:
            ns.joined[tile(own_rows + at.start, CHUNK), :] = (v * scale_of(v) * ns.gain_next[...]).astype(BF16)

    if last:
        late = [layer_out.pass_z, layer_out.pass_y]
    else:
        late = [next_qkv.forward, next_o.forward]
    collect(
        links, place, ns, partial(project_out, ns, ns.product, ns.wdown), result,
        before=[save_b.wait], sent=[weights.next], late=late,
    )
    if not last:
        layer_out.start()
        layer_out.pass_z()
        layer_out.pass_y()
    layer_out.pass_d()
    if not last:
        next_gate.forward()
        next_qkv.finish()
        next_o.finish()
    layer_out.own_ready()
    layer_out.z_ready()
    layer_out.y_ready()
    layer_out.d_ready()
    layer_out.drain()
    final = links.copy(ns.joined_grad if last else ns.joined, ns.save_next)
    final.start()
    if not last:
        next_gate.finish()
    for save in saves[-2:]:
        save.wait()
    for one in gathers:
        one.drain()
    final.wait()
    assert weights.at == len(gathers) and links.count <= ns.send.shape[0]


def call(kernel, ins, outs, scratch, collective_id, name):
    names = [*ins, *outs, *scratch]

    def run(*refs):
        kernel(SimpleNamespace(**dict(zip(names, refs))))

    def space(in_vmem):
        return pl.BlockSpec(memory_space=pltpu.VMEM if in_vmem else pl.ANY)

    results = pl.pallas_call(
        run,
        out_shape=[jax.ShapeDtypeStruct(shape, dtype) for shape, dtype, _ in outs.values()],
        in_specs=[space(v) for _, v in ins.values()],
        out_specs=[space(v) for _, _, v in outs.values()],
        scratch_shapes=list(scratch.values()),
        compiler_params=pltpu.CompilerParams(
            collective_id=collective_id, has_side_effects=True, vmem_limit_bytes=VMEM_LIMIT
        ),
        cost_estimate=pl.CostEstimate(
            flops=13 * 10**9, bytes_accessed=10**8, transcendentals=10**6
        ),
        name=name,
    )(*[array for array, _ in ins.values()])
    return SimpleNamespace(**dict(zip(outs, results)))


def exchange_scratch(rows, width):
    return dict(
        joined=pltpu.VMEM((8 * rows, width), BF16),
        part=pltpu.VMEM((8 * rows, width), BF16),
        core_in=pltpu.VMEM((4, rows, width), BF16),
        y_in=pltpu.VMEM((2, rows, width), BF16),
        z_in=pltpu.VMEM((rows, width), BF16),
        sums=pltpu.VMEM((3, rows, width), BF16),
    )


def forward_layer(layer, last, hidden, carry, masters, tables, gains, cotangent, spread):
    rows, width = hidden.shape
    query, keyvalue, output, mlp = masters
    first = layer == 0
    total = 8 * rows
    own = query.shape[1]
    d_rows = own * 4 * spread
    o, ff = query.shape[2] // 2, mlp.shape[3] // 2
    kv = keyvalue.shape[3] // 2
    qkv = o + 2 * kv
    cosine, sine, bias = tables

    def row(at, start, size):
        return (gains[at : at + 1, start : start + size], True)

    ins = dict(
        hidden=(hidden, True),
        query_weight=(query, False),
        keyvalue_weight=(keyvalue, False),
        output_weight=(output, False),
        mlp_weight=(mlp, False),
    )
    if first:
        ins.update(gain_attn=row(layer, 0, width))
    else:
        joined_in, wqkv_in, wo_in, wgate_in = ((one, False) for one in carry)
        ins.update(joined_in=joined_in, wqkv_in=wqkv_in, wo_in=wo_in, wgate_in=wgate_in)
    if last:
        ins.update(cotangent=(cotangent, True))
    else:
        ins.update(gain_next=row(layer + 1, 0, width))
    ins.update(gain_mlp=row(layer, width, width))
    ins.update(gain_q=row(layer, 2 * width, HD))
    ins.update(gain_k=row(layer, 2 * width + HD, HD))
    ins.update(cosine=(cosine, True), sine=(sine, True), bias=(bias, True))
    outs = dict(
        out=((rows, width), F32, True),
        mid=((rows, width), F32, True),
        raw=((total, o + 2 * kv), F32, True),
        q=((total, o), BF16, True),
        k=((total, kv), BF16, True),
        v=((total, kv), BF16, True),
        att=((total, o), BF16, True),
        product=((total, ff), BF16, True),
        save_gateup=((total, 2 * ff), BF16, False),
        save_b=((total, width), BF16, False),
        save_next=((total, width), BF16, False),
    )
    scratch = exchange_scratch(rows, width)
    scratch.update(gu_stage=pltpu.VMEM((2, 2 * rows, 2 * ff), BF16))
    scratch.update(stage=pltpu.VMEM((2, own, max(2 * ff, 2 * (o + 2 * kv))), F32))
    weight = lambda size: pltpu.VMEM((d_rows, size), BF16)
    mine = lambda size: pltpu.VMEM((2, own, size), BF16)
    saved = lambda size: ((d_rows, size), BF16, False)
    scratch.update(wqkv=weight(qkv), wo=weight(o), wgate=weight(ff), wup=weight(ff), wdown=weight(ff))
    scratch.update(own_up=mine(ff), own_down=mine(ff))
    outs.update(save_wup=saved(ff), save_wdown=saved(ff))
    if first:
        outs.update(save_a=((total, width), BF16, False))
        scratch.update(own_qkv=mine(qkv), own_o=mine(o), own_gate=mine(ff))
        outs.update(save_wqkv=saved(qkv), save_wo=saved(o), save_wgate=saved(ff))
    if last:
        scratch.update(joined_grad=pltpu.VMEM((total, width), BF16))
    else:
        scratch.update(wnext_qkv=weight(qkv), wnext_o=weight(o), wnext_gate=weight(ff))
        scratch.update(own_next_qkv=mine(qkv), own_next_o=mine(o), own_next_gate=mine(ff))
        outs.update(save_wnext_qkv=saved(qkv), save_wnext_o=saved(o), save_wnext_gate=saved(ff))
    count = 64 + 40 * spread
    scratch.update(send=pltpu.SemaphoreType.DMA((count,)))
    scratch.update(recv=pltpu.SemaphoreType.DMA((count,)))
    kernel = partial(forward_layer_kernel, layer, last, spread)
    return call(kernel, ins, outs, scratch, 1 + int(last) + 2 * int(not first), "forward_layer")


def mm_tn(a, b):
    return lax.dot_general(a, b, (((0,), (0,)), ((), ())), preferred_element_type=F32)


class Reduce:
    def __init__(self, links, place, blocks, x_in, z_in, outs):
        self.place, self.blocks, self.x_in, self.z_in, self.outs = place, blocks, x_in, z_in, outs
        spread = place.spread
        rows = blocks.shape[1] // spread
        self.rows = rows

        def block(q, r):
            return blocks.at[q, tile(r * rows, rows)]

        self.x_out = [
            [
                links.remote(
                    block(q, lax.rem(place.r + s, spread)), x_in.at[s - 1, q], place.r_id(s)
                )
                for s in range(1, spread)
            ]
            for q in range(4)
        ]
        self.z_out = [
            links.remote(block(q, place.r), z_in.at[q - 1], place.z_id(q)) for q in range(1, 4)
        ]

    def compute(self, q, left, right):
        part = self.blocks.shape[1]
        step = min(256, part)
        start = lax.rem(self.place.z + q, 4) * part

        def one(i, carry):
            product = mm_tn(left[:, tile(start + i * step, step)], right())
            self.blocks[q, tile(i * step, step), :] = product.astype(BF16)
            return carry

        lax.fori_loop(0, part // step, one, 0)
        for one_copy in self.x_out[q]:
            one_copy.start()

    def pass_on(self, q):
        for one in self.x_out[q]:
            one.wait_recv()
        step = min(64, self.rows)
        start = self.place.r * self.rows

        def add(i, carry):
            at = tile(start + i * step, step)
            total = self.blocks[q, at, :].astype(F32)
            for s in range(self.place.spread - 1):
                total = total + self.x_in[s, q, tile(i * step, step), :].astype(F32)
            self.blocks[q, at, :] = total.astype(BF16)
            return carry

        lax.fori_loop(0, self.rows // step, add, 0)
        if q:
            self.z_out[q - 1].start()

    def finish(self):
        for one in self.z_out:
            one.wait_recv()
        step = min(64, self.rows)
        low = self.place.low
        start = self.place.r * self.rows

        def add(i, carry):
            at = tile(i * step, step)
            near = self.blocks[0, tile(start + i * step, step), :].astype(F32)
            near = (near + self.z_in[1, at, :].astype(F32)).astype(BF16)
            far = self.z_in[0, at, :].astype(F32) + self.z_in[2, at, :].astype(F32)
            far = far.astype(BF16)
            first = 0
            for out, size in self.outs:
                out[at, tile(low * size, size)] = near[:, first : first + size]
                out[at, tile((1 - low) * size, size)] = far[:, first : first + size]
                first += size
            return carry

        lax.fori_loop(0, self.rows // step, add, 0)

    def drain(self):
        for group in self.x_out:
            for one in group:
                one.wait_send()
        for one in self.z_out:
            one.wait_send()


ORDER = (2, 1, 3, 0)


def gate_up_back(ns, pair, slot, width=256):
    span = ns.joined.shape[0] // 4
    rows = tile(pair * span, span)
    ff = ns.product.shape[1]

    def step(j, carry):
        here, there = tile(j * width, width), tile(ff + j * width, width)
        d_act = mm(ns.joined[rows, :], ns.wdown[:, here])
        gate = ns.stage[slot, :, here].astype(F32)
        up = ns.stage[slot, :, there].astype(F32)
        gated = 1.0 / (1.0 + jnp.exp(-gate))
        ns.d_gate[rows, here] = (d_act * up * gated * (1.0 + gate * (1.0 - gated))).astype(BF16)
        ns.d_up[rows, here] = (d_act * gate * gated).astype(BF16)
        return carry

    lax.fori_loop(0, ff // width, step, 0)


def head_back(ns, rows, d_out, raw, gain, d_gain, d_raw_columns):
    d_turned = d_out * ns.cosine[rows, :] + pltpu.roll(d_out * ns.sine[rows, :], HD // 2, axis=1)
    scale = scale_of(raw)
    normed = raw * scale
    d_gain[...] += jnp.sum(d_turned * normed, axis=0, keepdims=True)
    d_normed = d_turned * gain[...]
    inner = jnp.mean(d_normed * normed, axis=-1, keepdims=True)
    ns.d_raw[rows, d_raw_columns] = (scale * (d_normed - normed * inner)).astype(BF16)


def attend_back(ns):
    group = ns.bias.shape[1]
    span = ns.joined.shape[0] // 4
    q_size, kv_size = ns.q.shape[1], ns.k.shape[1]
    share = q_size // kv_size
    scale = HD**-0.5

    def one_group(b, carry):
        whole = tile(b * group, group)
        for kv in range(kv_size // HD):
            columns = slice(kv * HD, (kv + 1) * HD)
            ns.d_keys[...] = jnp.zeros_like(ns.d_keys)
            ns.d_values[...] = jnp.zeros_like(ns.d_values)
            for e in range(kv * share, (kv + 1) * share):
                mine = slice(e * HD, (e + 1) * HD)
                for half in range(group // span):
                    rows = tile(b * group + half * span, span)
                    seen = (half + 1) * span
                    keys = ns.k[whole, columns][:seen]
                    values = ns.v[whole, columns][:seen]
                    query = ns.q[rows, mine]
                    d_out = ns.d_att[rows, mine]
                    s = mm_nt(query, keys) * scale
                    s = s + ns.bias[b, half * span : (half + 1) * span, :seen].astype(F32)
                    p = jnp.exp(s - jnp.max(s, axis=-1, keepdims=True))
                    p = p / jnp.sum(p, axis=-1, keepdims=True)
                    d_p = mm_nt(d_out, values)
                    delta = jnp.sum(d_p * p, axis=-1, keepdims=True)
                    d_s = (p * (d_p - delta)).astype(BF16)
                    ns.d_values[:seen, :] += mm_tn(p.astype(BF16), d_out)
                    ns.d_keys[:seen, :] += mm_tn(d_s, query)
                    d_query = mm(d_s, keys) * scale
                    head_back(ns, rows, d_query, ns.raw[rows, mine], ns.gain_q, ns.d_gain_q, mine)
            key_columns = slice(q_size + kv * HD, q_size + (kv + 1) * HD)
            d_keys = ns.d_keys[...] * scale
            head_back(ns, whole, d_keys, ns.raw[whole, key_columns], ns.gain_k, ns.d_gain_k, key_columns)
            value_columns = slice(q_size + kv_size + kv * HD, q_size + kv_size + (kv + 1) * HD)
            ns.d_raw[whole, value_columns] = ns.d_values[...].astype(BF16)
        return carry

    lax.fori_loop(0, 2, one_group, 0)


class GainSum:
    def __init__(self, links, place, terms, came, came_r, total):
        spread = place.spread
        self.place, self.terms, self.came, self.came_r, self.total = place, terms, came, came_r, total
        ids = (place.core_id, place.y_id, place.low_id, place.z_id(2))
        self.pairs = [links.remote(terms.at[i], came.at[i], one) for i, one in enumerate(ids)]
        self.sides = [
            links.remote(terms.at[4], came_r.at[place.r], place.r_id(s)) for s in range(1, spread)
        ]
        self.at = 0

    def start(self):
        self.pairs[0].start()

    def step(self):
        i = self.at
        self.at += 1
        if i < 4:
            self.pairs[i].wait_recv()
            self.terms[i + 1] = self.terms[i] + self.came[i]
            if i < 3:
                self.pairs[i + 1].start()
                return
            self.came_r[self.place.r] = self.terms[4]
            for one in self.sides:
                one.start()
            return
        for one in self.sides:
            one.wait_recv()
        total = self.came_r[0]
        for r in range(1, self.place.spread):
            total = total + self.came_r[r]
        self.total[...] = total
        for one in self.pairs + self.sides:
            one.wait_send()


def backward_layer_kernel(layer, spread, ns):
    first = layer == 0
    place = Place(spread)
    links = Links(ns.send, ns.recv)
    local = ns.grad.shape[0]
    own_rows = (place.own_pair * 2 + place.core) * local
    span = 2 * local
    width = ns.grad.shape[1]
    qkv, o, ff = ns.wqkv_in.shape[1], ns.wo_in.shape[1], ns.wdown_in.shape[1]
    kv = (qkv - o) // 2
    diag, y, z, own = place.pairs

    def loads(*pairs):
        copies = [links.copy(src, dst) for src, dst in pairs]
        for one in copies:
            one.start()
        return copies

    def wait(copies):
        for one in copies:
            one.wait()

    def reduce(i, outs):
        return Reduce(links, place, ns.blocks.at[i], ns.x_in.at[i], ns.z_in_w.at[i], outs)

    red_down = reduce(0, [(ns.g_mlp.at[2], ff)])
    red_gate = reduce(1, [(ns.g_mlp.at[0], ff)])
    red_up = reduce(2, [(ns.g_mlp.at[1], ff)])
    red_o = Reduce(links, place, ns.blocks_o, ns.x_in_o, ns.z_in_o, [(ns.g_o, o)])
    red_qkv = Reduce(
        links, place, ns.blocks_qkv, ns.x_in_qkv, ns.z_in_qkv,
        [(ns.g_q, o), (ns.g_kv.at[0], kv), (ns.g_kv.at[1], kv)],
    )
    mid_in = Spread(links, place, ns.joined)
    if not first:
        layer_out = Spread(links, place, ns.joined)
    else:
        gain_sum = GainSum(links, place, ns.terms, ns.came, ns.came_r, ns.gain_total)

    def pass_all(one):
        for q in ORDER:
            one.pass_on(q)

    def compute_all(one, left, right):
        for q in ORDER:
            one.compute(q, left, right)

    def back_norm(value, grad, gain, d_gain, out, gather):
        def finish(at, total):
            v = value[at, :].astype(F32)
            scale = scale_of(v)
            normed = v * scale
            d_gain[...] += jnp.sum(total * normed, axis=0, keepdims=True)
            d_normed = total * gain[...]
            inner = jnp.mean(d_normed * normed, axis=-1, keepdims=True)
            g = grad[at, :].astype(F32) + scale * (d_normed - normed * inner)
            out[at, :] = g
            if gather:
                ns.joined[tile(own_rows + at.start, CHUNK), :] = g.astype(BF16)

        return finish

    for one in (ns.d_gain_attn, ns.d_gain_mlp, ns.d_gain_q, ns.d_gain_k):
        one[...] = jnp.zeros_like(one)

    def mlp_scope(wgate, wup, d_gate, d_up):
        ns.d_gate, ns.d_up = d_gate, d_up
        weight_loads = loads((ns.wgate_in, wgate), (ns.wup_in, wup))

        def down_scope(wdown, product, stage):
            ns.wdown, ns.product, ns.stage = wdown, product, stage
            first_loads = loads((ns.joined_in, ns.joined), (ns.product_in, product))
            down_load = loads((ns.wdown_in, wdown))
            gateup_loads = [
                links.copy(ns.gateup_in.at[tile(p * span, span)], stage.at[i % 2])
                for i, p in enumerate(place.pairs)
            ]
            for one in gateup_loads[:2]:
                one.start()
            place.greet()
            wait(first_loads)
            compute_all(red_down, ns.joined, lambda: product[...])
            wait(down_load)
            for i, pair in enumerate(place.pairs):
                gateup_loads[i].wait()
                gate_up_back(ns, pair, i % 2)
                if i + 2 < 4:
                    gateup_loads[i + 2].start()

        rows_all = ns.wdown_in.shape[0]
        pl.run_scoped(
            down_scope,
            pltpu.VMEM((rows_all, ff), BF16),
            pltpu.VMEM((8 * local, ff), BF16),
            pltpu.VMEM((2, span, 2 * ff), BF16),
        )

        def rest_scope(b):
            b_load = loads((ns.b_in, b))
            wait(weight_loads)

            def work(pair, columns=512):
                rows = tile(pair * span, span)

                def step(j, carry):
                    at = tile(j * columns, columns)
                    term = mm_nt(d_gate[rows, :], wgate[at, :]) + mm_nt(d_up[rows, :], wup[at, :])
                    ns.part[rows, at] = term.astype(BF16)
                    return carry

                lax.fori_loop(0, width // columns, step, 0)

            collect(
                links, place, ns, work,
                back_norm(ns.mid, ns.grad, ns.gain_mlp, ns.d_gain_mlp, ns.grad_mid, True),
                sent=[partial(wait, b_load), partial(compute_all, red_gate, b, lambda: d_gate[...])],
                late=[partial(compute_all, red_up, b, lambda: d_up[...])],
            )
            mid_in.start()
            pass_all(red_down)

        pl.run_scoped(rest_scope, pltpu.VMEM((8 * local, width), BF16))

    rows_all = ns.wdown_in.shape[0]
    total = 8 * local
    pl.run_scoped(
        mlp_scope,
        pltpu.VMEM((rows_all, ff), BF16),
        pltpu.VMEM((rows_all, ff), BF16),
        pltpu.VMEM((total, ff), BF16),
        pltpu.VMEM((total, ff), BF16),
    )

    def attention_scope(
        cosine, sine, bias, hidden, wqkv, wo, a, q, k, v, raw, att, d_att, d_raw, d_keys, d_values
    ):
        ns.cosine, ns.sine, ns.bias, ns.hidden = cosine, sine, bias, hidden
        ns.q, ns.k, ns.v, ns.raw, ns.att = q, k, v, raw, att
        ns.d_att, ns.d_raw, ns.d_keys, ns.d_values = d_att, d_raw, d_keys, d_values
        o_loads = loads((ns.wo_in, wo), (ns.att_in, att))
        other_loads = loads(
            (ns.q_in, q), (ns.k_in, k), (ns.v_in, v), (ns.raw_in, raw), (ns.cosine_in, cosine),
            (ns.sine_in, sine), (ns.bias_in, bias), (ns.a_in, a), (ns.wqkv_in, wqkv), (ns.hidden_in, hidden),
        )

        def d_attended(pair):
            rows = tile(pair * span, span)
            d_att[rows, :] = mm(ns.joined[rows, :], wo[...]).astype(BF16)

        mid_in.pass_z()
        mid_in.pass_y()
        wait(o_loads)
        mid_in.own_ready()
        d_attended(own)
        mid_in.z_ready()
        d_attended(z)
        mid_in.pass_d()
        mid_in.y_ready()
        d_attended(y)
        mid_in.d_ready()
        d_attended(diag)
        mid_in.drain()
        compute_all(red_o, ns.joined, lambda: att[...])
        pass_all(red_gate)
        wait(other_loads)
        attend_back(ns)
        pass_all(red_up)
        compute_all(red_qkv, a, lambda: d_raw[...])
        collect(
            links, place, ns, partial(project_out, ns, d_raw, wqkv),
            back_norm(hidden, ns.grad_mid, ns.gain_attn, ns.d_gain_attn, ns.out, not first),
            sent=[partial(pass_all, red_o)],
            late=[red_down.finish],
        )

    pl.run_scoped(
        attention_scope,
        pltpu.VMEM(ns.cosine_in.shape, F32),
        pltpu.VMEM(ns.sine_in.shape, F32),
        pltpu.VMEM(ns.bias_in.shape, BF16),
        pltpu.VMEM(ns.hidden_in.shape, ns.hidden_in.dtype),
        pltpu.VMEM((rows_all, qkv), BF16),
        pltpu.VMEM((rows_all, o), BF16),
        pltpu.VMEM((total, width), BF16),
        pltpu.VMEM(ns.q_in.shape, BF16),
        pltpu.VMEM(ns.k_in.shape, BF16),
        pltpu.VMEM(ns.v_in.shape, BF16),
        pltpu.VMEM(ns.raw_in.shape, F32),
        pltpu.VMEM(ns.att_in.shape, BF16),
        pltpu.VMEM((total, o), BF16),
        pltpu.VMEM((total, qkv), BF16),
        pltpu.VMEM((ns.bias_in.shape[1], HD), F32),
        pltpu.VMEM((ns.bias_in.shape[1], HD), F32),
    )
    if first:
        ns.terms[0] = jnp.zeros_like(ns.terms[0])
        earlier = (ns.later_attn, ns.later_mlp, ns.later_q, ns.later_k)
        here = (ns.d_gain_attn, ns.d_gain_mlp, ns.d_gain_q, ns.d_gain_k)
        for i, (attn, mlp, query, key) in enumerate((here, earlier)):
            ns.terms[0, 2 * i : 2 * i + 1, :width] = attn[...]
            ns.terms[0, 2 * i + 1 : 2 * i + 2, :width] = mlp[...]
            ns.terms[0, 2 * i : 2 * i + 1, width : width + HD] = query[...]
            ns.terms[0, 2 * i : 2 * i + 1, width + HD : width + 2 * HD] = key[...]
        gain_sum.start()
        for q in ORDER:
            red_qkv.pass_on(q)
            gain_sum.step()
        red_gate.finish()
        gain_sum.step()
    else:
        layer_out.start()
        layer_out.pass_z()
        layer_out.pass_y()
        pass_all(red_qkv)
        layer_out.own_ready()
        layer_out.z_ready()
        layer_out.pass_d()
        layer_out.y_ready()
        red_gate.finish()
        layer_out.d_ready()
        layer_out.drain()
        final = links.copy(ns.joined, ns.save_next)
        final.start()
    red_up.finish()
    red_o.finish()
    red_qkv.finish()
    for one in (red_down, red_gate, red_up, red_o, red_qkv):
        one.drain()
    if not first:
        final.wait()
    assert links.count <= ns.send.shape[0]


def backward_layer(layer, grad, grad_rows, kept, later, tables, gains, spread):
    rows, width = grad.shape
    first = layer == 0
    total = 8 * rows
    cosine, sine, bias = tables
    d_rows, ff = kept.save_wdown.shape
    o, qkv = kept.wo.shape[1], kept.wqkv.shape[1]
    part = d_rows // 4
    block = part // spread

    def row(start, size):
        return gains[layer : layer + 1, start : start + size]

    ins = dict(
        grad=(grad, True),
        joined_in=(grad_rows, False),
        mid=(kept.mid, True),
        hidden_in=(kept.hidden, False),
        product_in=(kept.product, False),
        gateup_in=(kept.save_gateup, False),
        b_in=(kept.save_b, False),
        a_in=(kept.a, False),
        wdown_in=(kept.save_wdown, False),
        wgate_in=(kept.wgate, False),
        wup_in=(kept.save_wup, False),
        wqkv_in=(kept.wqkv, False),
        wo_in=(kept.wo, False),
        q_in=(kept.q, False),
        k_in=(kept.k, False),
        v_in=(kept.v, False),
        raw_in=(kept.raw, False),
        att_in=(kept.att, False),
        gain_attn=(row(0, width), True),
        gain_mlp=(row(width, width), True),
        gain_q=(row(2 * width, HD), True),
        gain_k=(row(2 * width + HD, HD), True),
        cosine_in=(cosine, False),
        sine_in=(sine, False),
        bias_in=(bias, False),
    )
    outs = dict(
        out=((rows, width), F32, True),
        d_gain_attn=((1, width), F32, True),
        d_gain_mlp=((1, width), F32, True),
        d_gain_q=((1, HD), F32, True),
        d_gain_k=((1, HD), F32, True),
        g_q=((block, 2 * o), BF16, True),
        g_kv=((2, block, qkv - o), BF16, True),
        g_o=((block, 2 * o), BF16, True),
        g_mlp=((3, block, 2 * ff), BF16, True),
    )
    if first:
        ins.update(
            later_attn=(later.d_gain_attn, True), later_mlp=(later.d_gain_mlp, True),
            later_q=(later.d_gain_q, True), later_k=(later.d_gain_k, True),
        )
        outs.update(gain_total=((8, width + 2 * HD), F32, True))
    if not first:
        outs.update(save_next=((total, width), BF16, False))
    scratch = exchange_scratch(rows, width)
    side = spread - 1
    scratch.update(grad_mid=pltpu.VMEM((rows, width), F32))
    scratch.update(blocks=pltpu.VMEM((3, 4, part, ff), BF16))
    scratch.update(blocks_o=pltpu.VMEM((4, part, o), BF16))
    scratch.update(blocks_qkv=pltpu.VMEM((4, part, qkv), BF16))
    scratch.update(x_in=pltpu.VMEM((3, side, 4, block, ff), BF16))
    scratch.update(x_in_o=pltpu.VMEM((side, 4, block, o), BF16))
    scratch.update(x_in_qkv=pltpu.VMEM((side, 4, block, qkv), BF16))
    scratch.update(z_in_w=pltpu.VMEM((3, 3, block, ff), BF16))
    scratch.update(z_in_o=pltpu.VMEM((3, block, o), BF16))
    scratch.update(z_in_qkv=pltpu.VMEM((3, block, qkv), BF16))
    if first:
        small = (8, width + 2 * HD)
        scratch.update(terms=pltpu.VMEM((5, *small), F32))
        scratch.update(came=pltpu.VMEM((4, *small), F32))
        scratch.update(came_r=pltpu.VMEM((spread, *small), F32))
    count = 96 + 24 * spread
    scratch.update(send=pltpu.SemaphoreType.DMA((count,)))
    scratch.update(recv=pltpu.SemaphoreType.DMA((count,)))
    kernel = partial(backward_layer_kernel, layer, spread)
    return call(kernel, ins, outs, scratch, 6 if first else 5, "backward_layer")


def places(dp_size):
    spread = dp_size // 4
    me = lax.axis_index("dp")
    z = me // spread
    return spread, me, lax.rem(me, spread), lax.rem(z, 2), z // 2


def flip_lo(dp_size):
    spread = dp_size // 4
    return [(i, i + spread * (1 - 2 * ((i // spread) % 2))) for i in range(dp_size)]


def flip_hi(dp_size):
    spread = dp_size // 4
    return [(i, i + 2 * spread * (1 - 2 * (i // (2 * spread)))) for i in range(dp_size)]


def shift_r(dp_size, step):
    spread = dp_size // 4
    return [(i, (i // spread) * spread + (i % spread + step) % spread) for i in range(dp_size)]


def rope_tables(positions, head_size):
    half = head_size // 2
    frequency = jnp.power(THETA, -2.0 * jnp.arange(half, dtype=F32) / head_size)
    angle = positions.astype(F32)[:, None] * frequency[None, :]
    return (jnp.cos(angle)[:, None, :], jnp.sin(angle)[:, None, :])


def adamw(weight, first, second, grad, rate, decay):
    first_new = BETA_ONE * first + (1.0 - BETA_ONE) * grad
    second_new = BETA_TWO * second + (1.0 - BETA_TWO) * grad * grad
    first_hat = first_new / (1.0 - BETA_ONE**STEP)
    second_hat = second_new / (1.0 - BETA_TWO**STEP)
    weight_new = weight - rate * (first_hat / (jnp.sqrt(second_hat) + ADAM_EPS) + decay * weight)
    return (first_new, second_new, weight_new)


def body(
    tokens, cotangent, segment_ids, gains, gain_first, gain_second,
    query_weight, query_first, query_second,
    keyvalue_weight, keyvalue_first, keyvalue_second,
    output_weight, output_first, output_second,
    mlp_weight, mlp_first, mlp_second,
):
    dp_size = lax.axis_size("dp")
    spread, me, r, low, high = places(dp_size)
    layers = gains.shape[0]
    local_rows, width = tokens.shape
    group = segment_ids.shape[0]
    rows = 8 * local_rows
    index = jnp.arange(group, dtype=jnp.int32)
    other = lax.ppermute(segment_ids, "dp", flip_lo(dp_size))
    segments = jnp.stack([jnp.where(low == 0, segment_ids, other), jnp.where(low == 0, other, segment_ids)])
    positions = (index[None, :] - (segments - segments[:, :1])).reshape(rows)
    mask = (segments[:, :, None] == segments[:, None, :]) & (index[None, None, :] <= index[None, :, None])
    bias = jnp.where(mask, 0.0, -1e30).astype(BF16)
    cosine, sine = rope_tables(positions, HD)
    tables = (
        jnp.concatenate([cosine[:, 0], cosine[:, 0]], axis=1),
        jnp.concatenate([-sine[:, 0], sine[:, 0]], axis=1),
        bias,
    )
    masters = (query_weight, keyvalue_weight, output_weight, mlp_weight)

    hidden, carry = tokens, None
    saved = []
    for layer in range(layers):
        last = layer + 1 == layers
        kept = forward_layer(layer, last, hidden, carry, masters, tables, gains, cotangent, spread)
        if layer == 0:
            carry = (kept.save_a, kept.save_wqkv, kept.save_wo, kept.save_wgate)
        kept.hidden = hidden
        kept.a, kept.wqkv, kept.wo, kept.wgate = carry
        saved.append(kept)
        hidden = kept.out
        if not last:
            carry = (kept.save_next, kept.save_wnext_qkv, kept.save_wnext_o, kept.save_wnext_gate)

    block_output = hidden
    grad = cotangent
    grad_rows = saved[-1].save_next
    reduced = [None] * layers
    done = None
    for layer in reversed(range(layers)):
        done = backward_layer(layer, grad, grad_rows, saved[layer], done, tables, gains, spread)
        grad, grad_rows = done.out, None if layer == 0 else done.save_next
        reduced[layer] = [done.g_q, done.g_kv, done.g_o, done.g_mlp]
    stacked = [jnp.stack([entry[i] for entry in reduced]).astype(F32) for i in range(4)]
    sums = done.gain_total
    gain_total = jnp.stack(
        [
            jnp.concatenate([sums[2 * i, :width], sums[2 * i + 1, :width], sums[2 * i, width:]])
            for i in range(layers)
        ]
    )
    head_gain_grads = gain_total[:, 2 * width :]
    gain_new = adamw(gains, gain_first, gain_second, gain_total, GAIN_RATE, 0.0)
    query_new = adamw(query_weight, query_first, query_second, stacked[0], RATE, DECAY)
    keyvalue_new = adamw(keyvalue_weight, keyvalue_first, keyvalue_second, stacked[1], RATE, DECAY)
    output_new = adamw(output_weight, output_first, output_second, stacked[2], RATE * OUTPUT_FACTOR, DECAY)
    mlp_new = adamw(mlp_weight, mlp_first, mlp_second, stacked[3], RATE, DECAY)
    return (block_output, grad, *gain_new, head_gain_grads, *query_new, *keyvalue_new, *output_new, *mlp_new)


def solution(mesh):
    token = P(("dp", "tensor"), None)
    flat = P(None, "dp", "tensor")
    deep = P(None, None, "dp", "tensor")
    placed = (token, token, P("dp"), P(), P(), P(), *[flat] * 3, *[deep] * 3, *[flat] * 3, *[deep] * 3)
    outs = (token, token, P(), P(), P(), P(), *[flat] * 3, *[deep] * 3, *[flat] * 3, *[deep] * 3)
    return jax.shard_map(body, mesh=mesh, in_specs=placed, out_specs=outs, check_vma=False)
```

```python
from functools import partial
import math
from types import SimpleNamespace

import jax
import jax.numpy as jnp
from jax import lax
from jax.experimental import pallas as pl
from jax.experimental.pallas import tpu as pltpu
from jax.sharding import PartitionSpec as P

HD = 128
STEP = 10
EPSILON = 1e-06
THETA = 1000000.0
BETA_ONE = 0.9
BETA_TWO = 0.95
ADAM_EPS = 1e-08
DECAY = 0.1
RATE = 0.05
GAIN_RATE = 0.8
OUTPUT_FACTOR = math.sqrt(128)

BF16 = jnp.bfloat16
F32 = jnp.float32
MESH = pl.DeviceIdType.MESH
CHUNK = 32
VMEM_LIMIT = 62 * 1024 * 1024


class Place:
    def __init__(self, spread):
        self.spread = spread
        self.dp = lax.axis_index("dp")
        self.tensor = lax.axis_index("tensor")
        self.core = lax.rem(self.tensor, 2)
        self.y = self.tensor // 2
        self.z = self.dp // spread
        self.r = lax.rem(self.dp, spread)
        self.low = lax.rem(self.z, 2)
        self.core_id = {"dp": self.dp, "tensor": self.y * 2 + 1 - self.core}
        self.y_id = {"dp": self.dp, "tensor": (1 - self.y) * 2 + self.core}
        self.low_id = {"dp": self.dp + spread * (1 - 2 * self.low), "tensor": self.tensor}
        self.own_pair = self.low * 2 + self.y
        self.pairs = (
            (1 - self.low) * 2 + 1 - self.y,
            self.low * 2 + 1 - self.y,
            (1 - self.low) * 2 + self.y,
            self.own_pair,
        )

    def z_dp(self, step):
        return lax.rem(self.z + 4 + step, 4) * self.spread + self.r

    def z_id(self, step):
        return {"dp": self.z_dp(step), "tensor": self.tensor}

    def r_dp(self, step):
        return self.z * self.spread + lax.rem(self.r + self.spread + step, self.spread)

    def r_id(self, step):
        return {"dp": self.r_dp(step), "tensor": self.tensor}

    def greet(self):
        ids = [self.core_id, self.y_id]
        ids += [self.z_id(k) for k in range(1, 4)]
        ids += [self.r_id(k) for k in range(1, self.spread)]
        barrier = pltpu.get_barrier_semaphore()
        for one in ids:
            pl.semaphore_signal(barrier, inc=1, device_id=one, device_id_type=MESH)
        pl.semaphore_wait(barrier, len(ids))


class Links:
    def __init__(self, send, recv):
        self.send, self.recv, self.count = send, recv, 0
        self.local = []

    def remote(self, src, dst, to):
        slot = self.count
        self.count += 1
        return pltpu.make_async_remote_copy(
            src_ref=src, dst_ref=dst, send_sem=self.send.at[slot], recv_sem=self.recv.at[slot],
            device_id=to, device_id_type=MESH,
        )

    def copy(self, src, dst):
        slot = self.count
        self.count += 1
        return pltpu.make_async_copy(src, dst, self.send.at[slot])


def tile(start, size):
    return pl.ds(pl.multiple_of(start, size), size)


class Spread:
    def __init__(self, links, place, joined):
        rows = joined.shape[0] // 8

        def block(pair, core):
            return joined.at[tile((pair * 2 + core) * rows, rows)]

        c = place.core
        diag, y, z, own = place.pairs
        own, from_z, from_y, from_d = (block(p, c) for p in (own, z, y, diag))
        self.to_z = links.remote(own, own, place.low_id)
        self.to_y = links.remote(own, own, place.y_id)
        self.to_core = links.remote(own, own, place.core_id)
        self.on_y = links.remote(from_z, from_z, place.y_id)
        self.core_z = links.remote(from_z, from_z, place.core_id)
        self.core_y = links.remote(from_y, from_y, place.core_id)
        self.core_d = links.remote(from_d, from_d, place.core_id)

    def start(self):
        self.to_z.start()
        self.to_y.start()
        self.to_core.start()

    def own_ready(self):
        self.to_core.wait_recv()

    def pass_z(self):
        self.to_z.wait_recv()
        self.on_y.start()
        self.core_z.start()

    def pass_y(self):
        self.to_y.wait_recv()
        self.core_y.start()

    def z_ready(self):
        self.core_z.wait_recv()

    def y_ready(self):
        self.core_y.wait_recv()

    def pass_d(self):
        self.on_y.wait_recv()
        self.core_d.start()

    def d_ready(self):
        self.core_d.wait_recv()

    def drain(self):
        for one in (self.to_z, self.to_y, self.to_core, self.on_y, self.core_z, self.core_y, self.core_d):
            one.wait_send()


def collect(links, place, ns, work, finish, before=(), sent=(), late=()):
    part, core_in, y_in, z_in, sums = ns.part, ns.core_in, ns.y_in, ns.z_in, ns.sums
    rows = part.shape[0] // 8
    core = place.core

    def block(pair, c):
        return tile((pair * 2 + c) * rows, rows)

    across = [
        links.remote(part.at[block(p, 1 - core)], core_in.at[k], place.core_id)
        for k, p in enumerate(place.pairs)
    ]
    diag = links.remote(sums.at[0], y_in.at[0], place.y_id)
    to_y = links.remote(sums.at[1], y_in.at[1], place.y_id)
    to_z = links.remote(sums.at[2], z_in, place.low_id)

    def term(k, i):
        start = (place.pairs[k] * 2 + core) * rows + i * CHUNK
        at = tile(i * CHUNK, CHUNK)
        return part[tile(start, CHUNK), :].astype(F32) + core_in[k, at, :].astype(F32)

    def add(k, extra):
        def step(i, carry):
            at = tile(i * CHUNK, CHUNK)
            total = term(k, i)
            if extra is not None:
                total = total + extra[at, :].astype(F32)
            sums[k, at, :] = total.astype(BF16)
            return carry

        lax.fori_loop(0, rows // CHUNK, step, 0)

    work(place.pairs[0])
    across[0].start()
    work(place.pairs[1])
    across[1].start()
    across[0].wait_recv()
    add(0, None)
    diag.start()
    run(before)
    work(place.pairs[2])
    across[2].start()
    across[1].wait_recv()
    add(1, None)
    to_y.start()
    work(place.pairs[3])
    across[3].start()
    run(sent)
    across[2].wait_recv()
    diag.wait_recv()
    add(2, y_in.at[0])
    to_z.start()
    run(late)
    across[3].wait_recv()
    to_y.wait_recv()
    to_z.wait_recv()

    def last(i, carry):
        at = tile(i * CHUNK, CHUNK)
        total = term(3, i) + y_in[1, at, :].astype(F32) + z_in[at, :].astype(F32)
        finish(at, total)
        return carry

    lax.fori_loop(0, rows // CHUNK, last, 0)
    for one in (*across, diag, to_y, to_z):
        one.wait_send()


class Gather:
    def __init__(self, links, place, sources, own, stage, land, save):
        rows = own.shape[1]
        self.place, self.own, self.land, self.rows, self.stage = place, own, land, rows, stage
        self.starts, self.loads = [], []
        start = 0
        for one in sources:
            size = one.shape[1]
            self.starts.append((start, size // 2))
            self.loads.append(links.copy(one, stage.at[:, start : start + size]))
            start += size
        spread = place.spread

        def at(dp):
            return land.at[tile(dp * rows, rows)]

        mine = at(place.dp)
        self.out = [
            links.remote(own.at[lax.rem(place.low + k, 2)], mine, place.z_id(k)) for k in range(1, 4)
        ]
        self.side = [links.remote(own.at[place.low], mine, place.r_id(s)) for s in range(1, spread)]
        self.on = [
            [
                links.remote(at(place.z_dp(-k)), at(place.z_dp(-k)), place.r_id(s))
                for s in range(1, spread)
            ]
            for k in range(1, 4)
        ]
        self.save = links.copy(land, save)

    def load(self):
        for one in self.loads:
            one.start()

    def cast(self):
        for one in self.loads:
            one.wait()
        step = min(64, self.rows)

        def round_rows(i, carry):
            at = tile(i * step, step)
            for low in range(2):
                to = 0
                for start, half in self.starts:
                    piece = self.stage[at, start + low * half : start + (low + 1) * half]
                    self.own[low, at, to : to + half] = piece.astype(BF16)
                    to += half
            return carry

        lax.fori_loop(0, self.rows // step, round_rows, 0)

    def begin(self):
        for one in self.side:
            one.start()
        step = min(64, self.rows)

        def copy(i, carry):
            self.land[tile(self.place.dp * self.rows + i * step, step), :] = self.own[
                self.place.low, tile(i * step, step), :
            ]
            return carry

        lax.fori_loop(0, self.rows // step, copy, 0)

    def forward(self, k):
        self.out[k].wait_recv()
        for one in self.on[k]:
            one.start()

    def finish(self):
        for one in self.side:
            one.wait_recv()
        for group in self.on:
            for one in group:
                one.wait_recv()
        self.save.start()

    def drain(self):
        for one in self.out + self.side:
            one.wait_send()
        for group in self.on:
            for one in group:
                one.wait_send()
        self.save.wait()


class Stream:
    def __init__(self, groups):
        self.groups = groups
        self.order = [one for group in groups for one in group]
        self.items = [(group, k) for group in groups for k in range(3)]
        self.sent = self.passed = 0
        for one in self.order[:2]:
            one.load()

    def send(self, count=1):
        for group, k in self.items[self.sent : self.sent + count]:
            for one in group:
                if k == 0:
                    one.cast()
                    at = self.order.index(one) + 2
                    if at < len(self.order):
                        self.order[at].load()
                    one.begin()
                one.out[k].start()
            self.sent += 1

    def forward(self, count=1):
        for group, k in self.items[self.passed : min(self.passed + count, self.sent)]:
            for one in group:
                one.forward(k)
            self.passed += 1

    def tick(self, lag=2):
        self.send()
        if self.passed + lag < self.sent or self.sent == len(self.items):
            self.forward()

    def need(self, one):
        place = [i for i, group in enumerate(self.groups) if one in group][0] * 3 + 3
        self.send(max(0, place - self.sent))
        self.forward(max(0, place - self.passed))
        one.finish()

    def rest(self):
        self.send(len(self.items))
        self.forward(len(self.items))


def run(steps):
    for one in steps:
        one()


def scale_of(v):
    return lax.rsqrt(jnp.mean(v * v, axis=-1, keepdims=True) + EPSILON)


def mm(a, b):
    return jnp.dot(a, b, preferred_element_type=F32)


def mm_nt(a, b):
    return lax.dot_general(a, b, (((1,), (1,)), ((), ())), preferred_element_type=F32)


def project_heads(ns, pair):
    span = ns.joined.shape[0] // 4
    rows = tile(pair * span, span)
    raw = mm(ns.joined[rows, :], ns.wqkv[...])
    ns.raw[rows, :] = raw
    cosine, sine = ns.cosine[rows, :], ns.sine[rows, :]
    q_size, kv_size = ns.q.shape[1], ns.k.shape[1]

    def heads(out, start, size, gain):
        for h in range(size // HD):
            v = raw[:, start + h * HD : start + (h + 1) * HD]
            v = v * scale_of(v) * gain[...]
            turned = v * cosine + pltpu.roll(v, HD // 2, axis=1) * sine
            out[rows, h * HD : (h + 1) * HD] = turned.astype(BF16)

    heads(ns.q, 0, q_size, ns.gain_q)
    heads(ns.k, q_size, kv_size, ns.gain_k)
    ns.v[rows, :] = raw[:, q_size + kv_size :].astype(BF16)


def attend(ns, b):
    group = ns.bias.shape[1]
    span = ns.joined.shape[0] // 4
    q_heads = ns.q.shape[1] // HD
    share = q_heads // (ns.k.shape[1] // HD)
    scale = HD**-0.5

    for e in range(q_heads):
        kv = slice((e // share) * HD, (e // share + 1) * HD)
        for half in range(group // span):
            start = b * group + half * span
            rows = slice(start, start + span)
            seen = (half + 1) * span
            keys = ns.k[b * group : b * group + seen, kv]
            values = ns.v[b * group : b * group + seen, kv]
            s = mm_nt(ns.q[rows, e * HD : (e + 1) * HD], keys) * scale
            s = s + ns.bias[b, half * span : (half + 1) * span, :seen].astype(F32)
            p = jnp.exp(s - jnp.max(s, axis=-1, keepdims=True))
            p = p / jnp.sum(p, axis=-1, keepdims=True)
            ns.att[rows, e * HD : (e + 1) * HD] = mm(p.astype(BF16), values).astype(BF16)


def project_out(ns, source, weight, pair, width=512):
    span = ns.part.shape[0] // 4
    rows = tile(pair * span, span)

    def step(j, carry):
        at = tile(j * width, width)
        ns.part[rows, at] = mm_nt(source[rows, :], weight[at, :]).astype(BF16)
        return carry

    lax.fori_loop(0, ns.part.shape[1] // width, step, 0)


def gate_up(ns, pair, slot, width=256):
    span = ns.joined.shape[0] // 4
    rows = tile(pair * span, span)
    ff = ns.product.shape[1]

    def step(j, carry):
        here, there = tile(j * width, width), tile(ff + j * width, width)
        x = ns.joined[rows, :]
        gate = mm(x, ns.wgate[:, here])
        up = mm(x, ns.wup[:, here])
        ns.gu_stage[slot, :, here] = gate.astype(BF16)
        ns.gu_stage[slot, :, there] = up.astype(BF16)
        ns.product[rows, here] = (gate / (1.0 + jnp.exp(-gate)) * up).astype(BF16)
        return carry

    lax.fori_loop(0, ff // width, step, 0)


def forward_layer_kernel(layer, last, spread, ns):
    first = layer == 0
    place = Place(spread)
    links = Links(ns.send, ns.recv)
    local = ns.hidden.shape[0]
    own_rows = (place.own_pair * 2 + place.core) * local
    span = 2 * local
    gathers = []

    def gather(own, land, save, *sources):
        stage = ns.stage.at[len(gathers) % 2]
        gathers.append(Gather(links, place, sources, own, stage, land, save))
        return gathers[-1]

    def attention_weights(at):
        kv = ns.keyvalue_weight
        return (ns.query_weight.at[at], kv.at[at, 0], kv.at[at, 1]), ns.output_weight.at[at]

    mlp = ns.mlp_weight
    if first:
        qkv_source, o_source = attention_weights(layer)
        get_qkv = gather(ns.own_qkv, ns.wqkv, ns.save_wqkv, *qkv_source)
        get_o = gather(ns.own_o, ns.wo, ns.save_wo, o_source)
        get_gate = gather(ns.own_gate, ns.wgate, ns.save_wgate, mlp.at[layer, 0])
    get_up = gather(ns.own_up, ns.wup, ns.save_wup, mlp.at[layer, 1])
    get_down = gather(ns.own_down, ns.wdown, ns.save_wdown, mlp.at[layer, 2])
    if not last:
        qkv_source, o_source = attention_weights(layer + 1)
        next_qkv = gather(ns.own_next_qkv, ns.wnext_qkv, ns.save_wnext_qkv, *qkv_source)
        next_o = gather(ns.own_next_o, ns.wnext_o, ns.save_wnext_o, o_source)
        next_gate = gather(ns.own_next_gate, ns.wnext_gate, ns.save_wnext_gate, mlp.at[layer + 1, 0])
    groups = [[get_qkv], [get_o], [get_gate]] if first else []
    groups += [[get_up], [get_down]]
    if not last:
        groups += [[next_qkv, next_o], [next_gate]]
    stream = Stream(groups)
    tick = stream.tick
    if first:
        tokens_in = Spread(links, place, ns.joined)
    mlp_in = Spread(links, place, ns.joined)
    layer_out = Spread(links, place, ns.joined_grad if last else ns.joined)
    diag, y, z, own = place.pairs
    heads = partial(project_heads, ns)

    if first:
        def norm(i, carry):
            v = ns.hidden[tile(i * CHUNK, CHUNK), :].astype(F32)
            ns.joined[tile(own_rows + i * CHUNK, CHUNK), :] = (v * scale_of(v) * ns.gain_attn[...]).astype(BF16)
            return carry

        lax.fori_loop(0, local // CHUNK, norm, 0)
        place.greet()
        tokens_in.start()
        stream.send(3)
        tokens_in.pass_z()
        tokens_in.pass_y()
        stream.send()
        stream.forward()
        stream.send()
        stream.forward()
        stream.send()
        stream.forward()
        tokens_in.pass_d()
        tick()
        tick()
        tokens_in.own_ready()
        tokens_in.z_ready()
        tokens_in.y_ready()
        stream.need(get_qkv)
        heads(own)
        heads(z)
        tick()
        heads(y)
        tokens_in.d_ready()
        heads(diag)
        tokens_in.drain()
        save_a = links.copy(ns.joined, ns.save_a)
        save_a.start()
        tick()
    else:
        loads = [
            links.copy(ns.joined_in, ns.joined),
            links.copy(ns.wqkv_in, ns.wqkv),
            links.copy(ns.wo_in, ns.wo),
        ]
        gate_load = links.copy(ns.wgate_in, ns.wgate)
        for one in loads:
            one.start()
        gate_load.start()
        if last:
            def put(i, carry):
                at = tile(i * CHUNK, CHUNK)
                ns.joined_grad[tile(own_rows + i * CHUNK, CHUNK), :] = ns.cotangent[at, :]
                return carry

            lax.fori_loop(0, local // CHUNK, put, 0)
        place.greet()
        if last:
            layer_out.start()
        stream.send()
        for one in loads:
            one.wait()

        def every(i, carry):
            heads(i)
            return carry

        lax.fori_loop(0, 4, every, 0)
        gate_load.wait()
        if last:
            layer_out.pass_z()
            layer_out.pass_y()
        tick()

    attend(ns, 0)
    tick()
    attend(ns, 1)
    tick()
    if first:
        stream.need(get_o)
    if last:
        layer_out.pass_d()

    def middle(at, total):
        v = ns.hidden[at, :].astype(F32) + total
        ns.mid[at, :] = v
        ns.joined[tile(own_rows + at.start, CHUNK), :] = (v * scale_of(v) * ns.gain_mlp[...]).astype(BF16)

    collect(
        links, place, ns, partial(project_out, ns, ns.att, ns.wo), middle,
        before=[save_a.wait] if first else [], sent=[tick], late=[tick],
    )
    mlp_in.start()
    tick()
    mlp_in.pass_z()
    mlp_in.pass_y()
    tick()
    mlp_in.own_ready()
    if first:
        stream.need(get_gate)
    stream.need(get_up)
    saves = []

    def gate_up_pair(pair):
        slot = len(saves) % 2
        if len(saves) >= 2:
            saves[-2].wait()
        gate_up(ns, pair, slot)
        save = links.copy(ns.gu_stage.at[slot], ns.save_gateup.at[tile(pair * span, span)])
        save.start()
        saves.append(save)

    gate_up_pair(own)
    mlp_in.z_ready()
    gate_up_pair(z)
    mlp_in.pass_d()
    tick()
    mlp_in.y_ready()
    gate_up_pair(y)
    mlp_in.d_ready()
    gate_up_pair(diag)
    tick()
    mlp_in.drain()
    save_b = links.copy(ns.joined, ns.save_b)
    save_b.start()
    stream.need(get_down)

    def result(at, total):
        v = ns.mid[at, :] + total
        ns.out[at, :] = v
        if not last:
            ns.joined[tile(own_rows + at.start, CHUNK), :] = (v * scale_of(v) * ns.gain_next[...]).astype(BF16)

    collect(
        links, place, ns, partial(project_out, ns, ns.product, ns.wdown), result,
        before=[save_b.wait], sent=[tick], late=[tick],
    )
    if not last:
        layer_out.start()
        tick()
        layer_out.pass_z()
        layer_out.pass_y()
        tick()
        layer_out.pass_d()
        tick()
        stream.rest()
        for one in (next_qkv, next_o):
            stream.need(one)
    layer_out.own_ready()
    layer_out.z_ready()
    layer_out.y_ready()
    layer_out.d_ready()
    layer_out.drain()
    final = links.copy(ns.joined_grad if last else ns.joined, ns.save_next)
    final.start()
    if not last:
        stream.need(next_gate)
    for save in saves[-2:]:
        save.wait()
    for one in gathers:
        one.drain()
    final.wait()
    assert stream.passed == len(stream.items) and links.count <= ns.send.shape[0]


def call(kernel, ins, outs, scratch, collective_id, name):
    names = [*ins, *outs, *scratch]

    def run(*refs):
        kernel(SimpleNamespace(**dict(zip(names, refs))))

    def space(in_vmem):
        return pl.BlockSpec(memory_space=pltpu.VMEM if in_vmem else pl.ANY)

    results = pl.pallas_call(
        run,
        out_shape=[jax.ShapeDtypeStruct(shape, dtype) for shape, dtype, _ in outs.values()],
        in_specs=[space(v) for _, v in ins.values()],
        out_specs=[space(v) for _, _, v in outs.values()],
        scratch_shapes=list(scratch.values()),
        compiler_params=pltpu.CompilerParams(
            collective_id=collective_id, has_side_effects=True, vmem_limit_bytes=VMEM_LIMIT
        ),
        cost_estimate=pl.CostEstimate(
            flops=13 * 10**9, bytes_accessed=10**8, transcendentals=10**6
        ),
        name=name,
    )(*[array for array, _ in ins.values()])
    return SimpleNamespace(**dict(zip(outs, results)))


def exchange_scratch(rows, width):
    return dict(
        joined=pltpu.VMEM((8 * rows, width), BF16),
        part=pltpu.VMEM((8 * rows, width), BF16),
        core_in=pltpu.VMEM((4, rows, width), BF16),
        y_in=pltpu.VMEM((2, rows, width), BF16),
        z_in=pltpu.VMEM((rows, width), BF16),
        sums=pltpu.VMEM((3, rows, width), BF16),
    )


def forward_layer(layer, last, hidden, carry, masters, tables, gains, cotangent, spread):
    rows, width = hidden.shape
    query, keyvalue, output, mlp = masters
    first = layer == 0
    total = 8 * rows
    own = query.shape[1]
    d_rows = own * 4 * spread
    o, ff = query.shape[2] // 2, mlp.shape[3] // 2
    kv = keyvalue.shape[3] // 2
    qkv = o + 2 * kv
    cosine, sine, bias = tables

    def row(at, start, size):
        return (gains[at : at + 1, start : start + size], True)

    ins = dict(
        hidden=(hidden, True),
        query_weight=(query, False),
        keyvalue_weight=(keyvalue, False),
        output_weight=(output, False),
        mlp_weight=(mlp, False),
    )
    if first:
        ins.update(gain_attn=row(layer, 0, width))
    else:
        joined_in, wqkv_in, wo_in, wgate_in = ((one, False) for one in carry)
        ins.update(joined_in=joined_in, wqkv_in=wqkv_in, wo_in=wo_in, wgate_in=wgate_in)
    if last:
        ins.update(cotangent=(cotangent, True))
    else:
        ins.update(gain_next=row(layer + 1, 0, width))
    ins.update(gain_mlp=row(layer, width, width))
    ins.update(gain_q=row(layer, 2 * width, HD))
    ins.update(gain_k=row(layer, 2 * width + HD, HD))
    ins.update(cosine=(cosine, True), sine=(sine, True), bias=(bias, True))
    outs = dict(
        out=((rows, width), F32, True),
        mid=((rows, width), F32, True),
        raw=((total, o + 2 * kv), F32, True),
        q=((total, o), BF16, True),
        k=((total, kv), BF16, True),
        v=((total, kv), BF16, True),
        att=((total, o), BF16, True),
        product=((total, ff), BF16, True),
        save_gateup=((total, 2 * ff), BF16, False),
        save_b=((total, width), BF16, False),
        save_next=((total, width), BF16, False),
    )
    scratch = exchange_scratch(rows, width)
    scratch.update(gu_stage=pltpu.VMEM((2, 2 * rows, 2 * ff), BF16))
    scratch.update(stage=pltpu.VMEM((2, own, max(2 * ff, 2 * (o + 2 * kv))), F32))
    weight = lambda size: pltpu.VMEM((d_rows, size), BF16)
    mine = lambda size: pltpu.VMEM((2, own, size), BF16)
    saved = lambda size: ((d_rows, size), BF16, False)
    scratch.update(wqkv=weight(qkv), wo=weight(o), wgate=weight(ff), wup=weight(ff), wdown=weight(ff))
    scratch.update(own_up=mine(ff), own_down=mine(ff))
    outs.update(save_wup=saved(ff), save_wdown=saved(ff))
    if first:
        outs.update(save_a=((total, width), BF16, False))
        scratch.update(own_qkv=mine(qkv), own_o=mine(o), own_gate=mine(ff))
        outs.update(save_wqkv=saved(qkv), save_wo=saved(o), save_wgate=saved(ff))
    if last:
        scratch.update(joined_grad=pltpu.VMEM((total, width), BF16))
    else:
        scratch.update(wnext_qkv=weight(qkv), wnext_o=weight(o), wnext_gate=weight(ff))
        scratch.update(own_next_qkv=mine(qkv), own_next_o=mine(o), own_next_gate=mine(ff))
        outs.update(save_wnext_qkv=saved(qkv), save_wnext_o=saved(o), save_wnext_gate=saved(ff))
    count = 64 + 40 * spread
    scratch.update(send=pltpu.SemaphoreType.DMA((count,)))
    scratch.update(recv=pltpu.SemaphoreType.DMA((count,)))
    kernel = partial(forward_layer_kernel, layer, last, spread)
    return call(kernel, ins, outs, scratch, 1 + int(last) + 2 * int(not first), "forward_layer")


def mm_tn(a, b):
    return lax.dot_general(a, b, (((0,), (0,)), ((), ())), preferred_element_type=F32)


class Reduce:
    def __init__(self, links, place, blocks, x_in, z_in, outs):
        self.place, self.blocks, self.x_in, self.z_in, self.outs = place, blocks, x_in, z_in, outs
        spread = place.spread
        rows = blocks.shape[1] // spread
        self.rows = rows

        def block(q, r):
            return blocks.at[q, tile(r * rows, rows)]

        self.x_out = [
            [
                links.remote(
                    block(q, lax.rem(place.r + s, spread)), x_in.at[s - 1, q], place.r_id(s)
                )
                for s in range(1, spread)
            ]
            for q in range(4)
        ]
        self.z_out = [
            links.remote(block(q, place.r), z_in.at[q - 1], place.z_id(q)) for q in range(1, 4)
        ]

    def compute(self, q, left, right):
        part = self.blocks.shape[1]
        step = min(256, part)
        start = lax.rem(self.place.z + q, 4) * part

        def one(i, carry):
            product = mm_tn(left[:, tile(start + i * step, step)], right())
            self.blocks[q, tile(i * step, step), :] = product.astype(BF16)
            return carry

        lax.fori_loop(0, part // step, one, 0)
        for one_copy in self.x_out[q]:
            one_copy.start()

    def pass_on(self, q):
        for one in self.x_out[q]:
            one.wait_recv()
        step = min(64, self.rows)
        start = self.place.r * self.rows

        def add(i, carry):
            at = tile(start + i * step, step)
            total = self.blocks[q, at, :].astype(F32)
            for s in range(self.place.spread - 1):
                total = total + self.x_in[s, q, tile(i * step, step), :].astype(F32)
            self.blocks[q, at, :] = total.astype(BF16)
            return carry

        lax.fori_loop(0, self.rows // step, add, 0)
        if q:
            self.z_out[q - 1].start()

    def finish(self):
        for one in self.z_out:
            one.wait_recv()
        step = min(64, self.rows)
        low = self.place.low
        start = self.place.r * self.rows

        def add(i, carry):
            at = tile(i * step, step)
            near = self.blocks[0, tile(start + i * step, step), :].astype(F32)
            near = (near + self.z_in[1, at, :].astype(F32)).astype(BF16)
            far = self.z_in[0, at, :].astype(F32) + self.z_in[2, at, :].astype(F32)
            far = far.astype(BF16)
            first = 0
            for out, size in self.outs:
                out[at, tile(low * size, size)] = near[:, first : first + size]
                out[at, tile((1 - low) * size, size)] = far[:, first : first + size]
                first += size
            return carry

        lax.fori_loop(0, self.rows // step, add, 0)

    def drain(self):
        for group in self.x_out:
            for one in group:
                one.wait_send()
        for one in self.z_out:
            one.wait_send()


ORDER = (2, 1, 3, 0)


def gate_up_back(ns, pair, slot, width=256):
    span = ns.joined.shape[0] // 4
    rows = tile(pair * span, span)
    ff = ns.product.shape[1]

    def step(j, carry):
        here, there = tile(j * width, width), tile(ff + j * width, width)
        d_act = mm(ns.joined[rows, :], ns.wdown[:, here])
        gate = ns.stage[slot, :, here].astype(F32)
        up = ns.stage[slot, :, there].astype(F32)
        gated = 1.0 / (1.0 + jnp.exp(-gate))
        ns.d_gate[rows, here] = (d_act * up * gated * (1.0 + gate * (1.0 - gated))).astype(BF16)
        ns.d_up[rows, here] = (d_act * gate * gated).astype(BF16)
        return carry

    lax.fori_loop(0, ff // width, step, 0)


def head_back(ns, rows, d_out, raw, gain, d_gain, d_raw_columns):
    d_turned = d_out * ns.cosine[rows, :] + pltpu.roll(d_out * ns.sine[rows, :], HD // 2, axis=1)
    scale = scale_of(raw)
    normed = raw * scale
    d_gain[...] += jnp.sum(d_turned * normed, axis=0, keepdims=True)
    d_normed = d_turned * gain[...]
    inner = jnp.mean(d_normed * normed, axis=-1, keepdims=True)
    ns.d_raw[rows, d_raw_columns] = (scale * (d_normed - normed * inner)).astype(BF16)


def attend_back(ns, b):
    group = ns.bias.shape[1]
    span = ns.joined.shape[0] // 4
    q_size, kv_size = ns.q.shape[1], ns.k.shape[1]
    share = q_size // kv_size
    scale = HD**-0.5

    whole = slice(b * group, (b + 1) * group)
    for kv in range(kv_size // HD):
        columns = slice(kv * HD, (kv + 1) * HD)
        ns.d_keys[...] = jnp.zeros_like(ns.d_keys)
        ns.d_values[...] = jnp.zeros_like(ns.d_values)
        for e in range(kv * share, (kv + 1) * share):
            mine = slice(e * HD, (e + 1) * HD)
            for half in range(group // span):
                start = b * group + half * span
                rows = slice(start, start + span)
                seen = (half + 1) * span
                keys = ns.k[b * group : b * group + seen, columns]
                values = ns.v[b * group : b * group + seen, columns]
                query = ns.q[rows, mine]
                d_out = ns.d_att[rows, mine]
                s = mm_nt(query, keys) * scale
                s = s + ns.bias[b, half * span : (half + 1) * span, :seen].astype(F32)
                p = jnp.exp(s - jnp.max(s, axis=-1, keepdims=True))
                p = p / jnp.sum(p, axis=-1, keepdims=True)
                d_p = mm_nt(d_out, values)
                delta = jnp.sum(d_p * p, axis=-1, keepdims=True)
                d_s = (p * (d_p - delta)).astype(BF16)
                ns.d_values[:seen, :] += mm_tn(p.astype(BF16), d_out)
                ns.d_keys[:seen, :] += mm_tn(d_s, query)
                d_query = mm(d_s, keys) * scale
                head_back(ns, rows, d_query, ns.raw[rows, mine], ns.gain_q, ns.d_gain_q, mine)
        key_columns = slice(q_size + kv * HD, q_size + (kv + 1) * HD)
        d_keys = ns.d_keys[...] * scale
        head_back(ns, whole, d_keys, ns.raw[whole, key_columns], ns.gain_k, ns.d_gain_k, key_columns)
        value_columns = slice(q_size + kv_size + kv * HD, q_size + kv_size + (kv + 1) * HD)
        ns.d_raw[whole, value_columns] = ns.d_values[...].astype(BF16)


class GainSum:
    def __init__(self, links, place, terms, came, came_r, total):
        spread = place.spread
        self.place, self.terms, self.came, self.came_r, self.total = place, terms, came, came_r, total
        ids = (place.core_id, place.y_id, place.low_id, place.z_id(2))
        self.pairs = [links.remote(terms.at[i], came.at[i], one) for i, one in enumerate(ids)]
        self.sides = [
            links.remote(terms.at[4], came_r.at[place.r], place.r_id(s)) for s in range(1, spread)
        ]
        self.at = 0

    def start(self):
        self.pairs[0].start()

    def step(self):
        i = self.at
        self.at += 1
        if i < 4:
            self.pairs[i].wait_recv()
            self.terms[i + 1] = self.terms[i] + self.came[i]
            if i < 3:
                self.pairs[i + 1].start()
                return
            self.came_r[self.place.r] = self.terms[4]
            for one in self.sides:
                one.start()
            return
        for one in self.sides:
            one.wait_recv()
        total = self.came_r[0]
        for r in range(1, self.place.spread):
            total = total + self.came_r[r]
        self.total[...] = total
        for one in self.pairs + self.sides:
            one.wait_send()


def backward_layer_kernel(layer, spread, ns):
    first = layer == 0
    place = Place(spread)
    links = Links(ns.send, ns.recv)
    local = ns.grad.shape[0]
    own_rows = (place.own_pair * 2 + place.core) * local
    span = 2 * local
    width = ns.grad.shape[1]
    qkv, o, ff = ns.wqkv_in.shape[1], ns.wo_in.shape[1], ns.wdown_in.shape[1]
    kv = (qkv - o) // 2
    diag, y, z, own = place.pairs

    def loads(*pairs):
        copies = [links.copy(src, dst) for src, dst in pairs]
        for one in copies:
            one.start()
        return copies

    def wait(copies):
        for one in copies:
            one.wait()

    def reduce(i, outs):
        return Reduce(links, place, ns.blocks.at[i], ns.x_in.at[i], ns.z_in_w.at[i], outs)

    red_down = reduce(0, [(ns.g_mlp.at[2], ff)])
    red_gate = reduce(1, [(ns.g_mlp.at[0], ff)])
    red_up = reduce(2, [(ns.g_mlp.at[1], ff)])
    red_o = Reduce(links, place, ns.blocks_o, ns.x_in_o, ns.z_in_o, [(ns.g_o, o)])
    red_qkv = Reduce(
        links, place, ns.blocks_qkv, ns.x_in_qkv, ns.z_in_qkv,
        [(ns.g_q, o), (ns.g_kv.at[0], kv), (ns.g_kv.at[1], kv)],
    )
    mid_in = Spread(links, place, ns.joined)
    if not first:
        layer_out = Spread(links, place, ns.joined)
    else:
        gain_sum = GainSum(links, place, ns.terms, ns.came, ns.came_r, ns.gain_total)

    passes = [partial(one.pass_on, q) for one in (red_down, red_gate, red_up, red_o, red_qkv) for q in ORDER]

    def pass_next(count=1):
        for _ in range(count):
            passes.pop(0)()

    def compute_all(one, left, right):
        for q in ORDER:
            one.compute(q, left, right)

    def back_norm(value, grad, gain, d_gain, out, gather):
        def finish(at, total):
            v = value[at, :].astype(F32)
            scale = scale_of(v)
            normed = v * scale
            d_gain[...] += jnp.sum(total * normed, axis=0, keepdims=True)
            d_normed = total * gain[...]
            inner = jnp.mean(d_normed * normed, axis=-1, keepdims=True)
            g = grad[at, :].astype(F32) + scale * (d_normed - normed * inner)
            out[at, :] = g
            if gather:
                ns.joined[tile(own_rows + at.start, CHUNK), :] = g.astype(BF16)

        return finish

    for one in (ns.d_gain_attn, ns.d_gain_mlp, ns.d_gain_q, ns.d_gain_k):
        one[...] = jnp.zeros_like(one)

    def mlp_scope(wgate, wup, d_gate, d_up):
        ns.d_gate, ns.d_up = d_gate, d_up
        weight_loads = loads((ns.wgate_in, wgate), (ns.wup_in, wup))

        def down_scope(wdown, product, stage):
            ns.wdown, ns.product, ns.stage = wdown, product, stage
            first_loads = loads((ns.joined_in, ns.joined), (ns.product_in, product))
            down_load = loads((ns.wdown_in, wdown))
            gateup_loads = [
                links.copy(ns.gateup_in.at[tile(p * span, span)], stage.at[i % 2])
                for i, p in enumerate(place.pairs)
            ]
            for one in gateup_loads[:2]:
                one.start()
            place.greet()
            wait(first_loads)
            compute_all(red_down, ns.joined, lambda: product[...])
            wait(down_load)
            for i, pair in enumerate(place.pairs):
                gateup_loads[i].wait()
                gate_up_back(ns, pair, i % 2)
                if i + 2 < 4:
                    gateup_loads[i + 2].start()

        rows_all = ns.wdown_in.shape[0]
        pl.run_scoped(
            down_scope,
            pltpu.VMEM((rows_all, ff), BF16),
            pltpu.VMEM((8 * local, ff), BF16),
            pltpu.VMEM((2, span, 2 * ff), BF16),
        )

        def rest_scope(b):
            b_load = loads((ns.b_in, b))
            wait(weight_loads)

            def work(pair, columns=512):
                rows = tile(pair * span, span)

                def step(j, carry):
                    at = tile(j * columns, columns)
                    term = mm_nt(d_gate[rows, :], wgate[at, :]) + mm_nt(d_up[rows, :], wup[at, :])
                    ns.part[rows, at] = term.astype(BF16)
                    return carry

                lax.fori_loop(0, width // columns, step, 0)

            collect(
                links, place, ns, work,
                back_norm(ns.mid, ns.grad, ns.gain_mlp, ns.d_gain_mlp, ns.grad_mid, True),
                sent=[partial(wait, b_load), partial(compute_all, red_gate, b, lambda: d_gate[...]), pass_next],
                late=[partial(compute_all, red_up, b, lambda: d_up[...]), pass_next],
            )
            mid_in.start()
            pass_next()

        pl.run_scoped(rest_scope, pltpu.VMEM((8 * local, width), BF16))

    rows_all = ns.wdown_in.shape[0]
    total = 8 * local
    pl.run_scoped(
        mlp_scope,
        pltpu.VMEM((rows_all, ff), BF16),
        pltpu.VMEM((rows_all, ff), BF16),
        pltpu.VMEM((total, ff), BF16),
        pltpu.VMEM((total, ff), BF16),
    )

    def attention_scope(
        cosine, sine, bias, hidden, wqkv, wo, a, q, k, v, raw, att, d_att, d_raw, d_keys, d_values
    ):
        ns.cosine, ns.sine, ns.bias, ns.hidden = cosine, sine, bias, hidden
        ns.q, ns.k, ns.v, ns.raw, ns.att = q, k, v, raw, att
        ns.d_att, ns.d_raw, ns.d_keys, ns.d_values = d_att, d_raw, d_keys, d_values
        o_loads = loads((ns.wo_in, wo), (ns.att_in, att))
        other_loads = loads(
            (ns.q_in, q), (ns.k_in, k), (ns.v_in, v), (ns.raw_in, raw), (ns.cosine_in, cosine),
            (ns.sine_in, sine), (ns.bias_in, bias), (ns.a_in, a), (ns.wqkv_in, wqkv), (ns.hidden_in, hidden),
        )

        def d_attended(pair):
            rows = tile(pair * span, span)
            d_att[rows, :] = mm(ns.joined[rows, :], wo[...]).astype(BF16)

        mid_in.pass_z()
        mid_in.pass_y()
        pass_next()
        wait(o_loads)
        mid_in.own_ready()
        d_attended(own)
        mid_in.z_ready()
        d_attended(z)
        mid_in.pass_d()
        pass_next()
        mid_in.y_ready()
        d_attended(y)
        mid_in.d_ready()
        d_attended(diag)
        mid_in.drain()
        compute_all(red_o, ns.joined, lambda: att[...])
        pass_next()
        wait(other_loads)
        attend_back(ns, 0)
        pass_next(2)
        attend_back(ns, 1)
        pass_next(2)
        compute_all(red_qkv, a, lambda: d_raw[...])
        collect(
            links, place, ns, partial(project_out, ns, d_raw, wqkv),
            back_norm(hidden, ns.grad_mid, ns.gain_attn, ns.d_gain_attn, ns.out, not first),
            sent=[partial(pass_next, 2)],
            late=[partial(pass_next, 4), red_down.finish],
        )

    pl.run_scoped(
        attention_scope,
        pltpu.VMEM(ns.cosine_in.shape, F32),
        pltpu.VMEM(ns.sine_in.shape, F32),
        pltpu.VMEM(ns.bias_in.shape, BF16),
        pltpu.VMEM(ns.hidden_in.shape, ns.hidden_in.dtype),
        pltpu.VMEM((rows_all, qkv), BF16),
        pltpu.VMEM((rows_all, o), BF16),
        pltpu.VMEM((total, width), BF16),
        pltpu.VMEM(ns.q_in.shape, BF16),
        pltpu.VMEM(ns.k_in.shape, BF16),
        pltpu.VMEM(ns.v_in.shape, BF16),
        pltpu.VMEM(ns.raw_in.shape, F32),
        pltpu.VMEM(ns.att_in.shape, BF16),
        pltpu.VMEM((total, o), BF16),
        pltpu.VMEM((total, qkv), BF16),
        pltpu.VMEM((ns.bias_in.shape[1], HD), F32),
        pltpu.VMEM((ns.bias_in.shape[1], HD), F32),
    )
    if first:
        ns.terms[0] = jnp.zeros_like(ns.terms[0])
        earlier = (ns.later_attn, ns.later_mlp, ns.later_q, ns.later_k)
        here = (ns.d_gain_attn, ns.d_gain_mlp, ns.d_gain_q, ns.d_gain_k)
        for i, (attn, mlp, query, key) in enumerate((here, earlier)):
            ns.terms[0, 2 * i : 2 * i + 1, :width] = attn[...]
            ns.terms[0, 2 * i + 1 : 2 * i + 2, :width] = mlp[...]
            ns.terms[0, 2 * i : 2 * i + 1, width : width + HD] = query[...]
            ns.terms[0, 2 * i : 2 * i + 1, width + HD : width + 2 * HD] = key[...]
        gain_sum.start()
        for _ in range(4):
            pass_next()
            gain_sum.step()
        red_gate.finish()
        gain_sum.step()
    else:
        layer_out.start()
        pass_next()
        layer_out.pass_z()
        layer_out.pass_y()
        pass_next(2)
        layer_out.own_ready()
        layer_out.z_ready()
        layer_out.pass_d()
        pass_next()
        layer_out.y_ready()
        red_gate.finish()
        layer_out.d_ready()
        layer_out.drain()
        final = links.copy(ns.joined, ns.save_next)
        final.start()
    red_up.finish()
    red_o.finish()
    red_qkv.finish()
    for one in (red_down, red_gate, red_up, red_o, red_qkv):
        one.drain()
    if not first:
        final.wait()
    assert not passes and links.count <= ns.send.shape[0]


def backward_layer(layer, grad, grad_rows, kept, later, tables, gains, spread):
    rows, width = grad.shape
    first = layer == 0
    total = 8 * rows
    cosine, sine, bias = tables
    d_rows, ff = kept.save_wdown.shape
    o, qkv = kept.wo.shape[1], kept.wqkv.shape[1]
    part = d_rows // 4
    block = part // spread

    def row(start, size):
        return gains[layer : layer + 1, start : start + size]

    ins = dict(
        grad=(grad, True),
        joined_in=(grad_rows, False),
        mid=(kept.mid, True),
        hidden_in=(kept.hidden, False),
        product_in=(kept.product, False),
        gateup_in=(kept.save_gateup, False),
        b_in=(kept.save_b, False),
        a_in=(kept.a, False),
        wdown_in=(kept.save_wdown, False),
        wgate_in=(kept.wgate, False),
        wup_in=(kept.save_wup, False),
        wqkv_in=(kept.wqkv, False),
        wo_in=(kept.wo, False),
        q_in=(kept.q, False),
        k_in=(kept.k, False),
        v_in=(kept.v, False),
        raw_in=(kept.raw, False),
        att_in=(kept.att, False),
        gain_attn=(row(0, width), True),
        gain_mlp=(row(width, width), True),
        gain_q=(row(2 * width, HD), True),
        gain_k=(row(2 * width + HD, HD), True),
        cosine_in=(cosine, False),
        sine_in=(sine, False),
        bias_in=(bias, False),
    )
    outs = dict(
        out=((rows, width), F32, True),
        d_gain_attn=((1, width), F32, True),
        d_gain_mlp=((1, width), F32, True),
        d_gain_q=((1, HD), F32, True),
        d_gain_k=((1, HD), F32, True),
        g_q=((block, 2 * o), BF16, True),
        g_kv=((2, block, qkv - o), BF16, True),
        g_o=((block, 2 * o), BF16, True),
        g_mlp=((3, block, 2 * ff), BF16, True),
    )
    if first:
        ins.update(
            later_attn=(later.d_gain_attn, True), later_mlp=(later.d_gain_mlp, True),
            later_q=(later.d_gain_q, True), later_k=(later.d_gain_k, True),
        )
        outs.update(gain_total=((8, width + 2 * HD), F32, True))
    if not first:
        outs.update(save_next=((total, width), BF16, False))
    scratch = exchange_scratch(rows, width)
    side = spread - 1
    scratch.update(grad_mid=pltpu.VMEM((rows, width), F32))
    scratch.update(blocks=pltpu.VMEM((3, 4, part, ff), BF16))
    scratch.update(blocks_o=pltpu.VMEM((4, part, o), BF16))
    scratch.update(blocks_qkv=pltpu.VMEM((4, part, qkv), BF16))
    scratch.update(x_in=pltpu.VMEM((3, side, 4, block, ff), BF16))
    scratch.update(x_in_o=pltpu.VMEM((side, 4, block, o), BF16))
    scratch.update(x_in_qkv=pltpu.VMEM((side, 4, block, qkv), BF16))
    scratch.update(z_in_w=pltpu.VMEM((3, 3, block, ff), BF16))
    scratch.update(z_in_o=pltpu.VMEM((3, block, o), BF16))
    scratch.update(z_in_qkv=pltpu.VMEM((3, block, qkv), BF16))
    if first:
        small = (8, width + 2 * HD)
        scratch.update(terms=pltpu.VMEM((5, *small), F32))
        scratch.update(came=pltpu.VMEM((4, *small), F32))
        scratch.update(came_r=pltpu.VMEM((spread, *small), F32))
    count = 96 + 24 * spread
    scratch.update(send=pltpu.SemaphoreType.DMA((count,)))
    scratch.update(recv=pltpu.SemaphoreType.DMA((count,)))
    kernel = partial(backward_layer_kernel, layer, spread)
    return call(kernel, ins, outs, scratch, 6 if first else 5, "backward_layer")


def places(dp_size):
    spread = dp_size // 4
    me = lax.axis_index("dp")
    z = me // spread
    return spread, me, lax.rem(me, spread), lax.rem(z, 2), z // 2


def flip_lo(dp_size):
    spread = dp_size // 4
    return [(i, i + spread * (1 - 2 * ((i // spread) % 2))) for i in range(dp_size)]


def flip_hi(dp_size):
    spread = dp_size // 4
    return [(i, i + 2 * spread * (1 - 2 * (i // (2 * spread)))) for i in range(dp_size)]


def shift_r(dp_size, step):
    spread = dp_size // 4
    return [(i, (i // spread) * spread + (i % spread + step) % spread) for i in range(dp_size)]


def rope_tables(positions, head_size):
    half = head_size // 2
    frequency = jnp.power(THETA, -2.0 * jnp.arange(half, dtype=F32) / head_size)
    angle = positions.astype(F32)[:, None] * frequency[None, :]
    return (jnp.cos(angle)[:, None, :], jnp.sin(angle)[:, None, :])


def adamw(weight, first, second, grad, rate, decay):
    first_new = BETA_ONE * first + (1.0 - BETA_ONE) * grad
    second_new = BETA_TWO * second + (1.0 - BETA_TWO) * grad * grad
    first_hat = first_new / (1.0 - BETA_ONE**STEP)
    second_hat = second_new / (1.0 - BETA_TWO**STEP)
    weight_new = weight - rate * (first_hat / (jnp.sqrt(second_hat) + ADAM_EPS) + decay * weight)
    return (first_new, second_new, weight_new)


def body(
    tokens, cotangent, segment_ids, gains, gain_first, gain_second,
    query_weight, query_first, query_second,
    keyvalue_weight, keyvalue_first, keyvalue_second,
    output_weight, output_first, output_second,
    mlp_weight, mlp_first, mlp_second,
):
    dp_size = lax.axis_size("dp")
    spread, me, r, low, high = places(dp_size)
    layers = gains.shape[0]
    local_rows, width = tokens.shape
    group = segment_ids.shape[0]
    rows = 8 * local_rows
    index = jnp.arange(group, dtype=jnp.int32)
    other = lax.ppermute(segment_ids, "dp", flip_lo(dp_size))
    segments = jnp.stack([jnp.where(low == 0, segment_ids, other), jnp.where(low == 0, other, segment_ids)])
    positions = (index[None, :] - (segments - segments[:, :1])).reshape(rows)
    mask = (segments[:, :, None] == segments[:, None, :]) & (index[None, None, :] <= index[None, :, None])
    bias = jnp.where(mask, 0.0, -1e30).astype(BF16)
    cosine, sine = rope_tables(positions, HD)
    tables = (
        jnp.concatenate([cosine[:, 0], cosine[:, 0]], axis=1),
        jnp.concatenate([-sine[:, 0], sine[:, 0]], axis=1),
        bias,
    )
    masters = (query_weight, keyvalue_weight, output_weight, mlp_weight)

    hidden, carry = tokens, None
    saved = []
    for layer in range(layers):
        last = layer + 1 == layers
        kept = forward_layer(layer, last, hidden, carry, masters, tables, gains, cotangent, spread)
        if layer == 0:
            carry = (kept.save_a, kept.save_wqkv, kept.save_wo, kept.save_wgate)
        kept.hidden = hidden
        kept.a, kept.wqkv, kept.wo, kept.wgate = carry
        saved.append(kept)
        hidden = kept.out
        if not last:
            carry = (kept.save_next, kept.save_wnext_qkv, kept.save_wnext_o, kept.save_wnext_gate)

    block_output = hidden
    grad = cotangent
    grad_rows = saved[-1].save_next
    reduced = [None] * layers
    done = None
    for layer in reversed(range(layers)):
        done = backward_layer(layer, grad, grad_rows, saved[layer], done, tables, gains, spread)
        grad, grad_rows = done.out, None if layer == 0 else done.save_next
        reduced[layer] = [done.g_q, done.g_kv, done.g_o, done.g_mlp]
    stacked = [jnp.stack([entry[i] for entry in reduced]).astype(F32) for i in range(4)]
    sums = done.gain_total
    gain_total = jnp.stack(
        [
            jnp.concatenate([sums[2 * i, :width], sums[2 * i + 1, :width], sums[2 * i, width:]])
            for i in range(layers)
        ]
    )
    head_gain_grads = gain_total[:, 2 * width :]
    gain_new = adamw(gains, gain_first, gain_second, gain_total, GAIN_RATE, 0.0)
    query_new = adamw(query_weight, query_first, query_second, stacked[0], RATE, DECAY)
    keyvalue_new = adamw(keyvalue_weight, keyvalue_first, keyvalue_second, stacked[1], RATE, DECAY)
    output_new = adamw(output_weight, output_first, output_second, stacked[2], RATE * OUTPUT_FACTOR, DECAY)
    mlp_new = adamw(mlp_weight, mlp_first, mlp_second, stacked[3], RATE, DECAY)
    return (block_output, grad, *gain_new, head_gain_grads, *query_new, *keyvalue_new, *output_new, *mlp_new)


def solution(mesh):
    token = P(("dp", "tensor"), None)
    flat = P(None, "dp", "tensor")
    deep = P(None, None, "dp", "tensor")
    placed = (token, token, P("dp"), P(), P(), P(), *[flat] * 3, *[deep] * 3, *[flat] * 3, *[deep] * 3)
    outs = (token, token, P(), P(), P(), P(), *[flat] * 3, *[deep] * 3, *[flat] * 3, *[deep] * 3)
    return jax.shard_map(body, mesh=mesh, in_specs=placed, out_specs=outs, check_vma=False)
```

```python
from functools import partial
import math
from types import SimpleNamespace

import jax
import jax.numpy as jnp
from jax import lax
from jax.experimental import pallas as pl
from jax.experimental.pallas import tpu as pltpu
from jax.sharding import PartitionSpec as P

HD = 128
STEP = 10
EPSILON = 1e-06
THETA = 1000000.0
BETA_ONE = 0.9
BETA_TWO = 0.95
ADAM_EPS = 1e-08
DECAY = 0.1
RATE = 0.05
GAIN_RATE = 0.8
OUTPUT_FACTOR = math.sqrt(128)

BF16 = jnp.bfloat16
F32 = jnp.float32
MESH = pl.DeviceIdType.MESH
CHUNK = 32
VMEM_LIMIT = 62 * 1024 * 1024


class Place:
    def __init__(self, spread):
        self.spread = spread
        self.dp = lax.axis_index("dp")
        self.tensor = lax.axis_index("tensor")
        self.core = lax.rem(self.tensor, 2)
        self.y = self.tensor // 2
        self.z = self.dp // spread
        self.r = lax.rem(self.dp, spread)
        self.low = lax.rem(self.z, 2)
        self.core_id = {"dp": self.dp, "tensor": self.y * 2 + 1 - self.core}
        self.y_id = {"dp": self.dp, "tensor": (1 - self.y) * 2 + self.core}
        self.low_id = {"dp": self.dp + spread * (1 - 2 * self.low), "tensor": self.tensor}
        self.own_pair = self.low * 2 + self.y
        self.pairs = (
            (1 - self.low) * 2 + 1 - self.y,
            self.low * 2 + 1 - self.y,
            (1 - self.low) * 2 + self.y,
            self.own_pair,
        )

    def z_dp(self, step):
        return lax.rem(self.z + 4 + step, 4) * self.spread + self.r

    def z_id(self, step):
        return {"dp": self.z_dp(step), "tensor": self.tensor}

    def r_dp(self, step):
        return self.z * self.spread + lax.rem(self.r + self.spread + step, self.spread)

    def r_id(self, step):
        return {"dp": self.r_dp(step), "tensor": self.tensor}

    def greet(self):
        ids = [self.core_id, self.y_id]
        ids += [self.z_id(k) for k in range(1, 4)]
        ids += [self.r_id(k) for k in range(1, self.spread)]
        barrier = pltpu.get_barrier_semaphore()
        for one in ids:
            pl.semaphore_signal(barrier, inc=1, device_id=one, device_id_type=MESH)
        pl.semaphore_wait(barrier, len(ids))


class Links:
    def __init__(self, send, recv):
        self.send, self.recv, self.count = send, recv, 0
        self.local = []

    def remote(self, src, dst, to):
        slot = self.count
        self.count += 1
        return pltpu.make_async_remote_copy(
            src_ref=src, dst_ref=dst, send_sem=self.send.at[slot], recv_sem=self.recv.at[slot],
            device_id=to, device_id_type=MESH,
        )

    def copy(self, src, dst):
        slot = self.count
        self.count += 1
        return pltpu.make_async_copy(src, dst, self.send.at[slot])


def tile(start, size):
    return pl.ds(pl.multiple_of(start, size), size)


class Spread:
    def __init__(self, links, place, joined, start, rows):
        def block(pair, core):
            return joined.at[pair * 2 + core, pl.ds(start, rows)]

        c = place.core
        diag, y, z, own = place.pairs
        own, from_z, from_y, from_d = (block(p, c) for p in (own, z, y, diag))
        self.to_z = links.remote(own, own, place.low_id)
        self.to_y = links.remote(own, own, place.y_id)
        self.to_core = links.remote(own, own, place.core_id)
        self.on_y = links.remote(from_z, from_z, place.y_id)
        self.core_z = links.remote(from_z, from_z, place.core_id)
        self.core_y = links.remote(from_y, from_y, place.core_id)
        self.core_d = links.remote(from_d, from_d, place.core_id)

    def start(self):
        self.to_z.start()
        self.to_y.start()
        self.to_core.start()

    def pass_on(self):
        self.to_z.wait_recv()
        self.on_y.start()
        self.core_z.start()
        self.to_y.wait_recv()
        self.core_y.start()

    def pass_last(self):
        self.on_y.wait_recv()
        self.core_d.start()

    def ready(self):
        for one in (self.to_core, self.core_z, self.core_y, self.core_d):
            one.wait_recv()

    def drain(self):
        for one in (self.to_z, self.to_y, self.to_core, self.on_y, self.core_z, self.core_y, self.core_d):
            one.wait_send()


class Collect:
    def __init__(self, links, place, ns, start, rows):
        self.place, self.ns, self.start, self.rows = place, ns, start, rows
        here = pl.ds(start, rows)
        self.across = [
            links.remote(ns.part.at[p * 2 + 1 - place.core, here], ns.core_in.at[k, here], place.core_id)
            for k, p in enumerate(place.pairs)
        ]
        self.diag = links.remote(ns.sums.at[0, here], ns.y_in.at[0, here], place.y_id)
        self.to_y = links.remote(ns.sums.at[1, here], ns.y_in.at[1, here], place.y_id)
        self.to_z = links.remote(ns.sums.at[2, here], ns.z_in.at[here], place.low_id)

    def cross(self, *which):
        for k in which:
            self.across[k].start()

    def term(self, k, at):
        block = self.place.pairs[k] * 2 + self.place.core
        return self.ns.part[block, at, :].astype(F32) + self.ns.core_in[k, at, :].astype(F32)

    def each(self, work):
        def step(i, carry):
            work(tile(self.start + i * CHUNK, CHUNK))
            return carry

        lax.fori_loop(0, self.rows // CHUNK, step, 0)

    def add(self, k):
        def work(at):
            total = self.term(k, at)
            if k == 2:
                total = total + self.ns.y_in[0, at, :].astype(F32)
            self.ns.sums[k, at, :] = total.astype(BF16)

        self.each(work)

    def send_y(self):
        self.across[0].wait_recv()
        self.add(0)
        self.diag.start()
        self.across[1].wait_recv()
        self.add(1)
        self.to_y.start()

    def send_z(self):
        self.across[2].wait_recv()
        self.diag.wait_recv()
        self.add(2)
        self.to_z.start()

    def end(self, finish):
        self.across[3].wait_recv()
        self.to_y.wait_recv()
        self.to_z.wait_recv()

        def work(at):
            total = self.term(3, at) + self.ns.y_in[1, at, :].astype(F32) + self.ns.z_in[at, :].astype(F32)
            finish(at, total)

        self.each(work)
        for one in (*self.across, self.diag, self.to_y, self.to_z):
            one.wait_send()


class Halves:
    def __init__(self, links, place, ns, joined):
        rows = ns.part.shape[1] // 2
        self.size = rows
        self.starts = (0, rows)
        self.sums = [Collect(links, place, ns, start, rows) for start in self.starts]
        self.back = joined is not None
        if self.back:
            self.spread = [Spread(links, place, joined, start, rows) for start in self.starts]


def take(ref, pairs, start, size, columns=slice(None)):
    parts = [ref[pl.ds(p * 2, 2), start : start + size, columns] for p in pairs]
    return jnp.concatenate([one.reshape(2 * size, -1) for one in parts], axis=0)


def put(ref, pairs, start, size, value, columns=slice(None)):
    for i, p in enumerate(pairs):
        part = value[2 * i * size : 2 * (i + 1) * size]
        ref[pl.ds(p * 2, 2), start : start + size, columns] = part.reshape(2, size, -1)


class Gather:
    def __init__(self, links, place, sources, own, stage, land, save):
        rows = own.shape[1]
        self.place, self.own, self.land, self.rows, self.stage = place, own, land, rows, stage
        self.starts, self.loads = [], []
        start = 0
        for one in sources:
            size = one.shape[1]
            self.starts.append((start, size // 2))
            self.loads.append(links.copy(one, stage.at[:, start : start + size]))
            start += size
        spread = place.spread

        def at(dp):
            return land.at[tile(dp * rows, rows)]

        mine = at(place.dp)
        self.out = [
            links.remote(own.at[lax.rem(place.low + k, 2)], mine, place.z_id(k)) for k in range(1, 4)
        ]
        self.side = [links.remote(own.at[place.low], mine, place.r_id(s)) for s in range(1, spread)]
        self.on = [
            [
                links.remote(at(place.z_dp(-k)), at(place.z_dp(-k)), place.r_id(s))
                for s in range(1, spread)
            ]
            for k in range(1, 4)
        ]
        self.save = links.copy(land, save)

    def load(self):
        for one in self.loads:
            one.start()

    def cast(self):
        for one in self.loads:
            one.wait()
        step = min(64, self.rows)

        def round_rows(i, carry):
            at = tile(i * step, step)
            for low in range(2):
                to = 0
                for start, half in self.starts:
                    piece = self.stage[at, start + low * half : start + (low + 1) * half]
                    self.own[low, at, to : to + half] = piece.astype(BF16)
                    to += half
            return carry

        lax.fori_loop(0, self.rows // step, round_rows, 0)

    def begin(self):
        for one in self.side:
            one.start()
        step = min(64, self.rows)

        def copy(i, carry):
            self.land[tile(self.place.dp * self.rows + i * step, step), :] = self.own[
                self.place.low, tile(i * step, step), :
            ]
            return carry

        lax.fori_loop(0, self.rows // step, copy, 0)

    def forward(self, k):
        self.out[k].wait_recv()
        for one in self.on[k]:
            one.start()

    def finish(self):
        for one in self.side:
            one.wait_recv()
        for group in self.on:
            for one in group:
                one.wait_recv()
        self.save.start()

    def drain(self):
        for one in self.out + self.side:
            one.wait_send()
        for group in self.on:
            for one in group:
                one.wait_send()
        self.save.wait()


class Stream:
    def __init__(self, groups):
        self.groups = groups
        self.order = [one for group in groups for one in group]
        self.items = [(group, k) for group in groups for k in range(3)]
        self.sent = self.passed = 0
        for one in self.order[:2]:
            one.load()

    def send(self, count=1):
        for group, k in self.items[self.sent : self.sent + count]:
            for one in group:
                if k == 0:
                    one.cast()
                    at = self.order.index(one) + 2
                    if at < len(self.order):
                        self.order[at].load()
                    one.begin()
                one.out[k].start()
            self.sent += 1

    def forward(self, count=1):
        for group, k in self.items[self.passed : min(self.passed + count, self.sent)]:
            for one in group:
                one.forward(k)
            self.passed += 1

    def tick(self, lag=2):
        self.send()
        if self.passed + lag < self.sent or self.sent == len(self.items):
            self.forward()

    def need(self, one):
        place = [i for i, group in enumerate(self.groups) if one in group][0] * 3 + 3
        self.send(max(0, place - self.sent))
        self.forward(max(0, place - self.passed))
        one.finish()

    def rest(self):
        self.send(len(self.items))
        self.forward(len(self.items))


def scale_of(v):
    return lax.rsqrt(jnp.mean(v * v, axis=-1, keepdims=True) + EPSILON)


def mm(a, b):
    return jnp.dot(a, b, preferred_element_type=F32)


def mm_nt(a, b):
    return lax.dot_general(a, b, (((1,), (1,)), ((), ())), preferred_element_type=F32)


def project_heads(ns, pair):
    block = ns.joined.shape[1]
    two = pl.ds(pair * 2, 2)
    x = ns.joined[two].reshape(2 * block, -1)
    raw = mm(x, ns.wqkv[...])
    ns.raw[two] = raw.reshape(2, block, -1)
    cosine, sine = ns.cosine[two].reshape(2 * block, HD), ns.sine[two].reshape(2 * block, HD)
    q_size, kv_size = ns.q.shape[2], ns.k.shape[2]

    def heads(out, start, size, gain):
        for h in range(size // HD):
            v = raw[:, start + h * HD : start + (h + 1) * HD]
            v = v * scale_of(v) * gain[...]
            turned = v * cosine + pltpu.roll(v, HD // 2, axis=1) * sine
            out[two, :, h * HD : (h + 1) * HD] = turned.astype(BF16).reshape(2, block, HD)

    heads(ns.q, 0, q_size, ns.gain_q)
    heads(ns.k, q_size, kv_size, ns.gain_k)
    ns.v[two] = raw[:, q_size + kv_size :].astype(BF16).reshape(2, block, kv_size)


def softmax(ns, b, half, span, query, keys):
    seen = keys.shape[0]
    s = mm_nt(query, keys) * HD**-0.5
    s = s + ns.bias[b, half * span : (half + 1) * span, :seen].astype(F32)
    p = jnp.exp(s - jnp.max(s, axis=-1, keepdims=True))
    return p / jnp.sum(p, axis=-1, keepdims=True)


def attend(ns, b):
    block = ns.joined.shape[1]
    span = 2 * block
    q_heads = ns.q.shape[2] // HD
    share = q_heads // (ns.k.shape[2] // HD)
    for e in range(q_heads):
        kv = slice((e // share) * HD, (e // share + 1) * HD)
        mine = slice(e * HD, (e + 1) * HD)
        for half in range(2):
            rows = slice(4 * b + 2 * half, 4 * b + 2 * half + 2)
            seen = slice(4 * b, 4 * b + 2 * half + 2)
            keys = ns.k[seen, :, kv].reshape(-1, HD)
            values = ns.v[seen, :, kv].reshape(-1, HD)
            query = ns.q[rows, :, mine].reshape(span, HD)
            p = softmax(ns, b, half, span, query, keys)
            ns.att[rows, :, mine] = mm(p.astype(BF16), values).astype(BF16).reshape(2, block, HD)


def project_out(ns, source, weight, pairs, start, size, width=1024):
    x = take(source, pairs, start, size)

    def step(j, carry):
        at = tile(j * width, width)
        put(ns.part, pairs, start, size, mm_nt(x, weight[at, :]).astype(BF16), at)
        return carry

    lax.fori_loop(0, ns.part.shape[2] // width, step, 0)


def gate_up(ns, pairs, start, size, slot):
    ff = ns.product.shape[2]
    x = take(ns.joined, pairs, start, size)
    gate = mm(x, ns.wgate[...])
    up = mm(x, ns.wup[...])
    ns.gu_stage[slot, :, :, :ff] = gate.astype(BF16).reshape(4, size, ff)
    ns.gu_stage[slot, :, :, ff:] = up.astype(BF16).reshape(4, size, ff)
    put(ns.product, pairs, start, size, (gate / (1.0 + jnp.exp(-gate)) * up).astype(BF16))


def forward_layer_kernel(layer, last, spread, ns):
    first = layer == 0
    place = Place(spread)
    links = Links(ns.send, ns.recv)
    local = ns.hidden.shape[0]
    mine = place.own_pair * 2 + place.core
    gathers = []

    def gather(own, land, save, *sources):
        stage = ns.stage.at[len(gathers) % 2]
        gathers.append(Gather(links, place, sources, own, stage, land, save))
        return gathers[-1]

    def attention_weights(at):
        kv = ns.keyvalue_weight
        return (ns.query_weight.at[at], kv.at[at, 0], kv.at[at, 1]), ns.output_weight.at[at]

    mlp = ns.mlp_weight
    if first:
        qkv_source, o_source = attention_weights(layer)
        get_qkv = gather(ns.own_qkv, ns.wqkv, ns.save_wqkv, *qkv_source)
        get_o = gather(ns.own_o, ns.wo, ns.save_wo, o_source)
        get_gate = gather(ns.own_gate, ns.wgate, ns.save_wgate, mlp.at[layer, 0])
    get_up = gather(ns.own_up, ns.wup, ns.save_wup, mlp.at[layer, 1])
    get_down = gather(ns.own_down, ns.wdown, ns.save_wdown, mlp.at[layer, 2])
    if not last:
        qkv_source, o_source = attention_weights(layer + 1)
        next_qkv = gather(ns.own_next_qkv, ns.wnext_qkv, ns.save_wnext_qkv, *qkv_source)
        next_o = gather(ns.own_next_o, ns.wnext_o, ns.save_wnext_o, o_source)
        next_gate = gather(ns.own_next_gate, ns.wnext_gate, ns.save_wnext_gate, mlp.at[layer + 1, 0])
    groups = [[get_qkv], [get_o], [get_gate]] if first else []
    groups += [[get_up], [get_down]]
    if not last:
        groups += [[next_qkv, next_o], [next_gate]]
    stream = Stream(groups)
    tick = stream.tick
    diag, y, z, own = place.pairs
    first_pairs, last_pairs = (diag, y), (z, own)
    heads = partial(project_heads, ns)
    if first:
        tokens_in = Spread(links, place, ns.joined, 0, local)
    if last:
        grads_in = Spread(links, place, ns.joined_grad, 0, local)
    middle = Halves(links, place, ns, ns.joined)
    end = Halves(links, place, ns, None if last else ns.joined)
    size = middle.size

    if first:
        def norm(i, carry):
            at = tile(i * CHUNK, CHUNK)
            v = ns.hidden[at, :].astype(F32)
            ns.joined[mine, at, :] = (v * scale_of(v) * ns.gain_attn[...]).astype(BF16)
            return carry

        lax.fori_loop(0, local // CHUNK, norm, 0)
        place.greet()
        tokens_in.start()
        stream.send(3)
        tokens_in.pass_on()
        stream.send()
        stream.forward()
        stream.send()
        stream.forward()
        stream.send()
        stream.forward()
        tokens_in.pass_last()
        tick()
        tick()
        tokens_in.ready()
        stream.need(get_qkv)
        heads(own)
        heads(z)
        tick()
        heads(y)
        heads(diag)
        tokens_in.drain()
        save_a = links.copy(ns.joined, ns.save_a)
        save_a.start()
        tick()
    else:
        loads = [
            links.copy(ns.joined_in, ns.joined),
            links.copy(ns.wqkv_in, ns.wqkv),
            links.copy(ns.wo_in, ns.wo),
        ]
        gate_load = links.copy(ns.wgate_in, ns.wgate)
        for one in loads:
            one.start()
        gate_load.start()
        if last:
            ns.joined_grad[mine] = ns.cotangent[...]
        place.greet()
        if last:
            grads_in.start()
        stream.send()
        for one in loads:
            one.wait()

        def every(i, carry):
            heads(i)
            return carry

        lax.fori_loop(0, 4, every, 0)
        gate_load.wait()
        if last:
            grads_in.pass_on()
        tick()

    attend(ns, 0)
    tick()
    attend(ns, 1)
    tick()
    if first:
        stream.need(get_o)
    if last:
        grads_in.pass_last()

    def middle_rows(at, total):
        v = ns.hidden[at, :].astype(F32) + total
        ns.mid[at, :] = v
        ns.joined[mine, at, :] = (v * scale_of(v) * ns.gain_mlp[...]).astype(BF16)

    def result_rows(at, total):
        v = ns.mid[at, :] + total
        ns.out[at, :] = v
        if not last:
            ns.joined[mine, at, :] = (v * scale_of(v) * ns.gain_next[...]).astype(BF16)

    def part_of(source, weight, halves, h):
        start = halves.starts[h]
        project_out(ns, source, weight, first_pairs, start, size)
        halves.sums[h].cross(0, 1)
        project_out(ns, source, weight, last_pairs, start, size)
        halves.sums[h].cross(2, 3)

    if first:
        save_a.wait()
    part_of(ns.att, ns.wo, middle, 0)
    middle.sums[0].send_y()
    part_of(ns.att, ns.wo, middle, 1)
    middle.sums[1].send_y()
    tick()
    middle.sums[0].send_z()
    middle.sums[1].send_z()
    tick()
    middle.sums[0].end(middle_rows)
    middle.spread[0].start()
    middle.sums[1].end(middle_rows)
    middle.spread[1].start()
    tick()
    middle.spread[0].pass_on()
    middle.spread[1].pass_on()
    tick()
    if first:
        stream.need(get_gate)
    stream.need(get_up)
    middle.spread[0].pass_last()
    middle.spread[0].ready()
    middle.spread[0].drain()
    saves = []

    def gate_up_of(pairs, start):
        slot = (len(saves) // 2) % 2
        if len(saves) >= 4:
            for save in saves[-4:-2]:
                save.wait()
        gate_up(ns, pairs, start, size, slot)
        for i, p in enumerate(pairs):
            save = links.copy(
                ns.gu_stage.at[slot, 2 * i : 2 * i + 2], ns.save_gateup.at[pl.ds(p * 2, 2), pl.ds(start, size)]
            )
            save.start()
            saves.append(save)

    save_b = [
        links.copy(ns.joined.at[:, pl.ds(start, size)], ns.save_b.at[:, pl.ds(start, size)])
        for start in middle.starts
    ]
    save_b[0].start()
    gate_up_of(first_pairs, 0)
    tick()
    middle.spread[1].pass_last()
    gate_up_of(last_pairs, 0)
    stream.need(get_down)
    save_b[0].wait()
    part_of(ns.product, ns.wdown, end, 0)
    middle.spread[1].ready()
    middle.spread[1].drain()
    end.sums[0].send_y()
    save_b[1].start()
    gate_up_of(first_pairs, size)
    end.sums[0].send_z()
    tick()
    gate_up_of(last_pairs, size)
    save_b[1].wait()
    part_of(ns.product, ns.wdown, end, 1)
    end.sums[1].send_y()
    end.sums[0].end(result_rows)
    if not last:
        end.spread[0].start()
    tick()
    end.sums[1].send_z()
    if not last:
        end.spread[0].pass_on()
    tick()
    end.sums[1].end(result_rows)
    if not last:
        end.spread[1].start()
        tick()
        end.spread[0].pass_last()
        end.spread[1].pass_on()
        tick()
        stream.rest()
        for one in (next_qkv, next_o):
            stream.need(one)
        end.spread[1].pass_last()
        for one in end.spread:
            one.ready()
            one.drain()
        final = links.copy(ns.joined, ns.save_next)
    else:
        grads_in.ready()
        grads_in.drain()
        final = links.copy(ns.joined_grad, ns.save_next)
    final.start()
    if not last:
        stream.need(next_gate)
    for save in saves[-4:]:
        save.wait()
    for one in gathers:
        one.drain()
    final.wait()
    assert stream.passed == len(stream.items) and links.count <= ns.send.shape[0]


def call(kernel, ins, outs, scratch, collective_id, name):
    names = [*ins, *outs, *scratch]

    def run(*refs):
        kernel(SimpleNamespace(**dict(zip(names, refs))))

    def space(in_vmem):
        return pl.BlockSpec(memory_space=pltpu.VMEM if in_vmem else pl.ANY)

    results = pl.pallas_call(
        run,
        out_shape=[jax.ShapeDtypeStruct(shape, dtype) for shape, dtype, _ in outs.values()],
        in_specs=[space(v) for _, v in ins.values()],
        out_specs=[space(v) for _, _, v in outs.values()],
        scratch_shapes=list(scratch.values()),
        compiler_params=pltpu.CompilerParams(
            collective_id=collective_id, has_side_effects=True, vmem_limit_bytes=VMEM_LIMIT
        ),
        cost_estimate=pl.CostEstimate(
            flops=13 * 10**9, bytes_accessed=10**8, transcendentals=10**6
        ),
        name=name,
    )(*[array for array, _ in ins.values()])
    return SimpleNamespace(**dict(zip(outs, results)))


def exchange_scratch(rows, width):
    return dict(
        joined=pltpu.VMEM((8, rows, width), BF16),
        part=pltpu.VMEM((8, rows, width), BF16),
        core_in=pltpu.VMEM((4, rows, width), BF16),
        y_in=pltpu.VMEM((2, rows, width), BF16),
        z_in=pltpu.VMEM((rows, width), BF16),
        sums=pltpu.VMEM((3, rows, width), BF16),
    )


def forward_layer(layer, last, hidden, carry, masters, tables, gains, cotangent, spread):
    rows, width = hidden.shape
    query, keyvalue, output, mlp = masters
    first = layer == 0
    own = query.shape[1]
    d_rows = own * 4 * spread
    o, ff = query.shape[2] // 2, mlp.shape[3] // 2
    kv = keyvalue.shape[3] // 2
    qkv = o + 2 * kv
    cosine, sine, bias = tables

    def row(at, start, size):
        return (gains[at : at + 1, start : start + size], True)

    ins = dict(
        hidden=(hidden, True),
        query_weight=(query, False),
        keyvalue_weight=(keyvalue, False),
        output_weight=(output, False),
        mlp_weight=(mlp, False),
    )
    if first:
        ins.update(gain_attn=row(layer, 0, width))
    else:
        joined_in, wqkv_in, wo_in, wgate_in = ((one, False) for one in carry)
        ins.update(joined_in=joined_in, wqkv_in=wqkv_in, wo_in=wo_in, wgate_in=wgate_in)
    if last:
        ins.update(cotangent=(cotangent, True))
    else:
        ins.update(gain_next=row(layer + 1, 0, width))
    ins.update(gain_mlp=row(layer, width, width))
    ins.update(gain_q=row(layer, 2 * width, HD))
    ins.update(gain_k=row(layer, 2 * width + HD, HD))
    ins.update(cosine=(cosine, True), sine=(sine, True), bias=(bias, True))
    outs = dict(
        out=((rows, width), F32, True),
        mid=((rows, width), F32, True),
        raw=((8, rows, o + 2 * kv), F32, True),
        q=((8, rows, o), BF16, True),
        k=((8, rows, kv), BF16, True),
        v=((8, rows, kv), BF16, True),
        att=((8, rows, o), BF16, True),
        product=((8, rows, ff), BF16, True),
        save_gateup=((8, rows, 2 * ff), BF16, False),
        save_b=((8, rows, width), BF16, False),
        save_next=((8, rows, width), BF16, False),
    )
    scratch = exchange_scratch(rows, width)
    scratch.update(gu_stage=pltpu.VMEM((2, 4, rows // 2, 2 * ff), BF16))
    scratch.update(stage=pltpu.VMEM((2, own, max(2 * ff, 2 * (o + 2 * kv))), F32))
    weight = lambda size: pltpu.VMEM((d_rows, size), BF16)
    mine = lambda size: pltpu.VMEM((2, own, size), BF16)
    saved = lambda size: ((d_rows, size), BF16, False)
    scratch.update(wqkv=weight(qkv), wo=weight(o), wgate=weight(ff), wup=weight(ff), wdown=weight(ff))
    scratch.update(own_up=mine(ff), own_down=mine(ff))
    outs.update(save_wup=saved(ff), save_wdown=saved(ff))
    if first:
        outs.update(save_a=((8, rows, width), BF16, False))
        scratch.update(own_qkv=mine(qkv), own_o=mine(o), own_gate=mine(ff))
        outs.update(save_wqkv=saved(qkv), save_wo=saved(o), save_wgate=saved(ff))
    if last:
        scratch.update(joined_grad=pltpu.VMEM((8, rows, width), BF16))
    else:
        scratch.update(wnext_qkv=weight(qkv), wnext_o=weight(o), wnext_gate=weight(ff))
        scratch.update(own_next_qkv=mine(qkv), own_next_o=mine(o), own_next_gate=mine(ff))
        outs.update(save_wnext_qkv=saved(qkv), save_wnext_o=saved(o), save_wnext_gate=saved(ff))
    count = 72 + 40 * spread
    scratch.update(send=pltpu.SemaphoreType.DMA((count,)))
    scratch.update(recv=pltpu.SemaphoreType.DMA((count,)))
    kernel = partial(forward_layer_kernel, layer, last, spread)
    return call(kernel, ins, outs, scratch, 1 + int(last) + 2 * int(not first), "forward_layer")


def mm_tn(a, b):
    return lax.dot_general(a, b, (((0,), (0,)), ((), ())), preferred_element_type=F32)


class Reduce:
    def __init__(self, links, place, blocks, x_in, z_in, outs):
        self.place, self.blocks, self.x_in, self.z_in, self.outs = place, blocks, x_in, z_in, outs
        spread = place.spread
        rows = blocks.shape[1] // spread
        self.rows = rows

        def block(q, r):
            return blocks.at[q, tile(r * rows, rows)]

        self.x_out = [
            [
                links.remote(
                    block(q, lax.rem(place.r + s, spread)), x_in.at[s - 1, q], place.r_id(s)
                )
                for s in range(1, spread)
            ]
            for q in range(4)
        ]
        self.z_out = [
            links.remote(block(q, place.r), z_in.at[q - 1], place.z_id(q)) for q in range(1, 4)
        ]

    def compute(self, q, left, right):
        part = self.blocks.shape[1]
        step = min(256, part)
        start = lax.rem(self.place.z + q, 4) * part

        def one(i, carry):
            x = left[:, :, tile(start + i * step, step)]
            product = mm_tn(x.reshape(-1, step), right())
            self.blocks[q, tile(i * step, step), :] = product.astype(BF16)
            return carry

        lax.fori_loop(0, part // step, one, 0)
        for one_copy in self.x_out[q]:
            one_copy.start()

    def pass_on(self, q):
        for one in self.x_out[q]:
            one.wait_recv()
        step = min(64, self.rows)
        start = self.place.r * self.rows

        def add(i, carry):
            at = tile(start + i * step, step)
            total = self.blocks[q, at, :].astype(F32)
            for s in range(self.place.spread - 1):
                total = total + self.x_in[s, q, tile(i * step, step), :].astype(F32)
            self.blocks[q, at, :] = total.astype(BF16)
            return carry

        lax.fori_loop(0, self.rows // step, add, 0)
        if q:
            self.z_out[q - 1].start()

    def finish(self):
        for one in self.z_out:
            one.wait_recv()
        step = min(64, self.rows)
        low = self.place.low
        start = self.place.r * self.rows

        def add(i, carry):
            at = tile(i * step, step)
            near = self.blocks[0, tile(start + i * step, step), :].astype(F32)
            near = (near + self.z_in[1, at, :].astype(F32)).astype(BF16)
            far = self.z_in[0, at, :].astype(F32) + self.z_in[2, at, :].astype(F32)
            far = far.astype(BF16)
            first = 0
            for out, size in self.outs:
                out[at, tile(low * size, size)] = near[:, first : first + size]
                out[at, tile((1 - low) * size, size)] = far[:, first : first + size]
                first += size
            return carry

        lax.fori_loop(0, self.rows // step, add, 0)

    def drain(self):
        for group in self.x_out:
            for one in group:
                one.wait_send()
        for one in self.z_out:
            one.wait_send()


ORDER = (2, 1, 3, 0)


def gate_up_back(ns, pairs, start, size, slot):
    ff = ns.product.shape[2]
    d_act = mm(take(ns.joined, pairs, start, size), ns.wdown[...])
    gate = ns.stage[slot, :, :, :ff].reshape(4 * size, ff).astype(F32)
    up = ns.stage[slot, :, :, ff:].reshape(4 * size, ff).astype(F32)
    gated = 1.0 / (1.0 + jnp.exp(-gate))
    put(ns.d_gate, pairs, start, size, (d_act * up * gated * (1.0 + gate * (1.0 - gated))).astype(BF16))
    put(ns.d_up, pairs, start, size, (d_act * gate * gated).astype(BF16))


def head_back(ns, blocks, d_out, raw_columns, gain, d_gain):
    rows = d_out.shape[0]
    cosine, sine = ns.cosine[blocks].reshape(rows, HD), ns.sine[blocks].reshape(rows, HD)
    raw = ns.raw[blocks, :, raw_columns].reshape(rows, HD)
    d_turned = d_out * cosine + pltpu.roll(d_out * sine, HD // 2, axis=1)
    scale = scale_of(raw)
    normed = raw * scale
    d_gain[...] += jnp.sum(d_turned * normed, axis=0, keepdims=True)
    d_normed = d_turned * gain[...]
    inner = jnp.mean(d_normed * normed, axis=-1, keepdims=True)
    d_raw = (scale * (d_normed - normed * inner)).astype(BF16)
    ns.d_raw[blocks, :, raw_columns] = d_raw.reshape(-1, ns.raw.shape[1], HD)


def attend_back(ns, b):
    block = ns.joined.shape[1]
    span = 2 * block
    q_size, kv_size = ns.q.shape[2], ns.k.shape[2]
    share = q_size // kv_size
    scale = HD**-0.5
    whole = slice(4 * b, 4 * b + 4)
    for kv in range(kv_size // HD):
        columns = slice(kv * HD, (kv + 1) * HD)
        ns.d_keys[...] = jnp.zeros_like(ns.d_keys)
        ns.d_values[...] = jnp.zeros_like(ns.d_values)
        for e in range(kv * share, (kv + 1) * share):
            mine = slice(e * HD, (e + 1) * HD)
            for half in range(2):
                rows = slice(4 * b + 2 * half, 4 * b + 2 * half + 2)
                some = slice(4 * b, 4 * b + 2 * half + 2)
                seen = (half + 1) * span
                keys = ns.k[some, :, columns].reshape(seen, HD)
                values = ns.v[some, :, columns].reshape(seen, HD)
                query = ns.q[rows, :, mine].reshape(span, HD)
                d_out = ns.d_att[rows, :, mine].reshape(span, HD)
                p = softmax(ns, b, half, span, query, keys)
                d_p = mm_nt(d_out, values)
                delta = jnp.sum(d_p * p, axis=-1, keepdims=True)
                d_s = (p * (d_p - delta)).astype(BF16)
                ns.d_values[:seen, :] += mm_tn(p.astype(BF16), d_out)
                ns.d_keys[:seen, :] += mm_tn(d_s, query)
                head_back(ns, rows, mm(d_s, keys) * scale, mine, ns.gain_q, ns.d_gain_q)
        key_columns = slice(q_size + kv * HD, q_size + (kv + 1) * HD)
        head_back(ns, whole, ns.d_keys[...] * scale, key_columns, ns.gain_k, ns.d_gain_k)
        value_columns = slice(q_size + kv_size + kv * HD, q_size + kv_size + (kv + 1) * HD)
        ns.d_raw[whole, :, value_columns] = ns.d_values[...].astype(BF16).reshape(4, block, HD)


class GainSum:
    def __init__(self, links, place, terms, came, came_r, total):
        spread = place.spread
        self.place, self.terms, self.came, self.came_r, self.total = place, terms, came, came_r, total
        ids = (place.core_id, place.y_id, place.low_id, place.z_id(2))
        self.pairs = [links.remote(terms.at[i], came.at[i], one) for i, one in enumerate(ids)]
        self.sides = [
            links.remote(terms.at[4], came_r.at[place.r], place.r_id(s)) for s in range(1, spread)
        ]
        self.at = 0

    def start(self):
        self.pairs[0].start()

    def step(self):
        i = self.at
        self.at += 1
        if i < 4:
            self.pairs[i].wait_recv()
            self.terms[i + 1] = self.terms[i] + self.came[i]
            if i < 3:
                self.pairs[i + 1].start()
                return
            self.came_r[self.place.r] = self.terms[4]
            for one in self.sides:
                one.start()
            return
        for one in self.sides:
            one.wait_recv()
        total = self.came_r[0]
        for r in range(1, self.place.spread):
            total = total + self.came_r[r]
        self.total[...] = total
        for one in self.pairs + self.sides:
            one.wait_send()


def backward_layer_kernel(layer, spread, ns):
    first = layer == 0
    place = Place(spread)
    links = Links(ns.send, ns.recv)
    local = ns.grad_in.shape[0]
    mine = place.own_pair * 2 + place.core
    width = ns.grad_in.shape[1]
    qkv, o, ff = ns.wqkv_in.shape[1], ns.wo_in.shape[1], ns.wdown_in.shape[1]
    kv = (qkv - o) // 2
    diag, y, z, own = place.pairs

    def loads(*pairs):
        copies = [links.copy(src, dst) for src, dst in pairs]
        for one in copies:
            one.start()
        return copies

    def wait(copies):
        for one in copies:
            one.wait()

    def reduce(i, outs):
        return Reduce(links, place, ns.blocks.at[i], ns.x_in.at[i], ns.z_in_w.at[i], outs)

    red_down = reduce(0, [(ns.g_mlp.at[2], ff)])
    red_gate = reduce(1, [(ns.g_mlp.at[0], ff)])
    red_up = reduce(2, [(ns.g_mlp.at[1], ff)])
    red_o = Reduce(links, place, ns.blocks_o, ns.x_in_o, ns.z_in_o, [(ns.g_o, o)])
    red_qkv = Reduce(
        links, place, ns.blocks_qkv, ns.x_in_qkv, ns.z_in_qkv,
        [(ns.g_q, o), (ns.g_kv.at[0], kv), (ns.g_kv.at[1], kv)],
    )
    middle = Halves(links, place, ns, ns.joined)
    end = Halves(links, place, ns, None if first else ns.joined)
    size = middle.size
    first_pairs, last_pairs = (diag, y), (z, own)
    if first:
        gain_sum = GainSum(links, place, ns.terms, ns.came, ns.came_r, ns.gain_total)

    passes = [partial(one.pass_on, q) for one in (red_down, red_gate, red_up, red_o, red_qkv) for q in ORDER]

    def pass_next(count=1):
        for _ in range(count):
            passes.pop(0)()

    def compute_all(one, left, right):
        for q in ORDER:
            one.compute(q, left, right)

    def back_norm(value, grad, gain, d_gain, out, gather):
        def finish(at, total):
            v = value[at, :].astype(F32)
            scale = scale_of(v)
            normed = v * scale
            d_gain[...] += jnp.sum(total * normed, axis=0, keepdims=True)
            d_normed = total * gain[...]
            inner = jnp.mean(d_normed * normed, axis=-1, keepdims=True)
            g = grad[at, :].astype(F32) + scale * (d_normed - normed * inner)
            out[at, :] = g
            if gather:
                ns.joined[mine, at, :] = g.astype(BF16)

        return finish

    for one in (ns.d_gain_attn, ns.d_gain_mlp, ns.d_gain_q, ns.d_gain_k):
        one[...] = jnp.zeros_like(one)

    flat = lambda ref: lambda: ref[...].reshape(8 * local, -1)

    def mlp_scope(wgate, wup, d_gate, d_up):
        ns.d_gate, ns.d_up = d_gate, d_up
        weight_loads = loads((ns.wgate_in, wgate), (ns.wup_in, wup))

        def part_of(h, columns=1024):
            start = middle.starts[h]
            for which, pairs in ((0, first_pairs), (2, last_pairs)):
                gates, ups = take(d_gate, pairs, start, size), take(d_up, pairs, start, size)

                def step(j, carry):
                    at = tile(j * columns, columns)
                    term = mm_nt(gates, wgate[at, :]) + mm_nt(ups, wup[at, :])
                    put(ns.part, pairs, start, size, term.astype(BF16), at)
                    return carry

                lax.fori_loop(0, width // columns, step, 0)
                middle.sums[h].cross(which, which + 1)

        def down_scope(wdown, product, stage):
            ns.wdown, ns.product, ns.stage = wdown, product, stage
            first_loads = loads((ns.joined_in, ns.joined), (ns.product_in, product))
            down_load = loads((ns.wdown_in, wdown))
            chunks = [(start, pairs) for start in middle.starts for pairs in (first_pairs, last_pairs)]
            gateup_loads = [
                [
                    links.copy(
                        ns.gateup_in.at[pl.ds(p * 2, 2), pl.ds(start, size)], stage.at[i % 2, 2 * j : 2 * j + 2]
                    )
                    for j, p in enumerate(pairs)
                ]
                for i, (start, pairs) in enumerate(chunks)
            ]
            for group in gateup_loads[:2]:
                for one in group:
                    one.start()
            place.greet()
            wait(first_loads)
            compute_all(red_down, ns.joined, flat(product))
            wait(down_load)
            for i, (start, pairs) in enumerate(chunks):
                wait(gateup_loads[i])
                gate_up_back(ns, pairs, start, size, i % 2)
                if i < 2:
                    for one in gateup_loads[i + 2]:
                        one.start()
                if i == 1:
                    wait(weight_loads)
                    part_of(0)
                if i == 2:
                    middle.sums[0].send_y()

        pl.run_scoped(
            down_scope,
            pltpu.VMEM((rows_all, ff), BF16),
            pltpu.VMEM((8, local, ff), BF16),
            pltpu.VMEM((2, 4, size, 2 * ff), BF16),
        )

        def rest_scope(b, mid, grad):
            b_load = loads((ns.mid_in, mid), (ns.grad_in, grad), (ns.b_in, b))
            middle_rows = back_norm(mid, grad, ns.gain_mlp, ns.d_gain_mlp, ns.grad_mid, True)
            part_of(1)
            middle.sums[0].send_z()
            middle.sums[1].send_y()
            wait(b_load)
            compute_all(red_gate, b, flat(d_gate))
            middle.sums[0].end(middle_rows)
            middle.spread[0].start()
            middle.sums[1].send_z()
            pass_next()
            compute_all(red_up, b, flat(d_up))
            middle.sums[1].end(middle_rows)
            middle.spread[1].start()
            pass_next()

        pl.run_scoped(
            rest_scope,
            pltpu.VMEM((8, local, width), BF16),
            pltpu.VMEM((local, width), F32),
            pltpu.VMEM((local, width), ns.grad_in.dtype),
        )

    rows_all = ns.wdown_in.shape[0]
    group = ns.bias_in.shape[1]
    pl.run_scoped(
        mlp_scope,
        pltpu.VMEM((rows_all, ff), BF16),
        pltpu.VMEM((rows_all, ff), BF16),
        pltpu.VMEM((8, local, ff), BF16),
        pltpu.VMEM((8, local, ff), BF16),
    )

    def attention_scope(
        cosine, sine, bias, hidden, wqkv, wo, a, q, k, v, raw, att, d_att, d_raw, d_keys, d_values
    ):
        ns.cosine, ns.sine, ns.bias, ns.hidden = cosine, sine, bias, hidden
        ns.q, ns.k, ns.v, ns.raw, ns.att = q, k, v, raw, att
        ns.d_att, ns.d_raw, ns.d_keys, ns.d_values = d_att, d_raw, d_keys, d_values
        o_loads = loads((ns.wo_in, wo), (ns.att_in, att))
        other_loads = loads(
            (ns.q_in, q), (ns.k_in, k), (ns.v_in, v), (ns.raw_in, raw), (ns.cosine_in, cosine),
            (ns.sine_in, sine), (ns.bias_in, bias), (ns.a_in, a), (ns.wqkv_in, wqkv), (ns.hidden_in, hidden),
        )
        result_rows = back_norm(hidden, ns.grad_mid, ns.gain_attn, ns.d_gain_attn, ns.out, not first)

        def d_attended(h):
            start = middle.starts[h]
            middle.spread[h].ready()
            middle.spread[h].drain()
            for pairs in (first_pairs, last_pairs):
                put(d_att, pairs, start, size, mm(take(ns.joined, pairs, start, size), wo[...]).astype(BF16))

        def part_of(h):
            start = end.starts[h]
            project_out(ns, d_raw, wqkv, first_pairs, start, size)
            end.sums[h].cross(0, 1)
            project_out(ns, d_raw, wqkv, last_pairs, start, size)
            end.sums[h].cross(2, 3)

        middle.spread[0].pass_on()
        middle.spread[1].pass_on()
        pass_next()
        wait(o_loads)
        middle.spread[0].pass_last()
        d_attended(0)
        pass_next()
        middle.spread[1].pass_last()
        d_attended(1)
        compute_all(red_o, ns.joined, flat(att))
        pass_next(2)
        wait(other_loads)
        attend_back(ns, 0)
        pass_next(2)
        attend_back(ns, 1)
        pass_next(2)
        part_of(0)
        end.sums[0].send_y()
        part_of(1)
        end.sums[1].send_y()
        compute_all(red_qkv, a, flat(d_raw))
        end.sums[0].send_z()
        end.sums[1].send_z()
        pass_next(2)
        end.sums[0].end(result_rows)
        if not first:
            end.spread[0].start()
        pass_next(4)
        end.sums[1].end(result_rows)
        if not first:
            end.spread[1].start()
        red_down.finish()

    pl.run_scoped(
        attention_scope,
        pltpu.VMEM(ns.cosine_in.shape, F32),
        pltpu.VMEM(ns.sine_in.shape, F32),
        pltpu.VMEM(ns.bias_in.shape, BF16),
        pltpu.VMEM(ns.hidden_in.shape, ns.hidden_in.dtype),
        pltpu.VMEM((rows_all, qkv), BF16),
        pltpu.VMEM((rows_all, o), BF16),
        pltpu.VMEM((8, local, width), BF16),
        pltpu.VMEM(ns.q_in.shape, BF16),
        pltpu.VMEM(ns.k_in.shape, BF16),
        pltpu.VMEM(ns.v_in.shape, BF16),
        pltpu.VMEM(ns.raw_in.shape, F32),
        pltpu.VMEM(ns.att_in.shape, BF16),
        pltpu.VMEM((8, local, o), BF16),
        pltpu.VMEM((8, local, qkv), BF16),
        pltpu.VMEM((group, HD), F32),
        pltpu.VMEM((group, HD), F32),
    )
    if first:
        ns.terms[0] = jnp.zeros_like(ns.terms[0])
        earlier = (ns.later_attn, ns.later_mlp, ns.later_q, ns.later_k)
        here = (ns.d_gain_attn, ns.d_gain_mlp, ns.d_gain_q, ns.d_gain_k)
        for i, (attn, mlp, query, key) in enumerate((here, earlier)):
            ns.terms[0, 2 * i : 2 * i + 1, :width] = attn[...]
            ns.terms[0, 2 * i + 1 : 2 * i + 2, :width] = mlp[...]
            ns.terms[0, 2 * i : 2 * i + 1, width : width + HD] = query[...]
            ns.terms[0, 2 * i : 2 * i + 1, width + HD : width + 2 * HD] = key[...]
        gain_sum.start()
        for _ in range(4):
            pass_next()
            gain_sum.step()
        red_gate.finish()
        gain_sum.step()
    else:
        pass_next()
        end.spread[0].pass_on()
        end.spread[1].pass_on()
        pass_next(2)
        end.spread[0].pass_last()
        end.spread[1].pass_last()
        pass_next()
        red_gate.finish()
        for one in end.spread:
            one.ready()
            one.drain()
        final = links.copy(ns.joined, ns.save_next)
        final.start()
    red_up.finish()
    red_o.finish()
    red_qkv.finish()
    for one in (red_down, red_gate, red_up, red_o, red_qkv):
        one.drain()
    if not first:
        final.wait()
    assert not passes and links.count <= ns.send.shape[0]


def backward_layer(layer, grad, grad_rows, kept, later, tables, gains, spread):
    rows, width = grad.shape
    first = layer == 0
    cosine, sine, bias = tables
    d_rows, ff = kept.save_wdown.shape
    o, qkv = kept.wo.shape[1], kept.wqkv.shape[1]
    part = d_rows // 4
    block = part // spread

    def row(start, size):
        return gains[layer : layer + 1, start : start + size]

    ins = dict(
        grad_in=(grad, False),
        joined_in=(grad_rows, False),
        mid_in=(kept.mid, False),
        hidden_in=(kept.hidden, False),
        product_in=(kept.product, False),
        gateup_in=(kept.save_gateup, False),
        b_in=(kept.save_b, False),
        a_in=(kept.a, False),
        wdown_in=(kept.save_wdown, False),
        wgate_in=(kept.wgate, False),
        wup_in=(kept.save_wup, False),
        wqkv_in=(kept.wqkv, False),
        wo_in=(kept.wo, False),
        q_in=(kept.q, False),
        k_in=(kept.k, False),
        v_in=(kept.v, False),
        raw_in=(kept.raw, False),
        att_in=(kept.att, False),
        gain_attn=(row(0, width), True),
        gain_mlp=(row(width, width), True),
        gain_q=(row(2 * width, HD), True),
        gain_k=(row(2 * width + HD, HD), True),
        cosine_in=(cosine, False),
        sine_in=(sine, False),
        bias_in=(bias, False),
    )
    outs = dict(
        out=((rows, width), F32, True),
        d_gain_attn=((1, width), F32, True),
        d_gain_mlp=((1, width), F32, True),
        d_gain_q=((1, HD), F32, True),
        d_gain_k=((1, HD), F32, True),
        g_q=((block, 2 * o), BF16, True),
        g_kv=((2, block, qkv - o), BF16, True),
        g_o=((block, 2 * o), BF16, True),
        g_mlp=((3, block, 2 * ff), BF16, True),
    )
    if first:
        ins.update(
            later_attn=(later.d_gain_attn, True), later_mlp=(later.d_gain_mlp, True),
            later_q=(later.d_gain_q, True), later_k=(later.d_gain_k, True),
        )
        outs.update(gain_total=((8, width + 2 * HD), F32, True))
    if not first:
        outs.update(save_next=((8, rows, width), BF16, False))
    scratch = exchange_scratch(rows, width)
    side = spread - 1
    scratch.update(grad_mid=pltpu.VMEM((rows, width), F32))
    scratch.update(blocks=pltpu.VMEM((3, 4, part, ff), BF16))
    scratch.update(blocks_o=pltpu.VMEM((4, part, o), BF16))
    scratch.update(blocks_qkv=pltpu.VMEM((4, part, qkv), BF16))
    scratch.update(x_in=pltpu.VMEM((3, side, 4, block, ff), BF16))
    scratch.update(x_in_o=pltpu.VMEM((side, 4, block, o), BF16))
    scratch.update(x_in_qkv=pltpu.VMEM((side, 4, block, qkv), BF16))
    scratch.update(z_in_w=pltpu.VMEM((3, 3, block, ff), BF16))
    scratch.update(z_in_o=pltpu.VMEM((3, block, o), BF16))
    scratch.update(z_in_qkv=pltpu.VMEM((3, block, qkv), BF16))
    if first:
        small = (8, width + 2 * HD)
        scratch.update(terms=pltpu.VMEM((5, *small), F32))
        scratch.update(came=pltpu.VMEM((4, *small), F32))
        scratch.update(came_r=pltpu.VMEM((spread, *small), F32))
    count = 84 + 20 * spread
    scratch.update(send=pltpu.SemaphoreType.DMA((count,)))
    scratch.update(recv=pltpu.SemaphoreType.DMA((count,)))
    kernel = partial(backward_layer_kernel, layer, spread)
    return call(kernel, ins, outs, scratch, 6 if first else 5, "backward_layer")


def places(dp_size):
    spread = dp_size // 4
    me = lax.axis_index("dp")
    z = me // spread
    return spread, me, lax.rem(me, spread), lax.rem(z, 2), z // 2


def flip_lo(dp_size):
    spread = dp_size // 4
    return [(i, i + spread * (1 - 2 * ((i // spread) % 2))) for i in range(dp_size)]


def flip_hi(dp_size):
    spread = dp_size // 4
    return [(i, i + 2 * spread * (1 - 2 * (i // (2 * spread)))) for i in range(dp_size)]


def shift_r(dp_size, step):
    spread = dp_size // 4
    return [(i, (i // spread) * spread + (i % spread + step) % spread) for i in range(dp_size)]


def rope_tables(positions, head_size):
    half = head_size // 2
    frequency = jnp.power(THETA, -2.0 * jnp.arange(half, dtype=F32) / head_size)
    angle = positions.astype(F32)[:, None] * frequency[None, :]
    return (jnp.cos(angle)[:, None, :], jnp.sin(angle)[:, None, :])


def adamw(weight, first, second, grad, rate, decay):
    first_new = BETA_ONE * first + (1.0 - BETA_ONE) * grad
    second_new = BETA_TWO * second + (1.0 - BETA_TWO) * grad * grad
    first_hat = first_new / (1.0 - BETA_ONE**STEP)
    second_hat = second_new / (1.0 - BETA_TWO**STEP)
    weight_new = weight - rate * (first_hat / (jnp.sqrt(second_hat) + ADAM_EPS) + decay * weight)
    return (first_new, second_new, weight_new)


def body(
    tokens, cotangent, segment_ids, gains, gain_first, gain_second,
    query_weight, query_first, query_second,
    keyvalue_weight, keyvalue_first, keyvalue_second,
    output_weight, output_first, output_second,
    mlp_weight, mlp_first, mlp_second,
):
    dp_size = lax.axis_size("dp")
    spread, me, r, low, high = places(dp_size)
    layers = gains.shape[0]
    local_rows, width = tokens.shape
    group = segment_ids.shape[0]
    rows = 8 * local_rows
    index = jnp.arange(group, dtype=jnp.int32)
    other = lax.ppermute(segment_ids, "dp", flip_lo(dp_size))
    segments = jnp.stack([jnp.where(low == 0, segment_ids, other), jnp.where(low == 0, other, segment_ids)])
    positions = (index[None, :] - (segments - segments[:, :1])).reshape(rows)
    mask = (segments[:, :, None] == segments[:, None, :]) & (index[None, None, :] <= index[None, :, None])
    bias = jnp.where(mask, 0.0, -1e30).astype(BF16)
    cosine, sine = rope_tables(positions, HD)
    tables = (
        jnp.concatenate([cosine[:, 0], cosine[:, 0]], axis=1).reshape(8, local_rows, HD),
        jnp.concatenate([-sine[:, 0], sine[:, 0]], axis=1).reshape(8, local_rows, HD),
        bias,
    )
    masters = (query_weight, keyvalue_weight, output_weight, mlp_weight)

    hidden, carry = tokens, None
    saved = []
    for layer in range(layers):
        last = layer + 1 == layers
        kept = forward_layer(layer, last, hidden, carry, masters, tables, gains, cotangent, spread)
        if layer == 0:
            carry = (kept.save_a, kept.save_wqkv, kept.save_wo, kept.save_wgate)
        kept.hidden = hidden
        kept.a, kept.wqkv, kept.wo, kept.wgate = carry
        saved.append(kept)
        hidden = kept.out
        if not last:
            carry = (kept.save_next, kept.save_wnext_qkv, kept.save_wnext_o, kept.save_wnext_gate)

    block_output = hidden
    grad = cotangent
    grad_rows = saved[-1].save_next
    reduced = [None] * layers
    done = None
    for layer in reversed(range(layers)):
        done = backward_layer(layer, grad, grad_rows, saved[layer], done, tables, gains, spread)
        grad, grad_rows = done.out, None if layer == 0 else done.save_next
        reduced[layer] = [done.g_q, done.g_kv, done.g_o, done.g_mlp]
    stacked = [jnp.stack([entry[i] for entry in reduced]).astype(F32) for i in range(4)]
    sums = done.gain_total
    gain_total = jnp.stack(
        [
            jnp.concatenate([sums[2 * i, :width], sums[2 * i + 1, :width], sums[2 * i, width:]])
            for i in range(layers)
        ]
    )
    head_gain_grads = gain_total[:, 2 * width :]
    gain_new = adamw(gains, gain_first, gain_second, gain_total, GAIN_RATE, 0.0)
    query_new = adamw(query_weight, query_first, query_second, stacked[0], RATE, DECAY)
    keyvalue_new = adamw(keyvalue_weight, keyvalue_first, keyvalue_second, stacked[1], RATE, DECAY)
    output_new = adamw(output_weight, output_first, output_second, stacked[2], RATE * OUTPUT_FACTOR, DECAY)
    mlp_new = adamw(mlp_weight, mlp_first, mlp_second, stacked[3], RATE, DECAY)
    return (block_output, grad, *gain_new, head_gain_grads, *query_new, *keyvalue_new, *output_new, *mlp_new)


def solution(mesh):
    token = P(("dp", "tensor"), None)
    flat = P(None, "dp", "tensor")
    deep = P(None, None, "dp", "tensor")
    placed = (token, token, P("dp"), P(), P(), P(), *[flat] * 3, *[deep] * 3, *[flat] * 3, *[deep] * 3)
    outs = (token, token, P(), P(), P(), P(), *[flat] * 3, *[deep] * 3, *[flat] * 3, *[deep] * 3)
    return jax.shard_map(body, mesh=mesh, in_specs=placed, out_specs=outs, check_vma=False)
```

```python
from functools import partial
import math
from types import SimpleNamespace

import jax
import jax.numpy as jnp
from jax import lax
from jax.experimental import pallas as pl
from jax.experimental.pallas import tpu as pltpu
from jax.sharding import PartitionSpec as P

HD = 128
STEP = 10
EPSILON = 1e-06
THETA = 1000000.0
BETA_ONE = 0.9
BETA_TWO = 0.95
ADAM_EPS = 1e-08
DECAY = 0.1
RATE = 0.05
GAIN_RATE = 0.8
OUTPUT_FACTOR = math.sqrt(128)

BF16 = jnp.bfloat16
F32 = jnp.float32
MESH = pl.DeviceIdType.MESH
CHUNK = 32
VMEM_LIMIT = 62 * 1024 * 1024


class Place:
    def __init__(self, spread):
        self.spread = spread
        self.dp = lax.axis_index("dp")
        self.tensor = lax.axis_index("tensor")
        self.core = lax.rem(self.tensor, 2)
        self.y = self.tensor // 2
        self.z = self.dp // spread
        self.r = lax.rem(self.dp, spread)
        self.low = lax.rem(self.z, 2)
        self.core_id = {"dp": self.dp, "tensor": self.y * 2 + 1 - self.core}
        self.y_id = {"dp": self.dp, "tensor": (1 - self.y) * 2 + self.core}
        self.low_id = {"dp": self.dp + spread * (1 - 2 * self.low), "tensor": self.tensor}
        self.own_pair = self.low * 2 + self.y
        self.pairs = (
            (1 - self.low) * 2 + 1 - self.y,
            self.low * 2 + 1 - self.y,
            (1 - self.low) * 2 + self.y,
            self.own_pair,
        )

    def z_dp(self, step):
        return lax.rem(self.z + 4 + step, 4) * self.spread + self.r

    def z_id(self, step):
        return {"dp": self.z_dp(step), "tensor": self.tensor}

    def r_dp(self, step):
        return self.z * self.spread + lax.rem(self.r + self.spread + step, self.spread)

    def r_id(self, step):
        return {"dp": self.r_dp(step), "tensor": self.tensor}

    def greet(self):
        ids = [self.core_id, self.y_id]
        ids += [self.z_id(k) for k in range(1, 4)]
        ids += [self.r_id(k) for k in range(1, self.spread)]
        barrier = pltpu.get_barrier_semaphore()
        for one in ids:
            pl.semaphore_signal(barrier, inc=1, device_id=one, device_id_type=MESH)
        pl.semaphore_wait(barrier, len(ids))


class Links:
    def __init__(self, send, recv):
        self.send, self.recv, self.count = send, recv, 0
        self.local = []

    def remote(self, src, dst, to):
        slot = self.count
        self.count += 1
        return pltpu.make_async_remote_copy(
            src_ref=src, dst_ref=dst, send_sem=self.send.at[slot], recv_sem=self.recv.at[slot],
            device_id=to, device_id_type=MESH,
        )

    def copy(self, src, dst):
        slot = self.count
        self.count += 1
        return pltpu.make_async_copy(src, dst, self.send.at[slot])


def tile(start, size):
    return pl.ds(pl.multiple_of(start, size), size)


class Spread:
    def __init__(self, links, place, joined, h):
        rows = joined.shape[1] // 2
        self.own = place.low == h
        self.to_z, self.to_y, self.to_core, self.core_y = [], [], [], []
        for i in range(2):
            here = pl.ds(i * rows, rows)
            mine = joined.at[h * 4 + place.y * 2 + place.core, here]
            other = joined.at[h * 4 + (1 - place.y) * 2 + place.core, here]
            self.to_z.append(links.remote(mine, mine, place.low_id))
            self.to_y.append(links.remote(mine, mine, place.y_id))
            self.to_core.append(links.remote(mine, mine, place.core_id))
            self.core_y.append(links.remote(other, other, place.core_id))

    def start(self, i):
        self.to_z[i].start()
        self.to_y[i].start()
        self.to_core[i].start()

    def begin(self):
        @pl.when(self.own)
        def _():
            self.start(0)
            self.start(1)

    def pass_z(self):
        @pl.when(jnp.logical_not(self.own))
        def _():
            for i in range(2):
                self.to_z[i].wait_recv()
                self.to_y[i].start()
                self.to_core[i].start()

    def pass_y(self):
        for i in range(2):
            self.to_y[i].wait_recv()
            self.core_y[i].start()

    def ready(self):
        for one in self.to_core + self.core_y:
            one.wait_recv()
        for one in self.to_y + self.to_core + self.core_y:
            one.wait_send()

        @pl.when(self.own)
        def _():
            for one in self.to_z:
                one.wait_send()


class Collect:
    def __init__(self, links, place, ns, h):
        self.ns, self.own, self.count = ns, place.low == h, ns.part.shape[1] // 2
        self.pairs = (h * 2 + 1 - place.y, h * 2 + place.y)
        self.blocks = [p * 2 + place.core for p in self.pairs]
        self.core_in = [ns.core_in.at[h * 2 + k] for k in range(2)]
        self.y_in, self.sum_y = ns.y_in.at[h], ns.sums.at[h]
        self.across = [
            links.remote(ns.part.at[p * 2 + 1 - place.core], self.core_in[k], place.core_id)
            for k, p in enumerate(self.pairs)
        ]
        self.to_y, self.to_z = [], []
        for i in range(2):
            here = pl.ds(i * self.count, self.count)
            self.to_y.append(links.remote(self.sum_y.at[here], self.y_in.at[here], place.y_id))
            self.to_z.append(links.remote(ns.sums.at[2, here], ns.z_in.at[here], place.low_id))

    def work(self, fill):
        for k in range(2):
            fill(self.pairs[k])
            self.across[k].start()

    def each(self, i, work):
        def step(j, carry):
            work(tile(i * self.count + j * CHUNK, CHUNK))
            return carry

        lax.fori_loop(0, self.count // CHUNK, step, 0)

    def term(self, k, at):
        return self.ns.part[self.blocks[k], at, :].astype(F32) + self.core_in[k][at, :].astype(F32)

    def send_y(self):
        self.across[0].wait_recv()

        def add(at):
            self.sum_y[at, :] = self.term(0, at).astype(BF16)

        for i in range(2):
            self.each(i, add)
            self.to_y[i].start()

    def send_z(self):
        self.across[1].wait_recv()

        @pl.when(jnp.logical_not(self.own))
        def _():
            def add(at):
                total = self.term(1, at) + self.y_in[at, :].astype(F32)
                self.ns.sums[2, at, :] = total.astype(BF16)

            for i in range(2):
                self.to_y[i].wait_recv()
                self.each(i, add)
                self.to_z[i].start()

    def end(self, finish, spread=None):
        @pl.when(self.own)
        def _():
            def add(at):
                total = self.term(1, at) + self.y_in[at, :].astype(F32)
                finish(at, total + self.ns.z_in[at, :].astype(F32))

            for i in range(2):
                self.to_y[i].wait_recv()
                self.to_z[i].wait_recv()
                self.each(i, add)
                if spread is not None:
                    spread.start(i)

    def drain(self):
        for one in self.across + self.to_y:
            one.wait_send()

        @pl.when(jnp.logical_not(self.own))
        def _():
            for one in self.to_z:
                one.wait_send()


class Exchange:
    def __init__(self, links, place, ns, joined):
        self.sums = [Collect(links, place, ns, h) for h in range(2)]
        self.back = [None, None] if joined is None else [Spread(links, place, joined, h) for h in range(2)]

    def rest(self, finish, hooks=()):
        hooks = list(hooks)

        def hook():
            if hooks:
                hooks.pop(0)()

        first, second = self.sums
        first.send_z()
        second.send_y()
        hook()
        first.end(finish, self.back[0])
        second.send_z()
        hook()
        if self.back[0] is not None:
            self.back[0].pass_z()
        second.end(finish, self.back[1])
        hook()
        if self.back[0] is not None:
            self.back[0].pass_y()
            self.back[1].pass_z()
        for one in self.sums:
            one.drain()
        while hooks:
            hook()


def pair_rows(ref, pair):
    return ref[pl.ds(pair * 2, 2)].reshape(2 * ref.shape[1], -1)


def put_rows(ref, pair, value, columns=slice(None)):
    ref[pl.ds(pair * 2, 2), :, columns] = value.reshape(2, ref.shape[1], -1)


class Gather:
    def __init__(self, links, place, sources, own, stage, land, save):
        rows = own.shape[1]
        self.place, self.own, self.land, self.rows, self.stage = place, own, land, rows, stage
        self.starts, self.loads = [], []
        start = 0
        for one in sources:
            size = one.shape[1]
            self.starts.append((start, size // 2))
            self.loads.append(links.copy(one, stage.at[:, start : start + size]))
            start += size
        spread = place.spread

        def at(dp):
            return land.at[tile(dp * rows, rows)]

        mine = at(place.dp)
        self.out = [
            links.remote(own.at[lax.rem(place.low + k, 2)], mine, place.z_id(k)) for k in range(1, 4)
        ]
        self.side = [links.remote(own.at[place.low], mine, place.r_id(s)) for s in range(1, spread)]
        self.on = [
            [
                links.remote(at(place.z_dp(-k)), at(place.z_dp(-k)), place.r_id(s))
                for s in range(1, spread)
            ]
            for k in range(1, 4)
        ]
        self.save = links.copy(land, save)

    def load(self):
        for one in self.loads:
            one.start()

    def cast(self):
        for one in self.loads:
            one.wait()
        step = min(64, self.rows)

        def round_rows(i, carry):
            at = tile(i * step, step)
            for low in range(2):
                to = 0
                for start, half in self.starts:
                    piece = self.stage[at, start + low * half : start + (low + 1) * half]
                    self.own[low, at, to : to + half] = piece.astype(BF16)
                    to += half
            return carry

        lax.fori_loop(0, self.rows // step, round_rows, 0)

    def begin(self):
        for one in self.side:
            one.start()
        step = min(64, self.rows)

        def copy(i, carry):
            self.land[tile(self.place.dp * self.rows + i * step, step), :] = self.own[
                self.place.low, tile(i * step, step), :
            ]
            return carry

        lax.fori_loop(0, self.rows // step, copy, 0)

    def forward(self, k):
        self.out[k].wait_recv()
        for one in self.on[k]:
            one.start()

    def finish(self):
        for one in self.side:
            one.wait_recv()
        for group in self.on:
            for one in group:
                one.wait_recv()
        self.save.start()

    def drain(self):
        for one in self.out + self.side:
            one.wait_send()
        for group in self.on:
            for one in group:
                one.wait_send()
        self.save.wait()


class Stream:
    def __init__(self, groups):
        self.groups = groups
        self.order = [one for group in groups for one in group]
        self.items = [(group, k) for group in groups for k in range(3)]
        self.sent = self.passed = 0
        for one in self.order[:2]:
            one.load()

    def send(self, count=1):
        for group, k in self.items[self.sent : self.sent + count]:
            for one in group:
                if k == 0:
                    one.cast()
                    at = self.order.index(one) + 2
                    if at < len(self.order):
                        self.order[at].load()
                    one.begin()
                one.out[k].start()
            self.sent += 1

    def forward(self, count=1):
        for group, k in self.items[self.passed : min(self.passed + count, self.sent)]:
            for one in group:
                one.forward(k)
            self.passed += 1

    def tick(self, lag=2):
        self.send()
        if self.passed + lag < self.sent or self.sent == len(self.items):
            self.forward()

    def need(self, one):
        place = [i for i, group in enumerate(self.groups) if one in group][0] * 3 + 3
        self.send(max(0, place - self.sent))
        self.forward(max(0, place - self.passed))
        one.finish()

    def rest(self):
        self.send(len(self.items))
        self.forward(len(self.items))


def scale_of(v):
    return lax.rsqrt(jnp.mean(v * v, axis=-1, keepdims=True) + EPSILON)


def mm(a, b):
    return jnp.dot(a, b, preferred_element_type=F32)


def mm_nt(a, b):
    return lax.dot_general(a, b, (((1,), (1,)), ((), ())), preferred_element_type=F32)


def project_heads(ns, pair):
    block = ns.joined.shape[1]
    two = pl.ds(pair * 2, 2)
    x = ns.joined[two].reshape(2 * block, -1)
    raw = mm(x, ns.wqkv[...])
    ns.raw[two] = raw.reshape(2, block, -1)
    cosine, sine = ns.cosine[two].reshape(2 * block, HD), ns.sine[two].reshape(2 * block, HD)
    q_size, kv_size = ns.q.shape[2], ns.k.shape[2]

    def heads(out, start, size, gain):
        for h in range(size // HD):
            v = raw[:, start + h * HD : start + (h + 1) * HD]
            v = v * scale_of(v) * gain[...]
            turned = v * cosine + pltpu.roll(v, HD // 2, axis=1) * sine
            out[two, :, h * HD : (h + 1) * HD] = turned.astype(BF16).reshape(2, block, HD)

    heads(ns.q, 0, q_size, ns.gain_q)
    heads(ns.k, q_size, kv_size, ns.gain_k)
    ns.v[two] = raw[:, q_size + kv_size :].astype(BF16).reshape(2, block, kv_size)


def softmax(ns, b, half, span, query, keys):
    seen = keys.shape[0]
    s = mm_nt(query, keys) * HD**-0.5
    s = s + ns.bias[b, half * span : (half + 1) * span, :seen].astype(F32)
    p = jnp.exp(s - jnp.max(s, axis=-1, keepdims=True))
    return p / jnp.sum(p, axis=-1, keepdims=True)


def attend(ns, b):
    block = ns.joined.shape[1]
    span = 2 * block
    q_heads = ns.q.shape[2] // HD
    share = q_heads // (ns.k.shape[2] // HD)
    for e in range(q_heads):
        kv = slice((e // share) * HD, (e // share + 1) * HD)
        mine = slice(e * HD, (e + 1) * HD)
        for half in range(2):
            rows = slice(4 * b + 2 * half, 4 * b + 2 * half + 2)
            seen = slice(4 * b, 4 * b + 2 * half + 2)
            keys = ns.k[seen, :, kv].reshape(-1, HD)
            values = ns.v[seen, :, kv].reshape(-1, HD)
            query = ns.q[rows, :, mine].reshape(span, HD)
            p = softmax(ns, b, half, span, query, keys)
            ns.att[rows, :, mine] = mm(p.astype(BF16), values).astype(BF16).reshape(2, block, HD)


def project_out(ns, source, weight, pair, width=1024):
    x = pair_rows(source, pair)

    def step(j, carry):
        at = tile(j * width, width)
        put_rows(ns.part, pair, mm_nt(x, weight[at, :]).astype(BF16), at)
        return carry

    lax.fori_loop(0, ns.part.shape[2] // width, step, 0)


def gate_up(ns, pair, slot):
    ff = ns.product.shape[2]
    block = ns.joined.shape[1]
    x = pair_rows(ns.joined, pair)
    gate = mm(x, ns.wgate[...])
    up = mm(x, ns.wup[...])
    ns.gu_stage[slot, :, :, :ff] = gate.astype(BF16).reshape(2, block, ff)
    ns.gu_stage[slot, :, :, ff:] = up.astype(BF16).reshape(2, block, ff)
    put_rows(ns.product, pair, (gate / (1.0 + jnp.exp(-gate)) * up).astype(BF16))


def forward_layer_kernel(layer, last, spread, ns):
    first = layer == 0
    place = Place(spread)
    links = Links(ns.send, ns.recv)
    local = ns.hidden.shape[0]
    mine = place.own_pair * 2 + place.core
    gathers = []

    def gather(own, land, save, *sources):
        stage = ns.stage.at[len(gathers) % 2]
        gathers.append(Gather(links, place, sources, own, stage, land, save))
        return gathers[-1]

    def attention_weights(at):
        kv = ns.keyvalue_weight
        return (ns.query_weight.at[at], kv.at[at, 0], kv.at[at, 1]), ns.output_weight.at[at]

    mlp = ns.mlp_weight
    if first:
        qkv_source, o_source = attention_weights(layer)
        get_qkv = gather(ns.own_qkv, ns.wqkv, ns.save_wqkv, *qkv_source)
        get_o = gather(ns.own_o, ns.wo, ns.save_wo, o_source)
        get_gate = gather(ns.own_gate, ns.wgate, ns.save_wgate, mlp.at[layer, 0])
    get_up = gather(ns.own_up, ns.wup, ns.save_wup, mlp.at[layer, 1])
    get_down = gather(ns.own_down, ns.wdown, ns.save_wdown, mlp.at[layer, 2])
    if not last:
        qkv_source, o_source = attention_weights(layer + 1)
        next_qkv = gather(ns.own_next_qkv, ns.wnext_qkv, ns.save_wnext_qkv, *qkv_source)
        next_o = gather(ns.own_next_o, ns.wnext_o, ns.save_wnext_o, o_source)
        next_gate = gather(ns.own_next_gate, ns.wnext_gate, ns.save_wnext_gate, mlp.at[layer + 1, 0])
    groups = [[get_qkv], [get_o], [get_gate]] if first else []
    groups += [[get_up], [get_down]]
    if not last:
        groups += [[next_qkv, next_o], [next_gate]]
    stream = Stream(groups)
    tick = stream.tick
    heads = partial(project_heads, ns)
    if first:
        tokens_in = [Spread(links, place, ns.joined, h) for h in range(2)]
    if last:
        grads_in = [Spread(links, place, ns.joined_grad, h) for h in range(2)]
    middle = Exchange(links, place, ns, ns.joined)
    end = Exchange(links, place, ns, None if last else ns.joined)

    if first:
        def norm(i, carry):
            at = tile(i * CHUNK, CHUNK)
            v = ns.hidden[at, :].astype(F32)
            ns.joined[mine, at, :] = (v * scale_of(v) * ns.gain_attn[...]).astype(BF16)
            return carry

        lax.fori_loop(0, local // CHUNK, norm, 0)
        place.greet()
        for one in tokens_in:
            one.begin()
        stream.send(3)
        for one in tokens_in:
            one.pass_z()
        stream.send()
        stream.forward()
        for one in tokens_in:
            one.pass_y()
        stream.send()
        stream.forward()
        stream.send()
        stream.forward()
        tick()
        tick()
        for one in tokens_in:
            one.ready()
        save_a = links.copy(ns.joined, ns.save_a)
        save_a.start()
        stream.need(get_qkv)
    else:
        loads = [
            links.copy(ns.joined_in, ns.joined),
            links.copy(ns.wqkv_in, ns.wqkv),
            links.copy(ns.wo_in, ns.wo),
        ]
        gate_load = links.copy(ns.wgate_in, ns.wgate)
        for one in loads:
            one.start()
        gate_load.start()
        if last:
            ns.joined_grad[mine] = ns.cotangent[...]
        place.greet()
        if last:
            for one in grads_in:
                one.begin()
        stream.send()
        for one in loads:
            one.wait()
        gate_load.wait()

    def middle_rows(at, total):
        v = ns.hidden[at, :].astype(F32) + total
        ns.mid[at, :] = v
        ns.joined[mine, at, :] = (v * scale_of(v) * ns.gain_mlp[...]).astype(BF16)

    def result_rows(at, total):
        v = ns.mid[at, :] + total
        ns.out[at, :] = v
        if not last:
            ns.joined[mine, at, :] = (v * scale_of(v) * ns.gain_next[...]).astype(BF16)

    attention_part = partial(project_out, ns, ns.att, ns.wo)
    heads(0)
    heads(1)
    tick()
    attend(ns, 0)
    tick()
    heads(2)
    heads(3)
    if first:
        stream.need(get_o)
        save_a.wait()
    middle.sums[0].work(attention_part)
    if last:
        for one in grads_in:
            one.pass_z()
    tick()
    middle.sums[0].send_y()
    attend(ns, 1)
    middle.sums[1].work(attention_part)
    tick()
    hooks = [tick, tick, tick]
    if last:
        hooks += [grads_in[0].pass_y, grads_in[1].pass_y]
    middle.rest(middle_rows, hooks)
    tick()
    if first:
        stream.need(get_gate)
    stream.need(get_up)
    saves = []

    def gate_up_of(pair):
        slot = len(saves) % 2
        if len(saves) >= 2:
            saves[-2].wait()
        gate_up(ns, pair, slot)
        save = links.copy(ns.gu_stage.at[slot], ns.save_gateup.at[2 * pair : 2 * pair + 2])
        save.start()
        saves.append(save)

    save_b = [
        links.copy(ns.joined.at[4 * h : 4 * h + 4], ns.save_b.at[4 * h : 4 * h + 4]) for h in range(2)
    ]
    mlp_part = partial(project_out, ns, ns.product, ns.wdown)
    middle.back[0].ready()
    save_b[0].start()
    gate_up_of(0)
    middle.back[1].pass_y()
    gate_up_of(1)
    tick()
    stream.need(get_down)
    save_b[0].wait()
    end.sums[0].work(mlp_part)
    middle.back[1].ready()
    save_b[1].start()
    end.sums[0].send_y()
    gate_up_of(2)
    tick()
    gate_up_of(3)
    save_b[1].wait()
    end.sums[1].work(mlp_part)
    end.rest(result_rows, [tick, tick, tick])
    if not last:
        tick()
        end.back[1].pass_y()
        tick()
        stream.rest()
        for one in (next_qkv, next_o):
            stream.need(one)
        for one in end.back:
            one.ready()
        final = links.copy(ns.joined, ns.save_next)
    else:
        for one in grads_in:
            one.ready()
        final = links.copy(ns.joined_grad, ns.save_next)
    final.start()
    if not last:
        stream.need(next_gate)
    for save in saves[-2:]:
        save.wait()
    for one in gathers:
        one.drain()
    final.wait()
    assert stream.passed == len(stream.items) and links.count <= ns.send.shape[0]


def call(kernel, ins, outs, scratch, collective_id, name):
    names = [*ins, *outs, *scratch]

    def run(*refs):
        kernel(SimpleNamespace(**dict(zip(names, refs))))

    def space(in_vmem):
        return pl.BlockSpec(memory_space=pltpu.VMEM if in_vmem else pl.ANY)

    results = pl.pallas_call(
        run,
        out_shape=[jax.ShapeDtypeStruct(shape, dtype) for shape, dtype, _ in outs.values()],
        in_specs=[space(v) for _, v in ins.values()],
        out_specs=[space(v) for _, _, v in outs.values()],
        scratch_shapes=list(scratch.values()),
        compiler_params=pltpu.CompilerParams(
            collective_id=collective_id, has_side_effects=True, vmem_limit_bytes=VMEM_LIMIT
        ),
        cost_estimate=pl.CostEstimate(
            flops=13 * 10**9, bytes_accessed=10**8, transcendentals=10**6
        ),
        name=name,
    )(*[array for array, _ in ins.values()])
    return SimpleNamespace(**dict(zip(outs, results)))


def exchange_scratch(rows, width):
    return dict(
        joined=pltpu.VMEM((8, rows, width), BF16),
        part=pltpu.VMEM((8, rows, width), BF16),
        core_in=pltpu.VMEM((4, rows, width), BF16),
        y_in=pltpu.VMEM((2, rows, width), BF16),
        z_in=pltpu.VMEM((rows, width), BF16),
        sums=pltpu.VMEM((3, rows, width), BF16),
    )


def forward_layer(layer, last, hidden, carry, masters, tables, gains, cotangent, spread):
    rows, width = hidden.shape
    query, keyvalue, output, mlp = masters
    first = layer == 0
    own = query.shape[1]
    d_rows = own * 4 * spread
    o, ff = query.shape[2] // 2, mlp.shape[3] // 2
    kv = keyvalue.shape[3] // 2
    qkv = o + 2 * kv
    cosine, sine, bias = tables

    def row(at, start, size):
        return (gains[at : at + 1, start : start + size], True)

    ins = dict(
        hidden=(hidden, True),
        query_weight=(query, False),
        keyvalue_weight=(keyvalue, False),
        output_weight=(output, False),
        mlp_weight=(mlp, False),
    )
    if first:
        ins.update(gain_attn=row(layer, 0, width))
    else:
        joined_in, wqkv_in, wo_in, wgate_in = ((one, False) for one in carry)
        ins.update(joined_in=joined_in, wqkv_in=wqkv_in, wo_in=wo_in, wgate_in=wgate_in)
    if last:
        ins.update(cotangent=(cotangent, True))
    else:
        ins.update(gain_next=row(layer + 1, 0, width))
    ins.update(gain_mlp=row(layer, width, width))
    ins.update(gain_q=row(layer, 2 * width, HD))
    ins.update(gain_k=row(layer, 2 * width + HD, HD))
    ins.update(cosine=(cosine, True), sine=(sine, True), bias=(bias, True))
    outs = dict(
        out=((rows, width), F32, True),
        mid=((rows, width), F32, True),
        raw=((8, rows, o + 2 * kv), F32, True),
        q=((8, rows, o), BF16, True),
        k=((8, rows, kv), BF16, True),
        v=((8, rows, kv), BF16, True),
        att=((8, rows, o), BF16, True),
        product=((8, rows, ff), BF16, True),
        save_gateup=((8, rows, 2 * ff), BF16, False),
        save_b=((8, rows, width), BF16, False),
        save_next=((8, rows, width), BF16, False),
    )
    scratch = exchange_scratch(rows, width)
    scratch.update(gu_stage=pltpu.VMEM((2, 2, rows, 2 * ff), BF16))
    scratch.update(stage=pltpu.VMEM((2, own, max(2 * ff, 2 * (o + 2 * kv))), F32))
    weight = lambda size: pltpu.VMEM((d_rows, size), BF16)
    mine = lambda size: pltpu.VMEM((2, own, size), BF16)
    saved = lambda size: ((d_rows, size), BF16, False)
    scratch.update(wqkv=weight(qkv), wo=weight(o), wgate=weight(ff), wup=weight(ff), wdown=weight(ff))
    scratch.update(own_up=mine(ff), own_down=mine(ff))
    outs.update(save_wup=saved(ff), save_wdown=saved(ff))
    if first:
        outs.update(save_a=((8, rows, width), BF16, False))
        scratch.update(own_qkv=mine(qkv), own_o=mine(o), own_gate=mine(ff))
        outs.update(save_wqkv=saved(qkv), save_wo=saved(o), save_wgate=saved(ff))
    if last:
        scratch.update(joined_grad=pltpu.VMEM((8, rows, width), BF16))
    else:
        scratch.update(wnext_qkv=weight(qkv), wnext_o=weight(o), wnext_gate=weight(ff))
        scratch.update(own_next_qkv=mine(qkv), own_next_o=mine(o), own_next_gate=mine(ff))
        outs.update(save_wnext_qkv=saved(qkv), save_wnext_o=saved(o), save_wnext_gate=saved(ff))
    count = 80 + 40 * spread
    scratch.update(send=pltpu.SemaphoreType.DMA((count,)))
    scratch.update(recv=pltpu.SemaphoreType.DMA((count,)))
    kernel = partial(forward_layer_kernel, layer, last, spread)
    return call(kernel, ins, outs, scratch, 1 + int(last) + 2 * int(not first), "forward_layer")


def mm_tn(a, b):
    return lax.dot_general(a, b, (((0,), (0,)), ((), ())), preferred_element_type=F32)


class Reduce:
    def __init__(self, links, place, blocks, x_in, z_in, outs):
        self.place, self.blocks, self.x_in, self.z_in, self.outs = place, blocks, x_in, z_in, outs
        spread = place.spread
        rows = blocks.shape[1] // spread
        self.rows = rows

        def block(q, r):
            return blocks.at[q, tile(r * rows, rows)]

        self.x_out = [
            [
                links.remote(
                    block(q, lax.rem(place.r + s, spread)), x_in.at[s - 1, q], place.r_id(s)
                )
                for s in range(1, spread)
            ]
            for q in range(4)
        ]
        self.z_out = [
            links.remote(block(q, place.r), z_in.at[q - 1], place.z_id(q)) for q in range(1, 4)
        ]

    def compute(self, q, left, right):
        part = self.blocks.shape[1]
        step = min(256, part)
        start = lax.rem(self.place.z + q, 4) * part

        def one(i, carry):
            x = left[:, :, tile(start + i * step, step)]
            product = mm_tn(x.reshape(-1, step), right())
            self.blocks[q, tile(i * step, step), :] = product.astype(BF16)
            return carry

        lax.fori_loop(0, part // step, one, 0)
        for one_copy in self.x_out[q]:
            one_copy.start()

    def pass_on(self, q):
        for one in self.x_out[q]:
            one.wait_recv()
        step = min(64, self.rows)
        start = self.place.r * self.rows

        def add(i, carry):
            at = tile(start + i * step, step)
            total = self.blocks[q, at, :].astype(F32)
            for s in range(self.place.spread - 1):
                total = total + self.x_in[s, q, tile(i * step, step), :].astype(F32)
            self.blocks[q, at, :] = total.astype(BF16)
            return carry

        lax.fori_loop(0, self.rows // step, add, 0)
        if q:
            self.z_out[q - 1].start()

    def finish(self):
        for one in self.z_out:
            one.wait_recv()
        step = min(64, self.rows)
        low = self.place.low
        start = self.place.r * self.rows

        def add(i, carry):
            at = tile(i * step, step)
            near = self.blocks[0, tile(start + i * step, step), :].astype(F32)
            near = (near + self.z_in[1, at, :].astype(F32)).astype(BF16)
            far = self.z_in[0, at, :].astype(F32) + self.z_in[2, at, :].astype(F32)
            far = far.astype(BF16)
            first = 0
            for out, size in self.outs:
                out[at, tile(low * size, size)] = near[:, first : first + size]
                out[at, tile((1 - low) * size, size)] = far[:, first : first + size]
                first += size
            return carry

        lax.fori_loop(0, self.rows // step, add, 0)

    def drain(self):
        for group in self.x_out:
            for one in group:
                one.wait_send()
        for one in self.z_out:
            one.wait_send()


ORDER = (2, 1, 3, 0)


def gate_up_back(ns, pair, slot):
    ff = ns.product.shape[2]
    rows = 2 * ns.joined.shape[1]
    d_act = mm(pair_rows(ns.joined, pair), ns.wdown[...])
    gate = ns.stage[slot, :, :, :ff].reshape(rows, ff).astype(F32)
    up = ns.stage[slot, :, :, ff:].reshape(rows, ff).astype(F32)
    gated = 1.0 / (1.0 + jnp.exp(-gate))
    put_rows(ns.d_gate, pair, (d_act * up * gated * (1.0 + gate * (1.0 - gated))).astype(BF16))
    put_rows(ns.d_up, pair, (d_act * gate * gated).astype(BF16))


def head_back(ns, blocks, d_out, raw_columns, gain, d_gain):
    rows = d_out.shape[0]
    cosine, sine = ns.cosine[blocks].reshape(rows, HD), ns.sine[blocks].reshape(rows, HD)
    raw = ns.raw[blocks, :, raw_columns].reshape(rows, HD)
    d_turned = d_out * cosine + pltpu.roll(d_out * sine, HD // 2, axis=1)
    scale = scale_of(raw)
    normed = raw * scale
    d_gain[...] += jnp.sum(d_turned * normed, axis=0, keepdims=True)
    d_normed = d_turned * gain[...]
    inner = jnp.mean(d_normed * normed, axis=-1, keepdims=True)
    d_raw = (scale * (d_normed - normed * inner)).astype(BF16)
    ns.d_raw[blocks, :, raw_columns] = d_raw.reshape(-1, ns.raw.shape[1], HD)


def attend_back(ns, b):
    block = ns.joined.shape[1]
    span = 2 * block
    q_size, kv_size = ns.q.shape[2], ns.k.shape[2]
    share = q_size // kv_size
    scale = HD**-0.5
    whole = slice(4 * b, 4 * b + 4)
    for kv in range(kv_size // HD):
        columns = slice(kv * HD, (kv + 1) * HD)
        ns.d_keys[...] = jnp.zeros_like(ns.d_keys)
        ns.d_values[...] = jnp.zeros_like(ns.d_values)
        for e in range(kv * share, (kv + 1) * share):
            mine = slice(e * HD, (e + 1) * HD)
            for half in range(2):
                rows = slice(4 * b + 2 * half, 4 * b + 2 * half + 2)
                some = slice(4 * b, 4 * b + 2 * half + 2)
                seen = (half + 1) * span
                keys = ns.k[some, :, columns].reshape(seen, HD)
                values = ns.v[some, :, columns].reshape(seen, HD)
                query = ns.q[rows, :, mine].reshape(span, HD)
                d_out = ns.d_att[rows, :, mine].reshape(span, HD)
                p = softmax(ns, b, half, span, query, keys)
                d_p = mm_nt(d_out, values)
                delta = jnp.sum(d_p * p, axis=-1, keepdims=True)
                d_s = (p * (d_p - delta)).astype(BF16)
                ns.d_values[:seen, :] += mm_tn(p.astype(BF16), d_out)
                ns.d_keys[:seen, :] += mm_tn(d_s, query)
                head_back(ns, rows, mm(d_s, keys) * scale, mine, ns.gain_q, ns.d_gain_q)
        key_columns = slice(q_size + kv * HD, q_size + (kv + 1) * HD)
        head_back(ns, whole, ns.d_keys[...] * scale, key_columns, ns.gain_k, ns.d_gain_k)
        value_columns = slice(q_size + kv_size + kv * HD, q_size + kv_size + (kv + 1) * HD)
        ns.d_raw[whole, :, value_columns] = ns.d_values[...].astype(BF16).reshape(4, block, HD)


class GainSum:
    def __init__(self, links, place, terms, came, came_r, total):
        spread = place.spread
        self.place, self.terms, self.came, self.came_r, self.total = place, terms, came, came_r, total
        ids = (place.core_id, place.y_id, place.low_id, place.z_id(2))
        self.pairs = [links.remote(terms.at[i], came.at[i], one) for i, one in enumerate(ids)]
        self.sides = [
            links.remote(terms.at[4], came_r.at[place.r], place.r_id(s)) for s in range(1, spread)
        ]
        self.at = 0

    def start(self):
        self.pairs[0].start()

    def step(self):
        i = self.at
        self.at += 1
        if i < 4:
            self.pairs[i].wait_recv()
            self.terms[i + 1] = self.terms[i] + self.came[i]
            if i < 3:
                self.pairs[i + 1].start()
                return
            self.came_r[self.place.r] = self.terms[4]
            for one in self.sides:
                one.start()
            return
        for one in self.sides:
            one.wait_recv()
        total = self.came_r[0]
        for r in range(1, self.place.spread):
            total = total + self.came_r[r]
        self.total[...] = total
        for one in self.pairs + self.sides:
            one.wait_send()


def backward_layer_kernel(layer, spread, ns):
    first = layer == 0
    place = Place(spread)
    links = Links(ns.send, ns.recv)
    local = ns.grad_in.shape[0]
    mine = place.own_pair * 2 + place.core
    width = ns.grad_in.shape[1]
    qkv, o, ff = ns.wqkv_in.shape[1], ns.wo_in.shape[1], ns.wdown_in.shape[1]
    kv = (qkv - o) // 2

    def loads(*pairs):
        copies = [links.copy(src, dst) for src, dst in pairs]
        for one in copies:
            one.start()
        return copies

    def wait(copies):
        for one in copies:
            one.wait()

    def reduce(i, outs):
        return Reduce(links, place, ns.blocks.at[i], ns.x_in.at[i], ns.z_in_w.at[i], outs)

    red_down = reduce(0, [(ns.g_mlp.at[2], ff)])
    red_gate = reduce(1, [(ns.g_mlp.at[0], ff)])
    red_up = reduce(2, [(ns.g_mlp.at[1], ff)])
    red_o = Reduce(links, place, ns.blocks_o, ns.x_in_o, ns.z_in_o, [(ns.g_o, o)])
    red_qkv = Reduce(
        links, place, ns.blocks_qkv, ns.x_in_qkv, ns.z_in_qkv,
        [(ns.g_q, o), (ns.g_kv.at[0], kv), (ns.g_kv.at[1], kv)],
    )
    middle = Exchange(links, place, ns, ns.joined)
    end = Exchange(links, place, ns, None if first else ns.joined)
    if first:
        gain_sum = GainSum(links, place, ns.terms, ns.came, ns.came_r, ns.gain_total)

    passes = [partial(one.pass_on, q) for one in (red_down, red_gate, red_up, red_o, red_qkv) for q in ORDER]

    def pass_next(count=1):
        for _ in range(count):
            passes.pop(0)()

    def compute_all(one, left, right):
        for q in ORDER:
            one.compute(q, left, right)

    def back_norm(value, grad, gain, d_gain, out, gather):
        def finish(at, total):
            v = value[at, :].astype(F32)
            scale = scale_of(v)
            normed = v * scale
            d_gain[...] += jnp.sum(total * normed, axis=0, keepdims=True)
            d_normed = total * gain[...]
            inner = jnp.mean(d_normed * normed, axis=-1, keepdims=True)
            g = grad[at, :].astype(F32) + scale * (d_normed - normed * inner)
            out[at, :] = g
            if gather:
                ns.joined[mine, at, :] = g.astype(BF16)

        return finish

    for one in (ns.d_gain_attn, ns.d_gain_mlp, ns.d_gain_q, ns.d_gain_k):
        one[...] = jnp.zeros_like(one)

    flat = lambda ref: lambda: ref[...].reshape(8 * local, -1)

    def mlp_scope(wgate, wup, d_gate, d_up):
        ns.d_gate, ns.d_up = d_gate, d_up
        weight_loads = loads((ns.wgate_in, wgate), (ns.wup_in, wup))

        def part(pair, columns=1024):
            gates, ups = pair_rows(d_gate, pair), pair_rows(d_up, pair)

            def step(j, carry):
                at = tile(j * columns, columns)
                put_rows(ns.part, pair, (mm_nt(gates, wgate[at, :]) + mm_nt(ups, wup[at, :])).astype(BF16), at)
                return carry

            lax.fori_loop(0, width // columns, step, 0)

        def down_scope(wdown, product, stage):
            ns.wdown, ns.product, ns.stage = wdown, product, stage
            first_loads = loads((ns.joined_in, ns.joined), (ns.product_in, product))
            down_load = loads((ns.wdown_in, wdown))
            gateup_loads = [
                links.copy(ns.gateup_in.at[2 * i : 2 * i + 2], stage.at[i % 2]) for i in range(4)
            ]
            for one in gateup_loads[:2]:
                one.start()
            place.greet()
            wait(first_loads)
            compute_all(red_down, ns.joined, flat(product))
            wait(down_load)
            for i in range(4):
                gateup_loads[i].wait()
                gate_up_back(ns, i, i % 2)
                if i < 2:
                    gateup_loads[i + 2].start()
                if i == 1:
                    wait(weight_loads)
                    middle.sums[0].work(part)
                if i == 2:
                    middle.sums[0].send_y()

        pl.run_scoped(
            down_scope,
            pltpu.VMEM((rows_all, ff), BF16),
            pltpu.VMEM((8, local, ff), BF16),
            pltpu.VMEM((2, 2, local, 2 * ff), BF16),
        )

        def rest_scope(b, mid, grad):
            b_load = loads((ns.mid_in, mid), (ns.grad_in, grad), (ns.b_in, b))
            middle_rows = back_norm(mid, grad, ns.gain_mlp, ns.d_gain_mlp, ns.grad_mid, True)
            middle.sums[1].work(part)
            wait(b_load)
            middle.rest(
                middle_rows,
                [
                    partial(compute_all, red_gate, b, flat(d_gate)),
                    pass_next,
                    partial(compute_all, red_up, b, flat(d_up)),
                    pass_next,
                ],
            )

        pl.run_scoped(
            rest_scope,
            pltpu.VMEM((8, local, width), BF16),
            pltpu.VMEM((local, width), F32),
            pltpu.VMEM((local, width), ns.grad_in.dtype),
        )

    rows_all = ns.wdown_in.shape[0]
    group = ns.bias_in.shape[1]
    pl.run_scoped(
        mlp_scope,
        pltpu.VMEM((rows_all, ff), BF16),
        pltpu.VMEM((rows_all, ff), BF16),
        pltpu.VMEM((8, local, ff), BF16),
        pltpu.VMEM((8, local, ff), BF16),
    )

    def attention_scope(
        cosine, sine, bias, hidden, wqkv, wo, a, q, k, v, raw, att, d_att, d_raw, d_keys, d_values
    ):
        ns.cosine, ns.sine, ns.bias, ns.hidden = cosine, sine, bias, hidden
        ns.q, ns.k, ns.v, ns.raw, ns.att = q, k, v, raw, att
        ns.d_att, ns.d_raw, ns.d_keys, ns.d_values = d_att, d_raw, d_keys, d_values
        o_loads = loads((ns.wo_in, wo), (ns.att_in, att))
        other_loads = loads(
            (ns.q_in, q), (ns.k_in, k), (ns.v_in, v), (ns.raw_in, raw), (ns.cosine_in, cosine),
            (ns.sine_in, sine), (ns.bias_in, bias), (ns.a_in, a), (ns.wqkv_in, wqkv), (ns.hidden_in, hidden),
        )
        result_rows = back_norm(hidden, ns.grad_mid, ns.gain_attn, ns.d_gain_attn, ns.out, not first)

        def d_attended(h):
            middle.back[h].ready()
            for pair in (2 * h, 2 * h + 1):
                put_rows(d_att, pair, mm(pair_rows(ns.joined, pair), wo[...]).astype(BF16))

        part = partial(project_out, ns, d_raw, wqkv)
        wait(o_loads)
        d_attended(0)
        middle.back[1].pass_y()
        pass_next()
        wait(other_loads)
        attend_back(ns, 0)
        pass_next()
        d_attended(1)
        compute_all(red_o, ns.joined, flat(att))
        end.sums[0].work(part)
        pass_next(2)
        end.sums[0].send_y()
        attend_back(ns, 1)
        end.sums[1].work(part)
        pass_next(2)
        end.rest(
            result_rows,
            [
                partial(compute_all, red_qkv, a, flat(d_raw)),
                partial(pass_next, 4),
                partial(pass_next, 4),
            ],
        )
        red_down.finish()

    pl.run_scoped(
        attention_scope,
        pltpu.VMEM(ns.cosine_in.shape, F32),
        pltpu.VMEM(ns.sine_in.shape, F32),
        pltpu.VMEM(ns.bias_in.shape, BF16),
        pltpu.VMEM(ns.hidden_in.shape, ns.hidden_in.dtype),
        pltpu.VMEM((rows_all, qkv), BF16),
        pltpu.VMEM((rows_all, o), BF16),
        pltpu.VMEM((8, local, width), BF16),
        pltpu.VMEM(ns.q_in.shape, BF16),
        pltpu.VMEM(ns.k_in.shape, BF16),
        pltpu.VMEM(ns.v_in.shape, BF16),
        pltpu.VMEM(ns.raw_in.shape, F32),
        pltpu.VMEM(ns.att_in.shape, BF16),
        pltpu.VMEM((8, local, o), BF16),
        pltpu.VMEM((8, local, qkv), BF16),
        pltpu.VMEM((group, HD), F32),
        pltpu.VMEM((group, HD), F32),
    )
    if first:
        ns.terms[0] = jnp.zeros_like(ns.terms[0])
        earlier = (ns.later_attn, ns.later_mlp, ns.later_q, ns.later_k)
        here = (ns.d_gain_attn, ns.d_gain_mlp, ns.d_gain_q, ns.d_gain_k)
        for i, (attn, mlp, query, key) in enumerate((here, earlier)):
            ns.terms[0, 2 * i : 2 * i + 1, :width] = attn[...]
            ns.terms[0, 2 * i + 1 : 2 * i + 2, :width] = mlp[...]
            ns.terms[0, 2 * i : 2 * i + 1, width : width + HD] = query[...]
            ns.terms[0, 2 * i : 2 * i + 1, width + HD : width + 2 * HD] = key[...]
        gain_sum.start()
        for _ in range(4):
            pass_next()
            gain_sum.step()
        red_gate.finish()
        gain_sum.step()
    else:
        pass_next(2)
        end.back[1].pass_y()
        pass_next(2)
        red_gate.finish()
        for one in end.back:
            one.ready()
        final = links.copy(ns.joined, ns.save_next)
        final.start()
    red_up.finish()
    red_o.finish()
    red_qkv.finish()
    for one in (red_down, red_gate, red_up, red_o, red_qkv):
        one.drain()
    if not first:
        final.wait()
    assert not passes and links.count <= ns.send.shape[0]


def backward_layer(layer, grad, grad_rows, kept, later, tables, gains, spread):
    rows, width = grad.shape
    first = layer == 0
    cosine, sine, bias = tables
    d_rows, ff = kept.save_wdown.shape
    o, qkv = kept.wo.shape[1], kept.wqkv.shape[1]
    part = d_rows // 4
    block = part // spread

    def row(start, size):
        return gains[layer : layer + 1, start : start + size]

    ins = dict(
        grad_in=(grad, False),
        joined_in=(grad_rows, False),
        mid_in=(kept.mid, False),
        hidden_in=(kept.hidden, False),
        product_in=(kept.product, False),
        gateup_in=(kept.save_gateup, False),
        b_in=(kept.save_b, False),
        a_in=(kept.a, False),
        wdown_in=(kept.save_wdown, False),
        wgate_in=(kept.wgate, False),
        wup_in=(kept.save_wup, False),
        wqkv_in=(kept.wqkv, False),
        wo_in=(kept.wo, False),
        q_in=(kept.q, False),
        k_in=(kept.k, False),
        v_in=(kept.v, False),
        raw_in=(kept.raw, False),
        att_in=(kept.att, False),
        gain_attn=(row(0, width), True),
        gain_mlp=(row(width, width), True),
        gain_q=(row(2 * width, HD), True),
        gain_k=(row(2 * width + HD, HD), True),
        cosine_in=(cosine, False),
        sine_in=(sine, False),
        bias_in=(bias, False),
    )
    outs = dict(
        out=((rows, width), F32, True),
        d_gain_attn=((1, width), F32, True),
        d_gain_mlp=((1, width), F32, True),
        d_gain_q=((1, HD), F32, True),
        d_gain_k=((1, HD), F32, True),
        g_q=((block, 2 * o), BF16, True),
        g_kv=((2, block, qkv - o), BF16, True),
        g_o=((block, 2 * o), BF16, True),
        g_mlp=((3, block, 2 * ff), BF16, True),
    )
    if first:
        ins.update(
            later_attn=(later.d_gain_attn, True), later_mlp=(later.d_gain_mlp, True),
            later_q=(later.d_gain_q, True), later_k=(later.d_gain_k, True),
        )
        outs.update(gain_total=((8, width + 2 * HD), F32, True))
    if not first:
        outs.update(save_next=((8, rows, width), BF16, False))
    scratch = exchange_scratch(rows, width)
    side = spread - 1
    scratch.update(grad_mid=pltpu.VMEM((rows, width), F32))
    scratch.update(blocks=pltpu.VMEM((3, 4, part, ff), BF16))
    scratch.update(blocks_o=pltpu.VMEM((4, part, o), BF16))
    scratch.update(blocks_qkv=pltpu.VMEM((4, part, qkv), BF16))
    scratch.update(x_in=pltpu.VMEM((3, side, 4, block, ff), BF16))
    scratch.update(x_in_o=pltpu.VMEM((side, 4, block, o), BF16))
    scratch.update(x_in_qkv=pltpu.VMEM((side, 4, block, qkv), BF16))
    scratch.update(z_in_w=pltpu.VMEM((3, 3, block, ff), BF16))
    scratch.update(z_in_o=pltpu.VMEM((3, block, o), BF16))
    scratch.update(z_in_qkv=pltpu.VMEM((3, block, qkv), BF16))
    if first:
        small = (8, width + 2 * HD)
        scratch.update(terms=pltpu.VMEM((5, *small), F32))
        scratch.update(came=pltpu.VMEM((4, *small), F32))
        scratch.update(came_r=pltpu.VMEM((spread, *small), F32))
    count = 92 + 20 * spread
    scratch.update(send=pltpu.SemaphoreType.DMA((count,)))
    scratch.update(recv=pltpu.SemaphoreType.DMA((count,)))
    kernel = partial(backward_layer_kernel, layer, spread)
    return call(kernel, ins, outs, scratch, 6 if first else 5, "backward_layer")


def places(dp_size):
    spread = dp_size // 4
    me = lax.axis_index("dp")
    z = me // spread
    return spread, me, lax.rem(me, spread), lax.rem(z, 2), z // 2


def flip_lo(dp_size):
    spread = dp_size // 4
    return [(i, i + spread * (1 - 2 * ((i // spread) % 2))) for i in range(dp_size)]


def flip_hi(dp_size):
    spread = dp_size // 4
    return [(i, i + 2 * spread * (1 - 2 * (i // (2 * spread)))) for i in range(dp_size)]


def shift_r(dp_size, step):
    spread = dp_size // 4
    return [(i, (i // spread) * spread + (i % spread + step) % spread) for i in range(dp_size)]


def rope_tables(positions, head_size):
    half = head_size // 2
    frequency = jnp.power(THETA, -2.0 * jnp.arange(half, dtype=F32) / head_size)
    angle = positions.astype(F32)[:, None] * frequency[None, :]
    return (jnp.cos(angle)[:, None, :], jnp.sin(angle)[:, None, :])


def adamw(weight, first, second, grad, rate, decay):
    first_new = BETA_ONE * first + (1.0 - BETA_ONE) * grad
    second_new = BETA_TWO * second + (1.0 - BETA_TWO) * grad * grad
    first_hat = first_new / (1.0 - BETA_ONE**STEP)
    second_hat = second_new / (1.0 - BETA_TWO**STEP)
    weight_new = weight - rate * (first_hat / (jnp.sqrt(second_hat) + ADAM_EPS) + decay * weight)
    return (first_new, second_new, weight_new)


def body(
    tokens, cotangent, segment_ids, gains, gain_first, gain_second,
    query_weight, query_first, query_second,
    keyvalue_weight, keyvalue_first, keyvalue_second,
    output_weight, output_first, output_second,
    mlp_weight, mlp_first, mlp_second,
):
    dp_size = lax.axis_size("dp")
    spread, me, r, low, high = places(dp_size)
    layers = gains.shape[0]
    local_rows, width = tokens.shape
    group = segment_ids.shape[0]
    rows = 8 * local_rows
    index = jnp.arange(group, dtype=jnp.int32)
    other = lax.ppermute(segment_ids, "dp", flip_lo(dp_size))
    segments = jnp.stack([jnp.where(low == 0, segment_ids, other), jnp.where(low == 0, other, segment_ids)])
    positions = (index[None, :] - (segments - segments[:, :1])).reshape(rows)
    mask = (segments[:, :, None] == segments[:, None, :]) & (index[None, None, :] <= index[None, :, None])
    bias = jnp.where(mask, 0.0, -1e30).astype(BF16)
    cosine, sine = rope_tables(positions, HD)
    tables = (
        jnp.concatenate([cosine[:, 0], cosine[:, 0]], axis=1).reshape(8, local_rows, HD),
        jnp.concatenate([-sine[:, 0], sine[:, 0]], axis=1).reshape(8, local_rows, HD),
        bias,
    )
    masters = (query_weight, keyvalue_weight, output_weight, mlp_weight)

    hidden, carry = tokens, None
    saved = []
    for layer in range(layers):
        last = layer + 1 == layers
        kept = forward_layer(layer, last, hidden, carry, masters, tables, gains, cotangent, spread)
        if layer == 0:
            carry = (kept.save_a, kept.save_wqkv, kept.save_wo, kept.save_wgate)
        kept.hidden = hidden
        kept.a, kept.wqkv, kept.wo, kept.wgate = carry
        saved.append(kept)
        hidden = kept.out
        if not last:
            carry = (kept.save_next, kept.save_wnext_qkv, kept.save_wnext_o, kept.save_wnext_gate)

    block_output = hidden
    grad = cotangent
    grad_rows = saved[-1].save_next
    reduced = [None] * layers
    done = None
    for layer in reversed(range(layers)):
        done = backward_layer(layer, grad, grad_rows, saved[layer], done, tables, gains, spread)
        grad, grad_rows = done.out, None if layer == 0 else done.save_next
        reduced[layer] = [done.g_q, done.g_kv, done.g_o, done.g_mlp]
    stacked = [jnp.stack([entry[i] for entry in reduced]).astype(F32) for i in range(4)]
    sums = done.gain_total
    gain_total = jnp.stack(
        [
            jnp.concatenate([sums[2 * i, :width], sums[2 * i + 1, :width], sums[2 * i, width:]])
            for i in range(layers)
        ]
    )
    head_gain_grads = gain_total[:, 2 * width :]
    gain_new = adamw(gains, gain_first, gain_second, gain_total, GAIN_RATE, 0.0)
    query_new = adamw(query_weight, query_first, query_second, stacked[0], RATE, DECAY)
    keyvalue_new = adamw(keyvalue_weight, keyvalue_first, keyvalue_second, stacked[1], RATE, DECAY)
    output_new = adamw(output_weight, output_first, output_second, stacked[2], RATE * OUTPUT_FACTOR, DECAY)
    mlp_new = adamw(mlp_weight, mlp_first, mlp_second, stacked[3], RATE, DECAY)
    return (block_output, grad, *gain_new, head_gain_grads, *query_new, *keyvalue_new, *output_new, *mlp_new)


def solution(mesh):
    token = P(("dp", "tensor"), None)
    flat = P(None, "dp", "tensor")
    deep = P(None, None, "dp", "tensor")
    placed = (token, token, P("dp"), P(), P(), P(), *[flat] * 3, *[deep] * 3, *[flat] * 3, *[deep] * 3)
    outs = (token, token, P(), P(), P(), P(), *[flat] * 3, *[deep] * 3, *[flat] * 3, *[deep] * 3)
    return jax.shard_map(body, mesh=mesh, in_specs=placed, out_specs=outs, check_vma=False)
```

```python
from functools import partial
import math
from types import SimpleNamespace

import jax
import jax.numpy as jnp
from jax import lax
from jax.experimental import pallas as pl
from jax.experimental.pallas import tpu as pltpu
from jax.sharding import PartitionSpec as P

HD = 128
STEP = 10
EPSILON = 1e-06
THETA = 1000000.0
BETA_ONE = 0.9
BETA_TWO = 0.95
ADAM_EPS = 1e-08
DECAY = 0.1
RATE = 0.05
GAIN_RATE = 0.8
OUTPUT_FACTOR = math.sqrt(128)

BF16 = jnp.bfloat16
F32 = jnp.float32
MESH = pl.DeviceIdType.MESH
CHUNK = 32
VMEM_LIMIT = 62 * 1024 * 1024


class Place:
    def __init__(self, spread):
        self.spread = spread
        self.high, self.low = lax.axis_index("zh"), lax.axis_index("zl")
        self.r = lax.axis_index("r")
        self.tensor = lax.axis_index("tensor")
        self.core = lax.rem(self.tensor, 2)
        self.y = self.tensor // 2
        self.z = self.high * 2 + self.low
        self.dp = self.z * spread + self.r
        self.core_id = self.at(self.z, self.r, self.y * 2 + 1 - self.core)
        self.y_id = self.at(self.z, self.r, (1 - self.y) * 2 + self.core)
        self.low_id = self.at(self.z + 1 - 2 * self.low, self.r, self.tensor)
        self.own_pair = self.low * 2 + self.y
        self.pairs = (
            (1 - self.low) * 2 + 1 - self.y,
            self.low * 2 + 1 - self.y,
            (1 - self.low) * 2 + self.y,
            self.own_pair,
        )

    def at(self, z, r, tensor):
        return {"zh": z // 2, "zl": lax.rem(z, 2), "r": r, "tensor": tensor}

    def z_dp(self, step):
        return lax.rem(self.z + 4 + step, 4) * self.spread + self.r

    def z_id(self, step):
        return self.at(lax.rem(self.z + 4 + step, 4), self.r, self.tensor)

    def r_id(self, step):
        return self.at(self.z, lax.rem(self.r + self.spread + step, self.spread), self.tensor)

    def greet(self):
        ids = [self.core_id, self.y_id]
        ids += [self.z_id(k) for k in range(1, 4)]
        ids += [self.r_id(k) for k in range(1, self.spread)]
        barrier = pltpu.get_barrier_semaphore()
        for one in ids:
            pl.semaphore_signal(barrier, inc=1, device_id=one, device_id_type=MESH)
        pl.semaphore_wait(barrier, len(ids))


class Links:
    def __init__(self, send, recv, local):
        self.send, self.recv, self.local = send, recv, local
        self.count = self.copies = 0

    def remote(self, src, dst, to):
        slot = self.count
        self.count += 1
        return pltpu.make_async_remote_copy(
            src_ref=src, dst_ref=dst, send_sem=self.send.at[slot], recv_sem=self.recv.at[slot],
            device_id=to, device_id_type=MESH,
        )

    def copy(self, src, dst):
        slot = self.copies
        self.copies += 1
        return pltpu.make_async_copy(src, dst, self.local.at[slot])

    def check(self):
        assert self.count <= self.send.shape[0] and self.copies <= self.local.shape[0]


def tile(start, size):
    return pl.ds(pl.multiple_of(start, size), size)


class Spread:
    def __init__(self, links, place, joined, start, rows):
        def block(pair, core):
            return joined.at[pair * 2 + core, pl.ds(start, rows)]

        c = place.core
        diag, y, z, own = place.pairs
        own, from_z, from_y, from_d = (block(p, c) for p in (own, z, y, diag))
        self.to_z = links.remote(own, own, place.low_id)
        self.to_y = links.remote(own, own, place.y_id)
        self.to_core = links.remote(own, own, place.core_id)
        self.on_y = links.remote(from_z, from_z, place.y_id)
        self.core_z = links.remote(from_z, from_z, place.core_id)
        self.core_y = links.remote(from_y, from_y, place.core_id)
        self.core_d = links.remote(from_d, from_d, place.core_id)

    def start(self):
        self.to_z.start()
        self.to_y.start()
        self.to_core.start()

    def pass_on(self):
        self.to_z.wait_recv()
        self.on_y.start()
        self.core_z.start()
        self.to_y.wait_recv()
        self.core_y.start()

    def pass_last(self):
        self.on_y.wait_recv()
        self.core_d.start()

    def ready(self):
        for one in (self.to_core, self.core_z, self.core_y, self.core_d):
            one.wait_recv()

    def drain(self):
        for one in (self.to_z, self.to_y, self.to_core, self.on_y, self.core_z, self.core_y, self.core_d):
            one.wait_send()


class Collect:
    def __init__(self, links, place, ns, start, rows):
        self.place, self.ns, self.start, self.rows = place, ns, start, rows
        here = pl.ds(start, rows)
        self.across = [
            links.remote(ns.part.at[p * 2 + 1 - place.core, here], ns.core_in.at[k, here], place.core_id)
            for k, p in enumerate(place.pairs)
        ]
        self.diag = links.remote(ns.sums.at[0, here], ns.y_in.at[0, here], place.y_id)
        self.to_y = links.remote(ns.sums.at[1, here], ns.y_in.at[1, here], place.y_id)
        self.to_z = links.remote(ns.sums.at[2, here], ns.z_in.at[here], place.low_id)

    def cross(self, *which):
        for k in which:
            self.across[k].start()

    def term(self, k, at):
        block = self.place.pairs[k] * 2 + self.place.core
        return self.ns.part[block, at, :].astype(F32) + self.ns.core_in[k, at, :].astype(F32)

    def each(self, work):
        def step(i, carry):
            work(tile(self.start + i * CHUNK, CHUNK))
            return carry

        lax.fori_loop(0, self.rows // CHUNK, step, 0)

    def add(self, k):
        def work(at):
            total = self.term(k, at)
            if k == 2:
                total = total + self.ns.y_in[0, at, :].astype(F32)
            self.ns.sums[k, at, :] = total.astype(BF16)

        self.each(work)

    def send_y(self):
        self.across[0].wait_recv()
        self.add(0)
        self.diag.start()
        self.across[1].wait_recv()
        self.add(1)
        self.to_y.start()

    def send_z(self):
        self.across[2].wait_recv()
        self.diag.wait_recv()
        self.add(2)
        self.to_z.start()

    def end(self, finish):
        self.across[3].wait_recv()
        self.to_y.wait_recv()
        self.to_z.wait_recv()

        def work(at):
            total = self.term(3, at) + self.ns.y_in[1, at, :].astype(F32) + self.ns.z_in[at, :].astype(F32)
            finish(at, total)

        self.each(work)
        for one in (*self.across, self.diag, self.to_y, self.to_z):
            one.wait_send()


class Halves:
    def __init__(self, links, place, ns, joined):
        rows = ns.part.shape[1] // 2
        self.size = rows
        self.starts = (0, rows)
        self.sums = [Collect(links, place, ns, start, rows) for start in self.starts]
        self.back = joined is not None
        if self.back:
            self.spread = [Spread(links, place, joined, start, rows) for start in self.starts]


def take(ref, pairs, start, size, columns=slice(None)):
    parts = [ref[pl.ds(p * 2, 2), start : start + size, columns] for p in pairs]
    return jnp.concatenate([one.reshape(2 * size, -1) for one in parts], axis=0)


def put(ref, pairs, start, size, value, columns=slice(None)):
    for i, p in enumerate(pairs):
        part = value[2 * i * size : 2 * (i + 1) * size]
        ref[pl.ds(p * 2, 2), start : start + size, columns] = part.reshape(2, size, -1)


class Gather:
    def __init__(self, links, place, sources, own, stage, land, save):
        rows = own.shape[1]
        self.place, self.own, self.land, self.rows, self.stage = place, own, land, rows, stage
        self.starts, self.loads = [], []
        start = 0
        for one in sources:
            size = one.shape[1]
            self.starts.append((start, size // 2))
            self.loads.append(links.copy(one, stage.at[:, start : start + size]))
            start += size
        spread = place.spread

        def at(dp):
            return land.at[tile(dp * rows, rows)]

        mine = at(place.dp)
        self.out = [
            links.remote(own.at[lax.rem(place.low + k, 2)], mine, place.z_id(k)) for k in range(1, 4)
        ]
        self.side = [links.remote(own.at[place.low], mine, place.r_id(s)) for s in range(1, spread)]
        self.on = [
            [
                links.remote(at(place.z_dp(-k)), at(place.z_dp(-k)), place.r_id(s))
                for s in range(1, spread)
            ]
            for k in range(1, 4)
        ]
        self.save = links.copy(land, save)

    def load(self):
        for one in self.loads:
            one.start()

    def cast(self):
        for one in self.loads:
            one.wait()
        step = min(64, self.rows)

        def round_rows(i, carry):
            at = tile(i * step, step)
            for low in range(2):
                to = 0
                for start, half in self.starts:
                    piece = self.stage[at, start + low * half : start + (low + 1) * half]
                    self.own[low, at, to : to + half] = piece.astype(BF16)
                    to += half
            return carry

        lax.fori_loop(0, self.rows // step, round_rows, 0)

    def begin(self):
        for one in self.side:
            one.start()
        step = min(64, self.rows)

        def copy(i, carry):
            self.land[tile(self.place.dp * self.rows + i * step, step), :] = self.own[
                self.place.low, tile(i * step, step), :
            ]
            return carry

        lax.fori_loop(0, self.rows // step, copy, 0)

    def forward(self, k):
        self.out[k].wait_recv()
        for one in self.on[k]:
            one.start()

    def finish(self):
        for one in self.side:
            one.wait_recv()
        for group in self.on:
            for one in group:
                one.wait_recv()
        self.save.start()

    def drain(self):
        for one in self.out + self.side:
            one.wait_send()
        for group in self.on:
            for one in group:
                one.wait_send()
        self.save.wait()


class Stream:
    def __init__(self, groups):
        self.groups = groups
        self.order = [one for group in groups for one in group]
        self.items = [(group, k) for group in groups for k in range(3)]
        self.sent = self.passed = 0
        for one in self.order[:2]:
            one.load()

    def send(self, count=1):
        for group, k in self.items[self.sent : self.sent + count]:
            for one in group:
                if k == 0:
                    one.cast()
                    at = self.order.index(one) + 2
                    if at < len(self.order):
                        self.order[at].load()
                    one.begin()
                one.out[k].start()
            self.sent += 1

    def forward(self, count=1):
        for group, k in self.items[self.passed : min(self.passed + count, self.sent)]:
            for one in group:
                one.forward(k)
            self.passed += 1

    def tick(self, lag=2):
        self.send()
        if self.passed + lag < self.sent or self.sent == len(self.items):
            self.forward()

    def need(self, one):
        place = [i for i, group in enumerate(self.groups) if one in group][0] * 3 + 3
        self.send(max(0, place - self.sent))
        self.forward(max(0, place - self.passed))
        one.finish()

    def rest(self):
        self.send(len(self.items))
        self.forward(len(self.items))


def scale_of(v):
    return lax.rsqrt(jnp.mean(v * v, axis=-1, keepdims=True) + EPSILON)


def mm(a, b):
    return jnp.dot(a, b, preferred_element_type=F32)


def mm_nt(a, b):
    return lax.dot_general(a, b, (((1,), (1,)), ((), ())), preferred_element_type=F32)


def project_heads(ns, pair):
    block = ns.joined.shape[1]
    two = pl.ds(pair * 2, 2)
    x = ns.joined[two].reshape(2 * block, -1)
    raw = mm(x, ns.wqkv[...])
    ns.raw[two] = raw.reshape(2, block, -1)
    cosine, sine = ns.cosine[two].reshape(2 * block, HD), ns.sine[two].reshape(2 * block, HD)
    q_size, kv_size = ns.q.shape[2], ns.k.shape[2]

    def heads(out, start, size, gain):
        for h in range(size // HD):
            v = raw[:, start + h * HD : start + (h + 1) * HD]
            v = v * scale_of(v) * gain[...]
            turned = v * cosine + pltpu.roll(v, HD // 2, axis=1) * sine
            out[two, :, h * HD : (h + 1) * HD] = turned.astype(BF16).reshape(2, block, HD)

    heads(ns.q, 0, q_size, ns.gain_q)
    heads(ns.k, q_size, kv_size, ns.gain_k)
    ns.v[two] = raw[:, q_size + kv_size :].astype(BF16).reshape(2, block, kv_size)


def softmax(ns, b, half, span, query, keys):
    seen = keys.shape[0]
    s = mm_nt(query, keys) * HD**-0.5
    s = s + ns.bias[b, half * span : (half + 1) * span, :seen].astype(F32)
    p = jnp.exp(s - jnp.max(s, axis=-1, keepdims=True))
    return p / jnp.sum(p, axis=-1, keepdims=True)


def attend(ns, b):
    block = ns.joined.shape[1]
    span = 2 * block
    q_heads = ns.q.shape[2] // HD
    share = q_heads // (ns.k.shape[2] // HD)
    for e in range(q_heads):
        kv = slice((e // share) * HD, (e // share + 1) * HD)
        mine = slice(e * HD, (e + 1) * HD)
        for half in range(2):
            rows = slice(4 * b + 2 * half, 4 * b + 2 * half + 2)
            seen = slice(4 * b, 4 * b + 2 * half + 2)
            keys = ns.k[seen, :, kv].reshape(-1, HD)
            values = ns.v[seen, :, kv].reshape(-1, HD)
            query = ns.q[rows, :, mine].reshape(span, HD)
            p = softmax(ns, b, half, span, query, keys)
            ns.att[rows, :, mine] = mm(p.astype(BF16), values).astype(BF16).reshape(2, block, HD)


def project_out(ns, source, weight, pairs, start, size, width=1024):
    x = take(source, pairs, start, size)

    def step(j, carry):
        at = tile(j * width, width)
        put(ns.part, pairs, start, size, mm_nt(x, weight[at, :]).astype(BF16), at)
        return carry

    lax.fori_loop(0, ns.part.shape[2] // width, step, 0)


def gate_up(ns, pairs, start, size, slot):
    ff = ns.product.shape[2]
    x = take(ns.joined, pairs, start, size)
    gate = mm(x, ns.wgate[...])
    up = mm(x, ns.wup[...])
    ns.gu_stage[slot, :, :, :ff] = gate.astype(BF16).reshape(4, size, ff)
    ns.gu_stage[slot, :, :, ff:] = up.astype(BF16).reshape(4, size, ff)
    put(ns.product, pairs, start, size, (gate / (1.0 + jnp.exp(-gate)) * up).astype(BF16))


def forward_layer_kernel(layer, last, spread, ns):
    first = layer == 0
    place = Place(spread)
    links = Links(ns.send, ns.recv, ns.local)
    local = ns.hidden.shape[0]
    mine = place.own_pair * 2 + place.core
    gathers = []

    def gather(own, land, save, *sources):
        stage = ns.stage.at[len(gathers) % 2]
        gathers.append(Gather(links, place, sources, own, stage, land, save))
        return gathers[-1]

    def attention_weights(at):
        kv = ns.keyvalue_weight
        return (ns.query_weight.at[at], kv.at[at, 0], kv.at[at, 1]), ns.output_weight.at[at]

    mlp = ns.mlp_weight
    if first:
        qkv_source, o_source = attention_weights(layer)
        get_qkv = gather(ns.own_qkv, ns.wqkv, ns.save_wqkv, *qkv_source)
        get_o = gather(ns.own_o, ns.wo, ns.save_wo, o_source)
        get_gate = gather(ns.own_gate, ns.wgate, ns.save_wgate, mlp.at[layer, 0])
    get_up = gather(ns.own_up, ns.wup, ns.save_wup, mlp.at[layer, 1])
    get_down = gather(ns.own_down, ns.wdown, ns.save_wdown, mlp.at[layer, 2])
    if not last:
        qkv_source, o_source = attention_weights(layer + 1)
        next_qkv = gather(ns.own_next_qkv, ns.wnext_qkv, ns.save_wnext_qkv, *qkv_source)
        next_o = gather(ns.own_next_o, ns.wnext_o, ns.save_wnext_o, o_source)
        next_gate = gather(ns.own_next_gate, ns.wnext_gate, ns.save_wnext_gate, mlp.at[layer + 1, 0])
    groups = [[get_qkv], [get_o], [get_gate]] if first else []
    groups += [[get_up], [get_down]]
    if not last:
        groups += [[next_qkv, next_o], [next_gate]]
    stream = Stream(groups)
    tick = stream.tick
    diag, y, z, own = place.pairs
    first_pairs, last_pairs = (diag, y), (z, own)
    heads = partial(project_heads, ns)
    if first:
        tokens_in = Spread(links, place, ns.joined, 0, local)
    if last:
        grads_in = Spread(links, place, ns.joined_grad, 0, local)
    middle = Halves(links, place, ns, ns.joined)
    end = Halves(links, place, ns, None if last else ns.joined)
    size = middle.size

    if first:
        def norm(i, carry):
            at = tile(i * CHUNK, CHUNK)
            v = ns.hidden[at, :].astype(F32)
            ns.joined[mine, at, :] = (v * scale_of(v) * ns.gain_attn[...]).astype(BF16)
            return carry

        lax.fori_loop(0, local // CHUNK, norm, 0)
        place.greet()
        tokens_in.start()
        stream.send(3)
        tokens_in.pass_on()
        stream.send()
        stream.forward()
        stream.send()
        stream.forward()
        stream.send()
        stream.forward()
        tokens_in.pass_last()
        tick()
        tick()
        tokens_in.ready()
        stream.need(get_qkv)
        heads(own)
        heads(z)
        tick()
        heads(y)
        heads(diag)
        tokens_in.drain()
        save_a = links.copy(ns.joined, ns.save_a)
        save_a.start()
        tick()
    else:
        loads = [
            links.copy(ns.joined_in, ns.joined),
            links.copy(ns.wqkv_in, ns.wqkv),
            links.copy(ns.wo_in, ns.wo),
        ]
        gate_load = links.copy(ns.wgate_in, ns.wgate)
        for one in loads:
            one.start()
        gate_load.start()
        if last:
            ns.joined_grad[mine] = ns.cotangent[...]
        place.greet()
        if last:
            grads_in.start()
        stream.send()
        for one in loads:
            one.wait()

        def every(i, carry):
            heads(i)
            return carry

        lax.fori_loop(0, 4, every, 0)
        gate_load.wait()
        if last:
            grads_in.pass_on()
        tick()

    attend(ns, 0)
    tick()
    attend(ns, 1)
    tick()
    if first:
        stream.need(get_o)
    if last:
        grads_in.pass_last()

    def middle_rows(at, total):
        v = ns.hidden[at, :].astype(F32) + total
        ns.mid[at, :] = v
        ns.joined[mine, at, :] = (v * scale_of(v) * ns.gain_mlp[...]).astype(BF16)

    def result_rows(at, total):
        v = ns.mid[at, :] + total
        ns.out[at, :] = v
        if not last:
            ns.joined[mine, at, :] = (v * scale_of(v) * ns.gain_next[...]).astype(BF16)

    def part_of(source, weight, halves, h):
        start = halves.starts[h]
        project_out(ns, source, weight, first_pairs, start, size)
        halves.sums[h].cross(0, 1)
        project_out(ns, source, weight, last_pairs, start, size)
        halves.sums[h].cross(2, 3)

    if first:
        save_a.wait()
    part_of(ns.att, ns.wo, middle, 0)
    middle.sums[0].send_y()
    part_of(ns.att, ns.wo, middle, 1)
    middle.sums[1].send_y()
    tick()
    middle.sums[0].send_z()
    middle.sums[1].send_z()
    tick()
    middle.sums[0].end(middle_rows)
    middle.spread[0].start()
    middle.sums[1].end(middle_rows)
    middle.spread[1].start()
    tick()
    middle.spread[0].pass_on()
    middle.spread[1].pass_on()
    tick()
    if first:
        stream.need(get_gate)
    stream.need(get_up)
    middle.spread[0].pass_last()
    middle.spread[0].ready()
    middle.spread[0].drain()
    saves = []

    def gate_up_of(pairs, start):
        slot = (len(saves) // 2) % 2
        if len(saves) >= 4:
            for save in saves[-4:-2]:
                save.wait()
        gate_up(ns, pairs, start, size, slot)
        for i, p in enumerate(pairs):
            save = links.copy(
                ns.gu_stage.at[slot, 2 * i : 2 * i + 2], ns.save_gateup.at[pl.ds(p * 2, 2), pl.ds(start, size)]
            )
            save.start()
            saves.append(save)

    save_b = [
        links.copy(ns.joined.at[:, pl.ds(start, size)], ns.save_b.at[:, pl.ds(start, size)])
        for start in middle.starts
    ]
    save_b[0].start()
    gate_up_of(first_pairs, 0)
    tick()
    middle.spread[1].pass_last()
    gate_up_of(last_pairs, 0)
    stream.need(get_down)
    save_b[0].wait()
    part_of(ns.product, ns.wdown, end, 0)
    middle.spread[1].ready()
    middle.spread[1].drain()
    end.sums[0].send_y()
    save_b[1].start()
    gate_up_of(first_pairs, size)
    end.sums[0].send_z()
    tick()
    gate_up_of(last_pairs, size)
    save_b[1].wait()
    part_of(ns.product, ns.wdown, end, 1)
    end.sums[1].send_y()
    end.sums[0].end(result_rows)
    if not last:
        end.spread[0].start()
    tick()
    end.sums[1].send_z()
    if not last:
        end.spread[0].pass_on()
    tick()
    end.sums[1].end(result_rows)
    if not last:
        end.spread[1].start()
        tick()
        end.spread[0].pass_last()
        end.spread[1].pass_on()
        tick()
        stream.rest()
        for one in (next_qkv, next_o):
            stream.need(one)
        end.spread[1].pass_last()
        for one in end.spread:
            one.ready()
            one.drain()
        final = links.copy(ns.joined, ns.save_next)
    else:
        grads_in.ready()
        grads_in.drain()
        final = links.copy(ns.joined_grad, ns.save_next)
    final.start()
    if not last:
        stream.need(next_gate)
    for save in saves[-4:]:
        save.wait()
    for one in gathers:
        one.drain()
    final.wait()
    assert stream.passed == len(stream.items)
    links.check()


def call(kernel, ins, outs, scratch, collective_id, name):
    names = [*ins, *outs, *scratch]

    def run(*refs):
        kernel(SimpleNamespace(**dict(zip(names, refs))))

    def space(in_vmem):
        return pl.BlockSpec(memory_space=pltpu.VMEM if in_vmem else pl.ANY)

    results = pl.pallas_call(
        run,
        out_shape=[jax.ShapeDtypeStruct(shape, dtype) for shape, dtype, _ in outs.values()],
        in_specs=[space(v) for _, v in ins.values()],
        out_specs=[space(v) for _, _, v in outs.values()],
        scratch_shapes=list(scratch.values()),
        compiler_params=pltpu.CompilerParams(
            collective_id=collective_id, has_side_effects=True, vmem_limit_bytes=VMEM_LIMIT
        ),
        cost_estimate=pl.CostEstimate(
            flops=13 * 10**9, bytes_accessed=10**8, transcendentals=10**6
        ),
        name=name,
    )(*[array for array, _ in ins.values()])
    return SimpleNamespace(**dict(zip(outs, results)))


def exchange_scratch(rows, width):
    return dict(
        joined=pltpu.VMEM((8, rows, width), BF16),
        part=pltpu.VMEM((8, rows, width), BF16),
        core_in=pltpu.VMEM((4, rows, width), BF16),
        y_in=pltpu.VMEM((2, rows, width), BF16),
        z_in=pltpu.VMEM((rows, width), BF16),
        sums=pltpu.VMEM((3, rows, width), BF16),
    )


def forward_layer(layer, last, hidden, carry, masters, tables, gains, cotangent, spread):
    rows, width = hidden.shape
    query, keyvalue, output, mlp = masters
    first = layer == 0
    own = query.shape[1]
    d_rows = own * 4 * spread
    o, ff = query.shape[2] // 2, mlp.shape[3] // 2
    kv = keyvalue.shape[3] // 2
    qkv = o + 2 * kv
    cosine, sine, bias = tables

    def row(at, start, size):
        return (gains[at : at + 1, start : start + size], True)

    ins = dict(
        hidden=(hidden, True),
        query_weight=(query, False),
        keyvalue_weight=(keyvalue, False),
        output_weight=(output, False),
        mlp_weight=(mlp, False),
    )
    if first:
        ins.update(gain_attn=row(layer, 0, width))
    else:
        joined_in, wqkv_in, wo_in, wgate_in = ((one, False) for one in carry)
        ins.update(joined_in=joined_in, wqkv_in=wqkv_in, wo_in=wo_in, wgate_in=wgate_in)
    if last:
        ins.update(cotangent=(cotangent, True))
    else:
        ins.update(gain_next=row(layer + 1, 0, width))
    ins.update(gain_mlp=row(layer, width, width))
    ins.update(gain_q=row(layer, 2 * width, HD))
    ins.update(gain_k=row(layer, 2 * width + HD, HD))
    ins.update(cosine=(cosine, True), sine=(sine, True), bias=(bias, True))
    outs = dict(
        out=((rows, width), F32, True),
        mid=((rows, width), F32, True),
        raw=((8, rows, o + 2 * kv), F32, True),
        q=((8, rows, o), BF16, True),
        k=((8, rows, kv), BF16, True),
        v=((8, rows, kv), BF16, True),
        att=((8, rows, o), BF16, True),
        product=((8, rows, ff), BF16, True),
        save_gateup=((8, rows, 2 * ff), BF16, False),
        save_b=((8, rows, width), BF16, False),
        save_next=((8, rows, width), BF16, False),
    )
    scratch = exchange_scratch(rows, width)
    scratch.update(gu_stage=pltpu.VMEM((2, 4, rows // 2, 2 * ff), BF16))
    scratch.update(stage=pltpu.VMEM((2, own, max(2 * ff, 2 * (o + 2 * kv))), F32))
    weight = lambda size: pltpu.VMEM((d_rows, size), BF16)
    mine = lambda size: pltpu.VMEM((2, own, size), BF16)
    saved = lambda size: ((d_rows, size), BF16, False)
    scratch.update(wqkv=weight(qkv), wo=weight(o), wgate=weight(ff), wup=weight(ff), wdown=weight(ff))
    scratch.update(own_up=mine(ff), own_down=mine(ff))
    outs.update(save_wup=saved(ff), save_wdown=saved(ff))
    if first:
        outs.update(save_a=((8, rows, width), BF16, False))
        scratch.update(own_qkv=mine(qkv), own_o=mine(o), own_gate=mine(ff))
        outs.update(save_wqkv=saved(qkv), save_wo=saved(o), save_wgate=saved(ff))
    if last:
        scratch.update(joined_grad=pltpu.VMEM((8, rows, width), BF16))
    else:
        scratch.update(wnext_qkv=weight(qkv), wnext_o=weight(o), wnext_gate=weight(ff))
        scratch.update(own_next_qkv=mine(qkv), own_next_o=mine(o), own_next_gate=mine(ff))
        outs.update(save_wnext_qkv=saved(qkv), save_wnext_o=saved(o), save_wnext_gate=saved(ff))
    count = 64 + 36 * spread
    scratch.update(local=pltpu.SemaphoreType.DMA((48,)))
    scratch.update(send=pltpu.SemaphoreType.DMA((count,)))
    scratch.update(recv=pltpu.SemaphoreType.DMA((count,)))
    kernel = partial(forward_layer_kernel, layer, last, spread)
    return call(kernel, ins, outs, scratch, 1 + int(last) + 2 * int(not first), "forward_layer")


def mm_tn(a, b):
    return lax.dot_general(a, b, (((0,), (0,)), ((), ())), preferred_element_type=F32)


class Reduce:
    def __init__(self, links, place, blocks, x_in, z_in, outs):
        self.place, self.blocks, self.x_in, self.z_in, self.outs = place, blocks, x_in, z_in, outs
        spread = place.spread
        rows = blocks.shape[1] // spread
        self.rows = rows

        def block(q, r):
            return blocks.at[q, tile(r * rows, rows)]

        self.x_out = [
            [
                links.remote(
                    block(q, lax.rem(place.r + s, spread)), x_in.at[s - 1, q], place.r_id(s)
                )
                for s in range(1, spread)
            ]
            for q in range(4)
        ]
        self.z_out = [
            links.remote(block(q, place.r), z_in.at[q - 1], place.z_id(q)) for q in range(1, 4)
        ]

    def compute(self, q, left, right):
        part = self.blocks.shape[1]
        step = min(256, part)
        start = lax.rem(self.place.z + q, 4) * part

        def one(i, carry):
            x = left[:, :, tile(start + i * step, step)]
            product = mm_tn(x.reshape(-1, step), right())
            self.blocks[q, tile(i * step, step), :] = product.astype(BF16)
            return carry

        lax.fori_loop(0, part // step, one, 0)
        for one_copy in self.x_out[q]:
            one_copy.start()

    def pass_on(self, q):
        for one in self.x_out[q]:
            one.wait_recv()
        step = min(64, self.rows)
        start = self.place.r * self.rows

        def add(i, carry):
            at = tile(start + i * step, step)
            total = self.blocks[q, at, :].astype(F32)
            for s in range(self.place.spread - 1):
                total = total + self.x_in[s, q, tile(i * step, step), :].astype(F32)
            self.blocks[q, at, :] = total.astype(BF16)
            return carry

        lax.fori_loop(0, self.rows // step, add, 0)
        if q:
            self.z_out[q - 1].start()

    def finish(self):
        for one in self.z_out:
            one.wait_recv()
        step = min(64, self.rows)
        low = self.place.low
        start = self.place.r * self.rows

        def add(i, carry):
            at = tile(i * step, step)
            near = self.blocks[0, tile(start + i * step, step), :].astype(F32)
            near = (near + self.z_in[1, at, :].astype(F32)).astype(BF16)
            far = self.z_in[0, at, :].astype(F32) + self.z_in[2, at, :].astype(F32)
            far = far.astype(BF16)
            first = 0
            for out, size in self.outs:
                out[at, tile(low * size, size)] = near[:, first : first + size]
                out[at, tile((1 - low) * size, size)] = far[:, first : first + size]
                first += size
            return carry

        lax.fori_loop(0, self.rows // step, add, 0)

    def drain(self):
        for group in self.x_out:
            for one in group:
                one.wait_send()
        for one in self.z_out:
            one.wait_send()


ORDER = (2, 1, 3, 0)


def gate_up_back(ns, pairs, start, size, slot):
    ff = ns.product.shape[2]
    d_act = mm(take(ns.joined, pairs, start, size), ns.wdown[...])
    gate = ns.stage[slot, :, :, :ff].reshape(4 * size, ff).astype(F32)
    up = ns.stage[slot, :, :, ff:].reshape(4 * size, ff).astype(F32)
    gated = 1.0 / (1.0 + jnp.exp(-gate))
    put(ns.d_gate, pairs, start, size, (d_act * up * gated * (1.0 + gate * (1.0 - gated))).astype(BF16))
    put(ns.d_up, pairs, start, size, (d_act * gate * gated).astype(BF16))


def head_back(ns, blocks, d_out, raw_columns, gain, d_gain):
    rows = d_out.shape[0]
    cosine, sine = ns.cosine[blocks].reshape(rows, HD), ns.sine[blocks].reshape(rows, HD)
    raw = ns.raw[blocks, :, raw_columns].reshape(rows, HD)
    d_turned = d_out * cosine + pltpu.roll(d_out * sine, HD // 2, axis=1)
    scale = scale_of(raw)
    normed = raw * scale
    d_gain[...] += jnp.sum(d_turned * normed, axis=0, keepdims=True)
    d_normed = d_turned * gain[...]
    inner = jnp.mean(d_normed * normed, axis=-1, keepdims=True)
    d_raw = (scale * (d_normed - normed * inner)).astype(BF16)
    ns.d_raw[blocks, :, raw_columns] = d_raw.reshape(-1, ns.raw.shape[1], HD)


def attend_back(ns, b):
    block = ns.joined.shape[1]
    span = 2 * block
    q_size, kv_size = ns.q.shape[2], ns.k.shape[2]
    share = q_size // kv_size
    scale = HD**-0.5
    whole = slice(4 * b, 4 * b + 4)
    for kv in range(kv_size // HD):
        columns = slice(kv * HD, (kv + 1) * HD)
        ns.d_keys[...] = jnp.zeros_like(ns.d_keys)
        ns.d_values[...] = jnp.zeros_like(ns.d_values)
        for e in range(kv * share, (kv + 1) * share):
            mine = slice(e * HD, (e + 1) * HD)
            for half in range(2):
                rows = slice(4 * b + 2 * half, 4 * b + 2 * half + 2)
                some = slice(4 * b, 4 * b + 2 * half + 2)
                seen = (half + 1) * span
                keys = ns.k[some, :, columns].reshape(seen, HD)
                values = ns.v[some, :, columns].reshape(seen, HD)
                query = ns.q[rows, :, mine].reshape(span, HD)
                d_out = ns.d_att[rows, :, mine].reshape(span, HD)
                p = softmax(ns, b, half, span, query, keys)
                d_p = mm_nt(d_out, values)
                delta = jnp.sum(d_p * p, axis=-1, keepdims=True)
                d_s = (p * (d_p - delta)).astype(BF16)
                ns.d_values[:seen, :] += mm_tn(p.astype(BF16), d_out)
                ns.d_keys[:seen, :] += mm_tn(d_s, query)
                head_back(ns, rows, mm(d_s, keys) * scale, mine, ns.gain_q, ns.d_gain_q)
        key_columns = slice(q_size + kv * HD, q_size + (kv + 1) * HD)
        head_back(ns, whole, ns.d_keys[...] * scale, key_columns, ns.gain_k, ns.d_gain_k)
        value_columns = slice(q_size + kv_size + kv * HD, q_size + kv_size + (kv + 1) * HD)
        ns.d_raw[whole, :, value_columns] = ns.d_values[...].astype(BF16).reshape(4, block, HD)


class Keep:
    def __init__(self, links, place, blocks, out, start):
        self.place, self.blocks = place, blocks
        spread = place.spread
        rows, columns = blocks.shape[1] // spread, blocks.shape[2]
        self.copies = []
        for q in range(4):
            z = lax.rem(place.z + q, 4)
            self.copies.append(
                [
                    links.copy(
                        blocks.at[q, pl.ds(r * rows, rows)],
                        out.at[(z // 2) * spread + r, lax.rem(z, 2), :, pl.ds(start, columns)],
                    )
                    for r in range(spread)
                ]
            )

    def compute(self, q, left, right):
        part = self.blocks.shape[1]
        step = min(256, part)
        start = lax.rem(self.place.z + q, 4) * part

        def one(i, carry):
            x = left[:, :, tile(start + i * step, step)]
            product = mm_tn(x.reshape(-1, step), right())
            self.blocks[q, tile(i * step, step), :] = product.astype(BF16)
            return carry

        lax.fori_loop(0, part // step, one, 0)
        for one_copy in self.copies[q]:
            one_copy.start()

    def drain(self):
        for group in self.copies:
            for one in group:
                one.wait()


class GainSum:
    def __init__(self, links, place, terms, came, came_r, total):
        spread = place.spread
        self.place, self.terms, self.came, self.came_r, self.total = place, terms, came, came_r, total
        ids = (place.core_id, place.y_id, place.low_id, place.z_id(2))
        self.pairs = [links.remote(terms.at[i], came.at[i], one) for i, one in enumerate(ids)]
        self.sides = [
            links.remote(terms.at[4], came_r.at[place.r], place.r_id(s)) for s in range(1, spread)
        ]
        self.at = 0

    def start(self):
        self.pairs[0].start()

    def step(self):
        i = self.at
        self.at += 1
        if i < 4:
            self.pairs[i].wait_recv()
            self.terms[i + 1] = self.terms[i] + self.came[i]
            if i < 3:
                self.pairs[i + 1].start()
                return
            self.came_r[self.place.r] = self.terms[4]
            for one in self.sides:
                one.start()
            return
        for one in self.sides:
            one.wait_recv()
        total = self.came_r[0]
        for r in range(1, self.place.spread):
            total = total + self.came_r[r]
        self.total[...] = total
        for one in self.pairs + self.sides:
            one.wait_send()


def backward_layer_kernel(layer, spread, ns):
    first = layer == 0
    place = Place(spread)
    links = Links(ns.send, ns.recv, ns.local)
    local = ns.grad_in.shape[0]
    mine = place.own_pair * 2 + place.core
    width = ns.grad_in.shape[1]
    qkv, o, ff = ns.wqkv_in.shape[1], ns.wo_in.shape[1], ns.wdown_in.shape[1]
    kv = (qkv - o) // 2
    diag, y, z, own = place.pairs

    def loads(*pairs):
        copies = [links.copy(src, dst) for src, dst in pairs]
        for one in copies:
            one.start()
        return copies

    def wait(copies):
        for one in copies:
            one.wait()

    if first:
        def reduce(i, outs):
            return Reduce(links, place, ns.blocks.at[i], ns.x_in.at[i], ns.z_in_w.at[i], outs)

        red_down = reduce(0, [(ns.g_mlp.at[2], ff)])
        red_gate = reduce(1, [(ns.g_mlp.at[0], ff)])
        red_up = reduce(2, [(ns.g_mlp.at[1], ff)])
        red_o = Reduce(links, place, ns.blocks_o, ns.x_in_o, ns.z_in_o, [(ns.g_o, o)])
        red_qkv = Reduce(
            links, place, ns.blocks_qkv, ns.x_in_qkv, ns.z_in_qkv,
            [(ns.g_q, o), (ns.g_kv.at[0], kv), (ns.g_kv.at[1], kv)],
        )
    else:
        red_gate = Keep(links, place, ns.blocks.at[1], ns.terms_out, 0)
        red_up = Keep(links, place, ns.blocks.at[2], ns.terms_out, ff)
        red_down = Keep(links, place, ns.blocks.at[0], ns.terms_out, 2 * ff)
        red_o = Keep(links, place, ns.blocks_o, ns.terms_out, 3 * ff)
        red_qkv = Keep(links, place, ns.blocks_qkv, ns.terms_out, 3 * ff + o)
    middle = Halves(links, place, ns, ns.joined)
    end = Halves(links, place, ns, None if first else ns.joined)
    size = middle.size
    first_pairs, last_pairs = (diag, y), (z, own)
    if first:
        gain_sum = GainSum(links, place, ns.terms, ns.came, ns.came_r, ns.gain_total)

    passes = []
    if first:
        passes = [partial(one.pass_on, q) for one in (red_down, red_gate, red_up, red_o, red_qkv) for q in ORDER]

    def pass_next(count=1):
        for _ in range(min(count, len(passes))):
            passes.pop(0)()

    def compute_all(one, left, right):
        for q in ORDER:
            one.compute(q, left, right)

    def back_norm(value, grad, gain, d_gain, out, gather):
        def finish(at, total):
            v = value[at, :].astype(F32)
            scale = scale_of(v)
            normed = v * scale
            d_gain[...] += jnp.sum(total * normed, axis=0, keepdims=True)
            d_normed = total * gain[...]
            inner = jnp.mean(d_normed * normed, axis=-1, keepdims=True)
            g = grad[at, :].astype(F32) + scale * (d_normed - normed * inner)
            out[at, :] = g
            if gather:
                ns.joined[mine, at, :] = g.astype(BF16)

        return finish

    for one in (ns.d_gain_attn, ns.d_gain_mlp, ns.d_gain_q, ns.d_gain_k):
        one[...] = jnp.zeros_like(one)

    flat = lambda ref: lambda: ref[...].reshape(8 * local, -1)

    def mlp_scope(wgate, wup, d_gate, d_up):
        ns.d_gate, ns.d_up = d_gate, d_up
        weight_loads = loads((ns.wgate_in, wgate), (ns.wup_in, wup))

        def part_of(h, columns=1024):
            start = middle.starts[h]
            for which, pairs in ((0, first_pairs), (2, last_pairs)):
                gates, ups = take(d_gate, pairs, start, size), take(d_up, pairs, start, size)

                def step(j, carry):
                    at = tile(j * columns, columns)
                    term = mm_nt(gates, wgate[at, :]) + mm_nt(ups, wup[at, :])
                    put(ns.part, pairs, start, size, term.astype(BF16), at)
                    return carry

                lax.fori_loop(0, width // columns, step, 0)
                middle.sums[h].cross(which, which + 1)

        def down_scope(wdown, product, stage):
            ns.wdown, ns.product, ns.stage = wdown, product, stage
            first_loads = loads((ns.joined_in, ns.joined), (ns.product_in, product))
            down_load = loads((ns.wdown_in, wdown))
            chunks = [(start, pairs) for start in middle.starts for pairs in (first_pairs, last_pairs)]
            gateup_loads = [
                [
                    links.copy(
                        ns.gateup_in.at[pl.ds(p * 2, 2), pl.ds(start, size)], stage.at[i % 2, 2 * j : 2 * j + 2]
                    )
                    for j, p in enumerate(pairs)
                ]
                for i, (start, pairs) in enumerate(chunks)
            ]
            for group in gateup_loads[:2]:
                for one in group:
                    one.start()
            place.greet()
            wait(first_loads)
            compute_all(red_down, ns.joined, flat(product))
            wait(down_load)
            for i, (start, pairs) in enumerate(chunks):
                wait(gateup_loads[i])
                gate_up_back(ns, pairs, start, size, i % 2)
                if i < 2:
                    for one in gateup_loads[i + 2]:
                        one.start()
                if i == 1:
                    wait(weight_loads)
                    part_of(0)
                if i == 2:
                    middle.sums[0].send_y()

        pl.run_scoped(
            down_scope,
            pltpu.VMEM((rows_all, ff), BF16),
            pltpu.VMEM((8, local, ff), BF16),
            pltpu.VMEM((2, 4, size, 2 * ff), BF16),
        )

        def rest_scope(b, mid, grad):
            b_load = loads((ns.mid_in, mid), (ns.grad_in, grad), (ns.b_in, b))
            middle_rows = back_norm(mid, grad, ns.gain_mlp, ns.d_gain_mlp, ns.grad_mid, True)
            part_of(1)
            middle.sums[0].send_z()
            middle.sums[1].send_y()
            wait(b_load)
            compute_all(red_gate, b, flat(d_gate))
            middle.sums[0].end(middle_rows)
            middle.spread[0].start()
            middle.sums[1].send_z()
            pass_next()
            compute_all(red_up, b, flat(d_up))
            middle.sums[1].end(middle_rows)
            middle.spread[1].start()
            pass_next()

        pl.run_scoped(
            rest_scope,
            pltpu.VMEM((8, local, width), BF16),
            pltpu.VMEM((local, width), F32),
            pltpu.VMEM((local, width), ns.grad_in.dtype),
        )

    rows_all = ns.wdown_in.shape[0]
    group = ns.bias_in.shape[1]
    pl.run_scoped(
        mlp_scope,
        pltpu.VMEM((rows_all, ff), BF16),
        pltpu.VMEM((rows_all, ff), BF16),
        pltpu.VMEM((8, local, ff), BF16),
        pltpu.VMEM((8, local, ff), BF16),
    )

    def attention_scope(
        cosine, sine, bias, hidden, wqkv, wo, a, q, k, v, raw, att, d_att, d_raw, d_keys, d_values
    ):
        ns.cosine, ns.sine, ns.bias, ns.hidden = cosine, sine, bias, hidden
        ns.q, ns.k, ns.v, ns.raw, ns.att = q, k, v, raw, att
        ns.d_att, ns.d_raw, ns.d_keys, ns.d_values = d_att, d_raw, d_keys, d_values
        o_loads = loads((ns.wo_in, wo), (ns.att_in, att))
        other_loads = loads(
            (ns.q_in, q), (ns.k_in, k), (ns.v_in, v), (ns.raw_in, raw), (ns.cosine_in, cosine),
            (ns.sine_in, sine), (ns.bias_in, bias), (ns.a_in, a), (ns.wqkv_in, wqkv), (ns.hidden_in, hidden),
        )
        result_rows = back_norm(hidden, ns.grad_mid, ns.gain_attn, ns.d_gain_attn, ns.out, not first)

        def d_attended(h):
            start = middle.starts[h]
            middle.spread[h].ready()
            middle.spread[h].drain()
            for pairs in (first_pairs, last_pairs):
                put(d_att, pairs, start, size, mm(take(ns.joined, pairs, start, size), wo[...]).astype(BF16))

        def part_of(h):
            start = end.starts[h]
            project_out(ns, d_raw, wqkv, first_pairs, start, size)
            end.sums[h].cross(0, 1)
            project_out(ns, d_raw, wqkv, last_pairs, start, size)
            end.sums[h].cross(2, 3)

        middle.spread[0].pass_on()
        middle.spread[1].pass_on()
        pass_next()
        wait(o_loads)
        middle.spread[0].pass_last()
        d_attended(0)
        pass_next()
        middle.spread[1].pass_last()
        d_attended(1)
        compute_all(red_o, ns.joined, flat(att))
        pass_next(2)
        wait(other_loads)
        attend_back(ns, 0)
        pass_next(2)
        attend_back(ns, 1)
        pass_next(2)
        part_of(0)
        end.sums[0].send_y()
        part_of(1)
        end.sums[1].send_y()
        compute_all(red_qkv, a, flat(d_raw))
        end.sums[0].send_z()
        end.sums[1].send_z()
        pass_next(2)
        end.sums[0].end(result_rows)
        if not first:
            end.spread[0].start()
        pass_next(4)
        end.sums[1].end(result_rows)
        if not first:
            end.spread[1].start()
        else:
            red_down.finish()

    pl.run_scoped(
        attention_scope,
        pltpu.VMEM(ns.cosine_in.shape, F32),
        pltpu.VMEM(ns.sine_in.shape, F32),
        pltpu.VMEM(ns.bias_in.shape, BF16),
        pltpu.VMEM(ns.hidden_in.shape, ns.hidden_in.dtype),
        pltpu.VMEM((rows_all, qkv), BF16),
        pltpu.VMEM((rows_all, o), BF16),
        pltpu.VMEM((8, local, width), BF16),
        pltpu.VMEM(ns.q_in.shape, BF16),
        pltpu.VMEM(ns.k_in.shape, BF16),
        pltpu.VMEM(ns.v_in.shape, BF16),
        pltpu.VMEM(ns.raw_in.shape, F32),
        pltpu.VMEM(ns.att_in.shape, BF16),
        pltpu.VMEM((8, local, o), BF16),
        pltpu.VMEM((8, local, qkv), BF16),
        pltpu.VMEM((group, HD), F32),
        pltpu.VMEM((group, HD), F32),
    )
    if first:
        ns.terms[0] = jnp.zeros_like(ns.terms[0])
        earlier = (ns.later_attn, ns.later_mlp, ns.later_q, ns.later_k)
        here = (ns.d_gain_attn, ns.d_gain_mlp, ns.d_gain_q, ns.d_gain_k)
        for i, (attn, mlp, query, key) in enumerate((here, earlier)):
            ns.terms[0, 2 * i : 2 * i + 1, :width] = attn[...]
            ns.terms[0, 2 * i + 1 : 2 * i + 2, :width] = mlp[...]
            ns.terms[0, 2 * i : 2 * i + 1, width : width + HD] = query[...]
            ns.terms[0, 2 * i : 2 * i + 1, width + HD : width + 2 * HD] = key[...]
        gain_sum.start()
        for _ in range(4):
            pass_next()
            gain_sum.step()
        red_gate.finish()
        gain_sum.step()
    else:
        pass_next()
        end.spread[0].pass_on()
        end.spread[1].pass_on()
        pass_next(2)
        end.spread[0].pass_last()
        end.spread[1].pass_last()
        pass_next()
        for one in end.spread:
            one.ready()
            one.drain()
        final = links.copy(ns.joined, ns.save_next)
        final.start()
    if first:
        red_up.finish()
        red_o.finish()
        red_qkv.finish()
    for one in (red_down, red_gate, red_up, red_o, red_qkv):
        one.drain()
    if not first:
        final.wait()
    assert not passes
    links.check()


def backward_layer(layer, grad, grad_rows, kept, later, tables, gains, spread):
    rows, width = grad.shape
    first = layer == 0
    cosine, sine, bias = tables
    d_rows, ff = kept.save_wdown.shape
    o, qkv = kept.wo.shape[1], kept.wqkv.shape[1]
    part = d_rows // 4
    block = part // spread

    def row(start, size):
        return gains[layer : layer + 1, start : start + size]

    ins = dict(
        grad_in=(grad, False),
        joined_in=(grad_rows, False),
        mid_in=(kept.mid, False),
        hidden_in=(kept.hidden, False),
        product_in=(kept.product, False),
        gateup_in=(kept.save_gateup, False),
        b_in=(kept.save_b, False),
        a_in=(kept.a, False),
        wdown_in=(kept.save_wdown, False),
        wgate_in=(kept.wgate, False),
        wup_in=(kept.save_wup, False),
        wqkv_in=(kept.wqkv, False),
        wo_in=(kept.wo, False),
        q_in=(kept.q, False),
        k_in=(kept.k, False),
        v_in=(kept.v, False),
        raw_in=(kept.raw, False),
        att_in=(kept.att, False),
        gain_attn=(row(0, width), True),
        gain_mlp=(row(width, width), True),
        gain_q=(row(2 * width, HD), True),
        gain_k=(row(2 * width + HD, HD), True),
        cosine_in=(cosine, False),
        sine_in=(sine, False),
        bias_in=(bias, False),
    )
    outs = dict(
        out=((rows, width), F32, True),
        d_gain_attn=((1, width), F32, True),
        d_gain_mlp=((1, width), F32, True),
        d_gain_q=((1, HD), F32, True),
        d_gain_k=((1, HD), F32, True),
    )
    if first:
        outs.update(
            g_q=((block, 2 * o), BF16, True), g_kv=((2, block, qkv - o), BF16, True),
            g_o=((block, 2 * o), BF16, True), g_mlp=((3, block, 2 * ff), BF16, True),
        )
    else:
        outs.update(terms_out=((2 * spread, 2, block, 3 * ff + o + qkv), BF16, False))
    if first:
        ins.update(
            later_attn=(later.d_gain_attn, True), later_mlp=(later.d_gain_mlp, True),
            later_q=(later.d_gain_q, True), later_k=(later.d_gain_k, True),
        )
        outs.update(gain_total=((8, width + 2 * HD), F32, True))
    if not first:
        outs.update(save_next=((8, rows, width), BF16, False))
    scratch = exchange_scratch(rows, width)
    side = spread - 1
    scratch.update(grad_mid=pltpu.VMEM((rows, width), F32))
    scratch.update(blocks=pltpu.VMEM((3, 4, part, ff), BF16))
    scratch.update(blocks_o=pltpu.VMEM((4, part, o), BF16))
    scratch.update(blocks_qkv=pltpu.VMEM((4, part, qkv), BF16))
    if first:
        scratch.update(x_in=pltpu.VMEM((3, side, 4, block, ff), BF16))
        scratch.update(x_in_o=pltpu.VMEM((side, 4, block, o), BF16))
        scratch.update(x_in_qkv=pltpu.VMEM((side, 4, block, qkv), BF16))
        scratch.update(z_in_w=pltpu.VMEM((3, 3, block, ff), BF16))
        scratch.update(z_in_o=pltpu.VMEM((3, block, o), BF16))
        scratch.update(z_in_qkv=pltpu.VMEM((3, block, qkv), BF16))
    if first:
        small = (8, width + 2 * HD)
        scratch.update(terms=pltpu.VMEM((5, *small), F32))
        scratch.update(came=pltpu.VMEM((4, *small), F32))
        scratch.update(came_r=pltpu.VMEM((spread, *small), F32))
    count = 60 + 22 * spread
    scratch.update(local=pltpu.SemaphoreType.DMA((36 + (0 if first else 20 * spread),)))
    scratch.update(send=pltpu.SemaphoreType.DMA((count,)))
    scratch.update(recv=pltpu.SemaphoreType.DMA((count,)))
    kernel = partial(backward_layer_kernel, layer, spread)
    return call(kernel, ins, outs, scratch, 6 if first else 5, "backward_layer")


def swap(values):
    return lax.ppermute(values, "zl", [(0, 1), (1, 0)])


def sum_terms(terms, low, ff, o):
    total = lax.psum_scatter(terms, ("zh", "r"), scatter_dimension=0, tiled=True)[0]
    got = swap(jnp.where(low == 0, total[1], total[0]))
    keep = jnp.where(low == 0, total[0], total[1])
    halves = (jnp.where(low == 0, keep, got), jnp.where(low == 0, got, keep))

    def columns(start, size):
        return jnp.concatenate([one[:, start : start + size] for one in halves], axis=1)

    at = 3 * ff + o
    kv = (terms.shape[3] - at - o) // 2
    return [
        columns(at, o),
        jnp.stack([columns(at + o, kv), columns(at + o + kv, kv)]),
        columns(3 * ff, o),
        jnp.stack([columns(i * ff, ff) for i in range(3)]),
    ]


def rope_tables(positions, head_size):
    half = head_size // 2
    frequency = jnp.power(THETA, -2.0 * jnp.arange(half, dtype=F32) / head_size)
    angle = positions.astype(F32)[:, None] * frequency[None, :]
    return (jnp.cos(angle)[:, None, :], jnp.sin(angle)[:, None, :])


def adamw(weight, first, second, grad, rate, decay):
    first_new = BETA_ONE * first + (1.0 - BETA_ONE) * grad
    second_new = BETA_TWO * second + (1.0 - BETA_TWO) * grad * grad
    first_hat = first_new / (1.0 - BETA_ONE**STEP)
    second_hat = second_new / (1.0 - BETA_TWO**STEP)
    weight_new = weight - rate * (first_hat / (jnp.sqrt(second_hat) + ADAM_EPS) + decay * weight)
    return (first_new, second_new, weight_new)


def body(
    tokens, cotangent, segment_ids, gains, gain_first, gain_second,
    query_weight, query_first, query_second,
    keyvalue_weight, keyvalue_first, keyvalue_second,
    output_weight, output_first, output_second,
    mlp_weight, mlp_first, mlp_second,
):
    spread = lax.axis_size("r")
    low = lax.axis_index("zl")
    layers = gains.shape[0]
    local_rows, width = tokens.shape
    group = segment_ids.shape[0]
    rows = 8 * local_rows
    index = jnp.arange(group, dtype=jnp.int32)
    other = swap(segment_ids)
    segments = jnp.stack([jnp.where(low == 0, segment_ids, other), jnp.where(low == 0, other, segment_ids)])
    positions = (index[None, :] - (segments - segments[:, :1])).reshape(rows)
    mask = (segments[:, :, None] == segments[:, None, :]) & (index[None, None, :] <= index[None, :, None])
    bias = jnp.where(mask, 0.0, -1e30).astype(BF16)
    cosine, sine = rope_tables(positions, HD)
    tables = (
        jnp.concatenate([cosine[:, 0], cosine[:, 0]], axis=1).reshape(8, local_rows, HD),
        jnp.concatenate([-sine[:, 0], sine[:, 0]], axis=1).reshape(8, local_rows, HD),
        bias,
    )
    masters = (query_weight, keyvalue_weight, output_weight, mlp_weight)

    hidden, carry = tokens, None
    saved = []
    for layer in range(layers):
        last = layer + 1 == layers
        kept = forward_layer(layer, last, hidden, carry, masters, tables, gains, cotangent, spread)
        if layer == 0:
            carry = (kept.save_a, kept.save_wqkv, kept.save_wo, kept.save_wgate)
        kept.hidden = hidden
        kept.a, kept.wqkv, kept.wo, kept.wgate = carry
        saved.append(kept)
        hidden = kept.out
        if not last:
            carry = (kept.save_next, kept.save_wnext_qkv, kept.save_wnext_o, kept.save_wnext_gate)

    block_output = hidden
    grad = cotangent
    grad_rows = saved[-1].save_next
    reduced = [None] * layers
    done = None
    for layer in reversed(range(layers)):
        done = backward_layer(layer, grad, grad_rows, saved[layer], done, tables, gains, spread)
        grad, grad_rows = done.out, None if layer == 0 else done.save_next
        if layer > 0:
            kept = saved[layer]
            reduced[layer] = sum_terms(done.terms_out, low, kept.save_wdown.shape[1], kept.wo.shape[1])
        else:
            reduced[layer] = [done.g_q, done.g_kv, done.g_o, done.g_mlp]
    stacked = [jnp.stack([entry[i] for entry in reduced]).astype(F32) for i in range(4)]
    sums = done.gain_total
    gain_total = jnp.stack(
        [
            jnp.concatenate([sums[2 * i, :width], sums[2 * i + 1, :width], sums[2 * i, width:]])
            for i in range(layers)
        ]
    )
    head_gain_grads = gain_total[:, 2 * width :]
    gain_new = adamw(gains, gain_first, gain_second, gain_total, GAIN_RATE, 0.0)
    query_new = adamw(query_weight, query_first, query_second, stacked[0], RATE, DECAY)
    keyvalue_new = adamw(keyvalue_weight, keyvalue_first, keyvalue_second, stacked[1], RATE, DECAY)
    output_new = adamw(output_weight, output_first, output_second, stacked[2], RATE * OUTPUT_FACTOR, DECAY)
    mlp_new = adamw(mlp_weight, mlp_first, mlp_second, stacked[3], RATE, DECAY)
    return (block_output, grad, *gain_new, head_gain_grads, *query_new, *keyvalue_new, *output_new, *mlp_new)


def solution(mesh):
    devices = mesh.devices
    names = ("zh", "zl", "r", "tensor")
    parts = jax.sharding.Mesh(devices.reshape(2, 2, -1, devices.shape[1]), names)
    dp = names[:3]
    token = P(names, None)
    flat = P(None, dp, "tensor")
    deep = P(None, None, dp, "tensor")
    placed = (token, token, P(dp), P(), P(), P(), *[flat] * 3, *[deep] * 3, *[flat] * 3, *[deep] * 3)
    outs = (token, token, P(), P(), P(), P(), *[flat] * 3, *[deep] * 3, *[flat] * 3, *[deep] * 3)
    return jax.shard_map(body, mesh=parts, in_specs=placed, out_specs=outs, check_vma=False)
```

```python
from functools import partial
import math
from types import SimpleNamespace

import jax
import jax.numpy as jnp
from jax import lax
from jax.experimental import pallas as pl
from jax.experimental.pallas import tpu as pltpu
from jax.sharding import PartitionSpec as P

HD = 128
STEP = 10
EPSILON = 1e-06
THETA = 1000000.0
BETA_ONE = 0.9
BETA_TWO = 0.95
ADAM_EPS = 1e-08
DECAY = 0.1
RATE = 0.05
GAIN_RATE = 0.8
OUTPUT_FACTOR = math.sqrt(128)

BF16 = jnp.bfloat16
F32 = jnp.float32
MESH = pl.DeviceIdType.MESH
CHUNK = 32
VMEM_LIMIT = 62 * 1024 * 1024


class Place:
    def __init__(self, spread):
        self.spread = spread
        self.dp = lax.axis_index("dp")
        self.tensor = lax.axis_index("tensor")
        self.core = lax.rem(self.tensor, 2)
        self.y = self.tensor // 2
        self.z = self.dp // spread
        self.r = lax.rem(self.dp, spread)
        self.low = lax.rem(self.z, 2)
        self.core_id = {"dp": self.dp, "tensor": self.y * 2 + 1 - self.core}
        self.y_id = {"dp": self.dp, "tensor": (1 - self.y) * 2 + self.core}
        self.low_id = {"dp": self.dp + spread * (1 - 2 * self.low), "tensor": self.tensor}
        self.own_pair = self.low * 2 + self.y
        self.pairs = (
            (1 - self.low) * 2 + 1 - self.y,
            self.low * 2 + 1 - self.y,
            (1 - self.low) * 2 + self.y,
            self.own_pair,
        )

    def z_dp(self, step):
        return lax.rem(self.z + 4 + step, 4) * self.spread + self.r

    def z_id(self, step):
        return {"dp": self.z_dp(step), "tensor": self.tensor}

    def r_dp(self, step):
        return self.z * self.spread + lax.rem(self.r + self.spread + step, self.spread)

    def r_id(self, step):
        return {"dp": self.r_dp(step), "tensor": self.tensor}

    def greet(self):
        ids = [self.core_id, self.y_id]
        ids += [self.z_id(k) for k in range(1, 4)]
        ids += [self.r_id(k) for k in range(1, self.spread)]
        barrier = pltpu.get_barrier_semaphore()
        for one in ids:
            pl.semaphore_signal(barrier, inc=1, device_id=one, device_id_type=MESH)
        pl.semaphore_wait(barrier, len(ids))


class Links:
    def __init__(self, send, recv, local):
        self.send, self.recv, self.local = send, recv, local
        self.count = self.copies = 0

    def remote(self, src, dst, to):
        slot = self.count
        self.count += 1
        return pltpu.make_async_remote_copy(
            src_ref=src, dst_ref=dst, send_sem=self.send.at[slot], recv_sem=self.recv.at[slot],
            device_id=to, device_id_type=MESH,
        )

    def copy(self, src, dst):
        slot = self.copies
        self.copies += 1
        return pltpu.make_async_copy(src, dst, self.local.at[slot])

    def check(self):
        assert self.count <= self.send.shape[0] and self.copies <= self.local.shape[0]


def tile(start, size):
    return pl.ds(pl.multiple_of(start, size), size)


class Spread:
    def __init__(self, links, place, joined, start, rows):
        def block(pair, core):
            return joined.at[pair * 2 + core, pl.ds(start, rows)]

        c = place.core
        diag, y, z, own = place.pairs
        own, from_z, from_y, from_d = (block(p, c) for p in (own, z, y, diag))
        self.to_z = links.remote(own, own, place.low_id)
        self.to_y = links.remote(own, own, place.y_id)
        self.to_core = links.remote(own, own, place.core_id)
        self.on_y = links.remote(from_z, from_z, place.y_id)
        self.core_z = links.remote(from_z, from_z, place.core_id)
        self.core_y = links.remote(from_y, from_y, place.core_id)
        self.core_d = links.remote(from_d, from_d, place.core_id)

    def start(self):
        self.to_z.start()
        self.to_y.start()
        self.to_core.start()

    def pass_on(self):
        self.to_z.wait_recv()
        self.on_y.start()
        self.core_z.start()
        self.to_y.wait_recv()
        self.core_y.start()

    def pass_last(self):
        self.on_y.wait_recv()
        self.core_d.start()

    def ready(self):
        for one in (self.to_core, self.core_z, self.core_y, self.core_d):
            one.wait_recv()

    def drain(self):
        for one in (self.to_z, self.to_y, self.to_core, self.on_y, self.core_z, self.core_y, self.core_d):
            one.wait_send()


class Collect:
    def __init__(self, links, place, ns, start, rows):
        self.place, self.ns, self.start, self.rows = place, ns, start, rows
        here = pl.ds(start, rows)
        self.across = [
            links.remote(ns.part.at[p * 2 + 1 - place.core, here], ns.core_in.at[k, here], place.core_id)
            for k, p in enumerate(place.pairs)
        ]
        self.diag = links.remote(ns.sums.at[0, here], ns.y_in.at[0, here], place.y_id)
        self.to_y = links.remote(ns.sums.at[1, here], ns.y_in.at[1, here], place.y_id)
        self.to_z = links.remote(ns.sums.at[2, here], ns.z_in.at[here], place.low_id)

    def cross(self, *which):
        for k in which:
            self.across[k].start()

    def term(self, k, at):
        block = self.place.pairs[k] * 2 + self.place.core
        return self.ns.part[block, at, :].astype(F32) + self.ns.core_in[k, at, :].astype(F32)

    def each(self, work):
        def step(i, carry):
            work(tile(self.start + i * CHUNK, CHUNK))
            return carry

        lax.fori_loop(0, self.rows // CHUNK, step, 0)

    def add(self, k):
        def work(at):
            total = self.term(k, at)
            if k == 2:
                total = total + self.ns.y_in[0, at, :].astype(F32)
            self.ns.sums[k, at, :] = total.astype(BF16)

        self.each(work)

    def send_y(self):
        self.across[0].wait_recv()
        self.add(0)
        self.diag.start()
        self.across[1].wait_recv()
        self.add(1)
        self.to_y.start()

    def send_z(self):
        self.across[2].wait_recv()
        self.diag.wait_recv()
        self.add(2)
        self.to_z.start()

    def end(self, finish):
        self.across[3].wait_recv()
        self.to_y.wait_recv()
        self.to_z.wait_recv()

        def work(at):
            total = self.term(3, at) + self.ns.y_in[1, at, :].astype(F32) + self.ns.z_in[at, :].astype(F32)
            finish(at, total)

        self.each(work)
        for one in (*self.across, self.diag, self.to_y, self.to_z):
            one.wait_send()


class Halves:
    def __init__(self, links, place, ns, joined):
        rows = ns.part.shape[1] // 2
        self.size = rows
        self.starts = (0, rows)
        self.sums = [Collect(links, place, ns, start, rows) for start in self.starts]
        self.back = joined is not None
        if self.back:
            self.spread = [Spread(links, place, joined, start, rows) for start in self.starts]


def take(ref, pairs, start, size, columns=slice(None)):
    parts = [ref[pl.ds(p * 2, 2), start : start + size, columns] for p in pairs]
    return jnp.concatenate([one.reshape(2 * size, -1) for one in parts], axis=0)


def put(ref, pairs, start, size, value, columns=slice(None)):
    for i, p in enumerate(pairs):
        part = value[2 * i * size : 2 * (i + 1) * size]
        ref[pl.ds(p * 2, 2), start : start + size, columns] = part.reshape(2, size, -1)


class Gather:
    def __init__(self, links, place, sources, own, stage, land, save, earlier):
        rows = own.shape[1]
        self.earlier, self.own_free = earlier, False
        self.place, self.own, self.land, self.rows, self.stage = place, own, land, rows, stage
        self.starts, self.loads = [], []
        start = 0
        for one in sources:
            size = one.shape[1]
            self.starts.append((start, size // 2))
            self.loads.append(links.copy(one, stage.at[:, start : start + size]))
            start += size
        spread = place.spread

        def at(dp):
            return land.at[tile(dp * rows, rows)]

        mine = at(place.dp)
        self.out = [
            links.remote(own.at[lax.rem(place.low + k, 2)], mine, place.z_id(k)) for k in range(1, 4)
        ]
        self.side = [links.remote(own.at[place.low], mine, place.r_id(s)) for s in range(1, spread)]
        self.on = [
            [
                links.remote(at(place.z_dp(-k)), at(place.z_dp(-k)), place.r_id(s))
                for s in range(1, spread)
            ]
            for k in range(1, 4)
        ]
        self.save = links.copy(land, save)

    def load(self):
        for one in self.loads:
            one.start()

    def sent(self):
        for one in self.out + self.side:
            one.wait_send()

    def cast(self):
        for one in self.loads:
            one.wait()
        if self.earlier is not None:
            self.earlier.sent()
            self.earlier.own_free = True
        step = min(64, self.rows)

        def round_rows(i, carry):
            at = tile(i * step, step)
            for low in range(2):
                to = 0
                for start, half in self.starts:
                    piece = self.stage[at, start + low * half : start + (low + 1) * half]
                    self.own[low, at, to : to + half] = piece.astype(BF16)
                    to += half
            return carry

        lax.fori_loop(0, self.rows // step, round_rows, 0)

    def begin(self):
        for one in self.side:
            one.start()
        step = min(64, self.rows)

        def copy(i, carry):
            self.land[tile(self.place.dp * self.rows + i * step, step), :] = self.own[
                self.place.low, tile(i * step, step), :
            ]
            return carry

        lax.fori_loop(0, self.rows // step, copy, 0)

    def forward(self, k):
        self.out[k].wait_recv()
        for one in self.on[k]:
            one.start()

    def finish(self):
        for one in self.side:
            one.wait_recv()
        for group in self.on:
            for one in group:
                one.wait_recv()
        self.save.start()

    def drain(self):
        if not self.own_free:
            self.sent()
        for group in self.on:
            for one in group:
                one.wait_send()
        self.save.wait()


class Stream:
    def __init__(self, groups):
        self.groups = groups
        self.order = [one for group in groups for one in group]
        self.items = [(group, k) for group in groups for k in range(3)]
        self.sent = self.passed = 0
        self.order[0].load()

    def send(self, count=1):
        for group, k in self.items[self.sent : self.sent + count]:
            for one in group:
                if k == 0:
                    one.cast()
                    at = self.order.index(one) + 1
                    if at < len(self.order):
                        self.order[at].load()
                    one.begin()
                one.out[k].start()
            self.sent += 1

    def forward(self, count=1):
        for group, k in self.items[self.passed : min(self.passed + count, self.sent)]:
            for one in group:
                one.forward(k)
            self.passed += 1

    def tick(self, lag=2):
        self.send()
        if self.passed + lag < self.sent or self.sent == len(self.items):
            self.forward()

    def need(self, one):
        place = [i for i, group in enumerate(self.groups) if one in group][0] * 3 + 3
        self.send(max(0, place - self.sent))
        self.forward(max(0, place - self.passed))
        one.finish()

    def rest(self):
        self.send(len(self.items))
        self.forward(len(self.items))


def scale_of(v):
    return lax.rsqrt(jnp.mean(v * v, axis=-1, keepdims=True) + EPSILON)


def mm(a, b):
    return jnp.dot(a, b, preferred_element_type=F32)


def mm_nt(a, b):
    return lax.dot_general(a, b, (((1,), (1,)), ((), ())), preferred_element_type=F32)


def project_heads(ns, pair):
    block = ns.joined.shape[1]
    two = pl.ds(pair * 2, 2)
    x = ns.joined[two].reshape(2 * block, -1)
    raw = mm(x, ns.layer.wqkv[...])
    ns.raw[two] = raw.reshape(2, block, -1)
    cosine, sine = ns.cosine[two].reshape(2 * block, HD), ns.sine[two].reshape(2 * block, HD)
    q_size, kv_size = ns.q.shape[2], ns.k.shape[2]

    def heads(out, start, size, gain):
        for h in range(size // HD):
            v = raw[:, start + h * HD : start + (h + 1) * HD]
            v = v * scale_of(v) * gain[...]
            turned = v * cosine + pltpu.roll(v, HD // 2, axis=1) * sine
            out[two, :, h * HD : (h + 1) * HD] = turned.astype(BF16).reshape(2, block, HD)

    heads(ns.q, 0, q_size, ns.layer.gain_q)
    heads(ns.k, q_size, kv_size, ns.layer.gain_k)
    ns.v[two] = raw[:, q_size + kv_size :].astype(BF16).reshape(2, block, kv_size)


def softmax(ns, b, half, span, query, keys):
    seen = keys.shape[0]
    s = mm_nt(query, keys) * HD**-0.5
    s = s + ns.bias[b, half * span : (half + 1) * span, :seen].astype(F32)
    p = jnp.exp(s - jnp.max(s, axis=-1, keepdims=True))
    return p / jnp.sum(p, axis=-1, keepdims=True)


def attend(ns, b):
    block = ns.joined.shape[1]
    span = 2 * block
    q_heads = ns.q.shape[2] // HD
    share = q_heads // (ns.k.shape[2] // HD)
    for e in range(q_heads):
        kv = slice((e // share) * HD, (e // share + 1) * HD)
        mine = slice(e * HD, (e + 1) * HD)
        for half in range(2):
            rows = slice(4 * b + 2 * half, 4 * b + 2 * half + 2)
            seen = slice(4 * b, 4 * b + 2 * half + 2)
            keys = ns.k[seen, :, kv].reshape(-1, HD)
            values = ns.v[seen, :, kv].reshape(-1, HD)
            query = ns.q[rows, :, mine].reshape(span, HD)
            p = softmax(ns, b, half, span, query, keys)
            ns.att[rows, :, mine] = mm(p.astype(BF16), values).astype(BF16).reshape(2, block, HD)


def project_out(ns, source, weight, pairs, start, size, width=1024):
    x = take(source, pairs, start, size)

    def step(j, carry):
        at = tile(j * width, width)
        put(ns.part, pairs, start, size, mm_nt(x, weight[at, :]).astype(BF16), at)
        return carry

    lax.fori_loop(0, ns.part.shape[2] // width, step, 0)


def gate_up(ns, pairs, start, size, slot):
    ff = ns.product.shape[2]
    x = take(ns.joined, pairs, start, size)
    gate = mm(x, ns.layer.wgate[...])
    up = mm(x, ns.layer.wup[...])
    ns.gu_stage[slot, :, :, :ff] = gate.astype(BF16).reshape(4, size, ff)
    ns.gu_stage[slot, :, :, ff:] = up.astype(BF16).reshape(4, size, ff)
    put(ns.product, pairs, start, size, (gate / (1.0 + jnp.exp(-gate)) * up).astype(BF16))


def forward_kernel(layers, spread, ns):
    place = Place(spread)
    links = Links(ns.send, ns.recv, ns.local)
    local = ns.tokens.shape[0]
    mine = place.own_pair * 2 + place.core
    diag, y, z, own = place.pairs
    first_pairs, last_pairs = (diag, y), (z, own)

    def gathers_of(layer, before):
        kv = ns.keyvalue_weight.at[layer]
        mlp = ns.mlp_weight.at[layer]
        attention = [(ns.query_weight.at[layer], kv.at[0], kv.at[1]), (ns.output_weight.at[layer],)]
        sources = attention + [(mlp.at[i],) for i in range(3)]
        owns = (ns.own_qkv, ns.own_o, ns.own_gate, ns.own_up, ns.own_down)
        lands = (ns.wqkv, ns.wo, ns.wgate, ns.wup, ns.wdown)
        saves = (ns.save_wqkv, ns.save_wo, ns.save_wgate, ns.save_wup, ns.save_wdown)
        return [
            Gather(links, place, source, own_ref, ns.stage, land[layer], save[layer], earlier)
            for source, own_ref, land, save, earlier in zip(sources, owns, lands, saves, before)
        ]

    gathers = []
    for layer in range(layers):
        gathers.append(gathers_of(layer, gathers[-1] if gathers else [None] * 5))
    groups = [[one] for one in gathers[0]]
    for later in gathers[1:]:
        groups += [later[:2], *[[one] for one in later[2:]]]
    stream = Stream(groups)
    tick = stream.tick
    tokens_in = Spread(links, place, ns.joined, 0, local)
    grads_in = Spread(links, place, ns.joined_grad, 0, local)
    middle = Halves(links, place, ns, ns.joined)
    end = Halves(links, place, ns, ns.joined)
    size = middle.size
    rows_save = [links.copy(ns.joined, one) for one in ns.save_a]

    def norm(i, carry):
        at = tile(i * CHUNK, CHUNK)
        v = ns.tokens[at, :].astype(F32)
        ns.hidden[at, :] = v
        ns.joined[mine, at, :] = (v * scale_of(v) * ns.gain_attn[:1, :]).astype(BF16)
        return carry

    lax.fori_loop(0, local // CHUNK, norm, 0)
    place.greet()
    tokens_in.start()
    stream.send(3)
    tokens_in.pass_on()
    stream.send()
    stream.forward()
    stream.send()
    stream.forward()
    stream.send()
    stream.forward()
    tokens_in.pass_last()
    tick()
    tick()
    tokens_in.ready()
    tokens_in.drain()
    for layer in range(layers):
        first, last = layer == 0, layer + 1 == layers
        qkv, o, gate, up, down = gathers[layer]
        kept = [
            links.copy(src, dst[layer])
            for src, dst in (
                (ns.raw, ns.save_raw), (ns.q, ns.save_q), (ns.k, ns.save_k), (ns.v, ns.save_v),
                (ns.att, ns.save_att), (ns.product, ns.save_product), (ns.mid, ns.save_mid),
                (ns.hidden, ns.save_hidden),
            )
        ]
        kept_raw, kept_q, kept_k, kept_v, kept_att, kept_product, kept_mid, kept_hidden = kept
        ns.layer = SimpleNamespace(
            wqkv=ns.wqkv[layer], gain_q=ns.gain_q.at[pl.ds(layer, 1)], gain_k=ns.gain_k.at[pl.ds(layer, 1)],
            wgate=ns.wgate[layer], wup=ns.wup[layer],
        )
        save_a = rows_save[layer]
        save_a.start()
        kept_hidden.start()
        if last:
            ns.joined_grad[mine] = ns.cotangent[...]
            grads_in.start()
        stream.need(qkv)

        def every(i, carry):
            project_heads(ns, i)
            return carry

        lax.fori_loop(0, 2, every, 0)
        tick()
        lax.fori_loop(2, 4, every, 0)
        for one in (kept_raw, kept_q, kept_k, kept_v):
            one.start()
        if last:
            grads_in.pass_on()
        tick()
        attend(ns, 0)
        tick()
        attend(ns, 1)
        kept_att.start()
        tick()
        stream.need(o)
        if last:
            grads_in.pass_last()

        def middle_rows(at, total):
            v = ns.hidden[at, :] + total
            ns.mid[at, :] = v
            gain = ns.gain_mlp[layer : layer + 1, :]
            ns.joined[mine, at, :] = (v * scale_of(v) * gain).astype(BF16)

        def result_rows(at, total):
            v = ns.mid[at, :] + total
            ns.hidden[at, :] = v
            if not last:
                gain = ns.gain_attn[layer + 1 : layer + 2, :]
                ns.joined[mine, at, :] = (v * scale_of(v) * gain).astype(BF16)

        def part_of(source, weight, halves, h):
            start = halves.starts[h]
            project_out(ns, source, weight, first_pairs, start, size)
            halves.sums[h].cross(0, 1)
            project_out(ns, source, weight, last_pairs, start, size)
            halves.sums[h].cross(2, 3)

        save_a.wait()
        part_of(ns.att, ns.wo[layer], middle, 0)
        middle.sums[0].send_y()
        part_of(ns.att, ns.wo[layer], middle, 1)
        middle.sums[1].send_y()
        tick()
        middle.sums[0].send_z()
        middle.sums[1].send_z()
        tick()
        middle.sums[0].end(middle_rows)
        middle.spread[0].start()
        middle.sums[1].end(middle_rows)
        middle.spread[1].start()
        kept_mid.start()
        tick()
        middle.spread[0].pass_on()
        middle.spread[1].pass_on()
        tick()
        stream.need(gate)
        stream.need(up)
        middle.spread[0].pass_last()
        middle.spread[0].ready()
        middle.spread[0].drain()
        saves = []

        def gate_up_of(pairs, start):
            slot = (len(saves) // 2) % 2
            if len(saves) >= 4:
                for save in saves[-4:-2]:
                    save.wait()
            gate_up(ns, pairs, start, size, slot)
            for i, p in enumerate(pairs):
                save = links.copy(
                    ns.gu_stage.at[slot, 2 * i : 2 * i + 2],
                    ns.save_gateup[layer].at[pl.ds(p * 2, 2), pl.ds(start, size)],
                )
                save.start()
                saves.append(save)

        save_b = [
            links.copy(ns.joined.at[:, pl.ds(start, size)], ns.save_b[layer].at[:, pl.ds(start, size)])
            for start in middle.starts
        ]
        save_b[0].start()
        gate_up_of(first_pairs, 0)
        tick()
        middle.spread[1].pass_last()
        gate_up_of(last_pairs, 0)
        stream.need(down)
        save_b[0].wait()
        kept_hidden.wait()
        part_of(ns.product, ns.wdown[layer], end, 0)
        middle.spread[1].ready()
        middle.spread[1].drain()
        end.sums[0].send_y()
        save_b[1].start()
        gate_up_of(first_pairs, size)
        end.sums[0].send_z()
        tick()
        gate_up_of(last_pairs, size)
        kept_product.start()
        save_b[1].wait()
        part_of(ns.product, ns.wdown[layer], end, 1)
        end.sums[1].send_y()
        end.sums[0].end(result_rows)
        if not last:
            end.spread[0].start()
        tick()
        end.sums[1].send_z()
        if not last:
            end.spread[0].pass_on()
        tick()
        end.sums[1].end(result_rows)
        if not last:
            end.spread[1].start()
            tick()
            end.spread[0].pass_last()
            end.spread[1].pass_on()
            tick()
            end.spread[1].pass_last()
            for one in end.spread:
                one.ready()
                one.drain()
        for one in (*saves[-4:], kept_raw, kept_q, kept_k, kept_v, kept_att, kept_product, kept_mid):
            one.wait()
    result = links.copy(ns.hidden, ns.out)
    result.start()
    grads_in.ready()
    grads_in.drain()
    final = links.copy(ns.joined_grad, ns.save_grad)
    final.start()
    for group in gathers:
        for one in group:
            one.drain()
    result.wait()
    final.wait()
    assert stream.passed == len(stream.items)
    links.check()


def call(kernel, ins, outs, scratch, collective_id, name):
    groups = [ins, outs, scratch]
    sizes = [len(v) if isinstance(v, list) else 0 for group in groups for v in group.values()]
    names = [key for group in groups for key in group]

    def flat(group):
        return [one for v in group.values() for one in (v if isinstance(v, list) else [v])]

    def named(values, keys, counts):
        values = list(values)
        taken = {}
        for key, count in zip(keys, counts):
            taken[key] = [values.pop(0) for _ in range(count)] if count else values.pop(0)
        return SimpleNamespace(**taken)

    def run(*refs):
        kernel(named(refs, names, sizes))

    def space(in_vmem):
        return pl.BlockSpec(memory_space=pltpu.VMEM if in_vmem else pl.ANY)

    results = pl.pallas_call(
        run,
        out_shape=[jax.ShapeDtypeStruct(shape, dtype) for shape, dtype, _ in flat(outs)],
        in_specs=[space(v) for _, v in flat(ins)],
        out_specs=[space(v) for _, _, v in flat(outs)],
        scratch_shapes=flat(scratch),
        compiler_params=pltpu.CompilerParams(
            collective_id=collective_id, has_side_effects=True, vmem_limit_bytes=VMEM_LIMIT
        ),
        cost_estimate=pl.CostEstimate(
            flops=26 * 10**9, bytes_accessed=10**8, transcendentals=10**6
        ),
        name=name,
    )(*[array for array, _ in flat(ins)])
    return named(results, outs, sizes[len(ins) : len(ins) + len(outs)])


def exchange_scratch(rows, width):
    return dict(
        joined=pltpu.VMEM((8, rows, width), BF16),
        part=pltpu.VMEM((8, rows, width), BF16),
        core_in=pltpu.VMEM((4, rows, width), BF16),
        y_in=pltpu.VMEM((2, rows, width), BF16),
        z_in=pltpu.VMEM((rows, width), BF16),
        sums=pltpu.VMEM((3, rows, width), BF16),
    )


def forward(tokens, cotangent, masters, tables, gains, spread):
    rows, width = tokens.shape
    query, keyvalue, output, mlp = masters
    layers = gains.shape[0]
    own = query.shape[1]
    d_rows = own * 4 * spread
    o, ff = query.shape[2] // 2, mlp.shape[3] // 2
    kv = keyvalue.shape[3] // 2
    qkv = o + 2 * kv
    cosine, sine, bias = tables
    ins = dict(
        tokens=(tokens, True), cotangent=(cotangent, True),
        query_weight=(query, False), keyvalue_weight=(keyvalue, False),
        output_weight=(output, False), mlp_weight=(mlp, False),
        gain_attn=(gains[:, :width], True), gain_mlp=(gains[:, width : 2 * width], True),
        gain_q=(gains[:, 2 * width : 2 * width + HD], True), gain_k=(gains[:, 2 * width + HD :], True),
        cosine=(cosine, True), sine=(sine, True), bias=(bias, True),
    )

    def each(dtype, *shape):
        return [(shape, dtype, False)] * layers

    outs = dict(
        out=((rows, width), F32, False),
        save_hidden=each(F32, rows, width), save_mid=each(F32, rows, width),
        save_raw=each(F32, 8, rows, qkv), save_q=each(BF16, 8, rows, o),
        save_k=each(BF16, 8, rows, kv), save_v=each(BF16, 8, rows, kv),
        save_att=each(BF16, 8, rows, o), save_product=each(BF16, 8, rows, ff),
        save_gateup=each(BF16, 8, rows, 2 * ff),
        save_a=each(BF16, 8, rows, width), save_b=each(BF16, 8, rows, width),
        save_grad=((8, rows, width), BF16, False),
        save_wqkv=each(BF16, d_rows, qkv), save_wo=each(BF16, d_rows, o),
        save_wgate=each(BF16, d_rows, ff), save_wup=each(BF16, d_rows, ff), save_wdown=each(BF16, d_rows, ff),
    )
    scratch = exchange_scratch(rows, width)
    weight = lambda size: [pltpu.VMEM((d_rows, size), BF16)] * layers
    mine = lambda size: pltpu.VMEM((2, own, size), BF16)
    tokens_of = lambda size, dtype=BF16: pltpu.VMEM((8, rows, size), dtype)
    scratch.update(
        hidden=pltpu.VMEM((rows, width), F32), mid=pltpu.VMEM((rows, width), F32),
        joined_grad=tokens_of(width), gu_stage=pltpu.VMEM((2, 4, rows // 2, 2 * ff), BF16),
        stage=pltpu.VMEM((own, max(2 * ff, 2 * qkv)), F32),
        raw=tokens_of(qkv, F32), q=tokens_of(o), k=tokens_of(kv), v=tokens_of(kv), att=tokens_of(o),
        product=tokens_of(ff),
        wqkv=weight(qkv), wo=weight(o), wgate=weight(ff), wup=weight(ff), wdown=weight(ff),
        own_qkv=mine(qkv), own_o=mine(o), own_gate=mine(ff), own_up=mine(ff), own_down=mine(ff),
        local=pltpu.SemaphoreType.DMA((4 + 36 * layers,)),
    )
    count = 72 + 20 * spread * layers
    scratch.update(send=pltpu.SemaphoreType.DMA((count,)), recv=pltpu.SemaphoreType.DMA((count,)))
    return call(partial(forward_kernel, layers, spread), ins, outs, scratch, 1, "forward")


def mm_tn(a, b):
    return lax.dot_general(a, b, (((0,), (0,)), ((), ())), preferred_element_type=F32)


class Reduce:
    def __init__(self, links, place, blocks, x_in, z_in, outs):
        self.place, self.blocks, self.x_in, self.z_in, self.outs = place, blocks, x_in, z_in, outs
        spread = place.spread
        rows = blocks.shape[1] // spread
        self.rows = rows

        def block(q, r):
            return blocks.at[q, tile(r * rows, rows)]

        self.x_out = [
            [
                links.remote(
                    block(q, lax.rem(place.r + s, spread)), x_in.at[s - 1, q], place.r_id(s)
                )
                for s in range(1, spread)
            ]
            for q in range(4)
        ]
        self.z_out = [
            links.remote(block(q, place.r), z_in.at[q - 1], place.z_id(q)) for q in range(1, 4)
        ]

    def compute(self, q, left, right):
        part = self.blocks.shape[1]
        step = min(256, part)
        start = lax.rem(self.place.z + q, 4) * part

        def one(i, carry):
            x = left[:, :, tile(start + i * step, step)]
            product = mm_tn(x.reshape(-1, step), right())
            self.blocks[q, tile(i * step, step), :] = product.astype(BF16)
            return carry

        lax.fori_loop(0, part // step, one, 0)
        for one_copy in self.x_out[q]:
            one_copy.start()

    def pass_on(self, q):
        for one in self.x_out[q]:
            one.wait_recv()
        step = min(64, self.rows)
        start = self.place.r * self.rows

        def add(i, carry):
            at = tile(start + i * step, step)
            total = self.blocks[q, at, :].astype(F32)
            for s in range(self.place.spread - 1):
                total = total + self.x_in[s, q, tile(i * step, step), :].astype(F32)
            self.blocks[q, at, :] = total.astype(BF16)
            return carry

        lax.fori_loop(0, self.rows // step, add, 0)
        if q:
            self.z_out[q - 1].start()

    def finish(self):
        for one in self.z_out:
            one.wait_recv()
        step = min(64, self.rows)
        low = self.place.low
        start = self.place.r * self.rows

        def add(i, carry):
            at = tile(i * step, step)
            near = self.blocks[0, tile(start + i * step, step), :].astype(F32)
            near = (near + self.z_in[1, at, :].astype(F32)).astype(BF16)
            far = self.z_in[0, at, :].astype(F32) + self.z_in[2, at, :].astype(F32)
            far = far.astype(BF16)
            first = 0
            for out, size in self.outs:
                out[at, tile(low * size, size)] = near[:, first : first + size]
                out[at, tile((1 - low) * size, size)] = far[:, first : first + size]
                first += size
            return carry

        lax.fori_loop(0, self.rows // step, add, 0)

    def drain(self):
        for group in self.x_out:
            for one in group:
                one.wait_send()
        for one in self.z_out:
            one.wait_send()


ORDER = (2, 1, 3, 0)


def gate_up_back(ns, pairs, start, size, slot):
    ff = ns.product.shape[2]
    d_act = mm(take(ns.joined, pairs, start, size), ns.wdown[...])
    gate = ns.stage[slot, :, :, :ff].reshape(4 * size, ff).astype(F32)
    up = ns.stage[slot, :, :, ff:].reshape(4 * size, ff).astype(F32)
    gated = 1.0 / (1.0 + jnp.exp(-gate))
    put(ns.d_gate, pairs, start, size, (d_act * up * gated * (1.0 + gate * (1.0 - gated))).astype(BF16))
    put(ns.d_up, pairs, start, size, (d_act * gate * gated).astype(BF16))


def head_back(ns, blocks, d_out, raw_columns, gain, d_gain):
    rows = d_out.shape[0]
    cosine, sine = ns.cosine[blocks].reshape(rows, HD), ns.sine[blocks].reshape(rows, HD)
    raw = ns.raw[blocks, :, raw_columns].reshape(rows, HD)
    d_turned = d_out * cosine + pltpu.roll(d_out * sine, HD // 2, axis=1)
    scale = scale_of(raw)
    normed = raw * scale
    d_gain[...] += jnp.sum(d_turned * normed, axis=0, keepdims=True)
    d_normed = d_turned * gain[...]
    inner = jnp.mean(d_normed * normed, axis=-1, keepdims=True)
    d_raw = (scale * (d_normed - normed * inner)).astype(BF16)
    ns.d_raw[blocks, :, raw_columns] = d_raw.reshape(-1, ns.raw.shape[1], HD)


def attend_back(ns, b):
    block = ns.joined.shape[1]
    span = 2 * block
    q_size, kv_size = ns.q.shape[2], ns.k.shape[2]
    share = q_size // kv_size
    scale = HD**-0.5
    whole = slice(4 * b, 4 * b + 4)
    for kv in range(kv_size // HD):
        columns = slice(kv * HD, (kv + 1) * HD)
        ns.d_keys[...] = jnp.zeros_like(ns.d_keys)
        ns.d_values[...] = jnp.zeros_like(ns.d_values)
        for e in range(kv * share, (kv + 1) * share):
            mine = slice(e * HD, (e + 1) * HD)
            for half in range(2):
                rows = slice(4 * b + 2 * half, 4 * b + 2 * half + 2)
                some = slice(4 * b, 4 * b + 2 * half + 2)
                seen = (half + 1) * span
                keys = ns.k[some, :, columns].reshape(seen, HD)
                values = ns.v[some, :, columns].reshape(seen, HD)
                query = ns.q[rows, :, mine].reshape(span, HD)
                d_out = ns.d_att[rows, :, mine].reshape(span, HD)
                p = softmax(ns, b, half, span, query, keys)
                d_p = mm_nt(d_out, values)
                delta = jnp.sum(d_p * p, axis=-1, keepdims=True)
                d_s = (p * (d_p - delta)).astype(BF16)
                ns.d_values[:seen, :] += mm_tn(p.astype(BF16), d_out)
                ns.d_keys[:seen, :] += mm_tn(d_s, query)
                head_back(ns, rows, mm(d_s, keys) * scale, mine, ns.gain_q, ns.d_gain_q)
        key_columns = slice(q_size + kv * HD, q_size + (kv + 1) * HD)
        head_back(ns, whole, ns.d_keys[...] * scale, key_columns, ns.gain_k, ns.d_gain_k)
        value_columns = slice(q_size + kv_size + kv * HD, q_size + kv_size + (kv + 1) * HD)
        ns.d_raw[whole, :, value_columns] = ns.d_values[...].astype(BF16).reshape(4, block, HD)


class GainSum:
    def __init__(self, links, place, terms, came, came_r, total):
        spread = place.spread
        self.place, self.terms, self.came, self.came_r, self.total = place, terms, came, came_r, total
        ids = (place.core_id, place.y_id, place.low_id, place.z_id(2))
        self.pairs = [links.remote(terms.at[i], came.at[i], one) for i, one in enumerate(ids)]
        self.sides = [
            links.remote(terms.at[4], came_r.at[place.r], place.r_id(s)) for s in range(1, spread)
        ]
        self.at = 0

    def start(self):
        self.pairs[0].start()

    def step(self):
        i = self.at
        self.at += 1
        if i < 4:
            self.pairs[i].wait_recv()
            self.terms[i + 1] = self.terms[i] + self.came[i]
            if i < 3:
                self.pairs[i + 1].start()
                return
            self.came_r[self.place.r] = self.terms[4]
            for one in self.sides:
                one.start()
            return
        for one in self.sides:
            one.wait_recv()
        total = self.came_r[0]
        for r in range(1, self.place.spread):
            total = total + self.came_r[r]
        self.total[...] = total
        for one in self.pairs + self.sides:
            one.wait_send()


def backward_layer_kernel(layer, spread, ns):
    first = layer == 0
    place = Place(spread)
    links = Links(ns.send, ns.recv, ns.local)
    local = ns.grad_in.shape[0]
    mine = place.own_pair * 2 + place.core
    width = ns.grad_in.shape[1]
    qkv, o, ff = ns.wqkv_in.shape[1], ns.wo_in.shape[1], ns.wdown_in.shape[1]
    kv = (qkv - o) // 2
    diag, y, z, own = place.pairs

    def loads(*pairs):
        copies = [links.copy(src, dst) for src, dst in pairs]
        for one in copies:
            one.start()
        return copies

    def wait(copies):
        for one in copies:
            one.wait()

    def reduce(i, outs):
        return Reduce(links, place, ns.blocks.at[i], ns.x_in.at[i], ns.z_in_w.at[i], outs)

    red_down = reduce(0, [(ns.g_mlp.at[2], ff)])
    red_gate = reduce(1, [(ns.g_mlp.at[0], ff)])
    red_up = reduce(2, [(ns.g_mlp.at[1], ff)])
    red_o = Reduce(links, place, ns.blocks_o, ns.x_in_o, ns.z_in_o, [(ns.g_o, o)])
    red_qkv = Reduce(
        links, place, ns.blocks_qkv, ns.x_in_qkv, ns.z_in_qkv,
        [(ns.g_q, o), (ns.g_kv.at[0], kv), (ns.g_kv.at[1], kv)],
    )
    middle = Halves(links, place, ns, ns.joined)
    end = Halves(links, place, ns, None if first else ns.joined)
    size = middle.size
    first_pairs, last_pairs = (diag, y), (z, own)
    if first:
        gain_sum = GainSum(links, place, ns.terms, ns.came, ns.came_r, ns.gain_total)

    passes = [partial(one.pass_on, q) for one in (red_down, red_gate, red_up, red_o, red_qkv) for q in ORDER]

    def pass_next(count=1):
        for _ in range(count):
            passes.pop(0)()

    def compute_all(one, left, right):
        for q in ORDER:
            one.compute(q, left, right)

    def back_norm(value, grad, gain, d_gain, out, gather):
        def finish(at, total):
            v = value[at, :].astype(F32)
            scale = scale_of(v)
            normed = v * scale
            d_gain[...] += jnp.sum(total * normed, axis=0, keepdims=True)
            d_normed = total * gain[...]
            inner = jnp.mean(d_normed * normed, axis=-1, keepdims=True)
            g = grad[at, :].astype(F32) + scale * (d_normed - normed * inner)
            out[at, :] = g
            if gather:
                ns.joined[mine, at, :] = g.astype(BF16)

        return finish

    for one in (ns.d_gain_attn, ns.d_gain_mlp, ns.d_gain_q, ns.d_gain_k):
        one[...] = jnp.zeros_like(one)

    flat = lambda ref: lambda: ref[...].reshape(8 * local, -1)

    def mlp_scope(wgate, wup, d_gate, d_up):
        ns.d_gate, ns.d_up = d_gate, d_up
        weight_loads = loads((ns.wgate_in, wgate), (ns.wup_in, wup))

        def part_of(h, columns=1024):
            start = middle.starts[h]
            for which, pairs in ((0, first_pairs), (2, last_pairs)):
                gates, ups = take(d_gate, pairs, start, size), take(d_up, pairs, start, size)

                def step(j, carry):
                    at = tile(j * columns, columns)
                    term = mm_nt(gates, wgate[at, :]) + mm_nt(ups, wup[at, :])
                    put(ns.part, pairs, start, size, term.astype(BF16), at)
                    return carry

                lax.fori_loop(0, width // columns, step, 0)
                middle.sums[h].cross(which, which + 1)

        def down_scope(wdown, product, stage):
            ns.wdown, ns.product, ns.stage = wdown, product, stage
            first_loads = loads((ns.joined_in, ns.joined), (ns.product_in, product))
            down_load = loads((ns.wdown_in, wdown))
            chunks = [(start, pairs) for start in middle.starts for pairs in (first_pairs, last_pairs)]
            gateup_loads = [
                [
                    links.copy(
                        ns.gateup_in.at[pl.ds(p * 2, 2), pl.ds(start, size)], stage.at[i % 2, 2 * j : 2 * j + 2]
                    )
                    for j, p in enumerate(pairs)
                ]
                for i, (start, pairs) in enumerate(chunks)
            ]
            for group in gateup_loads[:2]:
                for one in group:
                    one.start()
            place.greet()
            wait(first_loads)
            compute_all(red_down, ns.joined, flat(product))
            wait(down_load)
            for i, (start, pairs) in enumerate(chunks):
                wait(gateup_loads[i])
                gate_up_back(ns, pairs, start, size, i % 2)
                if i < 2:
                    for one in gateup_loads[i + 2]:
                        one.start()
                if i == 1:
                    wait(weight_loads)
                    part_of(0)
                if i == 2:
                    middle.sums[0].send_y()

        pl.run_scoped(
            down_scope,
            pltpu.VMEM((rows_all, ff), BF16),
            pltpu.VMEM((8, local, ff), BF16),
            pltpu.VMEM((2, 4, size, 2 * ff), BF16),
        )

        def rest_scope(b, mid, grad):
            b_load = loads((ns.mid_in, mid), (ns.grad_in, grad), (ns.b_in, b))
            middle_rows = back_norm(mid, grad, ns.gain_mlp, ns.d_gain_mlp, ns.grad_mid, True)
            part_of(1)
            middle.sums[0].send_z()
            middle.sums[1].send_y()
            wait(b_load)
            compute_all(red_gate, b, flat(d_gate))
            middle.sums[0].end(middle_rows)
            middle.spread[0].start()
            middle.sums[1].send_z()
            pass_next()
            compute_all(red_up, b, flat(d_up))
            middle.sums[1].end(middle_rows)
            middle.spread[1].start()
            pass_next()

        pl.run_scoped(
            rest_scope,
            pltpu.VMEM((8, local, width), BF16),
            pltpu.VMEM((local, width), F32),
            pltpu.VMEM((local, width), ns.grad_in.dtype),
        )

    rows_all = ns.wdown_in.shape[0]
    group = ns.bias_in.shape[1]
    pl.run_scoped(
        mlp_scope,
        pltpu.VMEM((rows_all, ff), BF16),
        pltpu.VMEM((rows_all, ff), BF16),
        pltpu.VMEM((8, local, ff), BF16),
        pltpu.VMEM((8, local, ff), BF16),
    )

    def attention_scope(
        cosine, sine, bias, hidden, wqkv, wo, a, q, k, v, raw, att, d_att, d_raw, d_keys, d_values
    ):
        ns.cosine, ns.sine, ns.bias, ns.hidden = cosine, sine, bias, hidden
        ns.q, ns.k, ns.v, ns.raw, ns.att = q, k, v, raw, att
        ns.d_att, ns.d_raw, ns.d_keys, ns.d_values = d_att, d_raw, d_keys, d_values
        o_loads = loads((ns.wo_in, wo), (ns.att_in, att))
        other_loads = loads(
            (ns.q_in, q), (ns.k_in, k), (ns.v_in, v), (ns.raw_in, raw), (ns.cosine_in, cosine),
            (ns.sine_in, sine), (ns.bias_in, bias), (ns.a_in, a), (ns.wqkv_in, wqkv), (ns.hidden_in, hidden),
        )
        result_rows = back_norm(hidden, ns.grad_mid, ns.gain_attn, ns.d_gain_attn, ns.out, not first)

        def d_attended(h):
            start = middle.starts[h]
            middle.spread[h].ready()
            middle.spread[h].drain()
            for pairs in (first_pairs, last_pairs):
                put(d_att, pairs, start, size, mm(take(ns.joined, pairs, start, size), wo[...]).astype(BF16))

        def part_of(h):
            start = end.starts[h]
            project_out(ns, d_raw, wqkv, first_pairs, start, size)
            end.sums[h].cross(0, 1)
            project_out(ns, d_raw, wqkv, last_pairs, start, size)
            end.sums[h].cross(2, 3)

        middle.spread[0].pass_on()
        middle.spread[1].pass_on()
        pass_next()
        wait(o_loads)
        middle.spread[0].pass_last()
        d_attended(0)
        pass_next()
        middle.spread[1].pass_last()
        d_attended(1)
        compute_all(red_o, ns.joined, flat(att))
        pass_next(2)
        wait(other_loads)
        attend_back(ns, 0)
        pass_next(2)
        attend_back(ns, 1)
        pass_next(2)
        part_of(0)
        end.sums[0].send_y()
        part_of(1)
        end.sums[1].send_y()
        compute_all(red_qkv, a, flat(d_raw))
        end.sums[0].send_z()
        end.sums[1].send_z()
        pass_next(2)
        end.sums[0].end(result_rows)
        if not first:
            end.spread[0].start()
        pass_next(4)
        end.sums[1].end(result_rows)
        if not first:
            end.spread[1].start()
        red_down.finish()

    pl.run_scoped(
        attention_scope,
        pltpu.VMEM(ns.cosine_in.shape, F32),
        pltpu.VMEM(ns.sine_in.shape, F32),
        pltpu.VMEM(ns.bias_in.shape, BF16),
        pltpu.VMEM(ns.hidden_in.shape, ns.hidden_in.dtype),
        pltpu.VMEM((rows_all, qkv), BF16),
        pltpu.VMEM((rows_all, o), BF16),
        pltpu.VMEM((8, local, width), BF16),
        pltpu.VMEM(ns.q_in.shape, BF16),
        pltpu.VMEM(ns.k_in.shape, BF16),
        pltpu.VMEM(ns.v_in.shape, BF16),
        pltpu.VMEM(ns.raw_in.shape, F32),
        pltpu.VMEM(ns.att_in.shape, BF16),
        pltpu.VMEM((8, local, o), BF16),
        pltpu.VMEM((8, local, qkv), BF16),
        pltpu.VMEM((group, HD), F32),
        pltpu.VMEM((group, HD), F32),
    )
    if first:
        ns.terms[0] = jnp.zeros_like(ns.terms[0])
        earlier = (ns.later_attn, ns.later_mlp, ns.later_q, ns.later_k)
        here = (ns.d_gain_attn, ns.d_gain_mlp, ns.d_gain_q, ns.d_gain_k)
        for i, (attn, mlp, query, key) in enumerate((here, earlier)):
            ns.terms[0, 2 * i : 2 * i + 1, :width] = attn[...]
            ns.terms[0, 2 * i + 1 : 2 * i + 2, :width] = mlp[...]
            ns.terms[0, 2 * i : 2 * i + 1, width : width + HD] = query[...]
            ns.terms[0, 2 * i : 2 * i + 1, width + HD : width + 2 * HD] = key[...]
        gain_sum.start()
        for _ in range(4):
            pass_next()
            gain_sum.step()
        red_gate.finish()
        gain_sum.step()
    else:
        pass_next()
        end.spread[0].pass_on()
        end.spread[1].pass_on()
        pass_next(2)
        end.spread[0].pass_last()
        end.spread[1].pass_last()
        pass_next()
        red_gate.finish()
        for one in end.spread:
            one.ready()
            one.drain()
        final = links.copy(ns.joined, ns.save_next)
        final.start()
    red_up.finish()
    red_o.finish()
    red_qkv.finish()
    for one in (red_down, red_gate, red_up, red_o, red_qkv):
        one.drain()
    if not first:
        final.wait()
    assert not passes
    links.check()


def backward_layer(layer, grad, grad_rows, kept, later, tables, gains, spread):
    rows, width = grad.shape
    first = layer == 0
    cosine, sine, bias = tables
    d_rows, ff = kept.save_wdown[layer].shape
    o, qkv = kept.save_wo[layer].shape[1], kept.save_wqkv[layer].shape[1]
    part = d_rows // 4
    block = part // spread

    def row(start, size):
        return gains[layer : layer + 1, start : start + size]

    ins = dict(
        grad_in=(grad, False),
        joined_in=(grad_rows, False),
        mid_in=(kept.save_mid[layer], False),
        hidden_in=(kept.save_hidden[layer], False),
        product_in=(kept.save_product[layer], False),
        gateup_in=(kept.save_gateup[layer], False),
        b_in=(kept.save_b[layer], False),
        a_in=(kept.save_a[layer], False),
        wdown_in=(kept.save_wdown[layer], False),
        wgate_in=(kept.save_wgate[layer], False),
        wup_in=(kept.save_wup[layer], False),
        wqkv_in=(kept.save_wqkv[layer], False),
        wo_in=(kept.save_wo[layer], False),
        q_in=(kept.save_q[layer], False),
        k_in=(kept.save_k[layer], False),
        v_in=(kept.save_v[layer], False),
        raw_in=(kept.save_raw[layer], False),
        att_in=(kept.save_att[layer], False),
        gain_attn=(row(0, width), True),
        gain_mlp=(row(width, width), True),
        gain_q=(row(2 * width, HD), True),
        gain_k=(row(2 * width + HD, HD), True),
        cosine_in=(cosine, False),
        sine_in=(sine, False),
        bias_in=(bias, False),
    )
    outs = dict(
        out=((rows, width), F32, True),
        d_gain_attn=((1, width), F32, True),
        d_gain_mlp=((1, width), F32, True),
        d_gain_q=((1, HD), F32, True),
        d_gain_k=((1, HD), F32, True),
        g_q=((block, 2 * o), BF16, True),
        g_kv=((2, block, qkv - o), BF16, True),
        g_o=((block, 2 * o), BF16, True),
        g_mlp=((3, block, 2 * ff), BF16, True),
    )
    if first:
        ins.update(
            later_attn=(later.d_gain_attn, True), later_mlp=(later.d_gain_mlp, True),
            later_q=(later.d_gain_q, True), later_k=(later.d_gain_k, True),
        )
        outs.update(gain_total=((8, width + 2 * HD), F32, True))
    if not first:
        outs.update(save_next=((8, rows, width), BF16, False))
    scratch = exchange_scratch(rows, width)
    side = spread - 1
    scratch.update(grad_mid=pltpu.VMEM((rows, width), F32))
    scratch.update(blocks=pltpu.VMEM((3, 4, part, ff), BF16))
    scratch.update(blocks_o=pltpu.VMEM((4, part, o), BF16))
    scratch.update(blocks_qkv=pltpu.VMEM((4, part, qkv), BF16))
    scratch.update(x_in=pltpu.VMEM((3, side, 4, block, ff), BF16))
    scratch.update(x_in_o=pltpu.VMEM((side, 4, block, o), BF16))
    scratch.update(x_in_qkv=pltpu.VMEM((side, 4, block, qkv), BF16))
    scratch.update(z_in_w=pltpu.VMEM((3, 3, block, ff), BF16))
    scratch.update(z_in_o=pltpu.VMEM((3, block, o), BF16))
    scratch.update(z_in_qkv=pltpu.VMEM((3, block, qkv), BF16))
    if first:
        small = (8, width + 2 * HD)
        scratch.update(terms=pltpu.VMEM((5, *small), F32))
        scratch.update(came=pltpu.VMEM((4, *small), F32))
        scratch.update(came_r=pltpu.VMEM((spread, *small), F32))
    count = 60 + 22 * spread
    scratch.update(local=pltpu.SemaphoreType.DMA((36,)))
    scratch.update(send=pltpu.SemaphoreType.DMA((count,)))
    scratch.update(recv=pltpu.SemaphoreType.DMA((count,)))
    kernel = partial(backward_layer_kernel, layer, spread)
    return call(kernel, ins, outs, scratch, 6 if first else 5, "backward_layer")


def places(dp_size):
    spread = dp_size // 4
    me = lax.axis_index("dp")
    z = me // spread
    return spread, me, lax.rem(me, spread), lax.rem(z, 2), z // 2


def flip_lo(dp_size):
    spread = dp_size // 4
    return [(i, i + spread * (1 - 2 * ((i // spread) % 2))) for i in range(dp_size)]


def flip_hi(dp_size):
    spread = dp_size // 4
    return [(i, i + 2 * spread * (1 - 2 * (i // (2 * spread)))) for i in range(dp_size)]


def shift_r(dp_size, step):
    spread = dp_size // 4
    return [(i, (i // spread) * spread + (i % spread + step) % spread) for i in range(dp_size)]


def rope_tables(positions, head_size):
    half = head_size // 2
    frequency = jnp.power(THETA, -2.0 * jnp.arange(half, dtype=F32) / head_size)
    angle = positions.astype(F32)[:, None] * frequency[None, :]
    return (jnp.cos(angle)[:, None, :], jnp.sin(angle)[:, None, :])


def adamw(weight, first, second, grad, rate, decay):
    first_new = BETA_ONE * first + (1.0 - BETA_ONE) * grad
    second_new = BETA_TWO * second + (1.0 - BETA_TWO) * grad * grad
    first_hat = first_new / (1.0 - BETA_ONE**STEP)
    second_hat = second_new / (1.0 - BETA_TWO**STEP)
    weight_new = weight - rate * (first_hat / (jnp.sqrt(second_hat) + ADAM_EPS) + decay * weight)
    return (first_new, second_new, weight_new)


def body(
    tokens, cotangent, segment_ids, gains, gain_first, gain_second,
    query_weight, query_first, query_second,
    keyvalue_weight, keyvalue_first, keyvalue_second,
    output_weight, output_first, output_second,
    mlp_weight, mlp_first, mlp_second,
):
    dp_size = lax.axis_size("dp")
    spread, me, r, low, high = places(dp_size)
    layers = gains.shape[0]
    local_rows, width = tokens.shape
    group = segment_ids.shape[0]
    rows = 8 * local_rows
    index = jnp.arange(group, dtype=jnp.int32)
    other = lax.ppermute(segment_ids, "dp", flip_lo(dp_size))
    segments = jnp.stack([jnp.where(low == 0, segment_ids, other), jnp.where(low == 0, other, segment_ids)])
    positions = (index[None, :] - (segments - segments[:, :1])).reshape(rows)
    mask = (segments[:, :, None] == segments[:, None, :]) & (index[None, None, :] <= index[None, :, None])
    bias = jnp.where(mask, 0.0, -1e30).astype(BF16)
    cosine, sine = rope_tables(positions, HD)
    tables = (
        jnp.concatenate([cosine[:, 0], cosine[:, 0]], axis=1).reshape(8, local_rows, HD),
        jnp.concatenate([-sine[:, 0], sine[:, 0]], axis=1).reshape(8, local_rows, HD),
        bias,
    )
    masters = (query_weight, keyvalue_weight, output_weight, mlp_weight)

    kept = forward(tokens, cotangent, masters, tables, gains, spread)
    block_output = kept.out
    grad = cotangent
    grad_rows = kept.save_grad
    reduced = [None] * layers
    done = None
    for layer in reversed(range(layers)):
        done = backward_layer(layer, grad, grad_rows, kept, done, tables, gains, spread)
        grad, grad_rows = done.out, None if layer == 0 else done.save_next
        reduced[layer] = [done.g_q, done.g_kv, done.g_o, done.g_mlp]
    stacked = [jnp.stack([entry[i] for entry in reduced]).astype(F32) for i in range(4)]
    sums = done.gain_total
    gain_total = jnp.stack(
        [
            jnp.concatenate([sums[2 * i, :width], sums[2 * i + 1, :width], sums[2 * i, width:]])
            for i in range(layers)
        ]
    )
    head_gain_grads = gain_total[:, 2 * width :]
    gain_new = adamw(gains, gain_first, gain_second, gain_total, GAIN_RATE, 0.0)
    query_new = adamw(query_weight, query_first, query_second, stacked[0], RATE, DECAY)
    keyvalue_new = adamw(keyvalue_weight, keyvalue_first, keyvalue_second, stacked[1], RATE, DECAY)
    output_new = adamw(output_weight, output_first, output_second, stacked[2], RATE * OUTPUT_FACTOR, DECAY)
    mlp_new = adamw(mlp_weight, mlp_first, mlp_second, stacked[3], RATE, DECAY)
    return (block_output, grad, *gain_new, head_gain_grads, *query_new, *keyvalue_new, *output_new, *mlp_new)


def solution(mesh):
    token = P(("dp", "tensor"), None)
    flat = P(None, "dp", "tensor")
    deep = P(None, None, "dp", "tensor")
    placed = (token, token, P("dp"), P(), P(), P(), *[flat] * 3, *[deep] * 3, *[flat] * 3, *[deep] * 3)
    outs = (token, token, P(), P(), P(), P(), *[flat] * 3, *[deep] * 3, *[flat] * 3, *[deep] * 3)
    return jax.shard_map(body, mesh=mesh, in_specs=placed, out_specs=outs, check_vma=False)
```

```python
from functools import partial
import math
from types import SimpleNamespace

import jax
import jax.numpy as jnp
from jax import lax
from jax.experimental import pallas as pl
from jax.experimental.pallas import tpu as pltpu
from jax.sharding import PartitionSpec as P

HD = 128
STEP = 10
EPSILON = 1e-06
THETA = 1000000.0
BETA_ONE = 0.9
BETA_TWO = 0.95
ADAM_EPS = 1e-08
DECAY = 0.1
RATE = 0.05
GAIN_RATE = 0.8
OUTPUT_FACTOR = math.sqrt(128)

BF16 = jnp.bfloat16
F32 = jnp.float32
MESH = pl.DeviceIdType.MESH
CHUNK = 32
VMEM_LIMIT = 62 * 1024 * 1024


class Place:
    def __init__(self, spread):
        self.spread = spread
        self.dp = lax.axis_index("dp")
        self.tensor = lax.axis_index("tensor")
        self.core = lax.rem(self.tensor, 2)
        self.y = self.tensor // 2
        self.z = self.dp // spread
        self.r = lax.rem(self.dp, spread)
        self.low = lax.rem(self.z, 2)
        self.core_id = {"dp": self.dp, "tensor": self.y * 2 + 1 - self.core}
        self.y_id = {"dp": self.dp, "tensor": (1 - self.y) * 2 + self.core}
        self.low_id = {"dp": self.dp + spread * (1 - 2 * self.low), "tensor": self.tensor}
        self.own_pair = self.low * 2 + self.y
        self.pairs = (
            (1 - self.low) * 2 + 1 - self.y,
            self.low * 2 + 1 - self.y,
            (1 - self.low) * 2 + self.y,
            self.own_pair,
        )

    def z_dp(self, step):
        return lax.rem(self.z + 4 + step, 4) * self.spread + self.r

    def z_id(self, step):
        return {"dp": self.z_dp(step), "tensor": self.tensor}

    def r_dp(self, step):
        return self.z * self.spread + lax.rem(self.r + self.spread + step, self.spread)

    def r_id(self, step):
        return {"dp": self.r_dp(step), "tensor": self.tensor}

    def greet(self):
        ids = [self.core_id, self.y_id]
        ids += [self.z_id(k) for k in range(1, 4)]
        ids += [self.r_id(k) for k in range(1, self.spread)]
        barrier = pltpu.get_barrier_semaphore()
        for one in ids:
            pl.semaphore_signal(barrier, inc=1, device_id=one, device_id_type=MESH)
        pl.semaphore_wait(barrier, len(ids))


class Links:
    def __init__(self, send, recv, local):
        self.send, self.recv, self.local = send, recv, local
        self.count = self.copies = 0

    def remote(self, src, dst, to):
        slot = self.count
        self.count += 1
        return pltpu.make_async_remote_copy(
            src_ref=src, dst_ref=dst, send_sem=self.send.at[slot], recv_sem=self.recv.at[slot],
            device_id=to, device_id_type=MESH,
        )

    def copy(self, src, dst):
        slot = self.copies
        self.copies += 1
        return pltpu.make_async_copy(src, dst, self.local.at[slot])

    def check(self):
        assert self.count <= self.send.shape[0] and self.copies <= self.local.shape[0]


def tile(start, size):
    return pl.ds(pl.multiple_of(start, size), size)


class Spread:
    def __init__(self, links, place, joined, start, rows):
        def block(pair, core):
            return joined.at[pair * 2 + core, pl.ds(start, rows)]

        c = place.core
        diag, y, z, own = place.pairs
        own, from_z, from_y, from_d = (block(p, c) for p in (own, z, y, diag))
        self.to_z = links.remote(own, own, place.low_id)
        self.to_y = links.remote(own, own, place.y_id)
        self.to_core = links.remote(own, own, place.core_id)
        self.on_y = links.remote(from_z, from_z, place.y_id)
        self.core_z = links.remote(from_z, from_z, place.core_id)
        self.core_y = links.remote(from_y, from_y, place.core_id)
        self.core_d = links.remote(from_d, from_d, place.core_id)

    def start(self):
        self.to_z.start()
        self.to_y.start()
        self.to_core.start()

    def pass_on(self):
        self.to_z.wait_recv()
        self.on_y.start()
        self.core_z.start()
        self.to_y.wait_recv()
        self.core_y.start()

    def pass_last(self):
        self.on_y.wait_recv()
        self.core_d.start()

    def ready(self):
        for one in (self.to_core, self.core_z, self.core_y, self.core_d):
            one.wait_recv()

    def drain(self):
        for one in (self.to_z, self.to_y, self.to_core, self.on_y, self.core_z, self.core_y, self.core_d):
            one.wait_send()


class Collect:
    def __init__(self, links, place, ns, start, rows):
        self.place, self.ns, self.start, self.rows = place, ns, start, rows
        here = pl.ds(start, rows)
        self.across = [
            links.remote(ns.part.at[p * 2 + 1 - place.core, here], ns.core_in.at[k, here], place.core_id)
            for k, p in enumerate(place.pairs)
        ]
        self.diag = links.remote(ns.sums.at[0, here], ns.y_in.at[0, here], place.y_id)
        self.to_y = links.remote(ns.sums.at[1, here], ns.y_in.at[1, here], place.y_id)
        self.to_z = links.remote(ns.sums.at[2, here], ns.z_in.at[here], place.low_id)

    def cross(self, *which):
        for k in which:
            self.across[k].start()

    def term(self, k, at):
        block = self.place.pairs[k] * 2 + self.place.core
        return self.ns.part[block, at, :].astype(F32) + self.ns.core_in[k, at, :].astype(F32)

    def each(self, work):
        def step(i, carry):
            work(tile(self.start + i * CHUNK, CHUNK))
            return carry

        lax.fori_loop(0, self.rows // CHUNK, step, 0)

    def add(self, k):
        def work(at):
            total = self.term(k, at)
            if k == 2:
                total = total + self.ns.y_in[0, at, :].astype(F32)
            self.ns.sums[k, at, :] = total.astype(BF16)

        self.each(work)

    def send_y(self):
        self.across[0].wait_recv()
        self.add(0)
        self.diag.start()
        self.across[1].wait_recv()
        self.add(1)
        self.to_y.start()

    def send_z(self):
        self.across[2].wait_recv()
        self.diag.wait_recv()
        self.add(2)
        self.to_z.start()

    def end(self, finish):
        self.across[3].wait_recv()
        self.to_y.wait_recv()
        self.to_z.wait_recv()

        def work(at):
            total = self.term(3, at) + self.ns.y_in[1, at, :].astype(F32) + self.ns.z_in[at, :].astype(F32)
            finish(at, total)

        self.each(work)
        for one in (*self.across, self.diag, self.to_y, self.to_z):
            one.wait_send()


class Halves:
    def __init__(self, links, place, ns, joined):
        rows = ns.part.shape[1] // 2
        self.size = rows
        self.starts = (0, rows)
        self.sums = [Collect(links, place, ns, start, rows) for start in self.starts]
        self.back = joined is not None
        if self.back:
            self.spread = [Spread(links, place, joined, start, rows) for start in self.starts]


def take(ref, pairs, start, size, columns=slice(None)):
    parts = [ref[pl.ds(p * 2, 2), start : start + size, columns] for p in pairs]
    return jnp.concatenate([one.reshape(2 * size, -1) for one in parts], axis=0)


def put(ref, pairs, start, size, value, columns=slice(None)):
    for i, p in enumerate(pairs):
        part = value[2 * i * size : 2 * (i + 1) * size]
        ref[pl.ds(p * 2, 2), start : start + size, columns] = part.reshape(2, size, -1)


class Gather:
    def __init__(self, links, place, sources, own, stage, land, save, earlier):
        rows = own.shape[1]
        self.earlier, self.own_free = earlier, False
        self.place, self.own, self.land, self.rows, self.stage = place, own, land, rows, stage
        self.starts, self.loads = [], []
        start = 0
        for one in sources:
            size = one.shape[1]
            self.starts.append((start, size // 2))
            self.loads.append(links.copy(one, stage.at[:, start : start + size]))
            start += size
        spread = place.spread

        def at(dp):
            return land.at[tile(dp * rows, rows)]

        mine = at(place.dp)
        self.out = [
            links.remote(own.at[lax.rem(place.low + k, 2)], mine, place.z_id(k)) for k in range(1, 4)
        ]
        self.side = [links.remote(own.at[place.low], mine, place.r_id(s)) for s in range(1, spread)]
        self.on = [
            [
                links.remote(at(place.z_dp(-k)), at(place.z_dp(-k)), place.r_id(s))
                for s in range(1, spread)
            ]
            for k in range(1, 4)
        ]
        self.save = links.copy(land, save)

    def load(self):
        for one in self.loads:
            one.start()

    def sent(self):
        for one in self.out + self.side:
            one.wait_send()

    def cast(self):
        for one in self.loads:
            one.wait()
        if self.earlier is not None:
            self.earlier.sent()
            self.earlier.own_free = True
        step = min(64, self.rows)

        def round_rows(i, carry):
            at = tile(i * step, step)
            for low in range(2):
                to = 0
                for start, half in self.starts:
                    piece = self.stage[at, start + low * half : start + (low + 1) * half]
                    self.own[low, at, to : to + half] = piece.astype(BF16)
                    to += half
            return carry

        lax.fori_loop(0, self.rows // step, round_rows, 0)

    def begin(self):
        for one in self.side:
            one.start()
        step = min(64, self.rows)

        def copy(i, carry):
            self.land[tile(self.place.dp * self.rows + i * step, step), :] = self.own[
                self.place.low, tile(i * step, step), :
            ]
            return carry

        lax.fori_loop(0, self.rows // step, copy, 0)

    def forward(self, k):
        self.out[k].wait_recv()
        for one in self.on[k]:
            one.start()

    def finish(self):
        for one in self.side:
            one.wait_recv()
        for group in self.on:
            for one in group:
                one.wait_recv()
        self.save.start()

    def drain(self):
        if not self.own_free:
            self.sent()
        for group in self.on:
            for one in group:
                one.wait_send()
        self.save.wait()


class Stream:
    def __init__(self, groups):
        self.groups = groups
        self.order = [one for group in groups for one in group]
        self.items = [(group, k) for group in groups for k in range(3)]
        self.sent = self.passed = 0
        self.order[0].load()

    def send(self, count=1):
        for group, k in self.items[self.sent : self.sent + count]:
            for one in group:
                if k == 0:
                    one.cast()
                    at = self.order.index(one) + 1
                    if at < len(self.order):
                        self.order[at].load()
                    one.begin()
                one.out[k].start()
            self.sent += 1

    def forward(self, count=1):
        for group, k in self.items[self.passed : min(self.passed + count, self.sent)]:
            for one in group:
                one.forward(k)
            self.passed += 1

    def tick(self, lag=2):
        self.send()
        if self.passed + lag < self.sent or self.sent == len(self.items):
            self.forward()

    def need(self, one):
        place = [i for i, group in enumerate(self.groups) if one in group][0] * 3 + 3
        self.send(max(0, place - self.sent))
        self.forward(max(0, place - self.passed))
        one.finish()

    def rest(self):
        self.send(len(self.items))
        self.forward(len(self.items))


def scale_of(v):
    return lax.rsqrt(jnp.mean(v * v, axis=-1, keepdims=True) + EPSILON)


def mm(a, b):
    return jnp.dot(a, b, preferred_element_type=F32)


def mm_nt(a, b):
    return lax.dot_general(a, b, (((1,), (1,)), ((), ())), preferred_element_type=F32)


def project_heads(ns, pair):
    block = ns.joined.shape[1]
    two = pl.ds(pair * 2, 2)
    x = ns.joined[two].reshape(2 * block, -1)
    raw = mm(x, ns.layer.wqkv[...])
    ns.raw[two] = raw.reshape(2, block, -1)
    cosine, sine = ns.cosine[two].reshape(2 * block, HD), ns.sine[two].reshape(2 * block, HD)
    q_size, kv_size = ns.q.shape[2], ns.k.shape[2]

    def heads(out, start, size, gain):
        for h in range(size // HD):
            v = raw[:, start + h * HD : start + (h + 1) * HD]
            v = v * scale_of(v) * gain[...]
            turned = v * cosine + pltpu.roll(v, HD // 2, axis=1) * sine
            out[two, :, h * HD : (h + 1) * HD] = turned.astype(BF16).reshape(2, block, HD)

    heads(ns.q, 0, q_size, ns.layer.gain_q)
    heads(ns.k, q_size, kv_size, ns.layer.gain_k)
    ns.v[two] = raw[:, q_size + kv_size :].astype(BF16).reshape(2, block, kv_size)


def softmax(ns, b, half, span, query, keys):
    seen = keys.shape[0]
    s = mm_nt(query, keys) * HD**-0.5
    s = s + ns.bias[b, half * span : (half + 1) * span, :seen].astype(F32)
    p = jnp.exp(s - jnp.max(s, axis=-1, keepdims=True))
    return p / jnp.sum(p, axis=-1, keepdims=True)


def attend(ns, b):
    block = ns.joined.shape[1]
    span = 2 * block
    q_heads = ns.q.shape[2] // HD
    share = q_heads // (ns.k.shape[2] // HD)
    for e in range(q_heads):
        kv = slice((e // share) * HD, (e // share + 1) * HD)
        mine = slice(e * HD, (e + 1) * HD)
        for half in range(2):
            rows = slice(4 * b + 2 * half, 4 * b + 2 * half + 2)
            seen = slice(4 * b, 4 * b + 2 * half + 2)
            keys = ns.k[seen, :, kv].reshape(-1, HD)
            values = ns.v[seen, :, kv].reshape(-1, HD)
            query = ns.q[rows, :, mine].reshape(span, HD)
            p = softmax(ns, b, half, span, query, keys)
            ns.att[rows, :, mine] = mm(p.astype(BF16), values).astype(BF16).reshape(2, block, HD)


def project_out(ns, source, weight, pairs, start, size, width=1024):
    x = take(source, pairs, start, size)

    def step(j, carry):
        at = tile(j * width, width)
        put(ns.part, pairs, start, size, mm_nt(x, weight[at, :]).astype(BF16), at)
        return carry

    lax.fori_loop(0, ns.part.shape[2] // width, step, 0)


def gate_up(ns, pairs, start, size, slot):
    ff = ns.product.shape[2]
    x = take(ns.joined, pairs, start, size)
    gate = mm(x, ns.layer.wgate[...])
    up = mm(x, ns.layer.wup[...])
    ns.gu_stage[slot, :, :, :ff] = gate.astype(BF16).reshape(4, size, ff)
    ns.gu_stage[slot, :, :, ff:] = up.astype(BF16).reshape(4, size, ff)
    put(ns.product, pairs, start, size, (gate / (1.0 + jnp.exp(-gate)) * up).astype(BF16))


def forward_kernel(layers, spread, ns):
    place = Place(spread)
    links = Links(ns.send, ns.recv, ns.local)
    local = ns.tokens.shape[0]
    mine = place.own_pair * 2 + place.core
    diag, y, z, own = place.pairs
    first_pairs, last_pairs = (diag, y), (z, own)

    def gathers_of(layer, before):
        kv = ns.keyvalue_weight.at[layer]
        mlp = ns.mlp_weight.at[layer]
        attention = [(ns.query_weight.at[layer], kv.at[0], kv.at[1]), (ns.output_weight.at[layer],)]
        sources = attention + [(mlp.at[i],) for i in range(3)]
        owns = (ns.own_qkv, ns.own_o, ns.own_gate, ns.own_up, ns.own_down)
        lands = (ns.wqkv, ns.wo, ns.wgate, ns.wup, ns.wdown)
        saves = (ns.save_wqkv, ns.save_wo, ns.save_wgate, ns.save_wup, ns.save_wdown)
        return [
            Gather(links, place, source, own_ref, ns.stage, land[layer], save[layer], earlier)
            for source, own_ref, land, save, earlier in zip(sources, owns, lands, saves, before)
        ]

    gathers = []
    for layer in range(layers):
        gathers.append(gathers_of(layer, gathers[-1] if gathers else [None] * 5))
    groups = [[one] for one in gathers[0]]
    for later in gathers[1:]:
        groups += [later[:2], *[[one] for one in later[2:]]]
    stream = Stream(groups)
    tick = stream.tick
    tokens_in = Spread(links, place, ns.joined, 0, local)
    grads_in = Spread(links, place, ns.joined_grad, 0, local)
    middle = Halves(links, place, ns, ns.joined)
    end = Halves(links, place, ns, ns.joined)
    size = middle.size
    rows_save = [links.copy(ns.joined, one) for one in ns.save_a]

    def norm(i, carry):
        at = tile(i * CHUNK, CHUNK)
        v = ns.tokens[at, :].astype(F32)
        ns.hidden[at, :] = v
        ns.joined[mine, at, :] = (v * scale_of(v) * ns.gain_attn[:1, :]).astype(BF16)
        return carry

    lax.fori_loop(0, local // CHUNK, norm, 0)
    place.greet()
    tokens_in.start()
    stream.send(3)
    tokens_in.pass_on()
    stream.send()
    stream.forward()
    stream.send()
    stream.forward()
    stream.send()
    stream.forward()
    tokens_in.pass_last()
    tick()
    tick()
    tokens_in.ready()
    tokens_in.drain()
    for layer in range(layers):
        first, last = layer == 0, layer + 1 == layers
        qkv, o, gate, up, down = gathers[layer]
        kept = [
            links.copy(src, dst[layer])
            for src, dst in (
                (ns.raw, ns.save_raw), (ns.q, ns.save_q), (ns.k, ns.save_k), (ns.v, ns.save_v),
                (ns.att, ns.save_att), (ns.product, ns.save_product), (ns.mid, ns.save_mid),
                (ns.hidden, ns.save_hidden),
            )
        ]
        kept_raw, kept_q, kept_k, kept_v, kept_att, kept_product, kept_mid, kept_hidden = kept
        ns.layer = SimpleNamespace(
            wqkv=ns.wqkv[layer], gain_q=ns.gain_q.at[pl.ds(layer, 1)], gain_k=ns.gain_k.at[pl.ds(layer, 1)],
            wgate=ns.wgate[layer], wup=ns.wup[layer],
        )
        save_a = rows_save[layer]
        save_a.start()
        kept_hidden.start()
        if last:
            ns.joined_grad[mine] = ns.cotangent[...]
            grads_in.start()
        stream.need(qkv)

        def every(i, carry):
            project_heads(ns, i)
            return carry

        lax.fori_loop(0, 2, every, 0)
        tick()
        lax.fori_loop(2, 4, every, 0)
        for one in (kept_raw, kept_q, kept_k, kept_v):
            one.start()
        if last:
            grads_in.pass_on()
        tick()
        attend(ns, 0)
        tick()
        attend(ns, 1)
        kept_att.start()
        tick()
        stream.need(o)
        if last:
            grads_in.pass_last()

        def middle_rows(at, total):
            v = ns.hidden[at, :] + total
            ns.mid[at, :] = v
            gain = ns.gain_mlp[layer : layer + 1, :]
            ns.joined[mine, at, :] = (v * scale_of(v) * gain).astype(BF16)

        def result_rows(at, total):
            v = ns.mid[at, :] + total
            ns.hidden[at, :] = v
            if not last:
                gain = ns.gain_attn[layer + 1 : layer + 2, :]
                ns.joined[mine, at, :] = (v * scale_of(v) * gain).astype(BF16)

        def part_of(source, weight, halves, h):
            start = halves.starts[h]
            project_out(ns, source, weight, first_pairs, start, size)
            halves.sums[h].cross(0, 1)
            project_out(ns, source, weight, last_pairs, start, size)
            halves.sums[h].cross(2, 3)

        save_a.wait()
        part_of(ns.att, ns.wo[layer], middle, 0)
        middle.sums[0].send_y()
        part_of(ns.att, ns.wo[layer], middle, 1)
        middle.sums[1].send_y()
        tick()
        middle.sums[0].send_z()
        middle.sums[1].send_z()
        tick()
        middle.sums[0].end(middle_rows)
        middle.spread[0].start()
        middle.sums[1].end(middle_rows)
        middle.spread[1].start()
        kept_mid.start()
        tick()
        middle.spread[0].pass_on()
        middle.spread[1].pass_on()
        tick()
        stream.need(gate)
        stream.need(up)
        middle.spread[0].pass_last()
        middle.spread[0].ready()
        middle.spread[0].drain()
        saves = []

        def gate_up_of(pairs, start):
            slot = (len(saves) // 2) % 2
            if len(saves) >= 4:
                for save in saves[-4:-2]:
                    save.wait()
            gate_up(ns, pairs, start, size, slot)
            for i, p in enumerate(pairs):
                save = links.copy(
                    ns.gu_stage.at[slot, 2 * i : 2 * i + 2],
                    ns.save_gateup[layer].at[pl.ds(p * 2, 2), pl.ds(start, size)],
                )
                save.start()
                saves.append(save)

        save_b = [
            links.copy(ns.joined.at[:, pl.ds(start, size)], ns.save_b[layer].at[:, pl.ds(start, size)])
            for start in middle.starts
        ]
        save_b[0].start()
        gate_up_of(first_pairs, 0)
        tick()
        middle.spread[1].pass_last()
        gate_up_of(last_pairs, 0)
        stream.need(down)
        save_b[0].wait()
        kept_hidden.wait()
        part_of(ns.product, ns.wdown[layer], end, 0)
        middle.spread[1].ready()
        middle.spread[1].drain()
        end.sums[0].send_y()
        save_b[1].start()
        gate_up_of(first_pairs, size)
        end.sums[0].send_z()
        tick()
        gate_up_of(last_pairs, size)
        kept_product.start()
        save_b[1].wait()
        part_of(ns.product, ns.wdown[layer], end, 1)
        end.sums[1].send_y()
        end.sums[0].end(result_rows)
        if not last:
            end.spread[0].start()
        tick()
        end.sums[1].send_z()
        if not last:
            end.spread[0].pass_on()
        tick()
        end.sums[1].end(result_rows)
        if not last:
            end.spread[1].start()
            tick()
            end.spread[0].pass_last()
            end.spread[1].pass_on()
            tick()
            end.spread[1].pass_last()
            for one in end.spread:
                one.ready()
                one.drain()
        for one in (*saves[-4:], kept_raw, kept_q, kept_k, kept_v, kept_att, kept_product, kept_mid):
            one.wait()
    result = links.copy(ns.hidden, ns.out)
    result.start()
    grads_in.ready()
    grads_in.drain()
    final = links.copy(ns.joined_grad, ns.save_grad)
    final.start()
    for group in gathers:
        for one in group:
            one.drain()
    result.wait()
    final.wait()
    assert stream.passed == len(stream.items)
    links.check()


def call(kernel, ins, outs, scratch, collective_id, name):
    groups = [ins, outs, scratch]
    sizes = [len(v) if isinstance(v, list) else 0 for group in groups for v in group.values()]
    names = [key for group in groups for key in group]

    def flat(group):
        return [one for v in group.values() for one in (v if isinstance(v, list) else [v])]

    def named(values, keys, counts):
        values = list(values)
        taken = {}
        for key, count in zip(keys, counts):
            taken[key] = [values.pop(0) for _ in range(count)] if count else values.pop(0)
        return SimpleNamespace(**taken)

    def run(*refs):
        kernel(named(refs, names, sizes))

    def space(in_vmem):
        return pl.BlockSpec(memory_space=pltpu.VMEM if in_vmem else pl.ANY)

    results = pl.pallas_call(
        run,
        out_shape=[jax.ShapeDtypeStruct(shape, dtype) for shape, dtype, _ in flat(outs)],
        in_specs=[space(v) for _, v in flat(ins)],
        out_specs=[space(v) for _, _, v in flat(outs)],
        scratch_shapes=flat(scratch),
        compiler_params=pltpu.CompilerParams(
            collective_id=collective_id, has_side_effects=True, vmem_limit_bytes=VMEM_LIMIT
        ),
        cost_estimate=pl.CostEstimate(
            flops=26 * 10**9, bytes_accessed=10**8, transcendentals=10**6
        ),
        name=name,
    )(*[array for array, _ in flat(ins)])
    return named(results, outs, sizes[len(ins) : len(ins) + len(outs)])


def exchange_scratch(rows, width):
    return dict(
        joined=pltpu.VMEM((8, rows, width), BF16),
        part=pltpu.VMEM((8, rows, width), BF16),
        core_in=pltpu.VMEM((4, rows, width), BF16),
        y_in=pltpu.VMEM((2, rows, width), BF16),
        z_in=pltpu.VMEM((rows, width), BF16),
        sums=pltpu.VMEM((3, rows, width), BF16),
    )


def forward(tokens, cotangent, masters, tables, gains, spread):
    rows, width = tokens.shape
    query, keyvalue, output, mlp = masters
    layers = gains.shape[0]
    own = query.shape[1]
    d_rows = own * 4 * spread
    o, ff = query.shape[2] // 2, mlp.shape[3] // 2
    kv = keyvalue.shape[3] // 2
    qkv = o + 2 * kv
    cosine, sine, bias = tables
    ins = dict(
        tokens=(tokens, True), cotangent=(cotangent, True),
        query_weight=(query, False), keyvalue_weight=(keyvalue, False),
        output_weight=(output, False), mlp_weight=(mlp, False),
        gain_attn=(gains[:, :width], True), gain_mlp=(gains[:, width : 2 * width], True),
        gain_q=(gains[:, 2 * width : 2 * width + HD], True), gain_k=(gains[:, 2 * width + HD :], True),
        cosine=(cosine, True), sine=(sine, True), bias=(bias, True),
    )

    def each(dtype, *shape):
        return [(shape, dtype, False)] * layers

    outs = dict(
        out=((rows, width), F32, False),
        save_hidden=each(F32, rows, width), save_mid=each(F32, rows, width),
        save_raw=each(F32, 8, rows, qkv), save_q=each(BF16, 8, rows, o),
        save_k=each(BF16, 8, rows, kv), save_v=each(BF16, 8, rows, kv),
        save_att=each(BF16, 8, rows, o), save_product=each(BF16, 8, rows, ff),
        save_gateup=each(BF16, 8, rows, 2 * ff),
        save_a=each(BF16, 8, rows, width), save_b=each(BF16, 8, rows, width),
        save_grad=((8, rows, width), BF16, False),
        save_wqkv=each(BF16, d_rows, qkv), save_wo=each(BF16, d_rows, o),
        save_wgate=each(BF16, d_rows, ff), save_wup=each(BF16, d_rows, ff), save_wdown=each(BF16, d_rows, ff),
    )
    scratch = exchange_scratch(rows, width)
    weight = lambda size: [pltpu.VMEM((d_rows, size), BF16)] * layers
    mine = lambda size: pltpu.VMEM((2, own, size), BF16)
    tokens_of = lambda size, dtype=BF16: pltpu.VMEM((8, rows, size), dtype)
    scratch.update(
        hidden=pltpu.VMEM((rows, width), F32), mid=pltpu.VMEM((rows, width), F32),
        joined_grad=tokens_of(width), gu_stage=pltpu.VMEM((2, 4, rows // 2, 2 * ff), BF16),
        stage=pltpu.VMEM((own, max(2 * ff, 2 * qkv)), F32),
        raw=tokens_of(qkv, F32), q=tokens_of(o), k=tokens_of(kv), v=tokens_of(kv), att=tokens_of(o),
        product=tokens_of(ff),
        wqkv=weight(qkv), wo=weight(o), wgate=weight(ff), wup=weight(ff), wdown=weight(ff),
        own_qkv=mine(qkv), own_o=mine(o), own_gate=mine(ff), own_up=mine(ff), own_down=mine(ff),
        local=pltpu.SemaphoreType.DMA((4 + 36 * layers,)),
    )
    count = 72 + 20 * spread * layers
    scratch.update(send=pltpu.SemaphoreType.DMA((count,)), recv=pltpu.SemaphoreType.DMA((count,)))
    return call(partial(forward_kernel, layers, spread), ins, outs, scratch, 1, "forward")


def mm_tn(a, b):
    return lax.dot_general(a, b, (((0,), (0,)), ((), ())), preferred_element_type=F32)


class Reduce:
    def __init__(self, links, place, blocks, x_in, z_in, outs):
        self.place, self.blocks, self.x_in, self.z_in, self.outs = place, blocks, x_in, z_in, outs
        spread = place.spread
        rows = blocks.shape[1] // spread
        self.rows = rows

        def block(q, r):
            return blocks.at[q, tile(r * rows, rows)]

        self.x_out = [
            [
                links.remote(
                    block(q, lax.rem(place.r + s, spread)), x_in.at[s - 1, q], place.r_id(s)
                )
                for s in range(1, spread)
            ]
            for q in range(4)
        ]
        self.z_out = [
            links.remote(block(q, place.r), z_in.at[q - 1], place.z_id(q)) for q in range(1, 4)
        ]

    def compute(self, q, left, right):
        part = self.blocks.shape[1]
        step = min(256, part)
        start = lax.rem(self.place.z + q, 4) * part

        def one(i, carry):
            x = left[:, :, tile(start + i * step, step)]
            product = mm_tn(x.reshape(-1, step), right())
            self.blocks[q, tile(i * step, step), :] = product.astype(BF16)
            return carry

        lax.fori_loop(0, part // step, one, 0)
        for one_copy in self.x_out[q]:
            one_copy.start()

    def pass_on(self, q):
        for one in self.x_out[q]:
            one.wait_recv()
        step = min(64, self.rows)
        start = self.place.r * self.rows

        def add(i, carry):
            at = tile(start + i * step, step)
            total = self.blocks[q, at, :].astype(F32)
            for s in range(self.place.spread - 1):
                total = total + self.x_in[s, q, tile(i * step, step), :].astype(F32)
            self.blocks[q, at, :] = total.astype(BF16)
            return carry

        lax.fori_loop(0, self.rows // step, add, 0)
        if q:
            self.z_out[q - 1].start()

    def finish(self):
        for one in self.z_out:
            one.wait_recv()
        step = min(64, self.rows)
        low = self.place.low
        start = self.place.r * self.rows

        def add(i, carry):
            at = tile(i * step, step)
            near = self.blocks[0, tile(start + i * step, step), :].astype(F32)
            near = (near + self.z_in[1, at, :].astype(F32)).astype(BF16)
            far = self.z_in[0, at, :].astype(F32) + self.z_in[2, at, :].astype(F32)
            far = far.astype(BF16)
            first = 0
            for out, size in self.outs:
                out[at, tile(low * size, size)] = near[:, first : first + size]
                out[at, tile((1 - low) * size, size)] = far[:, first : first + size]
                first += size
            return carry

        lax.fori_loop(0, self.rows // step, add, 0)

    def drain(self):
        for group in self.x_out:
            for one in group:
                one.wait_send()
        for one in self.z_out:
            one.wait_send()


ORDER = (2, 1, 3, 0)


def gate_up_back(ns, pairs, start, size, slot):
    ff = ns.product.shape[2]
    d_act = mm(take(ns.joined, pairs, start, size), ns.wdown[...])
    gate = ns.stage[slot, :, :, :ff].reshape(4 * size, ff).astype(F32)
    up = ns.stage[slot, :, :, ff:].reshape(4 * size, ff).astype(F32)
    gated = 1.0 / (1.0 + jnp.exp(-gate))
    put(ns.d_gate, pairs, start, size, (d_act * up * gated * (1.0 + gate * (1.0 - gated))).astype(BF16))
    put(ns.d_up, pairs, start, size, (d_act * gate * gated).astype(BF16))


def head_back(ns, blocks, d_out, raw_columns, gain, d_gain):
    rows = d_out.shape[0]
    cosine, sine = ns.cosine[blocks].reshape(rows, HD), ns.sine[blocks].reshape(rows, HD)
    raw = ns.raw[blocks, :, raw_columns].reshape(rows, HD)
    d_turned = d_out * cosine + pltpu.roll(d_out * sine, HD // 2, axis=1)
    scale = scale_of(raw)
    normed = raw * scale
    d_gain[...] += jnp.sum(d_turned * normed, axis=0, keepdims=True)
    d_normed = d_turned * gain[...]
    inner = jnp.mean(d_normed * normed, axis=-1, keepdims=True)
    d_raw = (scale * (d_normed - normed * inner)).astype(BF16)
    ns.d_raw[blocks, :, raw_columns] = d_raw.reshape(-1, ns.raw.shape[1], HD)


def attend_back(ns, b):
    block = ns.joined.shape[1]
    span = 2 * block
    q_size, kv_size = ns.q.shape[2], ns.k.shape[2]
    share = q_size // kv_size
    scale = HD**-0.5
    whole = slice(4 * b, 4 * b + 4)
    for kv in range(kv_size // HD):
        columns = slice(kv * HD, (kv + 1) * HD)
        ns.d_keys[...] = jnp.zeros_like(ns.d_keys)
        ns.d_values[...] = jnp.zeros_like(ns.d_values)
        for e in range(kv * share, (kv + 1) * share):
            mine = slice(e * HD, (e + 1) * HD)
            for half in range(2):
                rows = slice(4 * b + 2 * half, 4 * b + 2 * half + 2)
                some = slice(4 * b, 4 * b + 2 * half + 2)
                seen = (half + 1) * span
                keys = ns.k[some, :, columns].reshape(seen, HD)
                values = ns.v[some, :, columns].reshape(seen, HD)
                query = ns.q[rows, :, mine].reshape(span, HD)
                d_out = ns.d_att[rows, :, mine].reshape(span, HD)
                p = softmax(ns, b, half, span, query, keys)
                d_p = mm_nt(d_out, values)
                delta = jnp.sum(d_p * p, axis=-1, keepdims=True)
                d_s = (p * (d_p - delta)).astype(BF16)
                ns.d_values[:seen, :] += mm_tn(p.astype(BF16), d_out)
                ns.d_keys[:seen, :] += mm_tn(d_s, query)
                head_back(ns, rows, mm(d_s, keys) * scale, mine, ns.gain_q, ns.d_gain_q)
        key_columns = slice(q_size + kv * HD, q_size + (kv + 1) * HD)
        head_back(ns, whole, ns.d_keys[...] * scale, key_columns, ns.gain_k, ns.d_gain_k)
        value_columns = slice(q_size + kv_size + kv * HD, q_size + kv_size + (kv + 1) * HD)
        ns.d_raw[whole, :, value_columns] = ns.d_values[...].astype(BF16).reshape(4, block, HD)


class GainSum:
    def __init__(self, links, place, terms, came, came_r, total):
        spread = place.spread
        self.place, self.terms, self.came, self.came_r, self.total = place, terms, came, came_r, total
        ids = (place.core_id, place.y_id, place.low_id, place.z_id(2))
        self.pairs = [links.remote(terms.at[i], came.at[i], one) for i, one in enumerate(ids)]
        self.sides = [
            links.remote(terms.at[4], came_r.at[place.r], place.r_id(s)) for s in range(1, spread)
        ]
        self.at = 0

    def start(self):
        self.pairs[0].start()

    def step(self):
        i = self.at
        self.at += 1
        if i < 4:
            self.pairs[i].wait_recv()
            self.terms[i + 1] = self.terms[i] + self.came[i]
            if i < 3:
                self.pairs[i + 1].start()
                return
            self.came_r[self.place.r] = self.terms[4]
            for one in self.sides:
                one.start()
            return
        for one in self.sides:
            one.wait_recv()
        total = self.came_r[0]
        for r in range(1, self.place.spread):
            total = total + self.came_r[r]
        self.total[...] = total
        for one in self.pairs + self.sides:
            one.wait_send()


def backward_kernel(layers, spread, ns):
    place = Place(spread)
    links = Links(ns.send, ns.recv, ns.local)
    local, width = ns.out.shape
    mine = place.own_pair * 2 + place.core
    qkv, o, ff = ns.wqkv_in[0].shape[1], ns.wo_in[0].shape[1], ns.wdown_in[0].shape[1]
    kv = (qkv - o) // 2
    rows_all = ns.wdown_in[0].shape[0]
    group = ns.bias_in.shape[1]
    diag, y, z, own = place.pairs
    first_pairs, last_pairs = (diag, y), (z, own)

    def loads(*pairs):
        copies = [links.copy(src, dst) for src, dst in pairs]
        for one in copies:
            one.start()
        return copies

    def wait(copies):
        for one in copies:
            one.wait()

    def reduce(i, outs):
        return Reduce(links, place, ns.blocks.at[i], ns.x_in.at[i], ns.z_in_w.at[i], outs)

    red_down = reduce(0, [(ns.g_mlp.at[2], ff)])
    red_gate = reduce(1, [(ns.g_mlp.at[0], ff)])
    red_up = reduce(2, [(ns.g_mlp.at[1], ff)])
    red_o = Reduce(links, place, ns.blocks_o, ns.x_in_o, ns.z_in_o, [(ns.g_o, o)])
    red_qkv = Reduce(
        links, place, ns.blocks_qkv, ns.x_in_qkv, ns.z_in_qkv,
        [(ns.g_q, o), (ns.g_kv.at[0], kv), (ns.g_kv.at[1], kv)],
    )
    reduces = (red_down, red_gate, red_up, red_o, red_qkv)
    middle = Halves(links, place, ns, ns.joined)
    end = Halves(links, place, ns, ns.joined)
    size = middle.size
    gain_sum = GainSum(links, place, ns.terms, ns.came, ns.came_r, ns.gain_total)
    passes = []
    going = [False]

    def pass_next(count=1):
        for _ in range(count):
            passes.pop(0)()

    def compute_all(one, left, right):
        if going[0]:
            one.drain()
        for q in ORDER:
            one.compute(q, left, right)

    def keep(layer):
        pairs = ((ns.g_q, ns.save_q), (ns.g_kv, ns.save_kv), (ns.g_o, ns.save_o), (ns.g_mlp, ns.save_mlp))
        return [links.copy(one, to[layer]) for one, to in pairs]

    for one in (*ns.d_attn, *ns.d_mlp, *ns.d_q, *ns.d_k):
        one[...] = jnp.zeros_like(one)
    first_rows = loads((ns.joined_in, ns.joined))
    place.greet()
    wait(first_rows)
    for layer in reversed(range(layers)):
        backward_layer(layer, layers, SimpleNamespace(**locals()))
    result = loads((ns.out, ns.input_grad))
    ns.terms[0] = jnp.zeros_like(ns.terms[0])
    for i in range(layers):
        ns.terms[0, 2 * i : 2 * i + 1, :width] = ns.d_attn[i][...]
        ns.terms[0, 2 * i + 1 : 2 * i + 2, :width] = ns.d_mlp[i][...]
        ns.terms[0, 2 * i : 2 * i + 1, width : width + HD] = ns.d_q[i][...]
        ns.terms[0, 2 * i : 2 * i + 1, width + HD : width + 2 * HD] = ns.d_k[i][...]
    gain_sum.start()
    for _ in range(4):
        pass_next()
        gain_sum.step()
    red_gate.finish()
    gain_sum.step()
    red_up.finish()
    red_o.finish()
    red_qkv.finish()
    for one in reduces:
        one.drain()
    last = keep(0)
    for one in last:
        one.start()
    wait(last)
    wait(result)
    assert not passes
    links.check()


def backward_layer(layer, layers, env):
    ns, place, links, loads, wait, local, width = (
        env.ns, env.place, env.links, env.loads, env.wait, env.local, env.width
    )
    middle, end, size, mine, passes, pass_next = env.middle, env.end, env.size, env.mine, env.passes, env.pass_next
    red_down, red_gate, red_up, red_o, red_qkv = env.reduces
    first_pairs, last_pairs, compute_all = env.first_pairs, env.last_pairs, env.compute_all
    first, started = layer == 0, layer + 1 < layers
    passes += [partial(one.pass_on, q) for one in env.reduces for q in ORDER]
    ns.gain_q, ns.gain_k = ns.gains_q.at[pl.ds(layer, 1)], ns.gains_k.at[pl.ds(layer, 1)]
    ns.d_gain_q, ns.d_gain_k = ns.d_q[layer], ns.d_k[layer]
    gain_mlp, gain_attn = ns.gains_mlp.at[pl.ds(layer, 1)], ns.gains_attn.at[pl.ds(layer, 1)]
    ff, qkv, o, rows_all, group = env.ff, env.qkv, env.o, env.rows_all, env.group
    kept = env.keep(layer + 1) if started else []

    def finish_later():
        if started:
            for one in (red_up, red_o, red_qkv):
                one.finish()
            for one in kept:
                one.start()
            for k in range(1, 4):
                pl.semaphore_signal(ns.credit, inc=1, device_id=place.z_id(k), device_id_type=MESH)

    def back_norm(value, grad, gain, d_gain, out, gather):
        def finish(at, total):
            v = value[at, :].astype(F32)
            scale = scale_of(v)
            normed = v * scale
            d_gain[...] += jnp.sum(total * normed, axis=0, keepdims=True)
            d_normed = total * gain[...]
            inner = jnp.mean(d_normed * normed, axis=-1, keepdims=True)
            g = grad[at, :].astype(F32) + scale * (d_normed - normed * inner)
            out[at, :] = g
            if gather:
                ns.joined[mine, at, :] = g.astype(BF16)

        return finish

    flat = lambda ref: lambda: ref[...].reshape(8 * local, -1)

    def mlp_scope(wgate, wup, d_gate, d_up):
        ns.d_gate, ns.d_up = d_gate, d_up
        weight_loads = loads((ns.wgate_in[layer], wgate), (ns.wup_in[layer], wup))

        def part_of(h, columns=1024):
            start = middle.starts[h]
            for which, pairs in ((0, first_pairs), (2, last_pairs)):
                gates, ups = take(d_gate, pairs, start, size), take(d_up, pairs, start, size)

                def step(j, carry):
                    at = tile(j * columns, columns)
                    term = mm_nt(gates, wgate[at, :]) + mm_nt(ups, wup[at, :])
                    put(ns.part, pairs, start, size, term.astype(BF16), at)
                    return carry

                lax.fori_loop(0, width // columns, step, 0)
                middle.sums[h].cross(which, which + 1)

        def down_scope(wdown, product, stage):
            ns.wdown, ns.product, ns.stage = wdown, product, stage
            first_loads = loads((ns.product_in[layer], product))
            down_load = loads((ns.wdown_in[layer], wdown))
            chunks = [(start, pairs) for start in middle.starts for pairs in (first_pairs, last_pairs)]
            gateup_loads = [
                [
                    links.copy(
                        ns.gateup_in[layer].at[pl.ds(p * 2, 2), pl.ds(start, size)], stage.at[i % 2, 2 * j : 2 * j + 2]
                    )
                    for j, p in enumerate(pairs)
                ]
                for i, (start, pairs) in enumerate(chunks)
            ]
            for group in gateup_loads[:2]:
                for one in group:
                    one.start()
            wait(first_loads)
            compute_all(red_down, ns.joined, flat(product))
            wait(down_load)
            for i, (start, pairs) in enumerate(chunks):
                wait(gateup_loads[i])
                gate_up_back(ns, pairs, start, size, i % 2)
                if i < 2:
                    for one in gateup_loads[i + 2]:
                        one.start()
                if i == 1:
                    wait(weight_loads)
                    part_of(0)
                if i == 2:
                    middle.sums[0].send_y()
            finish_later()

        pl.run_scoped(
            down_scope,
            pltpu.VMEM((rows_all, ff), BF16),
            pltpu.VMEM((8, local, ff), BF16),
            pltpu.VMEM((2, 4, size, 2 * ff), BF16),
        )

        def rest_scope(b, mid, grad=None):
            b_load = loads((ns.mid_in[layer], mid), (ns.b_in[layer], b))
            if grad is None:
                grad = ns.out
            else:
                b_load += loads((ns.grad_in, grad))
            middle_rows = back_norm(mid, grad, gain_mlp, ns.d_mlp[layer], ns.grad_mid, True)
            part_of(1)
            middle.sums[0].send_z()
            middle.sums[1].send_y()
            wait(b_load)
            compute_all(red_gate, b, flat(d_gate))
            middle.sums[0].end(middle_rows)
            middle.spread[0].start()
            middle.sums[1].send_z()
            if started:
                pl.semaphore_wait(ns.credit, 3)
            pass_next()
            compute_all(red_up, b, flat(d_up))
            middle.sums[1].end(middle_rows)
            middle.spread[1].start()
            pass_next()

        pl.run_scoped(
            rest_scope,
            pltpu.VMEM((8, local, width), BF16),
            pltpu.VMEM((local, width), F32),
            *([] if started else [pltpu.VMEM((local, width), ns.grad_in.dtype)]),
        )

    pl.run_scoped(
        mlp_scope,
        pltpu.VMEM((rows_all, ff), BF16),
        pltpu.VMEM((rows_all, ff), BF16),
        pltpu.VMEM((8, local, ff), BF16),
        pltpu.VMEM((8, local, ff), BF16),
    )

    def attention_scope(
        cosine, sine, bias, hidden, wqkv, wo, a, q, k, v, raw, att, d_att, d_raw, d_keys, d_values
    ):
        ns.cosine, ns.sine, ns.bias, ns.hidden = cosine, sine, bias, hidden
        ns.q, ns.k, ns.v, ns.raw, ns.att = q, k, v, raw, att
        ns.d_att, ns.d_raw, ns.d_keys, ns.d_values = d_att, d_raw, d_keys, d_values
        o_loads = loads((ns.wo_in[layer], wo), (ns.att_in[layer], att))
        other_loads = loads(
            (ns.q_in[layer], q), (ns.k_in[layer], k), (ns.v_in[layer], v), (ns.raw_in[layer], raw),
            (ns.cosine_in, cosine), (ns.sine_in, sine), (ns.bias_in, bias), (ns.a_in[layer], a),
            (ns.wqkv_in[layer], wqkv), (ns.hidden_in[layer], hidden),
        )
        result_rows = back_norm(hidden, ns.grad_mid, gain_attn, ns.d_attn[layer], ns.out, not first)

        def d_attended(h):
            start = middle.starts[h]
            middle.spread[h].ready()
            middle.spread[h].drain()
            for pairs in (first_pairs, last_pairs):
                put(d_att, pairs, start, size, mm(take(ns.joined, pairs, start, size), wo[...]).astype(BF16))

        def part_of(h):
            start = end.starts[h]
            project_out(ns, d_raw, wqkv, first_pairs, start, size)
            end.sums[h].cross(0, 1)
            project_out(ns, d_raw, wqkv, last_pairs, start, size)
            end.sums[h].cross(2, 3)

        middle.spread[0].pass_on()
        middle.spread[1].pass_on()
        pass_next()
        wait(o_loads)
        middle.spread[0].pass_last()
        d_attended(0)
        pass_next()
        middle.spread[1].pass_last()
        d_attended(1)
        compute_all(red_o, ns.joined, flat(att))
        pass_next(2)
        wait(other_loads)
        attend_back(ns, 0)
        pass_next(2)
        attend_back(ns, 1)
        pass_next(2)
        part_of(0)
        end.sums[0].send_y()
        part_of(1)
        end.sums[1].send_y()
        compute_all(red_qkv, a, flat(d_raw))
        end.sums[0].send_z()
        end.sums[1].send_z()
        pass_next(2)
        end.sums[0].end(result_rows)
        if not first:
            end.spread[0].start()
        pass_next(4)
        end.sums[1].end(result_rows)
        if not first:
            end.spread[1].start()
        wait(kept)
        red_down.finish()

    pl.run_scoped(
        attention_scope,
        pltpu.VMEM(ns.cosine_in.shape, F32),
        pltpu.VMEM(ns.sine_in.shape, F32),
        pltpu.VMEM(ns.bias_in.shape, BF16),
        pltpu.VMEM(ns.hidden_in[layer].shape, F32),
        pltpu.VMEM((rows_all, qkv), BF16),
        pltpu.VMEM((rows_all, o), BF16),
        pltpu.VMEM((8, local, width), BF16),
        pltpu.VMEM(ns.q_in[layer].shape, BF16),
        pltpu.VMEM(ns.k_in[layer].shape, BF16),
        pltpu.VMEM(ns.v_in[layer].shape, BF16),
        pltpu.VMEM(ns.raw_in[layer].shape, F32),
        pltpu.VMEM(ns.att_in[layer].shape, BF16),
        pltpu.VMEM((8, local, o), BF16),
        pltpu.VMEM((8, local, qkv), BF16),
        pltpu.VMEM((group, HD), F32),
        pltpu.VMEM((group, HD), F32),
    )
    if not first:
        pass_next()
        end.spread[0].pass_on()
        end.spread[1].pass_on()
        pass_next(2)
        end.spread[0].pass_last()
        end.spread[1].pass_last()
        pass_next()
        red_gate.finish()
        for one in end.spread:
            one.ready()
            one.drain()
        env.going[0] = True


def backward(cotangent, kept, tables, gains, spread):
    rows, width = cotangent.shape
    cosine, sine, bias = tables
    layers = gains.shape[0]
    d_rows, ff = kept.save_wdown[0].shape
    o, qkv = kept.save_wo[0].shape[1], kept.save_wqkv[0].shape[1]
    part = d_rows // 4
    block = part // spread
    small = (8, width + 2 * HD)

    def far(arrays):
        return [(one, False) for one in arrays]

    ins = dict(
        grad_in=(cotangent, False), joined_in=(kept.save_grad, False),
        mid_in=far(kept.save_mid), hidden_in=far(kept.save_hidden), product_in=far(kept.save_product),
        gateup_in=far(kept.save_gateup), b_in=far(kept.save_b), a_in=far(kept.save_a),
        wdown_in=far(kept.save_wdown), wgate_in=far(kept.save_wgate), wup_in=far(kept.save_wup),
        wqkv_in=far(kept.save_wqkv), wo_in=far(kept.save_wo), q_in=far(kept.save_q), k_in=far(kept.save_k),
        v_in=far(kept.save_v), raw_in=far(kept.save_raw), att_in=far(kept.save_att),
        gains_attn=(gains[:, :width], True), gains_mlp=(gains[:, width : 2 * width], True),
        gains_q=(gains[:, 2 * width : 2 * width + HD], True), gains_k=(gains[:, 2 * width + HD :], True),
        cosine_in=(cosine, False), sine_in=(sine, False), bias_in=(bias, False),
    )
    sums = dict(g_q=(block, 2 * o), g_kv=(2, block, qkv - o), g_o=(block, 2 * o), g_mlp=(3, block, 2 * ff))

    def each(name):
        return [(sums[name], BF16, False)] * layers

    outs = dict(
        input_grad=((rows, width), F32, False), gain_total=(small, F32, True),
        save_q=each("g_q"), save_kv=each("g_kv"), save_o=each("g_o"), save_mlp=each("g_mlp"),
    )
    scratch = exchange_scratch(rows, width)
    scratch.update({name: pltpu.VMEM(shape, BF16) for name, shape in sums.items()})
    side = spread - 1
    wide, thin = [pltpu.VMEM((1, width), F32)] * layers, [pltpu.VMEM((1, HD), F32)] * layers
    count = 88 + 22 * spread
    scratch.update(
        out=pltpu.VMEM((rows, width), F32), grad_mid=pltpu.VMEM((rows, width), F32),
        blocks=pltpu.VMEM((3, 4, part, ff), BF16),
        blocks_o=pltpu.VMEM((4, part, o), BF16), blocks_qkv=pltpu.VMEM((4, part, qkv), BF16),
        x_in=pltpu.VMEM((3, side, 4, block, ff), BF16),
        x_in_o=pltpu.VMEM((side, 4, block, o), BF16), x_in_qkv=pltpu.VMEM((side, 4, block, qkv), BF16),
        z_in_w=pltpu.VMEM((3, 3, block, ff), BF16),
        z_in_o=pltpu.VMEM((3, block, o), BF16), z_in_qkv=pltpu.VMEM((3, block, qkv), BF16),
        d_attn=wide, d_mlp=wide, d_q=thin, d_k=thin,
        terms=pltpu.VMEM((5, *small), F32), came=pltpu.VMEM((4, *small), F32),
        came_r=pltpu.VMEM((spread, *small), F32), credit=pltpu.SemaphoreType.REGULAR,
        local=pltpu.SemaphoreType.DMA((8 + 32 * layers,)),
        send=pltpu.SemaphoreType.DMA((count,)), recv=pltpu.SemaphoreType.DMA((count,)),
    )
    return call(partial(backward_kernel, layers, spread), ins, outs, scratch, 2, "backward")


def places(dp_size):
    spread = dp_size // 4
    me = lax.axis_index("dp")
    z = me // spread
    return spread, me, lax.rem(me, spread), lax.rem(z, 2), z // 2


def flip_lo(dp_size):
    spread = dp_size // 4
    return [(i, i + spread * (1 - 2 * ((i // spread) % 2))) for i in range(dp_size)]


def flip_hi(dp_size):
    spread = dp_size // 4
    return [(i, i + 2 * spread * (1 - 2 * (i // (2 * spread)))) for i in range(dp_size)]


def shift_r(dp_size, step):
    spread = dp_size // 4
    return [(i, (i // spread) * spread + (i % spread + step) % spread) for i in range(dp_size)]


def rope_tables(positions, head_size):
    half = head_size // 2
    frequency = jnp.power(THETA, -2.0 * jnp.arange(half, dtype=F32) / head_size)
    angle = positions.astype(F32)[:, None] * frequency[None, :]
    return (jnp.cos(angle)[:, None, :], jnp.sin(angle)[:, None, :])


def adamw(weight, first, second, grad, rate, decay):
    first_new = BETA_ONE * first + (1.0 - BETA_ONE) * grad
    second_new = BETA_TWO * second + (1.0 - BETA_TWO) * grad * grad
    first_hat = first_new / (1.0 - BETA_ONE**STEP)
    second_hat = second_new / (1.0 - BETA_TWO**STEP)
    weight_new = weight - rate * (first_hat / (jnp.sqrt(second_hat) + ADAM_EPS) + decay * weight)
    return (first_new, second_new, weight_new)


def body(
    tokens, cotangent, segment_ids, gains, gain_first, gain_second,
    query_weight, query_first, query_second,
    keyvalue_weight, keyvalue_first, keyvalue_second,
    output_weight, output_first, output_second,
    mlp_weight, mlp_first, mlp_second,
):
    dp_size = lax.axis_size("dp")
    spread, me, r, low, high = places(dp_size)
    layers = gains.shape[0]
    local_rows, width = tokens.shape
    group = segment_ids.shape[0]
    rows = 8 * local_rows
    index = jnp.arange(group, dtype=jnp.int32)
    other = lax.ppermute(segment_ids, "dp", flip_lo(dp_size))
    segments = jnp.stack([jnp.where(low == 0, segment_ids, other), jnp.where(low == 0, other, segment_ids)])
    positions = (index[None, :] - (segments - segments[:, :1])).reshape(rows)
    mask = (segments[:, :, None] == segments[:, None, :]) & (index[None, None, :] <= index[None, :, None])
    bias = jnp.where(mask, 0.0, -1e30).astype(BF16)
    cosine, sine = rope_tables(positions, HD)
    tables = (
        jnp.concatenate([cosine[:, 0], cosine[:, 0]], axis=1).reshape(8, local_rows, HD),
        jnp.concatenate([-sine[:, 0], sine[:, 0]], axis=1).reshape(8, local_rows, HD),
        bias,
    )
    masters = (query_weight, keyvalue_weight, output_weight, mlp_weight)

    kept = forward(tokens, cotangent, masters, tables, gains, spread)
    block_output = kept.out
    done = backward(cotangent, kept, tables, gains, spread)
    stacked = [
        jnp.stack(one).astype(F32) for one in (done.save_q, done.save_kv, done.save_o, done.save_mlp)
    ]
    sums = done.gain_total
    gain_total = jnp.stack(
        [
            jnp.concatenate([sums[2 * i, :width], sums[2 * i + 1, :width], sums[2 * i, width:]])
            for i in range(layers)
        ]
    )
    head_gain_grads = gain_total[:, 2 * width :]
    gain_new = adamw(gains, gain_first, gain_second, gain_total, GAIN_RATE, 0.0)
    query_new = adamw(query_weight, query_first, query_second, stacked[0], RATE, DECAY)
    keyvalue_new = adamw(keyvalue_weight, keyvalue_first, keyvalue_second, stacked[1], RATE, DECAY)
    output_new = adamw(output_weight, output_first, output_second, stacked[2], RATE * OUTPUT_FACTOR, DECAY)
    mlp_new = adamw(mlp_weight, mlp_first, mlp_second, stacked[3], RATE, DECAY)
    return (block_output, done.input_grad, *gain_new, head_gain_grads, *query_new, *keyvalue_new, *output_new, *mlp_new)


def solution(mesh):
    token = P(("dp", "tensor"), None)
    flat = P(None, "dp", "tensor")
    deep = P(None, None, "dp", "tensor")
    placed = (token, token, P("dp"), P(), P(), P(), *[flat] * 3, *[deep] * 3, *[flat] * 3, *[deep] * 3)
    outs = (token, token, P(), P(), P(), P(), *[flat] * 3, *[deep] * 3, *[flat] * 3, *[deep] * 3)
    return jax.shard_map(body, mesh=mesh, in_specs=placed, out_specs=outs, check_vma=False)
```

```python
from functools import partial
import math
from types import SimpleNamespace

import jax
import jax.numpy as jnp
from jax import lax
from jax.experimental import pallas as pl
from jax.experimental.pallas import tpu as pltpu
from jax.sharding import PartitionSpec as P

HD = 128
STEP = 10
EPSILON = 1e-06
THETA = 1000000.0
BETA_ONE = 0.9
BETA_TWO = 0.95
ADAM_EPS = 1e-08
DECAY = 0.1
RATE = 0.05
GAIN_RATE = 0.8
OUTPUT_FACTOR = math.sqrt(128)

BF16 = jnp.bfloat16
F32 = jnp.float32
MESH = pl.DeviceIdType.MESH
CHUNK = 32
VMEM_LIMIT = 62 * 1024 * 1024


class Place:
    def __init__(self, spread):
        self.spread = spread
        self.dp = lax.axis_index("dp")
        self.tensor = lax.axis_index("tensor")
        self.core = lax.rem(self.tensor, 2)
        self.y = self.tensor // 2
        self.z = self.dp // spread
        self.r = lax.rem(self.dp, spread)
        self.low = lax.rem(self.z, 2)
        self.core_id = {"dp": self.dp, "tensor": self.y * 2 + 1 - self.core}
        self.y_id = {"dp": self.dp, "tensor": (1 - self.y) * 2 + self.core}
        self.low_id = {"dp": self.dp + spread * (1 - 2 * self.low), "tensor": self.tensor}
        self.own_pair = self.low * 2 + self.y
        self.pairs = (
            (1 - self.low) * 2 + 1 - self.y,
            self.low * 2 + 1 - self.y,
            (1 - self.low) * 2 + self.y,
            self.own_pair,
        )

    def z_dp(self, step):
        return lax.rem(self.z + 4 + step, 4) * self.spread + self.r

    def z_id(self, step):
        return {"dp": self.z_dp(step), "tensor": self.tensor}

    def r_dp(self, step):
        return self.z * self.spread + lax.rem(self.r + self.spread + step, self.spread)

    def r_id(self, step):
        return {"dp": self.r_dp(step), "tensor": self.tensor}

    def greet(self):
        ids = [self.core_id, self.y_id]
        ids += [self.z_id(k) for k in range(1, 4)]
        ids += [self.r_id(k) for k in range(1, self.spread)]
        barrier = pltpu.get_barrier_semaphore()
        for one in ids:
            pl.semaphore_signal(barrier, inc=1, device_id=one, device_id_type=MESH)
        pl.semaphore_wait(barrier, len(ids))


class Links:
    def __init__(self, send, recv, local):
        self.send, self.recv, self.local = send, recv, local
        self.count = self.copies = 0

    def remote(self, src, dst, to):
        slot = self.count
        self.count += 1
        return pltpu.make_async_remote_copy(
            src_ref=src, dst_ref=dst, send_sem=self.send.at[slot], recv_sem=self.recv.at[slot],
            device_id=to, device_id_type=MESH,
        )

    def copy(self, src, dst):
        slot = self.copies
        self.copies += 1
        return pltpu.make_async_copy(src, dst, self.local.at[slot])

    def check(self):
        assert self.count <= self.send.shape[0] and self.copies <= self.local.shape[0]


def tile(start, size):
    return pl.ds(pl.multiple_of(start, size), size)


class Spread:
    def __init__(self, links, place, joined, start, rows):
        def block(pair, core):
            return joined.at[pair * 2 + core, pl.ds(start, rows)]

        c = place.core
        diag, y, z, own = place.pairs
        own, from_z, from_y, from_d = (block(p, c) for p in (own, z, y, diag))
        self.to_z = links.remote(own, own, place.low_id)
        self.to_y = links.remote(own, own, place.y_id)
        self.to_core = links.remote(own, own, place.core_id)
        self.on_y = links.remote(from_z, from_z, place.y_id)
        self.core_z = links.remote(from_z, from_z, place.core_id)
        self.core_y = links.remote(from_y, from_y, place.core_id)
        self.core_d = links.remote(from_d, from_d, place.core_id)

    def start(self):
        self.to_z.start()
        self.to_y.start()
        self.to_core.start()

    def pass_on(self):
        self.to_z.wait_recv()
        self.on_y.start()
        self.core_z.start()
        self.to_y.wait_recv()
        self.core_y.start()

    def pass_last(self):
        self.on_y.wait_recv()
        self.core_d.start()

    def ready(self):
        for one in (self.to_core, self.core_z, self.core_y, self.core_d):
            one.wait_recv()

    def drain(self):
        for one in (self.to_z, self.to_y, self.to_core, self.on_y, self.core_z, self.core_y, self.core_d):
            one.wait_send()


class Collect:
    def __init__(self, links, place, ns, start, rows):
        self.place, self.ns, self.start, self.rows = place, ns, start, rows
        here = pl.ds(start, rows)
        self.across = [
            links.remote(ns.part.at[p * 2 + 1 - place.core, here], ns.core_in.at[k, here], place.core_id)
            for k, p in enumerate(place.pairs)
        ]
        self.diag = links.remote(ns.sums.at[0, here], ns.y_in.at[0, here], place.y_id)
        self.to_y = links.remote(ns.sums.at[1, here], ns.y_in.at[1, here], place.y_id)
        self.to_z = links.remote(ns.sums.at[2, here], ns.z_in.at[here], place.low_id)

    def cross(self, *which):
        for k in which:
            self.across[k].start()

    def term(self, k, at):
        block = self.place.pairs[k] * 2 + self.place.core
        return self.ns.part[block, at, :].astype(F32) + self.ns.core_in[k, at, :].astype(F32)

    def each(self, work):
        def step(i, carry):
            work(tile(self.start + i * CHUNK, CHUNK))
            return carry

        lax.fori_loop(0, self.rows // CHUNK, step, 0)

    def add(self, k):
        def work(at):
            total = self.term(k, at)
            if k == 2:
                total = total + self.ns.y_in[0, at, :].astype(F32)
            self.ns.sums[k, at, :] = total.astype(BF16)

        self.each(work)

    def send_y(self):
        self.across[0].wait_recv()
        self.add(0)
        self.diag.start()
        self.across[1].wait_recv()
        self.add(1)
        self.to_y.start()

    def send_z(self):
        self.across[2].wait_recv()
        self.diag.wait_recv()
        self.add(2)
        self.to_z.start()

    def end(self, finish):
        self.across[3].wait_recv()
        self.to_y.wait_recv()
        self.to_z.wait_recv()

        def work(at):
            total = self.term(3, at) + self.ns.y_in[1, at, :].astype(F32) + self.ns.z_in[at, :].astype(F32)
            finish(at, total)

        self.each(work)
        for one in (*self.across, self.diag, self.to_y, self.to_z):
            one.wait_send()


class Halves:
    def __init__(self, links, place, ns, joined):
        rows = ns.part.shape[1] // 2
        self.size = rows
        self.starts = (0, rows)
        self.sums = [Collect(links, place, ns, start, rows) for start in self.starts]
        self.back = joined is not None
        if self.back:
            self.spread = [Spread(links, place, joined, start, rows) for start in self.starts]


def take(ref, pairs, start, size, columns=slice(None)):
    parts = [ref[pl.ds(p * 2, 2), start : start + size, columns] for p in pairs]
    return jnp.concatenate([one.reshape(2 * size, -1) for one in parts], axis=0)


def put(ref, pairs, start, size, value, columns=slice(None)):
    for i, p in enumerate(pairs):
        part = value[2 * i * size : 2 * (i + 1) * size]
        ref[pl.ds(p * 2, 2), start : start + size, columns] = part.reshape(2, size, -1)


class Gather:
    def __init__(self, links, place, sources, own, stage, land, save, earlier):
        rows = own.shape[1]
        self.earlier, self.own_free = earlier, False
        self.place, self.own, self.land, self.rows, self.stage = place, own, land, rows, stage
        self.starts, self.loads = [], []
        start = 0
        for one in sources:
            size = one.shape[1]
            self.starts.append((start, size // 2))
            self.loads.append(links.copy(one, stage.at[:, start : start + size]))
            start += size
        spread = place.spread

        def at(dp):
            return land.at[tile(dp * rows, rows)]

        mine = at(place.dp)
        self.out = [
            links.remote(own.at[lax.rem(place.low + k, 2)], mine, place.z_id(k)) for k in range(1, 4)
        ]
        self.side = [links.remote(own.at[place.low], mine, place.r_id(s)) for s in range(1, spread)]
        self.on = [
            [
                links.remote(at(place.z_dp(-k)), at(place.z_dp(-k)), place.r_id(s))
                for s in range(1, spread)
            ]
            for k in range(1, 4)
        ]
        self.save = links.copy(land, save)

    def load(self):
        for one in self.loads:
            one.start()

    def sent(self):
        for one in self.out + self.side:
            one.wait_send()

    def cast(self):
        for one in self.loads:
            one.wait()
        if self.earlier is not None:
            self.earlier.sent()
            self.earlier.own_free = True
        step = min(64, self.rows)

        def round_rows(i, carry):
            at = tile(i * step, step)
            for low in range(2):
                to = 0
                for start, half in self.starts:
                    piece = self.stage[at, start + low * half : start + (low + 1) * half]
                    self.own[low, at, to : to + half] = piece.astype(BF16)
                    to += half
            return carry

        lax.fori_loop(0, self.rows // step, round_rows, 0)

    def begin(self):
        for one in self.side:
            one.start()
        step = min(64, self.rows)

        def copy(i, carry):
            self.land[tile(self.place.dp * self.rows + i * step, step), :] = self.own[
                self.place.low, tile(i * step, step), :
            ]
            return carry

        lax.fori_loop(0, self.rows // step, copy, 0)

    def forward(self, k):
        self.out[k].wait_recv()
        for one in self.on[k]:
            one.start()

    def finish(self):
        for one in self.side:
            one.wait_recv()
        for group in self.on:
            for one in group:
                one.wait_recv()
        self.save.start()

    def drain(self):
        if not self.own_free:
            self.sent()
        for group in self.on:
            for one in group:
                one.wait_send()
        self.save.wait()


class Stream:
    def __init__(self, groups):
        self.groups = groups
        self.order = [one for group in groups for one in group]
        self.items = [(group, k) for group in groups for k in range(3)]
        self.sent = self.passed = 0
        self.order[0].load()

    def send(self, count=1):
        for group, k in self.items[self.sent : self.sent + count]:
            for one in group:
                if k == 0:
                    one.cast()
                    at = self.order.index(one) + 1
                    if at < len(self.order):
                        self.order[at].load()
                    one.begin()
                one.out[k].start()
            self.sent += 1

    def forward(self, count=1):
        for group, k in self.items[self.passed : min(self.passed + count, self.sent)]:
            for one in group:
                one.forward(k)
            self.passed += 1

    def tick(self, lag=2):
        self.send()
        if self.passed + lag < self.sent or self.sent == len(self.items):
            self.forward()

    def need(self, one):
        place = [i for i, group in enumerate(self.groups) if one in group][0] * 3 + 3
        self.send(max(0, place - self.sent))
        self.forward(max(0, place - self.passed))
        one.finish()

    def rest(self):
        self.send(len(self.items))
        self.forward(len(self.items))


def scale_of(v):
    return lax.rsqrt(jnp.mean(v * v, axis=-1, keepdims=True) + EPSILON)


def mm(a, b):
    return jnp.dot(a, b, preferred_element_type=F32)


def mm_nt(a, b):
    return lax.dot_general(a, b, (((1,), (1,)), ((), ())), preferred_element_type=F32)


def project_heads(ns, pair):
    block = ns.joined.shape[1]
    two = pl.ds(pair * 2, 2)
    x = ns.joined[two].reshape(2 * block, -1)
    raw = mm(x, ns.layer.wqkv[...])
    ns.raw[two] = raw.reshape(2, block, -1)
    cosine, sine = ns.cosine[two].reshape(2 * block, HD), ns.sine[two].reshape(2 * block, HD)
    q_size, kv_size = ns.q.shape[2], ns.k.shape[2]

    def heads(out, start, size, gain):
        for h in range(size // HD):
            v = raw[:, start + h * HD : start + (h + 1) * HD]
            v = v * scale_of(v) * gain[...]
            turned = v * cosine + pltpu.roll(v, HD // 2, axis=1) * sine
            out[two, :, h * HD : (h + 1) * HD] = turned.astype(BF16).reshape(2, block, HD)

    heads(ns.q, 0, q_size, ns.layer.gain_q)
    heads(ns.k, q_size, kv_size, ns.layer.gain_k)
    ns.v[two] = raw[:, q_size + kv_size :].astype(BF16).reshape(2, block, kv_size)


def softmax(ns, b, half, span, query, keys):
    seen = keys.shape[0]
    s = mm_nt(query, keys) * HD**-0.5
    s = s + ns.bias[b, half * span : (half + 1) * span, :seen].astype(F32)
    p = jnp.exp(s - jnp.max(s, axis=-1, keepdims=True))
    return p * (1.0 / jnp.sum(p, axis=-1, keepdims=True))


def attend(ns, b):
    block = ns.joined.shape[1]
    span = 2 * block
    q_heads = ns.q.shape[2] // HD
    share = q_heads // (ns.k.shape[2] // HD)
    for e in range(q_heads):
        kv = slice((e // share) * HD, (e // share + 1) * HD)
        mine = slice(e * HD, (e + 1) * HD)
        for half in range(2):
            rows = slice(4 * b + 2 * half, 4 * b + 2 * half + 2)
            seen = slice(4 * b, 4 * b + 2 * half + 2)
            keys = ns.k[seen, :, kv].reshape(-1, HD)
            values = ns.v[seen, :, kv].reshape(-1, HD)
            query = ns.q[rows, :, mine].reshape(span, HD)
            p = softmax(ns, b, half, span, query, keys)
            ns.att[rows, :, mine] = mm(p.astype(BF16), values).astype(BF16).reshape(2, block, HD)


def project_out(ns, source, weight, pairs, start, size, width=1024):
    x = take(source, pairs, start, size)

    def step(j, carry):
        at = tile(j * width, width)
        put(ns.part, pairs, start, size, mm_nt(x, weight[at, :]).astype(BF16), at)
        return carry

    lax.fori_loop(0, ns.part.shape[2] // width, step, 0)


def gate_up(ns, pairs, start, size, slot):
    ff = ns.product.shape[2]
    x = take(ns.joined, pairs, start, size)
    gate = mm(x, ns.layer.wgate[...])
    up = mm(x, ns.layer.wup[...])
    ns.gu_stage[slot, :, :, :ff] = gate.astype(BF16).reshape(4, size, ff)
    ns.gu_stage[slot, :, :, ff:] = up.astype(BF16).reshape(4, size, ff)
    put(ns.product, pairs, start, size, (gate / (1.0 + jnp.exp(-gate)) * up).astype(BF16))


def forward_kernel(layers, spread, ns):
    place = Place(spread)
    links = Links(ns.send, ns.recv, ns.local)
    local = ns.tokens.shape[0]
    mine = place.own_pair * 2 + place.core
    diag, y, z, own = place.pairs
    first_pairs, last_pairs = (diag, y), (z, own)

    def gathers_of(layer, before):
        kv = ns.keyvalue_weight.at[layer]
        mlp = ns.mlp_weight.at[layer]
        attention = [(ns.query_weight.at[layer], kv.at[0], kv.at[1]), (ns.output_weight.at[layer],)]
        sources = attention + [(mlp.at[i],) for i in range(3)]
        owns = (ns.own_qkv, ns.own_o, ns.own_gate, ns.own_up, ns.own_down)
        lands = (ns.wqkv, ns.wo, ns.wgate, ns.wup, ns.wdown)
        saves = (ns.save_wqkv, ns.save_wo, ns.save_wgate, ns.save_wup, ns.save_wdown)
        return [
            Gather(links, place, source, own_ref, ns.stage, land[layer], save[layer], earlier)
            for source, own_ref, land, save, earlier in zip(sources, owns, lands, saves, before)
        ]

    gathers = []
    for layer in range(layers):
        gathers.append(gathers_of(layer, gathers[-1] if gathers else [None] * 5))
    groups = [[one] for one in gathers[0]]
    for later in gathers[1:]:
        groups += [later[:2], *[[one] for one in later[2:]]]
    stream = Stream(groups)
    tick = stream.tick
    tokens_in = Spread(links, place, ns.joined, 0, local)
    grads_in = Spread(links, place, ns.joined_grad, 0, local)
    middle = Halves(links, place, ns, ns.joined)
    end = Halves(links, place, ns, ns.joined)
    size = middle.size
    rows_save = [links.copy(ns.joined, one) for one in ns.save_a]

    def norm(i, carry):
        at = tile(i * CHUNK, CHUNK)
        v = ns.tokens[at, :].astype(F32)
        ns.hidden[at, :] = v
        ns.joined[mine, at, :] = (v * scale_of(v) * ns.gain_attn[:1, :]).astype(BF16)
        return carry

    lax.fori_loop(0, local // CHUNK, norm, 0)
    place.greet()
    tokens_in.start()
    stream.send(3)
    tokens_in.pass_on()
    stream.send()
    stream.forward()
    stream.send()
    stream.forward()
    stream.send()
    stream.forward()
    tokens_in.pass_last()
    tick()
    tick()
    tokens_in.ready()
    tokens_in.drain()
    for layer in range(layers):
        first, last = layer == 0, layer + 1 == layers
        qkv, o, gate, up, down = gathers[layer]
        kept = [
            links.copy(src, dst[layer])
            for src, dst in (
                (ns.raw, ns.save_raw), (ns.q, ns.save_q), (ns.k, ns.save_k), (ns.v, ns.save_v),
                (ns.att, ns.save_att), (ns.product, ns.save_product), (ns.mid, ns.save_mid),
                (ns.hidden, ns.save_hidden),
            )
        ]
        kept_raw, kept_q, kept_k, kept_v, kept_att, kept_product, kept_mid, kept_hidden = kept
        ns.layer = SimpleNamespace(
            wqkv=ns.wqkv[layer], gain_q=ns.gain_q.at[pl.ds(layer, 1)], gain_k=ns.gain_k.at[pl.ds(layer, 1)],
            wgate=ns.wgate[layer], wup=ns.wup[layer],
        )
        save_a = rows_save[layer]
        save_a.start()
        kept_hidden.start()
        if last:
            ns.joined_grad[mine] = ns.cotangent[...]
            grads_in.start()
        stream.need(qkv)

        def every(i, carry):
            project_heads(ns, i)
            return carry

        lax.fori_loop(0, 2, every, 0)
        tick()
        lax.fori_loop(2, 4, every, 0)
        for one in (kept_raw, kept_q, kept_k, kept_v):
            one.start()
        if last:
            grads_in.pass_on()
        tick()
        attend(ns, 0)
        tick()
        attend(ns, 1)
        kept_att.start()
        tick()
        stream.need(o)
        if last:
            grads_in.pass_last()

        def middle_rows(at, total):
            v = ns.hidden[at, :] + total
            ns.mid[at, :] = v
            gain = ns.gain_mlp[layer : layer + 1, :]
            ns.joined[mine, at, :] = (v * scale_of(v) * gain).astype(BF16)

        def result_rows(at, total):
            v = ns.mid[at, :] + total
            ns.hidden[at, :] = v
            if not last:
                gain = ns.gain_attn[layer + 1 : layer + 2, :]
                ns.joined[mine, at, :] = (v * scale_of(v) * gain).astype(BF16)

        def part_of(source, weight, halves, h):
            start = halves.starts[h]
            project_out(ns, source, weight, first_pairs, start, size)
            halves.sums[h].cross(0, 1)
            project_out(ns, source, weight, last_pairs, start, size)
            halves.sums[h].cross(2, 3)

        save_a.wait()
        part_of(ns.att, ns.wo[layer], middle, 0)
        middle.sums[0].send_y()
        part_of(ns.att, ns.wo[layer], middle, 1)
        middle.sums[1].send_y()
        tick()
        middle.sums[0].send_z()
        middle.sums[1].send_z()
        tick()
        middle.sums[0].end(middle_rows)
        middle.spread[0].start()
        middle.sums[1].end(middle_rows)
        middle.spread[1].start()
        kept_mid.start()
        tick()
        middle.spread[0].pass_on()
        middle.spread[1].pass_on()
        tick()
        stream.need(gate)
        stream.need(up)
        middle.spread[0].pass_last()
        middle.spread[0].ready()
        middle.spread[0].drain()
        saves = []

        def gate_up_of(pairs, start):
            slot = (len(saves) // 2) % 2
            if len(saves) >= 4:
                for save in saves[-4:-2]:
                    save.wait()
            gate_up(ns, pairs, start, size, slot)
            for i, p in enumerate(pairs):
                save = links.copy(
                    ns.gu_stage.at[slot, 2 * i : 2 * i + 2],
                    ns.save_gateup[layer].at[pl.ds(p * 2, 2), pl.ds(start, size)],
                )
                save.start()
                saves.append(save)

        save_b = [
            links.copy(ns.joined.at[:, pl.ds(start, size)], ns.save_b[layer].at[:, pl.ds(start, size)])
            for start in middle.starts
        ]
        save_b[0].start()
        gate_up_of(first_pairs, 0)
        tick()
        middle.spread[1].pass_last()
        gate_up_of(last_pairs, 0)
        stream.need(down)
        save_b[0].wait()
        kept_hidden.wait()
        part_of(ns.product, ns.wdown[layer], end, 0)
        middle.spread[1].ready()
        middle.spread[1].drain()
        end.sums[0].send_y()
        save_b[1].start()
        gate_up_of(first_pairs, size)
        end.sums[0].send_z()
        tick()
        gate_up_of(last_pairs, size)
        kept_product.start()
        save_b[1].wait()
        part_of(ns.product, ns.wdown[layer], end, 1)
        end.sums[1].send_y()
        end.sums[0].end(result_rows)
        if not last:
            end.spread[0].start()
        tick()
        end.sums[1].send_z()
        if not last:
            end.spread[0].pass_on()
        tick()
        end.sums[1].end(result_rows)
        if not last:
            end.spread[1].start()
            tick()
            end.spread[0].pass_last()
            end.spread[1].pass_on()
            tick()
            end.spread[1].pass_last()
            for one in end.spread:
                one.ready()
                one.drain()
        for one in (*saves[-4:], kept_raw, kept_q, kept_k, kept_v, kept_att, kept_product, kept_mid):
            one.wait()
    result = links.copy(ns.hidden, ns.out)
    result.start()
    grads_in.ready()
    grads_in.drain()
    final = links.copy(ns.joined_grad, ns.save_grad)
    final.start()
    for group in gathers:
        for one in group:
            one.drain()
    result.wait()
    final.wait()
    assert stream.passed == len(stream.items)
    links.check()


def call(kernel, ins, outs, scratch, collective_id, name):
    groups = [ins, outs, scratch]
    sizes = [len(v) if isinstance(v, list) else 0 for group in groups for v in group.values()]
    names = [key for group in groups for key in group]

    def flat(group):
        return [one for v in group.values() for one in (v if isinstance(v, list) else [v])]

    def named(values, keys, counts):
        values = list(values)
        taken = {}
        for key, count in zip(keys, counts):
            taken[key] = [values.pop(0) for _ in range(count)] if count else values.pop(0)
        return SimpleNamespace(**taken)

    def run(*refs):
        kernel(named(refs, names, sizes))

    def space(in_vmem):
        return pl.BlockSpec(memory_space=pltpu.VMEM if in_vmem else pl.ANY)

    results = pl.pallas_call(
        run,
        out_shape=[jax.ShapeDtypeStruct(shape, dtype) for shape, dtype, _ in flat(outs)],
        in_specs=[space(v) for _, v in flat(ins)],
        out_specs=[space(v) for _, _, v in flat(outs)],
        scratch_shapes=flat(scratch),
        compiler_params=pltpu.CompilerParams(
            collective_id=collective_id, has_side_effects=True, vmem_limit_bytes=VMEM_LIMIT
        ),
        cost_estimate=pl.CostEstimate(
            flops=26 * 10**9, bytes_accessed=10**8, transcendentals=10**6
        ),
        name=name,
    )(*[array for array, _ in flat(ins)])
    return named(results, outs, sizes[len(ins) : len(ins) + len(outs)])


def exchange_scratch(rows, width):
    return dict(
        joined=pltpu.VMEM((8, rows, width), BF16),
        part=pltpu.VMEM((8, rows, width), BF16),
        core_in=pltpu.VMEM((4, rows, width), BF16),
        y_in=pltpu.VMEM((2, rows, width), BF16),
        z_in=pltpu.VMEM((rows, width), BF16),
        sums=pltpu.VMEM((3, rows, width), BF16),
    )


def forward(tokens, cotangent, masters, tables, gains, spread):
    rows, width = tokens.shape
    query, keyvalue, output, mlp = masters
    layers = gains.shape[0]
    own = query.shape[1]
    d_rows = own * 4 * spread
    o, ff = query.shape[2] // 2, mlp.shape[3] // 2
    kv = keyvalue.shape[3] // 2
    qkv = o + 2 * kv
    cosine, sine, bias = tables
    ins = dict(
        tokens=(tokens, True), cotangent=(cotangent, True),
        query_weight=(query, False), keyvalue_weight=(keyvalue, False),
        output_weight=(output, False), mlp_weight=(mlp, False),
        gain_attn=(gains[:, :width], True), gain_mlp=(gains[:, width : 2 * width], True),
        gain_q=(gains[:, 2 * width : 2 * width + HD], True), gain_k=(gains[:, 2 * width + HD :], True),
        cosine=(cosine, True), sine=(sine, True), bias=(bias, True),
    )

    def each(dtype, *shape):
        return [(shape, dtype, False)] * layers

    outs = dict(
        out=((rows, width), F32, False),
        save_hidden=each(F32, rows, width), save_mid=each(F32, rows, width),
        save_raw=each(F32, 8, rows, qkv), save_q=each(BF16, 8, rows, o),
        save_k=each(BF16, 8, rows, kv), save_v=each(BF16, 8, rows, kv),
        save_att=each(BF16, 8, rows, o), save_product=each(BF16, 8, rows, ff),
        save_gateup=each(BF16, 8, rows, 2 * ff),
        save_a=each(BF16, 8, rows, width), save_b=each(BF16, 8, rows, width),
        save_grad=((8, rows, width), BF16, False),
        save_wqkv=each(BF16, d_rows, qkv), save_wo=each(BF16, d_rows, o),
        save_wgate=each(BF16, d_rows, ff), save_wup=each(BF16, d_rows, ff), save_wdown=each(BF16, d_rows, ff),
    )
    scratch = exchange_scratch(rows, width)
    weight = lambda size: [pltpu.VMEM((d_rows, size), BF16)] * layers
    mine = lambda size: pltpu.VMEM((2, own, size), BF16)
    tokens_of = lambda size, dtype=BF16: pltpu.VMEM((8, rows, size), dtype)
    scratch.update(
        hidden=pltpu.VMEM((rows, width), F32), mid=pltpu.VMEM((rows, width), F32),
        joined_grad=tokens_of(width), gu_stage=pltpu.VMEM((2, 4, rows // 2, 2 * ff), BF16),
        stage=pltpu.VMEM((own, max(2 * ff, 2 * qkv)), F32),
        raw=tokens_of(qkv, F32), q=tokens_of(o), k=tokens_of(kv), v=tokens_of(kv), att=tokens_of(o),
        product=tokens_of(ff),
        wqkv=weight(qkv), wo=weight(o), wgate=weight(ff), wup=weight(ff), wdown=weight(ff),
        own_qkv=mine(qkv), own_o=mine(o), own_gate=mine(ff), own_up=mine(ff), own_down=mine(ff),
        local=pltpu.SemaphoreType.DMA((4 + 36 * layers,)),
    )
    count = 72 + 20 * spread * layers
    scratch.update(send=pltpu.SemaphoreType.DMA((count,)), recv=pltpu.SemaphoreType.DMA((count,)))
    return call(partial(forward_kernel, layers, spread), ins, outs, scratch, 1, "forward")


def mm_tn(a, b):
    return lax.dot_general(a, b, (((0,), (0,)), ((), ())), preferred_element_type=F32)


class Reduce:
    def __init__(self, links, place, blocks, x_in, z_in, outs):
        self.place, self.blocks, self.x_in, self.z_in, self.outs = place, blocks, x_in, z_in, outs
        spread = place.spread
        rows = blocks.shape[1] // spread
        self.rows = rows

        def block(q, r):
            return blocks.at[q, tile(r * rows, rows)]

        self.x_out = [
            [
                links.remote(
                    block(q, lax.rem(place.r + s, spread)), x_in.at[s - 1, q], place.r_id(s)
                )
                for s in range(1, spread)
            ]
            for q in range(4)
        ]
        self.z_out = [
            links.remote(block(q, place.r), z_in.at[q - 1], place.z_id(q)) for q in range(1, 4)
        ]

    def compute(self, q, left, right):
        part = self.blocks.shape[1]
        step = min(256, part)
        start = lax.rem(self.place.z + q, 4) * part

        def one(i, carry):
            x = left[:, :, tile(start + i * step, step)]
            product = mm_tn(x.reshape(-1, step), right())
            self.blocks[q, tile(i * step, step), :] = product.astype(BF16)
            return carry

        lax.fori_loop(0, part // step, one, 0)
        for one_copy in self.x_out[q]:
            one_copy.start()

    def compute_with(self, other, q, left, right):
        part, columns = self.blocks.shape[1:]
        step = min(256, part)
        start = lax.rem(self.place.z + q, 4) * part

        def one(i, carry):
            x = left[:, :, tile(start + i * step, step)]
            product = mm_tn(x.reshape(-1, step), right()).astype(BF16)
            self.blocks[q, tile(i * step, step), :] = product[:, :columns]
            other.blocks[q, tile(i * step, step), :] = product[:, columns:]
            return carry

        lax.fori_loop(0, part // step, one, 0)
        for one_copy in self.x_out[q] + other.x_out[q]:
            one_copy.start()

    def pass_on(self, q):
        for one in self.x_out[q]:
            one.wait_recv()
        step = min(64, self.rows)
        start = self.place.r * self.rows

        def add(i, carry):
            at = tile(start + i * step, step)
            if self.place.spread == 2:
                self.blocks[q, at, :] += self.x_in[0, q, tile(i * step, step), :]
                return carry
            total = self.blocks[q, at, :].astype(F32)
            for s in range(self.place.spread - 1):
                total = total + self.x_in[s, q, tile(i * step, step), :].astype(F32)
            self.blocks[q, at, :] = total.astype(BF16)
            return carry

        lax.fori_loop(0, self.rows // step, add, 0)
        if q:
            self.z_out[q - 1].start()

    def finish(self):
        for one in self.z_out:
            one.wait_recv()
        step = min(64, self.rows)
        low = self.place.low
        start = self.place.r * self.rows

        def add(i, carry):
            at = tile(i * step, step)
            near = self.blocks[0, tile(start + i * step, step), :] + self.z_in[1, at, :]
            far = self.z_in[0, at, :] + self.z_in[2, at, :]
            first = 0
            for out, size in self.outs:
                out[at, tile(low * size, size)] = near[:, first : first + size]
                out[at, tile((1 - low) * size, size)] = far[:, first : first + size]
                first += size
            return carry

        lax.fori_loop(0, self.rows // step, add, 0)

    def drain(self):
        for group in self.x_out:
            for one in group:
                one.wait_send()
        for one in self.z_out:
            one.wait_send()


ORDER = (2, 1, 3, 0)


def gate_up_back(ns, pairs, start, size, slot):
    ff = ns.product.shape[2]
    d_act = mm(take(ns.joined, pairs, start, size), ns.wdown[...])
    gate = ns.stage[slot, :, :, :ff].reshape(4 * size, ff).astype(F32)
    up = ns.stage[slot, :, :, ff:].reshape(4 * size, ff).astype(F32)
    gated = 1.0 / (1.0 + jnp.exp(-gate))
    d_gate = (d_act * up * gated * (1.0 + gate * (1.0 - gated))).astype(BF16)
    put(ns.d_gateup, pairs, start, size, d_gate, slice(0, ff))
    put(ns.d_gateup, pairs, start, size, (d_act * gate * gated).astype(BF16), slice(ff, 2 * ff))


def head_back(ns, blocks, d_out, raw_columns, gain, d_gain):
    rows = d_out.shape[0]
    cosine, sine = ns.cosine[blocks].reshape(rows, HD), ns.sine[blocks].reshape(rows, HD)
    raw = ns.raw[blocks, :, raw_columns].reshape(rows, HD)
    d_turned = d_out * cosine + pltpu.roll(d_out * sine, HD // 2, axis=1)
    scale = scale_of(raw)
    normed = raw * scale
    d_gain[...] += jnp.sum(d_turned * normed, axis=0, keepdims=True)
    d_normed = d_turned * gain[...]
    inner = jnp.mean(d_normed * normed, axis=-1, keepdims=True)
    d_raw = (scale * (d_normed - normed * inner)).astype(BF16)
    ns.d_raw[blocks, :, raw_columns] = d_raw.reshape(-1, ns.raw.shape[1], HD)


def attend_back(ns, b):
    block = ns.joined.shape[1]
    span = 2 * block
    q_size, kv_size = ns.q.shape[2], ns.k.shape[2]
    share = q_size // kv_size
    scale = HD**-0.5
    whole = slice(4 * b, 4 * b + 4)
    for kv in range(kv_size // HD):
        columns = slice(kv * HD, (kv + 1) * HD)
        ns.d_keys[...] = jnp.zeros_like(ns.d_keys)
        ns.d_values[...] = jnp.zeros_like(ns.d_values)
        for e in range(kv * share, (kv + 1) * share):
            mine = slice(e * HD, (e + 1) * HD)
            for half in range(2):
                rows = slice(4 * b + 2 * half, 4 * b + 2 * half + 2)
                some = slice(4 * b, 4 * b + 2 * half + 2)
                seen = (half + 1) * span
                keys = ns.k[some, :, columns].reshape(seen, HD)
                values = ns.v[some, :, columns].reshape(seen, HD)
                query = ns.q[rows, :, mine].reshape(span, HD)
                d_out = ns.d_att[rows, :, mine].reshape(span, HD)
                p = softmax(ns, b, half, span, query, keys)
                d_p = mm_nt(d_out, values)
                delta = jnp.sum(d_p * p, axis=-1, keepdims=True)
                d_s = (p * (d_p - delta)).astype(BF16)
                ns.d_values[:seen, :] += mm_tn(p.astype(BF16), d_out)
                ns.d_keys[:seen, :] += mm_tn(d_s, query)
                head_back(ns, rows, mm(d_s, keys) * scale, mine, ns.gain_q, ns.d_gain_q)
        key_columns = slice(q_size + kv * HD, q_size + (kv + 1) * HD)
        head_back(ns, whole, ns.d_keys[...] * scale, key_columns, ns.gain_k, ns.d_gain_k)
        value_columns = slice(q_size + kv_size + kv * HD, q_size + kv_size + (kv + 1) * HD)
        ns.d_raw[whole, :, value_columns] = ns.d_values[...].astype(BF16).reshape(4, block, HD)


class GainSum:
    def __init__(self, links, place, terms, came, came_r, total):
        spread = place.spread
        self.place, self.terms, self.came, self.came_r, self.total = place, terms, came, came_r, total
        ids = (place.core_id, place.y_id, place.low_id, place.z_id(2))
        self.pairs = [links.remote(terms.at[i], came.at[i], one) for i, one in enumerate(ids)]
        self.sides = [
            links.remote(terms.at[4], came_r.at[place.r], place.r_id(s)) for s in range(1, spread)
        ]
        self.at = 0

    def start(self):
        self.pairs[0].start()

    def step(self):
        i = self.at
        self.at += 1
        if i < 4:
            self.pairs[i].wait_recv()
            self.terms[i + 1] = self.terms[i] + self.came[i]
            if i < 3:
                self.pairs[i + 1].start()
                return
            self.came_r[self.place.r] = self.terms[4]
            for one in self.sides:
                one.start()
            return
        for one in self.sides:
            one.wait_recv()
        total = self.came_r[0]
        for r in range(1, self.place.spread):
            total = total + self.came_r[r]
        self.total[...] = total
        for one in self.pairs + self.sides:
            one.wait_send()


def backward_kernel(layers, spread, ns):
    place = Place(spread)
    links = Links(ns.send, ns.recv, ns.local)
    local, width = ns.out.shape
    mine = place.own_pair * 2 + place.core
    qkv, o, ff = ns.wqkv_in[0].shape[1], ns.wo_in[0].shape[1], ns.wdown_in[0].shape[1]
    kv = (qkv - o) // 2
    rows_all = ns.wdown_in[0].shape[0]
    group = ns.bias_in.shape[1]
    diag, y, z, own = place.pairs
    first_pairs, last_pairs = (diag, y), (z, own)

    def loads(*pairs):
        copies = [links.copy(src, dst) for src, dst in pairs]
        for one in copies:
            one.start()
        return copies

    def wait(copies):
        for one in copies:
            one.wait()

    def reduce(i, outs):
        return Reduce(links, place, ns.blocks.at[i], ns.x_in.at[i], ns.z_in_w.at[i], outs)

    red_down = reduce(0, [(ns.g_mlp.at[2], ff)])
    red_gate = reduce(1, [(ns.g_mlp.at[0], ff)])
    red_up = reduce(2, [(ns.g_mlp.at[1], ff)])
    red_o = Reduce(links, place, ns.blocks_o, ns.x_in_o, ns.z_in_o, [(ns.g_o, o)])
    red_qkv = Reduce(
        links, place, ns.blocks_qkv, ns.x_in_qkv, ns.z_in_qkv,
        [(ns.g_q, o), (ns.g_kv.at[0], kv), (ns.g_kv.at[1], kv)],
    )
    reduces = (red_down, red_gate, red_up, red_o, red_qkv)
    middle = Halves(links, place, ns, ns.joined)
    end = Halves(links, place, ns, ns.joined)
    size = middle.size
    gain_sum = GainSum(links, place, ns.terms, ns.came, ns.came_r, ns.gain_total)
    passes = []
    going = [False]

    def pass_next(count=1):
        for _ in range(count):
            passes.pop(0)()

    def compute_all(one, left, right):
        if going[0]:
            one.drain()
        for q in ORDER:
            one.compute(q, left, right)

    def keep(layer):
        pairs = ((ns.g_q, ns.save_q), (ns.g_kv, ns.save_kv), (ns.g_o, ns.save_o), (ns.g_mlp, ns.save_mlp))
        return [links.copy(one, to[layer]) for one, to in pairs]

    for one in (*ns.d_attn, *ns.d_mlp, *ns.d_q, *ns.d_k):
        one[...] = jnp.zeros_like(one)
    first_rows = loads((ns.joined_in, ns.joined))
    place.greet()
    wait(first_rows)
    for layer in reversed(range(layers)):
        backward_layer(layer, layers, SimpleNamespace(**locals()))
    result = loads((ns.out, ns.input_grad))
    ns.terms[0] = jnp.zeros_like(ns.terms[0])
    for i in range(layers):
        ns.terms[0, 2 * i : 2 * i + 1, :width] = ns.d_attn[i][...]
        ns.terms[0, 2 * i + 1 : 2 * i + 2, :width] = ns.d_mlp[i][...]
        ns.terms[0, 2 * i : 2 * i + 1, width : width + HD] = ns.d_q[i][...]
        ns.terms[0, 2 * i : 2 * i + 1, width + HD : width + 2 * HD] = ns.d_k[i][...]
    gain_sum.start()
    for _ in range(4):
        pass_next()
        gain_sum.step()
    red_gate.finish()
    gain_sum.step()
    red_up.finish()
    red_o.finish()
    red_qkv.finish()
    for one in reduces:
        one.drain()
    last = keep(0)
    for one in last:
        one.start()
    wait(last)
    wait(result)
    assert not passes
    links.check()


def backward_layer(layer, layers, env):
    ns, place, links, loads, wait, local, width = (
        env.ns, env.place, env.links, env.loads, env.wait, env.local, env.width
    )
    middle, end, size, mine, passes, pass_next = env.middle, env.end, env.size, env.mine, env.passes, env.pass_next
    red_down, red_gate, red_up, red_o, red_qkv = env.reduces
    first_pairs, last_pairs, compute_all = env.first_pairs, env.last_pairs, env.compute_all
    first, started = layer == 0, layer + 1 < layers
    passes += [partial(one.pass_on, q) for one in env.reduces for q in ORDER]
    ns.gain_q, ns.gain_k = ns.gains_q.at[pl.ds(layer, 1)], ns.gains_k.at[pl.ds(layer, 1)]
    ns.d_gain_q, ns.d_gain_k = ns.d_q[layer], ns.d_k[layer]
    gain_mlp, gain_attn = ns.gains_mlp.at[pl.ds(layer, 1)], ns.gains_attn.at[pl.ds(layer, 1)]
    ff, qkv, o, rows_all, group = env.ff, env.qkv, env.o, env.rows_all, env.group
    kept = env.keep(layer + 1) if started else []

    def finish_later():
        if started:
            for one in (red_up, red_o, red_qkv):
                one.finish()
            for one in kept:
                one.start()
            for k in range(1, 4):
                pl.semaphore_signal(ns.credit, inc=1, device_id=place.z_id(k), device_id_type=MESH)

    def back_norm(value, grad, gain, d_gain, out, gather):
        def finish(at, total):
            v = value[at, :].astype(F32)
            scale = scale_of(v)
            normed = v * scale
            d_gain[...] += jnp.sum(total * normed, axis=0, keepdims=True)
            d_normed = total * gain[...]
            inner = jnp.mean(d_normed * normed, axis=-1, keepdims=True)
            g = grad[at, :].astype(F32) + scale * (d_normed - normed * inner)
            out[at, :] = g
            if gather:
                ns.joined[mine, at, :] = g.astype(BF16)

        return finish

    flat = lambda ref: lambda: ref[...].reshape(8 * local, -1)

    def mlp_scope(wgate, wup, d_gateup):
        ns.d_gateup = d_gateup
        weight_loads = loads((ns.wgate_in[layer], wgate), (ns.wup_in[layer], wup))

        def part_of(h, columns=1024):
            start = middle.starts[h]
            for which, pairs in ((0, first_pairs), (2, last_pairs)):
                gates = take(d_gateup, pairs, start, size, slice(0, ff))
                ups = take(d_gateup, pairs, start, size, slice(ff, 2 * ff))

                def step(j, carry):
                    at = tile(j * columns, columns)
                    term = mm_nt(gates, wgate[at, :]) + mm_nt(ups, wup[at, :])
                    put(ns.part, pairs, start, size, term.astype(BF16), at)
                    return carry

                lax.fori_loop(0, width // columns, step, 0)
                middle.sums[h].cross(which, which + 1)

        def down_scope(wdown, product, stage):
            ns.wdown, ns.product, ns.stage = wdown, product, stage
            first_loads = loads((ns.product_in[layer], product))
            down_load = loads((ns.wdown_in[layer], wdown))
            chunks = [(start, pairs) for start in middle.starts for pairs in (first_pairs, last_pairs)]
            gateup_loads = [
                [
                    links.copy(
                        ns.gateup_in[layer].at[pl.ds(p * 2, 2), pl.ds(start, size)], stage.at[i % 2, 2 * j : 2 * j + 2]
                    )
                    for j, p in enumerate(pairs)
                ]
                for i, (start, pairs) in enumerate(chunks)
            ]
            for group in gateup_loads[:2]:
                for one in group:
                    one.start()
            wait(first_loads)
            compute_all(red_down, ns.joined, flat(product))
            wait(down_load)
            for i, (start, pairs) in enumerate(chunks):
                wait(gateup_loads[i])
                gate_up_back(ns, pairs, start, size, i % 2)
                if i < 2:
                    for one in gateup_loads[i + 2]:
                        one.start()
                if i == 1:
                    wait(weight_loads)
                    part_of(0)
                if i == 2:
                    middle.sums[0].send_y()
            finish_later()

        pl.run_scoped(
            down_scope,
            pltpu.VMEM((rows_all, ff), BF16),
            pltpu.VMEM((8, local, ff), BF16),
            pltpu.VMEM((2, 4, size, 2 * ff), BF16),
        )

        def rest_scope(b, mid, grad=None):
            b_load = loads((ns.mid_in[layer], mid), (ns.b_in[layer], b))
            if grad is None:
                grad = ns.out
            else:
                b_load += loads((ns.grad_in, grad))
            middle_rows = back_norm(mid, grad, gain_mlp, ns.d_mlp[layer], ns.grad_mid, True)
            part_of(1)
            middle.sums[0].send_z()
            middle.sums[1].send_y()
            wait(b_load)
            if started:
                red_gate.drain()
                red_up.drain()
            for q in ORDER[:2]:
                red_gate.compute_with(red_up, q, b, flat(d_gateup))
            middle.sums[0].end(middle_rows)
            middle.spread[0].start()
            middle.sums[1].send_z()
            if started:
                pl.semaphore_wait(ns.credit, 3)
            pass_next()
            for q in ORDER[2:]:
                red_gate.compute_with(red_up, q, b, flat(d_gateup))
            middle.sums[1].end(middle_rows)
            middle.spread[1].start()
            pass_next()

        pl.run_scoped(
            rest_scope,
            pltpu.VMEM((8, local, width), BF16),
            pltpu.VMEM((local, width), F32),
            *([] if started else [pltpu.VMEM((local, width), ns.grad_in.dtype)]),
        )

    pl.run_scoped(
        mlp_scope,
        pltpu.VMEM((rows_all, ff), BF16),
        pltpu.VMEM((rows_all, ff), BF16),
        pltpu.VMEM((8, local, 2 * ff), BF16),
    )

    def attention_scope(
        cosine, sine, bias, hidden, wqkv, wo, a, q, k, v, raw, att, d_att, d_raw, d_keys, d_values
    ):
        ns.cosine, ns.sine, ns.bias, ns.hidden = cosine, sine, bias, hidden
        ns.q, ns.k, ns.v, ns.raw, ns.att = q, k, v, raw, att
        ns.d_att, ns.d_raw, ns.d_keys, ns.d_values = d_att, d_raw, d_keys, d_values
        o_loads = loads((ns.wo_in[layer], wo), (ns.att_in[layer], att))
        other_loads = loads(
            (ns.q_in[layer], q), (ns.k_in[layer], k), (ns.v_in[layer], v), (ns.raw_in[layer], raw),
            (ns.cosine_in, cosine), (ns.sine_in, sine), (ns.bias_in, bias), (ns.a_in[layer], a),
            (ns.wqkv_in[layer], wqkv), (ns.hidden_in[layer], hidden),
        )
        result_rows = back_norm(hidden, ns.grad_mid, gain_attn, ns.d_attn[layer], ns.out, not first)

        def d_attended(h):
            start = middle.starts[h]
            middle.spread[h].ready()
            middle.spread[h].drain()
            for pairs in (first_pairs, last_pairs):
                put(d_att, pairs, start, size, mm(take(ns.joined, pairs, start, size), wo[...]).astype(BF16))

        def part_of(h):
            start = end.starts[h]
            project_out(ns, d_raw, wqkv, first_pairs, start, size)
            end.sums[h].cross(0, 1)
            project_out(ns, d_raw, wqkv, last_pairs, start, size)
            end.sums[h].cross(2, 3)

        middle.spread[0].pass_on()
        middle.spread[1].pass_on()
        pass_next()
        wait(o_loads)
        middle.spread[0].pass_last()
        d_attended(0)
        pass_next()
        middle.spread[1].pass_last()
        d_attended(1)
        compute_all(red_o, ns.joined, flat(att))
        pass_next(2)
        wait(other_loads)
        attend_back(ns, 0)
        pass_next(2)
        attend_back(ns, 1)
        pass_next(2)
        part_of(0)
        end.sums[0].send_y()
        part_of(1)
        end.sums[1].send_y()
        compute_all(red_qkv, a, flat(d_raw))
        end.sums[0].send_z()
        end.sums[1].send_z()
        pass_next(2)
        end.sums[0].end(result_rows)
        if not first:
            end.spread[0].start()
        pass_next(4)
        end.sums[1].end(result_rows)
        if not first:
            end.spread[1].start()
        wait(kept)
        red_down.finish()

    pl.run_scoped(
        attention_scope,
        pltpu.VMEM(ns.cosine_in.shape, F32),
        pltpu.VMEM(ns.sine_in.shape, F32),
        pltpu.VMEM(ns.bias_in.shape, BF16),
        pltpu.VMEM(ns.hidden_in[layer].shape, F32),
        pltpu.VMEM((rows_all, qkv), BF16),
        pltpu.VMEM((rows_all, o), BF16),
        pltpu.VMEM((8, local, width), BF16),
        pltpu.VMEM(ns.q_in[layer].shape, BF16),
        pltpu.VMEM(ns.k_in[layer].shape, BF16),
        pltpu.VMEM(ns.v_in[layer].shape, BF16),
        pltpu.VMEM(ns.raw_in[layer].shape, F32),
        pltpu.VMEM(ns.att_in[layer].shape, BF16),
        pltpu.VMEM((8, local, o), BF16),
        pltpu.VMEM((8, local, qkv), BF16),
        pltpu.VMEM((group, HD), F32),
        pltpu.VMEM((group, HD), F32),
    )
    if not first:
        pass_next()
        end.spread[0].pass_on()
        end.spread[1].pass_on()
        pass_next(2)
        end.spread[0].pass_last()
        end.spread[1].pass_last()
        pass_next()
        red_gate.finish()
        for one in end.spread:
            one.ready()
            one.drain()
        env.going[0] = True


def backward(cotangent, kept, tables, gains, spread):
    rows, width = cotangent.shape
    cosine, sine, bias = tables
    layers = gains.shape[0]
    d_rows, ff = kept.save_wdown[0].shape
    o, qkv = kept.save_wo[0].shape[1], kept.save_wqkv[0].shape[1]
    part = d_rows // 4
    block = part // spread
    small = (8, width + 2 * HD)

    def far(arrays):
        return [(one, False) for one in arrays]

    ins = dict(
        grad_in=(cotangent, False), joined_in=(kept.save_grad, False),
        mid_in=far(kept.save_mid), hidden_in=far(kept.save_hidden), product_in=far(kept.save_product),
        gateup_in=far(kept.save_gateup), b_in=far(kept.save_b), a_in=far(kept.save_a),
        wdown_in=far(kept.save_wdown), wgate_in=far(kept.save_wgate), wup_in=far(kept.save_wup),
        wqkv_in=far(kept.save_wqkv), wo_in=far(kept.save_wo), q_in=far(kept.save_q), k_in=far(kept.save_k),
        v_in=far(kept.save_v), raw_in=far(kept.save_raw), att_in=far(kept.save_att),
        gains_attn=(gains[:, :width], True), gains_mlp=(gains[:, width : 2 * width], True),
        gains_q=(gains[:, 2 * width : 2 * width + HD], True), gains_k=(gains[:, 2 * width + HD :], True),
        cosine_in=(cosine, False), sine_in=(sine, False), bias_in=(bias, False),
    )
    sums = dict(g_q=(block, 2 * o), g_kv=(2, block, qkv - o), g_o=(block, 2 * o), g_mlp=(3, block, 2 * ff))

    def each(name):
        return [(sums[name], BF16, False)] * layers

    outs = dict(
        input_grad=((rows, width), F32, False), gain_total=(small, F32, True),
        save_q=each("g_q"), save_kv=each("g_kv"), save_o=each("g_o"), save_mlp=each("g_mlp"),
    )
    scratch = exchange_scratch(rows, width)
    scratch.update({name: pltpu.VMEM(shape, BF16) for name, shape in sums.items()})
    side = spread - 1
    wide, thin = [pltpu.VMEM((1, width), F32)] * layers, [pltpu.VMEM((1, HD), F32)] * layers
    count = 88 + 22 * spread
    scratch.update(
        out=pltpu.VMEM((rows, width), F32), grad_mid=pltpu.VMEM((rows, width), F32),
        blocks=pltpu.VMEM((3, 4, part, ff), BF16),
        blocks_o=pltpu.VMEM((4, part, o), BF16), blocks_qkv=pltpu.VMEM((4, part, qkv), BF16),
        x_in=pltpu.VMEM((3, side, 4, block, ff), BF16),
        x_in_o=pltpu.VMEM((side, 4, block, o), BF16), x_in_qkv=pltpu.VMEM((side, 4, block, qkv), BF16),
        z_in_w=pltpu.VMEM((3, 3, block, ff), BF16),
        z_in_o=pltpu.VMEM((3, block, o), BF16), z_in_qkv=pltpu.VMEM((3, block, qkv), BF16),
        d_attn=wide, d_mlp=wide, d_q=thin, d_k=thin,
        terms=pltpu.VMEM((5, *small), F32), came=pltpu.VMEM((4, *small), F32),
        came_r=pltpu.VMEM((spread, *small), F32), credit=pltpu.SemaphoreType.REGULAR,
        local=pltpu.SemaphoreType.DMA((8 + 32 * layers,)),
        send=pltpu.SemaphoreType.DMA((count,)), recv=pltpu.SemaphoreType.DMA((count,)),
    )
    return call(partial(backward_kernel, layers, spread), ins, outs, scratch, 2, "backward")


def places(dp_size):
    spread = dp_size // 4
    me = lax.axis_index("dp")
    z = me // spread
    return spread, me, lax.rem(me, spread), lax.rem(z, 2), z // 2


def flip_lo(dp_size):
    spread = dp_size // 4
    return [(i, i + spread * (1 - 2 * ((i // spread) % 2))) for i in range(dp_size)]


def flip_hi(dp_size):
    spread = dp_size // 4
    return [(i, i + 2 * spread * (1 - 2 * (i // (2 * spread)))) for i in range(dp_size)]


def shift_r(dp_size, step):
    spread = dp_size // 4
    return [(i, (i // spread) * spread + (i % spread + step) % spread) for i in range(dp_size)]


def rope_tables(positions, head_size):
    half = head_size // 2
    frequency = jnp.power(THETA, -2.0 * jnp.arange(half, dtype=F32) / head_size)
    angle = positions.astype(F32)[:, None] * frequency[None, :]
    return (jnp.cos(angle)[:, None, :], jnp.sin(angle)[:, None, :])


def adamw(weight, first, second, grad, rate, decay):
    first_new = BETA_ONE * first + (1.0 - BETA_ONE) * grad
    second_new = BETA_TWO * second + (1.0 - BETA_TWO) * grad * grad
    first_hat = first_new / (1.0 - BETA_ONE**STEP)
    second_hat = second_new / (1.0 - BETA_TWO**STEP)
    weight_new = weight - rate * (first_hat / (jnp.sqrt(second_hat) + ADAM_EPS) + decay * weight)
    return (first_new, second_new, weight_new)


def body(
    tokens, cotangent, segment_ids, gains, gain_first, gain_second,
    query_weight, query_first, query_second,
    keyvalue_weight, keyvalue_first, keyvalue_second,
    output_weight, output_first, output_second,
    mlp_weight, mlp_first, mlp_second,
):
    dp_size = lax.axis_size("dp")
    spread, me, r, low, high = places(dp_size)
    layers = gains.shape[0]
    local_rows, width = tokens.shape
    group = segment_ids.shape[0]
    rows = 8 * local_rows
    index = jnp.arange(group, dtype=jnp.int32)
    other = lax.ppermute(segment_ids, "dp", flip_lo(dp_size))
    segments = jnp.stack([jnp.where(low == 0, segment_ids, other), jnp.where(low == 0, other, segment_ids)])
    positions = (index[None, :] - (segments - segments[:, :1])).reshape(rows)
    mask = (segments[:, :, None] == segments[:, None, :]) & (index[None, None, :] <= index[None, :, None])
    bias = jnp.where(mask, 0.0, -1e30).astype(BF16)
    cosine, sine = rope_tables(positions, HD)
    tables = (
        jnp.concatenate([cosine[:, 0], cosine[:, 0]], axis=1).reshape(8, local_rows, HD),
        jnp.concatenate([-sine[:, 0], sine[:, 0]], axis=1).reshape(8, local_rows, HD),
        bias,
    )
    masters = (query_weight, keyvalue_weight, output_weight, mlp_weight)

    kept = forward(tokens, cotangent, masters, tables, gains, spread)
    block_output = kept.out
    done = backward(cotangent, kept, tables, gains, spread)
    stacked = [
        jnp.stack(one).astype(F32) for one in (done.save_q, done.save_kv, done.save_o, done.save_mlp)
    ]
    sums = done.gain_total
    gain_total = jnp.stack(
        [
            jnp.concatenate([sums[2 * i, :width], sums[2 * i + 1, :width], sums[2 * i, width:]])
            for i in range(layers)
        ]
    )
    head_gain_grads = gain_total[:, 2 * width :]
    gain_new = adamw(gains, gain_first, gain_second, gain_total, GAIN_RATE, 0.0)
    query_new = adamw(query_weight, query_first, query_second, stacked[0], RATE, DECAY)
    keyvalue_new = adamw(keyvalue_weight, keyvalue_first, keyvalue_second, stacked[1], RATE, DECAY)
    output_new = adamw(output_weight, output_first, output_second, stacked[2], RATE * OUTPUT_FACTOR, DECAY)
    mlp_new = adamw(mlp_weight, mlp_first, mlp_second, stacked[3], RATE, DECAY)
    return (block_output, done.input_grad, *gain_new, head_gain_grads, *query_new, *keyvalue_new, *output_new, *mlp_new)


def solution(mesh):
    token = P(("dp", "tensor"), None)
    flat = P(None, "dp", "tensor")
    deep = P(None, None, "dp", "tensor")
    placed = (token, token, P("dp"), P(), P(), P(), *[flat] * 3, *[deep] * 3, *[flat] * 3, *[deep] * 3)
    outs = (token, token, P(), P(), P(), P(), *[flat] * 3, *[deep] * 3, *[flat] * 3, *[deep] * 3)
    return jax.shard_map(body, mesh=mesh, in_specs=placed, out_specs=outs, check_vma=False)
```

```python
from functools import partial
import math
from types import SimpleNamespace

import jax
import jax.numpy as jnp
from jax import lax
from jax.experimental import pallas as pl
from jax.experimental.pallas import tpu as pltpu
from jax.sharding import PartitionSpec as P

HD = 128
STEP = 10
EPSILON = 1e-06
THETA = 1000000.0
BETA_ONE = 0.9
BETA_TWO = 0.95
ADAM_EPS = 1e-08
DECAY = 0.1
RATE = 0.05
GAIN_RATE = 0.8
OUTPUT_FACTOR = math.sqrt(128)

BF16 = jnp.bfloat16
F32 = jnp.float32
MESH = pl.DeviceIdType.MESH
CHUNK = 32
VMEM_LIMIT = 62 * 1024 * 1024


class Place:
    def __init__(self, spread):
        self.spread = spread
        self.dp = lax.axis_index("dp")
        self.tensor = lax.axis_index("tensor")
        self.core = lax.rem(self.tensor, 2)
        self.y = self.tensor // 2
        self.z = self.dp // spread
        self.r = lax.rem(self.dp, spread)
        self.low = lax.rem(self.z, 2)
        self.core_id = {"dp": self.dp, "tensor": self.y * 2 + 1 - self.core}
        self.y_id = {"dp": self.dp, "tensor": (1 - self.y) * 2 + self.core}
        self.low_id = {"dp": self.dp + spread * (1 - 2 * self.low), "tensor": self.tensor}
        self.own_pair = self.low * 2 + self.y
        self.pairs = (
            (1 - self.low) * 2 + 1 - self.y,
            self.low * 2 + 1 - self.y,
            (1 - self.low) * 2 + self.y,
            self.own_pair,
        )

    def z_dp(self, step):
        return lax.rem(self.z + 4 + step, 4) * self.spread + self.r

    def z_id(self, step):
        return {"dp": self.z_dp(step), "tensor": self.tensor}

    def r_dp(self, step):
        return self.z * self.spread + lax.rem(self.r + self.spread + step, self.spread)

    def r_id(self, step):
        return {"dp": self.r_dp(step), "tensor": self.tensor}

    def greet(self):
        ids = [self.core_id, self.y_id]
        ids += [self.z_id(k) for k in range(1, 4)]
        ids += [self.r_id(k) for k in range(1, self.spread)]
        barrier = pltpu.get_barrier_semaphore()
        for one in ids:
            pl.semaphore_signal(barrier, inc=1, device_id=one, device_id_type=MESH)
        pl.semaphore_wait(barrier, len(ids))


class Links:
    def __init__(self, send, recv, local):
        self.send, self.recv, self.local = send, recv, local
        self.count = self.copies = 0

    def remote(self, src, dst, to):
        slot = self.count
        self.count += 1
        return pltpu.make_async_remote_copy(
            src_ref=src, dst_ref=dst, send_sem=self.send.at[slot], recv_sem=self.recv.at[slot],
            device_id=to, device_id_type=MESH,
        )

    def copy(self, src, dst):
        slot = self.copies
        self.copies += 1
        return pltpu.make_async_copy(src, dst, self.local.at[slot])

    def check(self):
        assert self.count <= self.send.shape[0] and self.copies <= self.local.shape[0]


def tile(start, size):
    return pl.ds(pl.multiple_of(start, size), size)


class Spread:
    def __init__(self, links, place, joined, start, rows):
        def block(pair, core):
            return joined.at[pair * 2 + core, pl.ds(start, rows)]

        c = place.core
        diag, y, z, own = place.pairs
        own, from_z, from_y, from_d = (block(p, c) for p in (own, z, y, diag))
        self.to_z = links.remote(own, own, place.low_id)
        self.to_y = links.remote(own, own, place.y_id)
        self.to_core = links.remote(own, own, place.core_id)
        self.on_y = links.remote(from_z, from_z, place.y_id)
        self.core_z = links.remote(from_z, from_z, place.core_id)
        self.core_y = links.remote(from_y, from_y, place.core_id)
        self.core_d = links.remote(from_d, from_d, place.core_id)

    def start(self):
        self.to_z.start()
        self.to_y.start()
        self.to_core.start()

    def pass_on(self):
        self.to_z.wait_recv()
        self.on_y.start()
        self.core_z.start()
        self.to_y.wait_recv()
        self.core_y.start()

    def pass_last(self):
        self.on_y.wait_recv()
        self.core_d.start()

    def ready(self):
        for one in (self.to_core, self.core_z, self.core_y, self.core_d):
            one.wait_recv()

    def drain(self):
        for one in (self.to_z, self.to_y, self.to_core, self.on_y, self.core_z, self.core_y, self.core_d):
            one.wait_send()


class Collect:
    def __init__(self, links, place, ns, start, rows):
        self.place, self.ns, self.start, self.rows = place, ns, start, rows
        here = pl.ds(start, rows)
        self.across = [
            links.remote(ns.part.at[p * 2 + 1 - place.core, here], ns.core_in.at[k, here], place.core_id)
            for k, p in enumerate(place.pairs)
        ]
        self.diag = links.remote(ns.sums.at[0, here], ns.y_in.at[0, here], place.y_id)
        self.to_y = links.remote(ns.sums.at[1, here], ns.y_in.at[1, here], place.y_id)
        self.to_z = links.remote(ns.sums.at[2, here], ns.z_in.at[here], place.low_id)

    def cross(self, *which):
        for k in which:
            self.across[k].start()

    def term(self, k, at):
        block = self.place.pairs[k] * 2 + self.place.core
        return self.ns.part[block, at, :].astype(F32) + self.ns.core_in[k, at, :].astype(F32)

    def each(self, work):
        def step(i, carry):
            work(tile(self.start + i * CHUNK, CHUNK))
            return carry

        lax.fori_loop(0, self.rows // CHUNK, step, 0)

    def add(self, k):
        def work(at):
            total = self.term(k, at)
            if k == 2:
                total = total + self.ns.y_in[0, at, :].astype(F32)
            self.ns.sums[k, at, :] = total.astype(BF16)

        self.each(work)

    def send_y(self):
        self.across[0].wait_recv()
        self.add(0)
        self.diag.start()
        self.across[1].wait_recv()
        self.add(1)
        self.to_y.start()

    def send_z(self):
        self.across[2].wait_recv()
        self.diag.wait_recv()
        self.add(2)
        self.to_z.start()

    def end(self, finish):
        self.across[3].wait_recv()
        self.to_y.wait_recv()
        self.to_z.wait_recv()

        def work(at):
            total = self.term(3, at) + self.ns.y_in[1, at, :].astype(F32) + self.ns.z_in[at, :].astype(F32)
            finish(at, total)

        self.each(work)
        for one in (*self.across, self.diag, self.to_y, self.to_z):
            one.wait_send()


class Halves:
    def __init__(self, links, place, ns, joined):
        rows = ns.part.shape[1] // 2
        self.size = rows
        self.starts = (0, rows)
        self.sums = [Collect(links, place, ns, start, rows) for start in self.starts]
        self.back = joined is not None
        if self.back:
            self.spread = [Spread(links, place, joined, start, rows) for start in self.starts]


def take(ref, pairs, start, size, columns=slice(None)):
    parts = [ref[pl.ds(p * 2, 2), start : start + size, columns] for p in pairs]
    return jnp.concatenate([one.reshape(2 * size, -1) for one in parts], axis=0)


def put(ref, pairs, start, size, value, columns=slice(None)):
    for i, p in enumerate(pairs):
        part = value[2 * i * size : 2 * (i + 1) * size]
        ref[pl.ds(p * 2, 2), start : start + size, columns] = part.reshape(2, size, -1)


class Gather:
    def __init__(self, links, place, sources, own, stage, land, save, earlier):
        rows = own.shape[1]
        self.earlier, self.own_free = earlier, False
        self.place, self.own, self.land, self.rows, self.stage = place, own, land, rows, stage
        self.starts, self.loads = [], []
        start = 0
        for one in sources:
            size = one.shape[1]
            self.starts.append((start, size // 2))
            self.loads.append(links.copy(one, stage.at[:, start : start + size]))
            start += size
        spread = place.spread

        def at(dp):
            return land.at[tile(dp * rows, rows)]

        mine = at(place.dp)
        self.out = [
            links.remote(own.at[lax.rem(place.low + k, 2)], mine, place.z_id(k)) for k in range(1, 4)
        ]
        self.side = [links.remote(own.at[place.low], mine, place.r_id(s)) for s in range(1, spread)]
        self.on = [
            [
                links.remote(at(place.z_dp(-k)), at(place.z_dp(-k)), place.r_id(s))
                for s in range(1, spread)
            ]
            for k in range(1, 4)
        ]
        self.save = links.copy(land, save)

    def load(self):
        for one in self.loads:
            one.start()

    def sent(self):
        for one in self.out + self.side:
            one.wait_send()

    def cast(self):
        for one in self.loads:
            one.wait()
        if self.earlier is not None:
            self.earlier.sent()
            self.earlier.own_free = True
        step = min(64, self.rows)

        def round_rows(i, carry):
            at = tile(i * step, step)
            for low in range(2):
                to = 0
                for start, half in self.starts:
                    piece = self.stage[at, start + low * half : start + (low + 1) * half]
                    self.own[low, at, to : to + half] = piece.astype(BF16)
                    to += half
            return carry

        lax.fori_loop(0, self.rows // step, round_rows, 0)

    def begin(self):
        for one in self.side:
            one.start()
        step = min(64, self.rows)

        def copy(i, carry):
            self.land[tile(self.place.dp * self.rows + i * step, step), :] = self.own[
                self.place.low, tile(i * step, step), :
            ]
            return carry

        lax.fori_loop(0, self.rows // step, copy, 0)

    def forward(self, k):
        self.out[k].wait_recv()
        for one in self.on[k]:
            one.start()

    def finish(self):
        for one in self.side:
            one.wait_recv()
        for group in self.on:
            for one in group:
                one.wait_recv()
        self.save.start()

    def drain(self):
        if not self.own_free:
            self.sent()
        for group in self.on:
            for one in group:
                one.wait_send()
        self.save.wait()


class Stream:
    def __init__(self, groups):
        self.groups = groups
        self.order = [one for group in groups for one in group]
        self.items = [(group, k) for group in groups for k in range(3)]
        self.sent = self.passed = 0
        self.order[0].load()

    def send(self, count=1):
        for group, k in self.items[self.sent : self.sent + count]:
            for one in group:
                if k == 0:
                    one.cast()
                    at = self.order.index(one) + 1
                    if at < len(self.order):
                        self.order[at].load()
                    one.begin()
                one.out[k].start()
            self.sent += 1

    def forward(self, count=1):
        for group, k in self.items[self.passed : min(self.passed + count, self.sent)]:
            for one in group:
                one.forward(k)
            self.passed += 1

    def tick(self, lag=2):
        self.send()
        if self.passed + lag < self.sent or self.sent == len(self.items):
            self.forward()

    def need(self, one):
        place = [i for i, group in enumerate(self.groups) if one in group][0] * 3 + 3
        self.send(max(0, place - self.sent))
        self.forward(max(0, place - self.passed))
        one.finish()

    def rest(self):
        self.send(len(self.items))
        self.forward(len(self.items))


def scale_of(v):
    return lax.rsqrt(jnp.mean(v * v, axis=-1, keepdims=True) + EPSILON)


def mm(a, b):
    return jnp.dot(a, b, preferred_element_type=F32)


def mm_nt(a, b):
    return lax.dot_general(a, b, (((1,), (1,)), ((), ())), preferred_element_type=F32)


def project_heads(ns, pair):
    block = ns.joined.shape[1]
    two = pl.ds(pair * 2, 2)
    x = ns.joined[two].reshape(2 * block, -1)
    raw = mm(x, ns.layer.wqkv[...])
    ns.raw[two] = raw.reshape(2, block, -1)
    cosine, sine = ns.cosine[two].reshape(2 * block, HD), ns.sine[two].reshape(2 * block, HD)
    q_size, kv_size = ns.q.shape[2], ns.k.shape[2]

    def heads(out, start, size, gain):
        for h in range(size // HD):
            v = raw[:, start + h * HD : start + (h + 1) * HD]
            v = v * scale_of(v) * gain[...]
            turned = v * cosine + pltpu.roll(v, HD // 2, axis=1) * sine
            out[two, :, h * HD : (h + 1) * HD] = turned.astype(BF16).reshape(2, block, HD)

    heads(ns.q, 0, q_size, ns.layer.gain_q)
    heads(ns.k, q_size, kv_size, ns.layer.gain_k)
    ns.v[two] = raw[:, q_size + kv_size :].astype(BF16).reshape(2, block, kv_size)


def softmax(ns, b, half, span, query, keys):
    seen = keys.shape[0]
    s = mm_nt(query, keys) * HD**-0.5
    s = s + ns.bias[b, half * span : (half + 1) * span, :seen].astype(F32)
    p = jnp.exp(s - jnp.max(s, axis=-1, keepdims=True))
    return p * (1.0 / jnp.sum(p, axis=-1, keepdims=True))


def attend(ns, b):
    block = ns.joined.shape[1]
    span = 2 * block
    q_heads = ns.q.shape[2] // HD
    share = q_heads // (ns.k.shape[2] // HD)
    for e in range(q_heads):
        kv = slice((e // share) * HD, (e // share + 1) * HD)
        mine = slice(e * HD, (e + 1) * HD)
        for half in range(2):
            rows = slice(4 * b + 2 * half, 4 * b + 2 * half + 2)
            seen = slice(4 * b, 4 * b + 2 * half + 2)
            keys = ns.k[seen, :, kv].reshape(-1, HD)
            values = ns.v[seen, :, kv].reshape(-1, HD)
            query = ns.q[rows, :, mine].reshape(span, HD)
            p = softmax(ns, b, half, span, query, keys)
            ns.att[rows, :, mine] = mm(p.astype(BF16), values).astype(BF16).reshape(2, block, HD)


def project_out(ns, source, weight, pairs, start, size, width=1024):
    x = take(source, pairs, start, size)

    def step(j, carry):
        at = tile(j * width, width)
        put(ns.part, pairs, start, size, mm_nt(x, weight[at, :]).astype(BF16), at)
        return carry

    lax.fori_loop(0, ns.part.shape[2] // width, step, 0)


def gate_up(ns, pairs, start, size, slot):
    ff = ns.product.shape[2]
    x = take(ns.joined, pairs, start, size)
    gate = mm(x, ns.layer.wgate[...])
    up = mm(x, ns.layer.wup[...])
    ns.gu_stage[slot, :, :, :ff] = gate.astype(BF16).reshape(4, size, ff)
    ns.gu_stage[slot, :, :, ff:] = up.astype(BF16).reshape(4, size, ff)
    put(ns.product, pairs, start, size, (gate / (1.0 + jnp.exp(-gate)) * up).astype(BF16))


def forward_kernel(layers, spread, ns):
    place = Place(spread)
    links = Links(ns.send, ns.recv, ns.local)
    local = ns.tokens.shape[0]
    mine = place.own_pair * 2 + place.core
    diag, y, z, own = place.pairs
    first_pairs, last_pairs = (diag, y), (z, own)

    def gathers_of(layer, before):
        kv = ns.keyvalue_weight.at[layer]
        mlp = ns.mlp_weight.at[layer]
        attention = [(ns.query_weight.at[layer], kv.at[0], kv.at[1]), (ns.output_weight.at[layer],)]
        sources = attention + [(mlp.at[i],) for i in range(3)]
        owns = (ns.own_qkv, ns.own_o, ns.own_gate, ns.own_up, ns.own_down)
        lands = (ns.wqkv, ns.wo, ns.wgate, ns.wup, ns.wdown)
        saves = (ns.save_wqkv, ns.save_wo, ns.save_wgate, ns.save_wup, ns.save_wdown)
        return [
            Gather(links, place, source, own_ref, ns.stage, land[layer], save[layer], earlier)
            for source, own_ref, land, save, earlier in zip(sources, owns, lands, saves, before)
        ]

    gathers = []
    for layer in range(layers):
        gathers.append(gathers_of(layer, gathers[-1] if gathers else [None] * 5))
    groups = [[one] for one in gathers[0]]
    for later in gathers[1:]:
        groups += [later[:2], *[[one] for one in later[2:]]]
    stream = Stream(groups)
    tick = stream.tick
    tokens_in = Spread(links, place, ns.joined, 0, local)
    grads_in = Spread(links, place, ns.joined_grad, 0, local)
    middle = Halves(links, place, ns, ns.joined)
    end = Halves(links, place, ns, ns.joined)
    size = middle.size
    rows_save = [links.copy(ns.joined, one) for one in ns.save_a]

    def norm(i, carry):
        at = tile(i * CHUNK, CHUNK)
        v = ns.tokens[at, :].astype(F32)
        ns.hidden[at, :] = v
        ns.joined[mine, at, :] = (v * scale_of(v) * ns.gain_attn[:1, :]).astype(BF16)
        return carry

    lax.fori_loop(0, local // CHUNK, norm, 0)
    place.greet()
    tokens_in.start()
    stream.send(3)
    tokens_in.pass_on()
    stream.send()
    stream.forward()
    stream.send()
    stream.forward()
    stream.send()
    stream.forward()
    tokens_in.pass_last()
    tick()
    tick()
    tokens_in.ready()
    tokens_in.drain()
    for layer in range(layers):
        first, last = layer == 0, layer + 1 == layers
        qkv, o, gate, up, down = gathers[layer]
        kept = [
            links.copy(src, dst[layer])
            for src, dst in (
                (ns.raw, ns.save_raw), (ns.q, ns.save_q), (ns.k, ns.save_k), (ns.v, ns.save_v),
                (ns.att, ns.save_att), (ns.product, ns.save_product), (ns.mid, ns.save_mid),
                (ns.hidden, ns.save_hidden),
            )
        ]
        kept_raw, kept_q, kept_k, kept_v, kept_att, kept_product, kept_mid, kept_hidden = kept
        ns.layer = SimpleNamespace(
            wqkv=ns.wqkv[layer], gain_q=ns.gain_q.at[pl.ds(layer, 1)], gain_k=ns.gain_k.at[pl.ds(layer, 1)],
            wgate=ns.wgate[layer], wup=ns.wup[layer],
        )
        save_a = rows_save[layer]
        save_a.start()
        kept_hidden.start()
        if last:
            ns.joined_grad[mine] = ns.cotangent[...]
            grads_in.start()
        stream.need(qkv)

        def every(i, carry):
            project_heads(ns, i)
            return carry

        lax.fori_loop(0, 2, every, 0)
        tick()
        lax.fori_loop(2, 4, every, 0)
        for one in (kept_raw, kept_q, kept_k, kept_v):
            one.start()
        if last:
            grads_in.pass_on()
        tick()
        attend(ns, 0)
        tick()
        attend(ns, 1)
        kept_att.start()
        tick()
        stream.need(o)
        if last:
            grads_in.pass_last()

        def middle_rows(at, total):
            v = ns.hidden[at, :] + total
            ns.mid[at, :] = v
            gain = ns.gain_mlp[layer : layer + 1, :]
            ns.joined[mine, at, :] = (v * scale_of(v) * gain).astype(BF16)

        def result_rows(at, total):
            v = ns.mid[at, :] + total
            ns.hidden[at, :] = v
            if not last:
                gain = ns.gain_attn[layer + 1 : layer + 2, :]
                ns.joined[mine, at, :] = (v * scale_of(v) * gain).astype(BF16)

        def part_of(source, weight, halves, h):
            start = halves.starts[h]
            project_out(ns, source, weight, first_pairs, start, size)
            halves.sums[h].cross(0, 1)
            project_out(ns, source, weight, last_pairs, start, size)
            halves.sums[h].cross(2, 3)

        save_a.wait()
        part_of(ns.att, ns.wo[layer], middle, 0)
        middle.sums[0].send_y()
        part_of(ns.att, ns.wo[layer], middle, 1)
        middle.sums[1].send_y()
        tick()
        middle.sums[0].send_z()
        middle.sums[1].send_z()
        tick()
        middle.sums[0].end(middle_rows)
        middle.spread[0].start()
        middle.sums[1].end(middle_rows)
        middle.spread[1].start()
        kept_mid.start()
        tick()
        middle.spread[0].pass_on()
        middle.spread[1].pass_on()
        tick()
        stream.need(gate)
        stream.need(up)
        middle.spread[0].pass_last()
        middle.spread[0].ready()
        middle.spread[0].drain()
        saves = []

        def gate_up_of(pairs, start):
            slot = (len(saves) // 2) % 2
            if len(saves) >= 4:
                for save in saves[-4:-2]:
                    save.wait()
            gate_up(ns, pairs, start, size, slot)
            for i, p in enumerate(pairs):
                save = links.copy(
                    ns.gu_stage.at[slot, 2 * i : 2 * i + 2],
                    ns.save_gateup[layer].at[pl.ds(p * 2, 2), pl.ds(start, size)],
                )
                save.start()
                saves.append(save)

        save_b = [
            links.copy(ns.joined.at[:, pl.ds(start, size)], ns.save_b[layer].at[:, pl.ds(start, size)])
            for start in middle.starts
        ]
        save_b[0].start()
        gate_up_of(first_pairs, 0)
        tick()
        middle.spread[1].pass_last()
        gate_up_of(last_pairs, 0)
        stream.need(down)
        save_b[0].wait()
        kept_hidden.wait()
        part_of(ns.product, ns.wdown[layer], end, 0)
        middle.spread[1].ready()
        middle.spread[1].drain()
        end.sums[0].send_y()
        save_b[1].start()
        gate_up_of(first_pairs, size)
        end.sums[0].send_z()
        tick()
        gate_up_of(last_pairs, size)
        kept_product.start()
        save_b[1].wait()
        part_of(ns.product, ns.wdown[layer], end, 1)
        end.sums[1].send_y()
        end.sums[0].end(result_rows)
        if not last:
            end.spread[0].start()
        tick()
        end.sums[1].send_z()
        if not last:
            end.spread[0].pass_on()
        tick()
        end.sums[1].end(result_rows)
        if not last:
            end.spread[1].start()
            tick()
            end.spread[0].pass_last()
            end.spread[1].pass_on()
            tick()
            end.spread[1].pass_last()
            for one in end.spread:
                one.ready()
                one.drain()
        for one in (*saves[-4:], kept_raw, kept_q, kept_k, kept_v, kept_att, kept_product, kept_mid):
            one.wait()
    result = links.copy(ns.hidden, ns.out)
    result.start()
    grads_in.ready()
    grads_in.drain()
    final = links.copy(ns.joined_grad, ns.save_grad)
    final.start()
    for group in gathers:
        for one in group:
            one.drain()
    result.wait()
    final.wait()
    assert stream.passed == len(stream.items)
    links.check()


def call(kernel, ins, outs, scratch, collective_id, name):
    groups = [ins, outs, scratch]
    sizes = [len(v) if isinstance(v, list) else 0 for group in groups for v in group.values()]
    names = [key for group in groups for key in group]

    def flat(group):
        return [one for v in group.values() for one in (v if isinstance(v, list) else [v])]

    def named(values, keys, counts):
        values = list(values)
        taken = {}
        for key, count in zip(keys, counts):
            taken[key] = [values.pop(0) for _ in range(count)] if count else values.pop(0)
        return SimpleNamespace(**taken)

    def run(*refs):
        kernel(named(refs, names, sizes))

    def space(in_vmem):
        return pl.BlockSpec(memory_space=pltpu.VMEM if in_vmem else pl.ANY)

    results = pl.pallas_call(
        run,
        out_shape=[jax.ShapeDtypeStruct(shape, dtype) for shape, dtype, _ in flat(outs)],
        in_specs=[space(v) for _, v in flat(ins)],
        out_specs=[space(v) for _, _, v in flat(outs)],
        scratch_shapes=flat(scratch),
        compiler_params=pltpu.CompilerParams(
            collective_id=collective_id, has_side_effects=True, vmem_limit_bytes=VMEM_LIMIT
        ),
        cost_estimate=pl.CostEstimate(
            flops=26 * 10**9, bytes_accessed=10**8, transcendentals=10**6
        ),
        name=name,
    )(*[array for array, _ in flat(ins)])
    return named(results, outs, sizes[len(ins) : len(ins) + len(outs)])


def exchange_scratch(rows, width):
    return dict(
        joined=pltpu.VMEM((8, rows, width), BF16),
        part=pltpu.VMEM((8, rows, width), BF16),
        core_in=pltpu.VMEM((4, rows, width), BF16),
        y_in=pltpu.VMEM((2, rows, width), BF16),
        z_in=pltpu.VMEM((rows, width), BF16),
        sums=pltpu.VMEM((3, rows, width), BF16),
    )


def forward(tokens, cotangent, masters, tables, gains, spread):
    rows, width = tokens.shape
    query, keyvalue, output, mlp = masters
    layers = gains.shape[0]
    own = query.shape[1]
    d_rows = own * 4 * spread
    o, ff = query.shape[2] // 2, mlp.shape[3] // 2
    kv = keyvalue.shape[3] // 2
    qkv = o + 2 * kv
    cosine, sine, bias = tables
    ins = dict(
        tokens=(tokens, True), cotangent=(cotangent, True),
        query_weight=(query, False), keyvalue_weight=(keyvalue, False),
        output_weight=(output, False), mlp_weight=(mlp, False),
        gain_attn=(gains[:, :width], True), gain_mlp=(gains[:, width : 2 * width], True),
        gain_q=(gains[:, 2 * width : 2 * width + HD], True), gain_k=(gains[:, 2 * width + HD :], True),
        cosine=(cosine, True), sine=(sine, True), bias=(bias, True),
    )

    def each(dtype, *shape):
        return [(shape, dtype, False)] * layers

    outs = dict(
        out=((rows, width), F32, False),
        save_hidden=each(F32, rows, width), save_mid=each(F32, rows, width),
        save_raw=each(F32, 8, rows, qkv), save_q=each(BF16, 8, rows, o),
        save_k=each(BF16, 8, rows, kv), save_v=each(BF16, 8, rows, kv),
        save_att=each(BF16, 8, rows, o), save_product=each(BF16, 8, rows, ff),
        save_gateup=each(BF16, 8, rows, 2 * ff),
        save_a=each(BF16, 8, rows, width), save_b=each(BF16, 8, rows, width),
        save_grad=((8, rows, width), BF16, False),
        save_wqkv=each(BF16, d_rows, qkv), save_wo=each(BF16, d_rows, o),
        save_wgate=each(BF16, d_rows, ff), save_wup=each(BF16, d_rows, ff), save_wdown=each(BF16, d_rows, ff),
    )
    scratch = exchange_scratch(rows, width)
    weight = lambda size: [pltpu.VMEM((d_rows, size), BF16)] * layers
    mine = lambda size: pltpu.VMEM((2, own, size), BF16)
    tokens_of = lambda size, dtype=BF16: pltpu.VMEM((8, rows, size), dtype)
    scratch.update(
        hidden=pltpu.VMEM((rows, width), F32), mid=pltpu.VMEM((rows, width), F32),
        joined_grad=tokens_of(width), gu_stage=pltpu.VMEM((2, 4, rows // 2, 2 * ff), BF16),
        stage=pltpu.VMEM((own, max(2 * ff, 2 * qkv)), F32),
        raw=tokens_of(qkv, F32), q=tokens_of(o), k=tokens_of(kv), v=tokens_of(kv), att=tokens_of(o),
        product=tokens_of(ff),
        wqkv=weight(qkv), wo=weight(o), wgate=weight(ff), wup=weight(ff), wdown=weight(ff),
        own_qkv=mine(qkv), own_o=mine(o), own_gate=mine(ff), own_up=mine(ff), own_down=mine(ff),
        local=pltpu.SemaphoreType.DMA((4 + 36 * layers,)),
    )
    count = 72 + 20 * spread * layers
    scratch.update(send=pltpu.SemaphoreType.DMA((count,)), recv=pltpu.SemaphoreType.DMA((count,)))
    return call(partial(forward_kernel, layers, spread), ins, outs, scratch, 1, "forward")


def mm_tn(a, b):
    return lax.dot_general(a, b, (((0,), (0,)), ((), ())), preferred_element_type=F32)


class Reduce:
    def __init__(self, links, place, blocks, x_in, z_in, outs):
        self.place, self.blocks, self.x_in, self.z_in, self.outs = place, blocks, x_in, z_in, outs
        spread = place.spread
        rows = blocks.shape[1] // spread
        self.rows = rows

        def block(q, r):
            return blocks.at[q, tile(r * rows, rows)]

        self.x_out = [
            [
                links.remote(
                    block(q, lax.rem(place.r + s, spread)), x_in.at[s - 1, q], place.r_id(s)
                )
                for s in range(1, spread)
            ]
            for q in range(4)
        ]
        self.z_out = [
            links.remote(block(q, place.r), z_in.at[q - 1], place.z_id(q)) for q in range(1, 4)
        ]

    def compute(self, q, left, right):
        part = self.blocks.shape[1]
        step = min(256, part)
        start = lax.rem(self.place.z + q, 4) * part

        def one(i, carry):
            x = left[:, :, tile(start + i * step, step)]
            product = mm_tn(x.reshape(-1, step), right())
            self.blocks[q, tile(i * step, step), :] = product.astype(BF16)
            return carry

        lax.fori_loop(0, part // step, one, 0)

    def send(self, q):
        for one in self.x_out[q]:
            one.start()

    def pass_on(self, q):
        for one in self.x_out[q]:
            one.wait_recv()
        step = min(64, self.rows)
        start = self.place.r * self.rows

        def add(i, carry):
            at = tile(start + i * step, step)
            if self.place.spread == 2:
                self.blocks[q, at, :] += self.x_in[0, q, tile(i * step, step), :]
                return carry
            total = self.blocks[q, at, :].astype(F32)
            for s in range(self.place.spread - 1):
                total = total + self.x_in[s, q, tile(i * step, step), :].astype(F32)
            self.blocks[q, at, :] = total.astype(BF16)
            return carry

        lax.fori_loop(0, self.rows // step, add, 0)
        if q:
            self.z_out[q - 1].start()

    def finish(self):
        for one in self.z_out:
            one.wait_recv()
        step = min(64, self.rows)
        low = self.place.low
        start = self.place.r * self.rows

        def add(i, carry):
            at = tile(i * step, step)
            near = self.blocks[0, tile(start + i * step, step), :] + self.z_in[1, at, :]
            far = self.z_in[0, at, :] + self.z_in[2, at, :]
            first = 0
            for out, size in self.outs:
                out[at, tile(low * size, size)] = near[:, first : first + size]
                out[at, tile((1 - low) * size, size)] = far[:, first : first + size]
                first += size
            return carry

        lax.fori_loop(0, self.rows // step, add, 0)

    def drain(self):
        for group in self.x_out:
            for one in group:
                one.wait_send()
        for one in self.z_out:
            one.wait_send()


ORDER = (2, 1, 3, 0)


def gate_up_back(ns, pairs, start, size, slot):
    ff = ns.product.shape[2]
    d_act = mm(take(ns.joined, pairs, start, size), ns.wdown[...])
    gate = ns.stage[slot, :, :, :ff].reshape(4 * size, ff).astype(F32)
    up = ns.stage[slot, :, :, ff:].reshape(4 * size, ff).astype(F32)
    gated = 1.0 / (1.0 + jnp.exp(-gate))
    put(ns.d_gate, pairs, start, size, (d_act * up * gated * (1.0 + gate * (1.0 - gated))).astype(BF16))
    put(ns.d_up, pairs, start, size, (d_act * gate * gated).astype(BF16))


def head_back(ns, blocks, d_out, raw_columns, gain, d_gain):
    rows = d_out.shape[0]
    cosine, sine = ns.cosine[blocks].reshape(rows, HD), ns.sine[blocks].reshape(rows, HD)
    raw = ns.raw[blocks, :, raw_columns].reshape(rows, HD)
    d_turned = d_out * cosine + pltpu.roll(d_out * sine, HD // 2, axis=1)
    scale = scale_of(raw)
    normed = raw * scale
    d_gain[...] += jnp.sum(d_turned * normed, axis=0, keepdims=True)
    d_normed = d_turned * gain[...]
    inner = jnp.mean(d_normed * normed, axis=-1, keepdims=True)
    d_raw = (scale * (d_normed - normed * inner)).astype(BF16)
    ns.d_raw[blocks, :, raw_columns] = d_raw.reshape(-1, ns.raw.shape[1], HD)


def attend_back(ns, b):
    block = ns.joined.shape[1]
    span = 2 * block
    q_size, kv_size = ns.q.shape[2], ns.k.shape[2]
    share = q_size // kv_size
    scale = HD**-0.5
    whole = slice(4 * b, 4 * b + 4)
    for kv in range(kv_size // HD):
        columns = slice(kv * HD, (kv + 1) * HD)
        ns.d_keys[...] = jnp.zeros_like(ns.d_keys)
        ns.d_values[...] = jnp.zeros_like(ns.d_values)
        for e in range(kv * share, (kv + 1) * share):
            mine = slice(e * HD, (e + 1) * HD)
            for half in range(2):
                rows = slice(4 * b + 2 * half, 4 * b + 2 * half + 2)
                some = slice(4 * b, 4 * b + 2 * half + 2)
                seen = (half + 1) * span
                keys = ns.k[some, :, columns].reshape(seen, HD)
                values = ns.v[some, :, columns].reshape(seen, HD)
                query = ns.q[rows, :, mine].reshape(span, HD)
                d_out = ns.d_att[rows, :, mine].reshape(span, HD)
                p = softmax(ns, b, half, span, query, keys)
                d_p = mm_nt(d_out, values)
                delta = jnp.sum(d_p * p, axis=-1, keepdims=True)
                d_s = (p * (d_p - delta)).astype(BF16)
                ns.d_values[:seen, :] += mm_tn(p.astype(BF16), d_out)
                ns.d_keys[:seen, :] += mm_tn(d_s, query)
                head_back(ns, rows, mm(d_s, keys) * scale, mine, ns.gain_q, ns.d_gain_q)
        key_columns = slice(q_size + kv * HD, q_size + (kv + 1) * HD)
        head_back(ns, whole, ns.d_keys[...] * scale, key_columns, ns.gain_k, ns.d_gain_k)
        value_columns = slice(q_size + kv_size + kv * HD, q_size + kv_size + (kv + 1) * HD)
        ns.d_raw[whole, :, value_columns] = ns.d_values[...].astype(BF16).reshape(4, block, HD)


class GainSum:
    def __init__(self, links, place, terms, came, came_r, total):
        spread = place.spread
        self.place, self.terms, self.came, self.came_r, self.total = place, terms, came, came_r, total
        ids = (place.core_id, place.y_id, place.low_id, place.z_id(2))
        self.pairs = [links.remote(terms.at[i], came.at[i], one) for i, one in enumerate(ids)]
        self.sides = [
            links.remote(terms.at[4], came_r.at[place.r], place.r_id(s)) for s in range(1, spread)
        ]
        self.at = 0

    def start(self):
        self.pairs[0].start()

    def step(self):
        i = self.at
        self.at += 1
        if i < 4:
            self.pairs[i].wait_recv()
            self.terms[i + 1] = self.terms[i] + self.came[i]
            if i < 3:
                self.pairs[i + 1].start()
                return
            self.came_r[self.place.r] = self.terms[4]
            for one in self.sides:
                one.start()
            return
        for one in self.sides:
            one.wait_recv()
        total = self.came_r[0]
        for r in range(1, self.place.spread):
            total = total + self.came_r[r]
        self.total[...] = total
        for one in self.pairs + self.sides:
            one.wait_send()


def backward_kernel(layers, spread, ns):
    place = Place(spread)
    links = Links(ns.send, ns.recv, ns.local)
    local, width = ns.out.shape
    mine = place.own_pair * 2 + place.core
    qkv, o, ff = ns.wqkv_in[0].shape[1], ns.wo_in[0].shape[1], ns.wdown_in[0].shape[1]
    kv = (qkv - o) // 2
    rows_all = ns.wdown_in[0].shape[0]
    group = ns.bias_in.shape[1]
    diag, y, z, own = place.pairs
    first_pairs, last_pairs = (diag, y), (z, own)

    def loads(*pairs):
        copies = [links.copy(src, dst) for src, dst in pairs]
        for one in copies:
            one.start()
        return copies

    def wait(copies):
        for one in copies:
            one.wait()

    def reduce(i, outs):
        return Reduce(links, place, ns.blocks.at[i], ns.x_in.at[i], ns.z_in_w.at[i], outs)

    red_down = reduce(0, [(ns.g_mlp.at[2], ff)])
    red_gate = reduce(1, [(ns.g_mlp.at[0], ff)])
    red_up = reduce(2, [(ns.g_mlp.at[1], ff)])
    red_o = Reduce(links, place, ns.blocks_o, ns.x_in_o, ns.z_in_o, [(ns.g_o, o)])
    red_qkv = Reduce(
        links, place, ns.blocks_qkv, ns.x_in_qkv, ns.z_in_qkv,
        [(ns.g_q, o), (ns.g_kv.at[0], kv), (ns.g_kv.at[1], kv)],
    )
    reduces = (red_down, red_gate, red_up, red_o, red_qkv)
    middle = Halves(links, place, ns, ns.joined)
    end = Halves(links, place, ns, ns.joined)
    size = middle.size
    gain_sum = GainSum(links, place, ns.terms, ns.came, ns.came_r, ns.gain_total)
    passes = []
    going = [False]

    def pass_next(count=1):
        for _ in range(count):
            passes.pop(0)()

    def compute_all(one, left, right, send=True):
        if going[0]:
            one.drain()
        for q in ORDER:
            one.compute(q, left, right)
            if send:
                one.send(q)

    def keep(layer):
        pairs = ((ns.g_q, ns.save_q), (ns.g_kv, ns.save_kv), (ns.g_o, ns.save_o), (ns.g_mlp, ns.save_mlp))
        return [links.copy(one, to.at[layer]) for one, to in pairs]

    for one in (*ns.d_attn, *ns.d_mlp, *ns.d_q, *ns.d_k):
        one[...] = jnp.zeros_like(one)
    first_rows = loads((ns.joined_in, ns.joined))
    place.greet()
    wait(first_rows)
    for layer in reversed(range(layers)):
        backward_layer(layer, layers, SimpleNamespace(**locals()))
    result = loads((ns.out, ns.input_grad))
    ns.terms[0] = jnp.zeros_like(ns.terms[0])
    for i in range(layers):
        ns.terms[0, 2 * i : 2 * i + 1, :width] = ns.d_attn[i][...]
        ns.terms[0, 2 * i + 1 : 2 * i + 2, :width] = ns.d_mlp[i][...]
        ns.terms[0, 2 * i : 2 * i + 1, width : width + HD] = ns.d_q[i][...]
        ns.terms[0, 2 * i : 2 * i + 1, width + HD : width + 2 * HD] = ns.d_k[i][...]
    gain_sum.start()
    for _ in range(4):
        pass_next()
        gain_sum.step()
    red_gate.finish()
    gain_sum.step()
    red_up.finish()
    red_o.finish()
    red_qkv.finish()
    for one in reduces:
        one.drain()
    last = keep(0)
    for one in last:
        one.start()
    wait(last)
    wait(result)
    assert not passes
    links.check()


def backward_layer(layer, layers, env):
    ns, place, links, loads, wait, local, width = (
        env.ns, env.place, env.links, env.loads, env.wait, env.local, env.width
    )
    middle, end, size, mine, passes, pass_next = env.middle, env.end, env.size, env.mine, env.passes, env.pass_next
    red_down, red_gate, red_up, red_o, red_qkv = env.reduces
    first_pairs, last_pairs, compute_all = env.first_pairs, env.last_pairs, env.compute_all
    first, started = layer == 0, layer + 1 < layers
    passes += [partial(one.pass_on, q) for one in env.reduces for q in ORDER]
    ns.gain_q, ns.gain_k = ns.gains_q.at[pl.ds(layer, 1)], ns.gains_k.at[pl.ds(layer, 1)]
    ns.d_gain_q, ns.d_gain_k = ns.d_q[layer], ns.d_k[layer]
    gain_mlp, gain_attn = ns.gains_mlp.at[pl.ds(layer, 1)], ns.gains_attn.at[pl.ds(layer, 1)]
    ff, qkv, o, rows_all, group = env.ff, env.qkv, env.o, env.rows_all, env.group
    kept = env.keep(layer + 1) if started else []

    def finish_later():
        if started:
            for one in (red_up, red_o, red_qkv):
                one.finish()
            for one in kept:
                one.start()
            for k in range(1, 4):
                pl.semaphore_signal(ns.credit, inc=1, device_id=place.z_id(k), device_id_type=MESH)

    def back_norm(value, grad, gain, d_gain, out, gather):
        def finish(at, total):
            v = value[at, :].astype(F32)
            scale = scale_of(v)
            normed = v * scale
            d_gain[...] += jnp.sum(total * normed, axis=0, keepdims=True)
            d_normed = total * gain[...]
            inner = jnp.mean(d_normed * normed, axis=-1, keepdims=True)
            g = grad[at, :].astype(F32) + scale * (d_normed - normed * inner)
            out[at, :] = g
            if gather:
                ns.joined[mine, at, :] = g.astype(BF16)

        return finish

    flat = lambda ref: lambda: ref[...].reshape(8 * local, -1)

    def mlp_scope(wgate, wup, d_gate, d_up):
        ns.d_gate, ns.d_up = d_gate, d_up
        weight_loads = loads((ns.wgate_in[layer], wgate), (ns.wup_in[layer], wup))

        def part_of(h, columns=1024):
            start = middle.starts[h]
            for which, pairs in ((0, first_pairs), (2, last_pairs)):
                gates, ups = take(d_gate, pairs, start, size), take(d_up, pairs, start, size)

                def step(j, carry):
                    at = tile(j * columns, columns)
                    term = mm_nt(gates, wgate[at, :]) + mm_nt(ups, wup[at, :])
                    put(ns.part, pairs, start, size, term.astype(BF16), at)
                    return carry

                lax.fori_loop(0, width // columns, step, 0)
                middle.sums[h].cross(which, which + 1)

        def down_scope(wdown, product, stage):
            ns.wdown, ns.product, ns.stage = wdown, product, stage
            first_loads = loads((ns.product_in[layer], product))
            down_load = loads((ns.wdown_in[layer], wdown))
            chunks = [(start, pairs) for start in middle.starts for pairs in (first_pairs, last_pairs)]
            gateup_loads = [
                [
                    links.copy(
                        ns.gateup_in[layer].at[pl.ds(p * 2, 2), pl.ds(start, size)], stage.at[i % 2, 2 * j : 2 * j + 2]
                    )
                    for j, p in enumerate(pairs)
                ]
                for i, (start, pairs) in enumerate(chunks)
            ]
            for group in gateup_loads[:2]:
                for one in group:
                    one.start()
            wait(first_loads)
            compute_all(red_down, ns.joined, flat(product))
            wait(down_load)
            for i, (start, pairs) in enumerate(chunks):
                wait(gateup_loads[i])
                gate_up_back(ns, pairs, start, size, i % 2)
                if i < 2:
                    for one in gateup_loads[i + 2]:
                        one.start()
                if i == 1:
                    wait(weight_loads)
                    part_of(0)
                if i == 2:
                    middle.sums[0].send_y()
            finish_later()

        pl.run_scoped(
            down_scope,
            pltpu.VMEM((rows_all, ff), BF16),
            pltpu.VMEM((8, local, ff), BF16),
            pltpu.VMEM((2, 4, size, 2 * ff), BF16),
        )

        def rest_scope(b, mid, grad=None):
            b_load = loads((ns.mid_in[layer], mid), (ns.b_in[layer], b))
            if grad is None:
                grad = ns.out
            else:
                b_load += loads((ns.grad_in, grad))
            middle_rows = back_norm(mid, grad, gain_mlp, ns.d_mlp[layer], ns.grad_mid, True)
            part_of(1)
            middle.sums[0].send_z()
            middle.sums[1].send_y()
            wait(b_load)
            compute_all(red_gate, b, flat(d_gate))
            middle.sums[0].end(middle_rows)
            middle.spread[0].start()
            middle.sums[1].send_z()
            if started:
                pl.semaphore_wait(ns.credit, 3)
            pass_next()
            compute_all(red_up, b, flat(d_up), send=False)
            middle.sums[1].end(middle_rows)
            middle.spread[1].start()
            pass_next()

        pl.run_scoped(
            rest_scope,
            pltpu.VMEM((8, local, width), BF16),
            pltpu.VMEM((local, width), F32),
            *([] if started else [pltpu.VMEM((local, width), ns.grad_in.dtype)]),
        )

    pl.run_scoped(
        mlp_scope,
        pltpu.VMEM((rows_all, ff), BF16),
        pltpu.VMEM((rows_all, ff), BF16),
        pltpu.VMEM((8, local, ff), BF16),
        pltpu.VMEM((8, local, ff), BF16),
    )

    def attention_scope(
        cosine, sine, bias, hidden, wqkv, wo, a, q, k, v, raw, att, d_att, d_raw, d_keys, d_values
    ):
        ns.cosine, ns.sine, ns.bias, ns.hidden = cosine, sine, bias, hidden
        ns.q, ns.k, ns.v, ns.raw, ns.att = q, k, v, raw, att
        ns.d_att, ns.d_raw, ns.d_keys, ns.d_values = d_att, d_raw, d_keys, d_values
        o_loads = loads((ns.wo_in[layer], wo), (ns.att_in[layer], att))
        other_loads = loads(
            (ns.q_in[layer], q), (ns.k_in[layer], k), (ns.v_in[layer], v), (ns.raw_in[layer], raw),
            (ns.cosine_in, cosine), (ns.sine_in, sine), (ns.bias_in, bias), (ns.a_in[layer], a),
            (ns.wqkv_in[layer], wqkv), (ns.hidden_in[layer], hidden),
        )
        result_rows = back_norm(hidden, ns.grad_mid, gain_attn, ns.d_attn[layer], ns.out, not first)

        def d_attended(h):
            start = middle.starts[h]
            middle.spread[h].ready()
            middle.spread[h].drain()
            for pairs in (first_pairs, last_pairs):
                put(d_att, pairs, start, size, mm(take(ns.joined, pairs, start, size), wo[...]).astype(BF16))

        def part_of(h):
            start = end.starts[h]
            project_out(ns, d_raw, wqkv, first_pairs, start, size)
            end.sums[h].cross(0, 1)
            project_out(ns, d_raw, wqkv, last_pairs, start, size)
            end.sums[h].cross(2, 3)

        middle.spread[0].pass_on()
        middle.spread[1].pass_on()
        pass_next()
        wait(o_loads)
        middle.spread[0].pass_last()
        d_attended(0)
        pass_next()
        middle.spread[1].pass_last()
        d_attended(1)
        for q_part in ORDER:
            red_up.send(q_part)
        compute_all(red_o, ns.joined, flat(att))
        pass_next(2)
        wait(other_loads)
        attend_back(ns, 0)
        pass_next(2)
        attend_back(ns, 1)
        pass_next(2)
        part_of(0)
        end.sums[0].send_y()
        part_of(1)
        end.sums[1].send_y()
        compute_all(red_qkv, a, flat(d_raw))
        end.sums[0].send_z()
        end.sums[1].send_z()
        pass_next(2)
        end.sums[0].end(result_rows)
        if not first:
            end.spread[0].start()
        pass_next(4)
        end.sums[1].end(result_rows)
        if not first:
            end.spread[1].start()
        wait(kept)
        red_down.finish()

    pl.run_scoped(
        attention_scope,
        pltpu.VMEM(ns.cosine_in.shape, F32),
        pltpu.VMEM(ns.sine_in.shape, F32),
        pltpu.VMEM(ns.bias_in.shape, BF16),
        pltpu.VMEM(ns.hidden_in[layer].shape, F32),
        pltpu.VMEM((rows_all, qkv), BF16),
        pltpu.VMEM((rows_all, o), BF16),
        pltpu.VMEM((8, local, width), BF16),
        pltpu.VMEM(ns.q_in[layer].shape, BF16),
        pltpu.VMEM(ns.k_in[layer].shape, BF16),
        pltpu.VMEM(ns.v_in[layer].shape, BF16),
        pltpu.VMEM(ns.raw_in[layer].shape, F32),
        pltpu.VMEM(ns.att_in[layer].shape, BF16),
        pltpu.VMEM((8, local, o), BF16),
        pltpu.VMEM((8, local, qkv), BF16),
        pltpu.VMEM((group, HD), F32),
        pltpu.VMEM((group, HD), F32),
    )
    if not first:
        pass_next()
        end.spread[0].pass_on()
        end.spread[1].pass_on()
        pass_next(2)
        end.spread[0].pass_last()
        end.spread[1].pass_last()
        pass_next()
        red_gate.finish()
        for one in end.spread:
            one.ready()
            one.drain()
        env.going[0] = True


def backward(cotangent, kept, tables, gains, spread):
    rows, width = cotangent.shape
    cosine, sine, bias = tables
    layers = gains.shape[0]
    d_rows, ff = kept.save_wdown[0].shape
    o, qkv = kept.save_wo[0].shape[1], kept.save_wqkv[0].shape[1]
    part = d_rows // 4
    block = part // spread
    small = (8, width + 2 * HD)

    def far(arrays):
        return [(one, False) for one in arrays]

    ins = dict(
        grad_in=(cotangent, False), joined_in=(kept.save_grad, False),
        mid_in=far(kept.save_mid), hidden_in=far(kept.save_hidden), product_in=far(kept.save_product),
        gateup_in=far(kept.save_gateup), b_in=far(kept.save_b), a_in=far(kept.save_a),
        wdown_in=far(kept.save_wdown), wgate_in=far(kept.save_wgate), wup_in=far(kept.save_wup),
        wqkv_in=far(kept.save_wqkv), wo_in=far(kept.save_wo), q_in=far(kept.save_q), k_in=far(kept.save_k),
        v_in=far(kept.save_v), raw_in=far(kept.save_raw), att_in=far(kept.save_att),
        gains_attn=(gains[:, :width], True), gains_mlp=(gains[:, width : 2 * width], True),
        gains_q=(gains[:, 2 * width : 2 * width + HD], True), gains_k=(gains[:, 2 * width + HD :], True),
        cosine_in=(cosine, False), sine_in=(sine, False), bias_in=(bias, False),
    )
    sums = dict(g_q=(block, 2 * o), g_kv=(2, block, qkv - o), g_o=(block, 2 * o), g_mlp=(3, block, 2 * ff))

    def each(name):
        return ((layers, *sums[name]), BF16, False)

    outs = dict(
        input_grad=((rows, width), F32, False), gain_total=(small, F32, True),
        save_q=each("g_q"), save_kv=each("g_kv"), save_o=each("g_o"), save_mlp=each("g_mlp"),
    )
    scratch = exchange_scratch(rows, width)
    scratch.update({name: pltpu.VMEM(shape, BF16) for name, shape in sums.items()})
    side = spread - 1
    wide, thin = [pltpu.VMEM((1, width), F32)] * layers, [pltpu.VMEM((1, HD), F32)] * layers
    count = 88 + 22 * spread
    scratch.update(
        out=pltpu.VMEM((rows, width), F32), grad_mid=pltpu.VMEM((rows, width), F32),
        blocks=pltpu.VMEM((3, 4, part, ff), BF16),
        blocks_o=pltpu.VMEM((4, part, o), BF16), blocks_qkv=pltpu.VMEM((4, part, qkv), BF16),
        x_in=pltpu.VMEM((3, side, 4, block, ff), BF16),
        x_in_o=pltpu.VMEM((side, 4, block, o), BF16), x_in_qkv=pltpu.VMEM((side, 4, block, qkv), BF16),
        z_in_w=pltpu.VMEM((3, 3, block, ff), BF16),
        z_in_o=pltpu.VMEM((3, block, o), BF16), z_in_qkv=pltpu.VMEM((3, block, qkv), BF16),
        d_attn=wide, d_mlp=wide, d_q=thin, d_k=thin,
        terms=pltpu.VMEM((5, *small), F32), came=pltpu.VMEM((4, *small), F32),
        came_r=pltpu.VMEM((spread, *small), F32), credit=pltpu.SemaphoreType.REGULAR,
        local=pltpu.SemaphoreType.DMA((8 + 32 * layers,)),
        send=pltpu.SemaphoreType.DMA((count,)), recv=pltpu.SemaphoreType.DMA((count,)),
    )
    return call(partial(backward_kernel, layers, spread), ins, outs, scratch, 2, "backward")


def places(dp_size):
    spread = dp_size // 4
    me = lax.axis_index("dp")
    z = me // spread
    return spread, me, lax.rem(me, spread), lax.rem(z, 2), z // 2


def flip_lo(dp_size):
    spread = dp_size // 4
    return [(i, i + spread * (1 - 2 * ((i // spread) % 2))) for i in range(dp_size)]


def flip_hi(dp_size):
    spread = dp_size // 4
    return [(i, i + 2 * spread * (1 - 2 * (i // (2 * spread)))) for i in range(dp_size)]


def shift_r(dp_size, step):
    spread = dp_size // 4
    return [(i, (i // spread) * spread + (i % spread + step) % spread) for i in range(dp_size)]


def rope_tables(positions, head_size):
    half = head_size // 2
    frequency = jnp.power(THETA, -2.0 * jnp.arange(half, dtype=F32) / head_size)
    angle = positions.astype(F32)[:, None] * frequency[None, :]
    return (jnp.cos(angle)[:, None, :], jnp.sin(angle)[:, None, :])


def adamw(weight, first, second, grad, rate, decay):
    first_new = BETA_ONE * first + (1.0 - BETA_ONE) * grad
    second_new = BETA_TWO * second + (1.0 - BETA_TWO) * grad * grad
    first_hat = first_new / (1.0 - BETA_ONE**STEP)
    second_hat = second_new / (1.0 - BETA_TWO**STEP)
    weight_new = weight - rate * (first_hat / (jnp.sqrt(second_hat) + ADAM_EPS) + decay * weight)
    return (first_new, second_new, weight_new)


def body(
    tokens, cotangent, segment_ids, gains, gain_first, gain_second,
    query_weight, query_first, query_second,
    keyvalue_weight, keyvalue_first, keyvalue_second,
    output_weight, output_first, output_second,
    mlp_weight, mlp_first, mlp_second,
):
    dp_size = lax.axis_size("dp")
    spread, me, r, low, high = places(dp_size)
    layers = gains.shape[0]
    local_rows, width = tokens.shape
    group = segment_ids.shape[0]
    rows = 8 * local_rows
    index = jnp.arange(group, dtype=jnp.int32)
    other = lax.ppermute(segment_ids, "dp", flip_lo(dp_size))
    segments = jnp.stack([jnp.where(low == 0, segment_ids, other), jnp.where(low == 0, other, segment_ids)])
    positions = (index[None, :] - (segments - segments[:, :1])).reshape(rows)
    mask = (segments[:, :, None] == segments[:, None, :]) & (index[None, None, :] <= index[None, :, None])
    bias = jnp.where(mask, 0.0, -1e30).astype(BF16)
    cosine, sine = rope_tables(positions, HD)
    tables = (
        jnp.concatenate([cosine[:, 0], cosine[:, 0]], axis=1).reshape(8, local_rows, HD),
        jnp.concatenate([-sine[:, 0], sine[:, 0]], axis=1).reshape(8, local_rows, HD),
        bias,
    )
    masters = (query_weight, keyvalue_weight, output_weight, mlp_weight)

    kept = forward(tokens, cotangent, masters, tables, gains, spread)
    block_output = kept.out
    done = backward(cotangent, kept, tables, gains, spread)
    stacked = [one.astype(F32) for one in (done.save_q, done.save_kv, done.save_o, done.save_mlp)]
    sums = done.gain_total
    gain_total = jnp.stack(
        [
            jnp.concatenate([sums[2 * i, :width], sums[2 * i + 1, :width], sums[2 * i, width:]])
            for i in range(layers)
        ]
    )
    head_gain_grads = gain_total[:, 2 * width :]
    gain_new = adamw(gains, gain_first, gain_second, gain_total, GAIN_RATE, 0.0)
    query_new = adamw(query_weight, query_first, query_second, stacked[0], RATE, DECAY)
    keyvalue_new = adamw(keyvalue_weight, keyvalue_first, keyvalue_second, stacked[1], RATE, DECAY)
    output_new = adamw(output_weight, output_first, output_second, stacked[2], RATE * OUTPUT_FACTOR, DECAY)
    mlp_new = adamw(mlp_weight, mlp_first, mlp_second, stacked[3], RATE, DECAY)
    return (block_output, done.input_grad, *gain_new, head_gain_grads, *query_new, *keyvalue_new, *output_new, *mlp_new)


def solution(mesh):
    token = P(("dp", "tensor"), None)
    flat = P(None, "dp", "tensor")
    deep = P(None, None, "dp", "tensor")
    placed = (token, token, P("dp"), P(), P(), P(), *[flat] * 3, *[deep] * 3, *[flat] * 3, *[deep] * 3)
    outs = (token, token, P(), P(), P(), P(), *[flat] * 3, *[deep] * 3, *[flat] * 3, *[deep] * 3)
    return jax.shard_map(body, mesh=mesh, in_specs=placed, out_specs=outs, check_vma=False)
```

```python
from functools import partial
import math
from types import SimpleNamespace

import jax
import jax.numpy as jnp
from jax import lax
from jax.experimental import pallas as pl
from jax.experimental.pallas import tpu as pltpu
from jax.sharding import PartitionSpec as P

HD = 128
STEP = 10
EPSILON = 1e-06
THETA = 1000000.0
BETA_ONE = 0.9
BETA_TWO = 0.95
ADAM_EPS = 1e-08
DECAY = 0.1
RATE = 0.05
GAIN_RATE = 0.8
OUTPUT_FACTOR = math.sqrt(128)

BF16 = jnp.bfloat16
F32 = jnp.float32
MESH = pl.DeviceIdType.MESH
CHUNK = 32
VMEM_LIMIT = 62 * 1024 * 1024


class Place:
    def __init__(self, spread):
        self.spread = spread
        self.dp = lax.axis_index("dp")
        self.tensor = lax.axis_index("tensor")
        self.core = lax.rem(self.tensor, 2)
        self.y = self.tensor // 2
        self.z = self.dp // spread
        self.r = lax.rem(self.dp, spread)
        self.low = lax.rem(self.z, 2)
        self.core_id = {"dp": self.dp, "tensor": self.y * 2 + 1 - self.core}
        self.y_id = {"dp": self.dp, "tensor": (1 - self.y) * 2 + self.core}
        self.low_id = {"dp": self.dp + spread * (1 - 2 * self.low), "tensor": self.tensor}
        self.own_pair = self.low * 2 + self.y
        self.pairs = (
            (1 - self.low) * 2 + 1 - self.y,
            self.low * 2 + 1 - self.y,
            (1 - self.low) * 2 + self.y,
            self.own_pair,
        )

    def z_dp(self, step):
        return lax.rem(self.z + 4 + step, 4) * self.spread + self.r

    def z_id(self, step):
        return {"dp": self.z_dp(step), "tensor": self.tensor}

    def r_dp(self, step):
        return self.z * self.spread + lax.rem(self.r + self.spread + step, self.spread)

    def r_id(self, step):
        return {"dp": self.r_dp(step), "tensor": self.tensor}

    def greet(self):
        ids = [self.core_id, self.y_id]
        ids += [self.z_id(k) for k in range(1, 4)]
        ids += [self.r_id(k) for k in range(1, self.spread)]
        barrier = pltpu.get_barrier_semaphore()
        for one in ids:
            pl.semaphore_signal(barrier, inc=1, device_id=one, device_id_type=MESH)
        pl.semaphore_wait(barrier, len(ids))


class Links:
    def __init__(self, send, recv, local):
        self.send, self.recv, self.local = send, recv, local
        self.count = self.copies = 0

    def remote(self, src, dst, to):
        slot = self.count
        self.count += 1
        return pltpu.make_async_remote_copy(
            src_ref=src, dst_ref=dst, send_sem=self.send.at[slot], recv_sem=self.recv.at[slot],
            device_id=to, device_id_type=MESH,
        )

    def copy(self, src, dst):
        slot = self.copies
        self.copies += 1
        return pltpu.make_async_copy(src, dst, self.local.at[slot])

    def check(self):
        assert self.count <= self.send.shape[0] and self.copies <= self.local.shape[0]


def tile(start, size):
    return pl.ds(pl.multiple_of(start, size), size)


class Spread:
    def __init__(self, links, place, joined, start, rows):
        def block(pair, core):
            return joined.at[pair * 2 + core, pl.ds(start, rows)]

        c = place.core
        diag, y, z, own = place.pairs
        own, from_z, from_y, from_d = (block(p, c) for p in (own, z, y, diag))
        self.to_z = links.remote(own, own, place.low_id)
        self.to_y = links.remote(own, own, place.y_id)
        self.to_core = links.remote(own, own, place.core_id)
        self.on_y = links.remote(from_z, from_z, place.y_id)
        self.core_z = links.remote(from_z, from_z, place.core_id)
        self.core_y = links.remote(from_y, from_y, place.core_id)
        self.core_d = links.remote(from_d, from_d, place.core_id)

    def start(self):
        self.to_z.start()
        self.to_y.start()
        self.to_core.start()

    def pass_on(self):
        self.to_z.wait_recv()
        self.on_y.start()
        self.core_z.start()
        self.to_y.wait_recv()
        self.core_y.start()

    def pass_last(self):
        self.on_y.wait_recv()
        self.core_d.start()

    def ready(self):
        for one in (self.to_core, self.core_z, self.core_y, self.core_d):
            one.wait_recv()

    def drain(self):
        for one in (self.to_z, self.to_y, self.to_core, self.on_y, self.core_z, self.core_y, self.core_d):
            one.wait_send()


class Collect:
    def __init__(self, links, place, ns, start, rows):
        self.place, self.ns, self.start, self.rows = place, ns, start, rows
        here = pl.ds(start, rows)
        self.across = [
            links.remote(ns.part.at[p * 2 + 1 - place.core, here], ns.core_in.at[k, here], place.core_id)
            for k, p in enumerate(place.pairs)
        ]
        self.diag = links.remote(ns.sums.at[0, here], ns.y_in.at[0, here], place.y_id)
        self.to_y = links.remote(ns.sums.at[1, here], ns.y_in.at[1, here], place.y_id)
        self.to_z = links.remote(ns.sums.at[2, here], ns.z_in.at[here], place.low_id)

    def cross(self, *which):
        for k in which:
            self.across[k].start()

    def term(self, k, at):
        block = self.place.pairs[k] * 2 + self.place.core
        return self.ns.part[block, at, :].astype(F32) + self.ns.core_in[k, at, :].astype(F32)

    def each(self, work):
        def step(i, carry):
            work(tile(self.start + i * CHUNK, CHUNK))
            return carry

        lax.fori_loop(0, self.rows // CHUNK, step, 0)

    def add(self, k):
        def work(at):
            total = self.term(k, at)
            if k == 2:
                total = total + self.ns.y_in[0, at, :].astype(F32)
            self.ns.sums[k, at, :] = total.astype(BF16)

        self.each(work)

    def send_y(self):
        self.across[0].wait_recv()
        self.add(0)
        self.diag.start()
        self.across[1].wait_recv()
        self.add(1)
        self.to_y.start()

    def send_z(self):
        self.across[2].wait_recv()
        self.diag.wait_recv()
        self.add(2)
        self.to_z.start()

    def end(self, finish):
        self.across[3].wait_recv()
        self.to_y.wait_recv()
        self.to_z.wait_recv()

        def work(at):
            total = self.term(3, at) + self.ns.y_in[1, at, :].astype(F32) + self.ns.z_in[at, :].astype(F32)
            finish(at, total)

        self.each(work)
        for one in (*self.across, self.diag, self.to_y, self.to_z):
            one.wait_send()


class Halves:
    def __init__(self, links, place, ns, joined):
        rows = ns.part.shape[1] // 2
        self.size = rows
        self.starts = (0, rows)
        self.sums = [Collect(links, place, ns, start, rows) for start in self.starts]
        self.back = joined is not None
        if self.back:
            self.spread = [Spread(links, place, joined, start, rows) for start in self.starts]


def take(ref, pairs, start, size, columns=slice(None)):
    parts = [ref[pl.ds(p * 2, 2), start : start + size, columns] for p in pairs]
    return jnp.concatenate([one.reshape(2 * size, -1) for one in parts], axis=0)


def put(ref, pairs, start, size, value, columns=slice(None)):
    for i, p in enumerate(pairs):
        part = value[2 * i * size : 2 * (i + 1) * size]
        ref[pl.ds(p * 2, 2), start : start + size, columns] = part.reshape(2, size, -1)


class Gather:
    def __init__(self, links, place, sources, own, stage, land, save, earlier):
        rows = own.shape[1]
        self.earlier, self.own_free = earlier, False
        self.place, self.own, self.land, self.rows, self.stage = place, own, land, rows, stage
        self.starts, self.loads = [], []
        start = 0
        for one in sources:
            size = one.shape[1]
            self.starts.append((start, size // 2))
            self.loads.append(links.copy(one, stage.at[:, start : start + size]))
            start += size
        spread = place.spread

        def at(dp):
            return land.at[tile(dp * rows, rows)]

        mine = at(place.dp)
        self.out = [
            links.remote(own.at[lax.rem(place.low + k, 2)], mine, place.z_id(k)) for k in range(1, 4)
        ]
        self.side = [links.remote(own.at[place.low], mine, place.r_id(s)) for s in range(1, spread)]
        self.on = [
            [
                links.remote(at(place.z_dp(-k)), at(place.z_dp(-k)), place.r_id(s))
                for s in range(1, spread)
            ]
            for k in range(1, 4)
        ]
        self.save = links.copy(land, save)

    def load(self):
        for one in self.loads:
            one.start()

    def sent(self):
        for one in self.out + self.side:
            one.wait_send()

    def cast(self):
        for one in self.loads:
            one.wait()
        if self.earlier is not None:
            self.earlier.sent()
            self.earlier.own_free = True
        step = min(64, self.rows)

        def round_rows(i, carry):
            at = tile(i * step, step)
            for low in range(2):
                to = 0
                for start, half in self.starts:
                    piece = self.stage[at, start + low * half : start + (low + 1) * half]
                    self.own[low, at, to : to + half] = piece.astype(BF16)
                    to += half
            return carry

        lax.fori_loop(0, self.rows // step, round_rows, 0)

    def begin(self):
        for one in self.side:
            one.start()
        step = min(64, self.rows)

        def copy(i, carry):
            self.land[tile(self.place.dp * self.rows + i * step, step), :] = self.own[
                self.place.low, tile(i * step, step), :
            ]
            return carry

        lax.fori_loop(0, self.rows // step, copy, 0)

    def forward(self, k):
        self.out[k].wait_recv()
        for one in self.on[k]:
            one.start()

    def finish(self):
        for one in self.side:
            one.wait_recv()
        for group in self.on:
            for one in group:
                one.wait_recv()
        self.save.start()

    def drain(self):
        if not self.own_free:
            self.sent()
        for group in self.on:
            for one in group:
                one.wait_send()
        self.save.wait()


class Stream:
    def __init__(self, groups):
        self.groups = groups
        self.order = [one for group in groups for one in group]
        self.items = [(group, k) for group in groups for k in range(3)]
        self.sent = self.passed = 0
        self.order[0].load()

    def send(self, count=1):
        for group, k in self.items[self.sent : self.sent + count]:
            for one in group:
                if k == 0:
                    one.cast()
                    at = self.order.index(one) + 1
                    if at < len(self.order):
                        self.order[at].load()
                    one.begin()
                one.out[k].start()
            self.sent += 1

    def forward(self, count=1):
        for group, k in self.items[self.passed : min(self.passed + count, self.sent)]:
            for one in group:
                one.forward(k)
            self.passed += 1

    def tick(self, lag=1):
        self.send()
        if self.passed + lag < self.sent or self.sent == len(self.items):
            self.forward()

    def need(self, one):
        place = [i for i, group in enumerate(self.groups) if one in group][0] * 3 + 3
        self.send(max(0, place - self.sent))
        self.forward(max(0, place - self.passed))
        one.finish()

    def rest(self):
        self.send(len(self.items))
        self.forward(len(self.items))


def scale_of(v):
    return lax.rsqrt(jnp.mean(v * v, axis=-1, keepdims=True) + EPSILON)


def mm(a, b):
    return jnp.dot(a, b, preferred_element_type=F32)


def mm_nt(a, b):
    return lax.dot_general(a, b, (((1,), (1,)), ((), ())), preferred_element_type=F32)


def project_heads(ns, pair):
    block = ns.joined.shape[1]
    two = pl.ds(pair * 2, 2)
    x = ns.joined[two].reshape(2 * block, -1)
    raw = mm(x, ns.layer.wqkv[...])
    ns.raw[two] = raw.reshape(2, block, -1)
    cosine, sine = ns.cosine[two].reshape(2 * block, HD), ns.sine[two].reshape(2 * block, HD)
    q_size, kv_size = ns.q.shape[2], ns.k.shape[2]

    def heads(out, start, size, gain):
        for h in range(size // HD):
            v = raw[:, start + h * HD : start + (h + 1) * HD]
            v = v * scale_of(v) * gain[...]
            turned = v * cosine + pltpu.roll(v, HD // 2, axis=1) * sine
            out[two, :, h * HD : (h + 1) * HD] = turned.astype(BF16).reshape(2, block, HD)

    heads(ns.q, 0, q_size, ns.layer.gain_q)
    heads(ns.k, q_size, kv_size, ns.layer.gain_k)
    ns.v[two] = raw[:, q_size + kv_size :].astype(BF16).reshape(2, block, kv_size)


def softmax(ns, b, half, span, query, keys):
    seen = keys.shape[0]
    s = mm_nt(query, keys) * HD**-0.5
    s = s + ns.bias[b, half * span : (half + 1) * span, :seen].astype(F32)
    p = jnp.exp(s - jnp.max(s, axis=-1, keepdims=True))
    return p * (1.0 / jnp.sum(p, axis=-1, keepdims=True))


def attend(ns, b):
    block = ns.joined.shape[1]
    span = 2 * block
    q_heads = ns.q.shape[2] // HD
    share = q_heads // (ns.k.shape[2] // HD)
    for e in range(q_heads):
        kv = slice((e // share) * HD, (e // share + 1) * HD)
        mine = slice(e * HD, (e + 1) * HD)
        for half in range(2):
            rows = slice(4 * b + 2 * half, 4 * b + 2 * half + 2)
            seen = slice(4 * b, 4 * b + 2 * half + 2)
            keys = ns.k[seen, :, kv].reshape(-1, HD)
            values = ns.v[seen, :, kv].reshape(-1, HD)
            query = ns.q[rows, :, mine].reshape(span, HD)
            p = softmax(ns, b, half, span, query, keys)
            ns.att[rows, :, mine] = mm(p.astype(BF16), values).astype(BF16).reshape(2, block, HD)


def project_out(ns, source, weight, pairs, start, size, width=1024):
    x = take(source, pairs, start, size)

    def step(j, carry):
        at = tile(j * width, width)
        put(ns.part, pairs, start, size, mm_nt(x, weight[at, :]).astype(BF16), at)
        return carry

    lax.fori_loop(0, ns.part.shape[2] // width, step, 0)


def gate_up(ns, pairs, start, size, slot):
    ff = ns.product.shape[2]
    x = take(ns.joined, pairs, start, size)
    gate = mm(x, ns.layer.wgate[...])
    up = mm(x, ns.layer.wup[...])
    ns.gu_stage[slot, :, :, :ff] = gate.astype(BF16).reshape(4, size, ff)
    ns.gu_stage[slot, :, :, ff:] = up.astype(BF16).reshape(4, size, ff)
    put(ns.product, pairs, start, size, (gate / (1.0 + jnp.exp(-gate)) * up).astype(BF16))


def forward_kernel(layers, spread, ns):
    place = Place(spread)
    links = Links(ns.send, ns.recv, ns.local)
    local = ns.tokens.shape[0]
    mine = place.own_pair * 2 + place.core
    diag, y, z, own = place.pairs
    first_pairs, last_pairs = (diag, y), (z, own)

    def gathers_of(layer, before):
        kv = ns.keyvalue_weight.at[layer]
        mlp = ns.mlp_weight.at[layer]
        attention = [(ns.query_weight.at[layer], kv.at[0], kv.at[1]), (ns.output_weight.at[layer],)]
        sources = attention + [(mlp.at[i],) for i in range(3)]
        owns = (ns.own_qkv, ns.own_o, ns.own_gate, ns.own_up, ns.own_down)
        lands = (ns.wqkv, ns.wo, ns.wgate, ns.wup, ns.wdown)
        saves = (ns.save_wqkv, ns.save_wo, ns.save_wgate, ns.save_wup, ns.save_wdown)
        return [
            Gather(links, place, source, own_ref, ns.stage, land[layer], save[layer], earlier)
            for source, own_ref, land, save, earlier in zip(sources, owns, lands, saves, before)
        ]

    gathers = []
    for layer in range(layers):
        gathers.append(gathers_of(layer, gathers[-1] if gathers else [None] * 5))
    groups = [[one] for one in gathers[0]]
    for later in gathers[1:]:
        groups += [later[:2], *[[one] for one in later[2:]]]
    stream = Stream(groups)
    tick = stream.tick
    tokens_in = Spread(links, place, ns.joined, 0, local)
    grads_in = Spread(links, place, ns.joined_grad, 0, local)
    middle = Halves(links, place, ns, ns.joined)
    end = Halves(links, place, ns, ns.joined)
    size = middle.size
    rows_save = [links.copy(ns.joined, one) for one in ns.save_a]

    def norm(i, carry):
        at = tile(i * CHUNK, CHUNK)
        v = ns.tokens[at, :].astype(F32)
        ns.hidden[at, :] = v
        ns.joined[mine, at, :] = (v * scale_of(v) * ns.gain_attn[:1, :]).astype(BF16)
        return carry

    lax.fori_loop(0, local // CHUNK, norm, 0)
    place.greet()
    tokens_in.start()
    stream.send(3)
    tokens_in.pass_on()
    stream.send()
    stream.forward()
    stream.send()
    stream.forward()
    stream.send()
    stream.forward()
    tokens_in.pass_last()
    tick()
    tick()
    tokens_in.ready()
    tokens_in.drain()
    for layer in range(layers):
        first, last = layer == 0, layer + 1 == layers
        qkv, o, gate, up, down = gathers[layer]
        kept = [
            links.copy(src, dst[layer])
            for src, dst in (
                (ns.raw, ns.save_raw), (ns.q, ns.save_q), (ns.k, ns.save_k), (ns.v, ns.save_v),
                (ns.att, ns.save_att), (ns.product, ns.save_product), (ns.mid, ns.save_mid),
                (ns.hidden, ns.save_hidden),
            )
        ]
        kept_raw, kept_q, kept_k, kept_v, kept_att, kept_product, kept_mid, kept_hidden = kept
        ns.layer = SimpleNamespace(
            wqkv=ns.wqkv[layer], gain_q=ns.gain_q.at[pl.ds(layer, 1)], gain_k=ns.gain_k.at[pl.ds(layer, 1)],
            wgate=ns.wgate[layer], wup=ns.wup[layer],
        )
        save_a = rows_save[layer]
        save_a.start()
        kept_hidden.start()
        if last:
            ns.joined_grad[mine] = ns.cotangent[...]
            grads_in.start()
        stream.need(qkv)

        def every(i, carry):
            project_heads(ns, i)
            return carry

        lax.fori_loop(0, 2, every, 0)
        tick()
        lax.fori_loop(2, 4, every, 0)
        for one in (kept_raw, kept_q, kept_k, kept_v):
            one.start()
        if last:
            grads_in.pass_on()
        tick()
        attend(ns, 0)
        tick()
        attend(ns, 1)
        kept_att.start()
        tick()
        stream.need(o)
        if last:
            grads_in.pass_last()

        def middle_rows(at, total):
            v = ns.hidden[at, :] + total
            ns.mid[at, :] = v
            gain = ns.gain_mlp[layer : layer + 1, :]
            ns.joined[mine, at, :] = (v * scale_of(v) * gain).astype(BF16)

        def result_rows(at, total):
            v = ns.mid[at, :] + total
            ns.hidden[at, :] = v
            if not last:
                gain = ns.gain_attn[layer + 1 : layer + 2, :]
                ns.joined[mine, at, :] = (v * scale_of(v) * gain).astype(BF16)

        def part_of(source, weight, halves, h):
            start = halves.starts[h]
            project_out(ns, source, weight, first_pairs, start, size)
            halves.sums[h].cross(0, 1)
            project_out(ns, source, weight, last_pairs, start, size)
            halves.sums[h].cross(2, 3)

        save_a.wait()
        part_of(ns.att, ns.wo[layer], middle, 0)
        middle.sums[0].send_y()
        part_of(ns.att, ns.wo[layer], middle, 1)
        middle.sums[1].send_y()
        tick()
        middle.sums[0].send_z()
        middle.sums[1].send_z()
        tick()
        middle.sums[0].end(middle_rows)
        middle.spread[0].start()
        middle.sums[1].end(middle_rows)
        middle.spread[1].start()
        kept_mid.start()
        tick()
        middle.spread[0].pass_on()
        middle.spread[1].pass_on()
        tick()
        stream.need(gate)
        stream.need(up)
        middle.spread[0].pass_last()
        middle.spread[0].ready()
        middle.spread[0].drain()
        saves = []

        def gate_up_of(pairs, start):
            slot = (len(saves) // 2) % 2
            if len(saves) >= 4:
                for save in saves[-4:-2]:
                    save.wait()
            gate_up(ns, pairs, start, size, slot)
            for i, p in enumerate(pairs):
                save = links.copy(
                    ns.gu_stage.at[slot, 2 * i : 2 * i + 2],
                    ns.save_gateup[layer].at[pl.ds(p * 2, 2), pl.ds(start, size)],
                )
                save.start()
                saves.append(save)

        save_b = [
            links.copy(ns.joined.at[:, pl.ds(start, size)], ns.save_b[layer].at[:, pl.ds(start, size)])
            for start in middle.starts
        ]
        save_b[0].start()
        gate_up_of(first_pairs, 0)
        tick()
        middle.spread[1].pass_last()
        gate_up_of(last_pairs, 0)
        stream.need(down)
        save_b[0].wait()
        kept_hidden.wait()
        part_of(ns.product, ns.wdown[layer], end, 0)
        middle.spread[1].ready()
        middle.spread[1].drain()
        end.sums[0].send_y()
        save_b[1].start()
        gate_up_of(first_pairs, size)
        end.sums[0].send_z()
        tick()
        gate_up_of(last_pairs, size)
        kept_product.start()
        save_b[1].wait()
        part_of(ns.product, ns.wdown[layer], end, 1)
        end.sums[1].send_y()
        end.sums[0].end(result_rows)
        if not last:
            end.spread[0].start()
        tick()
        end.sums[1].send_z()
        if not last:
            end.spread[0].pass_on()
        tick()
        end.sums[1].end(result_rows)
        if not last:
            end.spread[1].start()
            tick()
            end.spread[0].pass_last()
            end.spread[1].pass_on()
            tick()
            end.spread[1].pass_last()
            for one in end.spread:
                one.ready()
                one.drain()
        for one in (*saves[-4:], kept_raw, kept_q, kept_k, kept_v, kept_att, kept_product, kept_mid):
            one.wait()
    result = links.copy(ns.hidden, ns.out)
    result.start()
    grads_in.ready()
    grads_in.drain()
    final = links.copy(ns.joined_grad, ns.save_grad)
    final.start()
    for group in gathers:
        for one in group:
            one.drain()
    result.wait()
    final.wait()
    assert stream.passed == len(stream.items)
    links.check()


def call(kernel, ins, outs, scratch, collective_id, name):
    groups = [ins, outs, scratch]
    sizes = [len(v) if isinstance(v, list) else 0 for group in groups for v in group.values()]
    names = [key for group in groups for key in group]

    def flat(group):
        return [one for v in group.values() for one in (v if isinstance(v, list) else [v])]

    def named(values, keys, counts):
        values = list(values)
        taken = {}
        for key, count in zip(keys, counts):
            taken[key] = [values.pop(0) for _ in range(count)] if count else values.pop(0)
        return SimpleNamespace(**taken)

    def run(*refs):
        kernel(named(refs, names, sizes))

    def space(in_vmem):
        return pl.BlockSpec(memory_space=pltpu.VMEM if in_vmem else pl.ANY)

    results = pl.pallas_call(
        run,
        out_shape=[jax.ShapeDtypeStruct(shape, dtype) for shape, dtype, _ in flat(outs)],
        in_specs=[space(v) for _, v in flat(ins)],
        out_specs=[space(v) for _, _, v in flat(outs)],
        scratch_shapes=flat(scratch),
        compiler_params=pltpu.CompilerParams(
            collective_id=collective_id, has_side_effects=True, vmem_limit_bytes=VMEM_LIMIT
        ),
        cost_estimate=pl.CostEstimate(
            flops=26 * 10**9, bytes_accessed=10**8, transcendentals=10**6
        ),
        name=name,
    )(*[array for array, _ in flat(ins)])
    return named(results, outs, sizes[len(ins) : len(ins) + len(outs)])


def exchange_scratch(rows, width):
    return dict(
        joined=pltpu.VMEM((8, rows, width), BF16),
        part=pltpu.VMEM((8, rows, width), BF16),
        core_in=pltpu.VMEM((4, rows, width), BF16),
        y_in=pltpu.VMEM((2, rows, width), BF16),
        z_in=pltpu.VMEM((rows, width), BF16),
        sums=pltpu.VMEM((3, rows, width), BF16),
    )


def forward(tokens, cotangent, masters, tables, gains, spread):
    rows, width = tokens.shape
    query, keyvalue, output, mlp = masters
    layers = gains.shape[0]
    own = query.shape[1]
    d_rows = own * 4 * spread
    o, ff = query.shape[2] // 2, mlp.shape[3] // 2
    kv = keyvalue.shape[3] // 2
    qkv = o + 2 * kv
    cosine, sine, bias = tables
    ins = dict(
        tokens=(tokens, True), cotangent=(cotangent, True),
        query_weight=(query, False), keyvalue_weight=(keyvalue, False),
        output_weight=(output, False), mlp_weight=(mlp, False),
        gain_attn=(gains[:, :width], True), gain_mlp=(gains[:, width : 2 * width], True),
        gain_q=(gains[:, 2 * width : 2 * width + HD], True), gain_k=(gains[:, 2 * width + HD :], True),
        cosine=(cosine, True), sine=(sine, True), bias=(bias, True),
    )

    def each(dtype, *shape):
        return [(shape, dtype, False)] * layers

    outs = dict(
        out=((rows, width), F32, False),
        save_hidden=each(F32, rows, width), save_mid=each(F32, rows, width),
        save_raw=each(F32, 8, rows, qkv), save_q=each(BF16, 8, rows, o),
        save_k=each(BF16, 8, rows, kv), save_v=each(BF16, 8, rows, kv),
        save_att=each(BF16, 8, rows, o), save_product=each(BF16, 8, rows, ff),
        save_gateup=each(BF16, 8, rows, 2 * ff),
        save_a=each(BF16, 8, rows, width), save_b=each(BF16, 8, rows, width),
        save_grad=((8, rows, width), BF16, False),
        save_wqkv=each(BF16, d_rows, qkv), save_wo=each(BF16, d_rows, o),
        save_wgate=each(BF16, d_rows, ff), save_wup=each(BF16, d_rows, ff), save_wdown=each(BF16, d_rows, ff),
    )
    scratch = exchange_scratch(rows, width)
    weight = lambda size: [pltpu.VMEM((d_rows, size), BF16)] * layers
    mine = lambda size: pltpu.VMEM((2, own, size), BF16)
    tokens_of = lambda size, dtype=BF16: pltpu.VMEM((8, rows, size), dtype)
    scratch.update(
        hidden=pltpu.VMEM((rows, width), F32), mid=pltpu.VMEM((rows, width), F32),
        joined_grad=tokens_of(width), gu_stage=pltpu.VMEM((2, 4, rows // 2, 2 * ff), BF16),
        stage=pltpu.VMEM((own, max(2 * ff, 2 * qkv)), F32),
        raw=tokens_of(qkv, F32), q=tokens_of(o), k=tokens_of(kv), v=tokens_of(kv), att=tokens_of(o),
        product=tokens_of(ff),
        wqkv=weight(qkv), wo=weight(o), wgate=weight(ff), wup=weight(ff), wdown=weight(ff),
        own_qkv=mine(qkv), own_o=mine(o), own_gate=mine(ff), own_up=mine(ff), own_down=mine(ff),
        local=pltpu.SemaphoreType.DMA((4 + 36 * layers,)),
    )
    count = 72 + 20 * spread * layers
    scratch.update(send=pltpu.SemaphoreType.DMA((count,)), recv=pltpu.SemaphoreType.DMA((count,)))
    return call(partial(forward_kernel, layers, spread), ins, outs, scratch, 1, "forward")


def mm_tn(a, b):
    return lax.dot_general(a, b, (((0,), (0,)), ((), ())), preferred_element_type=F32)


class Reduce:
    def __init__(self, links, place, blocks, x_in, z_in, outs):
        self.place, self.blocks, self.x_in, self.z_in, self.outs = place, blocks, x_in, z_in, outs
        spread = place.spread
        rows = blocks.shape[1] // spread
        self.rows = rows

        def block(q, r):
            return blocks.at[q, tile(r * rows, rows)]

        self.x_out = [
            [
                links.remote(
                    block(q, lax.rem(place.r + s, spread)), x_in.at[s - 1, q], place.r_id(s)
                )
                for s in range(1, spread)
            ]
            for q in range(4)
        ]
        self.z_out = [
            links.remote(block(q, place.r), z_in.at[q - 1], place.z_id(q)) for q in range(1, 4)
        ]

    def compute(self, q, left, right):
        part = self.blocks.shape[1]
        step = min(256, part)
        start = lax.rem(self.place.z + q, 4) * part

        def one(i, carry):
            x = left[:, :, tile(start + i * step, step)]
            product = mm_tn(x.reshape(-1, step), right())
            self.blocks[q, tile(i * step, step), :] = product.astype(BF16)
            return carry

        lax.fori_loop(0, part // step, one, 0)

    def send(self, q):
        for one in self.x_out[q]:
            one.start()

    def pass_on(self, q):
        for one in self.x_out[q]:
            one.wait_recv()
        step = min(64, self.rows)
        start = self.place.r * self.rows

        def add(i, carry):
            at = tile(start + i * step, step)
            if self.place.spread == 2:
                self.blocks[q, at, :] += self.x_in[0, q, tile(i * step, step), :]
                return carry
            total = self.blocks[q, at, :].astype(F32)
            for s in range(self.place.spread - 1):
                total = total + self.x_in[s, q, tile(i * step, step), :].astype(F32)
            self.blocks[q, at, :] = total.astype(BF16)
            return carry

        lax.fori_loop(0, self.rows // step, add, 0)
        if q:
            self.z_out[q - 1].start()

    def finish(self):
        for one in self.z_out:
            one.wait_recv()
        step = min(64, self.rows)
        low = self.place.low
        start = self.place.r * self.rows

        def add(i, carry):
            at = tile(i * step, step)
            near = self.blocks[0, tile(start + i * step, step), :] + self.z_in[1, at, :]
            far = self.z_in[0, at, :] + self.z_in[2, at, :]
            first = 0
            for out, size in self.outs:
                out[at, tile(low * size, size)] = near[:, first : first + size]
                out[at, tile((1 - low) * size, size)] = far[:, first : first + size]
                first += size
            return carry

        lax.fori_loop(0, self.rows // step, add, 0)

    def drain(self):
        for group in self.x_out:
            for one in group:
                one.wait_send()
        for one in self.z_out:
            one.wait_send()


ORDER = (2, 1, 3, 0)


def gate_up_back(ns, pairs, start, size, slot):
    ff = ns.product.shape[2]
    d_act = mm(take(ns.joined, pairs, start, size), ns.wdown[...])
    gate = ns.stage[slot, :, :, :ff].reshape(4 * size, ff).astype(F32)
    up = ns.stage[slot, :, :, ff:].reshape(4 * size, ff).astype(F32)
    gated = 1.0 / (1.0 + jnp.exp(-gate))
    put(ns.d_gate, pairs, start, size, (d_act * up * gated * (1.0 + gate * (1.0 - gated))).astype(BF16))
    put(ns.d_up, pairs, start, size, (d_act * gate * gated).astype(BF16))


def head_back(ns, blocks, d_out, raw_columns, gain, d_gain):
    rows = d_out.shape[0]
    cosine, sine = ns.cosine[blocks].reshape(rows, HD), ns.sine[blocks].reshape(rows, HD)
    raw = ns.raw[blocks, :, raw_columns].reshape(rows, HD)
    d_turned = d_out * cosine + pltpu.roll(d_out * sine, HD // 2, axis=1)
    scale = scale_of(raw)
    normed = raw * scale
    d_gain[...] += jnp.sum(d_turned * normed, axis=0, keepdims=True)
    d_normed = d_turned * gain[...]
    inner = jnp.mean(d_normed * normed, axis=-1, keepdims=True)
    d_raw = (scale * (d_normed - normed * inner)).astype(BF16)
    ns.d_raw[blocks, :, raw_columns] = d_raw.reshape(-1, ns.raw.shape[1], HD)


def attend_back(ns, b):
    block = ns.joined.shape[1]
    span = 2 * block
    q_size, kv_size = ns.q.shape[2], ns.k.shape[2]
    share = q_size // kv_size
    scale = HD**-0.5
    whole = slice(4 * b, 4 * b + 4)
    for kv in range(kv_size // HD):
        columns = slice(kv * HD, (kv + 1) * HD)
        ns.d_keys[...] = jnp.zeros_like(ns.d_keys)
        ns.d_values[...] = jnp.zeros_like(ns.d_values)
        for e in range(kv * share, (kv + 1) * share):
            mine = slice(e * HD, (e + 1) * HD)
            for half in range(2):
                rows = slice(4 * b + 2 * half, 4 * b + 2 * half + 2)
                some = slice(4 * b, 4 * b + 2 * half + 2)
                seen = (half + 1) * span
                keys = ns.k[some, :, columns].reshape(seen, HD)
                values = ns.v[some, :, columns].reshape(seen, HD)
                query = ns.q[rows, :, mine].reshape(span, HD)
                d_out = ns.d_att[rows, :, mine].reshape(span, HD)
                p = softmax(ns, b, half, span, query, keys)
                d_p = mm_nt(d_out, values)
                delta = jnp.sum(d_p * p, axis=-1, keepdims=True)
                d_s = (p * (d_p - delta)).astype(BF16)
                ns.d_values[:seen, :] += mm_tn(p.astype(BF16), d_out)
                ns.d_keys[:seen, :] += mm_tn(d_s, query)
                head_back(ns, rows, mm(d_s, keys) * scale, mine, ns.gain_q, ns.d_gain_q)
        key_columns = slice(q_size + kv * HD, q_size + (kv + 1) * HD)
        head_back(ns, whole, ns.d_keys[...] * scale, key_columns, ns.gain_k, ns.d_gain_k)
        value_columns = slice(q_size + kv_size + kv * HD, q_size + kv_size + (kv + 1) * HD)
        ns.d_raw[whole, :, value_columns] = ns.d_values[...].astype(BF16).reshape(4, block, HD)


class GainSum:
    def __init__(self, links, place, terms, came, came_r, total):
        spread = place.spread
        self.place, self.terms, self.came, self.came_r, self.total = place, terms, came, came_r, total
        ids = (place.core_id, place.y_id, place.low_id, place.z_id(2))
        self.pairs = [links.remote(terms.at[i], came.at[i], one) for i, one in enumerate(ids)]
        self.sides = [
            links.remote(terms.at[4], came_r.at[place.r], place.r_id(s)) for s in range(1, spread)
        ]
        self.at = 0

    def start(self):
        self.pairs[0].start()

    def step(self):
        i = self.at
        self.at += 1
        if i < 4:
            self.pairs[i].wait_recv()
            self.terms[i + 1] = self.terms[i] + self.came[i]
            if i < 3:
                self.pairs[i + 1].start()
                return
            self.came_r[self.place.r] = self.terms[4]
            for one in self.sides:
                one.start()
            return
        for one in self.sides:
            one.wait_recv()
        total = self.came_r[0]
        for r in range(1, self.place.spread):
            total = total + self.came_r[r]
        self.total[...] = total
        for one in self.pairs + self.sides:
            one.wait_send()


def backward_kernel(layers, spread, ns):
    place = Place(spread)
    links = Links(ns.send, ns.recv, ns.local)
    local, width = ns.out.shape
    mine = place.own_pair * 2 + place.core
    qkv, o, ff = ns.wqkv_in[0].shape[1], ns.wo_in[0].shape[1], ns.wdown_in[0].shape[1]
    kv = (qkv - o) // 2
    rows_all = ns.wdown_in[0].shape[0]
    group = ns.bias_in.shape[1]
    diag, y, z, own = place.pairs
    first_pairs, last_pairs = (diag, y), (z, own)

    def loads(*pairs):
        copies = [links.copy(src, dst) for src, dst in pairs]
        for one in copies:
            one.start()
        return copies

    def wait(copies):
        for one in copies:
            one.wait()

    def reduce(i, outs):
        return Reduce(links, place, ns.blocks.at[i], ns.x_in.at[i], ns.z_in_w.at[i], outs)

    red_down = reduce(0, [(ns.g_mlp.at[2], ff)])
    red_gate = reduce(1, [(ns.g_mlp.at[0], ff)])
    red_up = reduce(2, [(ns.g_mlp.at[1], ff)])
    red_o = Reduce(links, place, ns.blocks_o, ns.x_in_o, ns.z_in_o, [(ns.g_o, o)])
    red_qkv = Reduce(
        links, place, ns.blocks_qkv, ns.x_in_qkv, ns.z_in_qkv,
        [(ns.g_q, o), (ns.g_kv.at[0], kv), (ns.g_kv.at[1], kv)],
    )
    reduces = (red_down, red_gate, red_up, red_o, red_qkv)
    middle = Halves(links, place, ns, ns.joined)
    end = Halves(links, place, ns, ns.joined)
    size = middle.size
    gain_sum = GainSum(links, place, ns.terms, ns.came, ns.came_r, ns.gain_total)
    passes = []
    going = [False]

    def pass_next(count=1):
        for _ in range(count):
            passes.pop(0)()

    def compute_all(one, left, right, send=True):
        if going[0]:
            one.drain()
        for q in ORDER:
            one.compute(q, left, right)
            if send:
                one.send(q)

    def keep(layer):
        pairs = ((ns.g_q, ns.save_q), (ns.g_kv, ns.save_kv), (ns.g_o, ns.save_o), (ns.g_mlp, ns.save_mlp))
        return [links.copy(one, to.at[layer]) for one, to in pairs]

    for one in (*ns.d_attn, *ns.d_mlp, *ns.d_q, *ns.d_k):
        one[...] = jnp.zeros_like(one)
    first_rows = loads((ns.joined_in, ns.joined))
    place.greet()
    wait(first_rows)
    for layer in reversed(range(layers)):
        backward_layer(layer, layers, SimpleNamespace(**locals()))
    result = loads((ns.out, ns.input_grad))
    ns.terms[0] = jnp.zeros_like(ns.terms[0])
    for i in range(layers):
        ns.terms[0, 2 * i : 2 * i + 1, :width] = ns.d_attn[i][...]
        ns.terms[0, 2 * i + 1 : 2 * i + 2, :width] = ns.d_mlp[i][...]
        ns.terms[0, 2 * i : 2 * i + 1, width : width + HD] = ns.d_q[i][...]
        ns.terms[0, 2 * i : 2 * i + 1, width + HD : width + 2 * HD] = ns.d_k[i][...]
    gain_sum.start()
    for _ in range(4):
        pass_next()
        gain_sum.step()
    red_gate.finish()
    gain_sum.step()
    red_up.finish()
    red_o.finish()
    red_qkv.finish()
    for one in reduces:
        one.drain()
    last = keep(0)
    for one in last:
        one.start()
    wait(last)
    wait(result)
    assert not passes
    links.check()


def backward_layer(layer, layers, env):
    ns, place, links, loads, wait, local, width = (
        env.ns, env.place, env.links, env.loads, env.wait, env.local, env.width
    )
    middle, end, size, mine, passes, pass_next = env.middle, env.end, env.size, env.mine, env.passes, env.pass_next
    red_down, red_gate, red_up, red_o, red_qkv = env.reduces
    first_pairs, last_pairs, compute_all = env.first_pairs, env.last_pairs, env.compute_all
    first, started = layer == 0, layer + 1 < layers
    passes += [partial(one.pass_on, q) for one in env.reduces for q in ORDER]
    ns.gain_q, ns.gain_k = ns.gains_q.at[pl.ds(layer, 1)], ns.gains_k.at[pl.ds(layer, 1)]
    ns.d_gain_q, ns.d_gain_k = ns.d_q[layer], ns.d_k[layer]
    gain_mlp, gain_attn = ns.gains_mlp.at[pl.ds(layer, 1)], ns.gains_attn.at[pl.ds(layer, 1)]
    ff, qkv, o, rows_all, group = env.ff, env.qkv, env.o, env.rows_all, env.group
    kept = env.keep(layer + 1) if started else []

    def finish_later():
        if started:
            for one in (red_up, red_o, red_qkv):
                one.finish()
            for one in kept:
                one.start()
            for k in range(1, 4):
                pl.semaphore_signal(ns.credit, inc=1, device_id=place.z_id(k), device_id_type=MESH)

    def back_norm(value, grad, gain, d_gain, out, gather):
        def finish(at, total):
            v = value[at, :].astype(F32)
            scale = scale_of(v)
            normed = v * scale
            d_gain[...] += jnp.sum(total * normed, axis=0, keepdims=True)
            d_normed = total * gain[...]
            inner = jnp.mean(d_normed * normed, axis=-1, keepdims=True)
            g = grad[at, :].astype(F32) + scale * (d_normed - normed * inner)
            out[at, :] = g
            if gather:
                ns.joined[mine, at, :] = g.astype(BF16)

        return finish

    flat = lambda ref: lambda: ref[...].reshape(8 * local, -1)

    def mlp_scope(wgate, wup, d_gate, d_up):
        ns.d_gate, ns.d_up = d_gate, d_up
        weight_loads = loads((ns.wgate_in[layer], wgate), (ns.wup_in[layer], wup))

        def part_of(h, columns=1024):
            start = middle.starts[h]
            for which, pairs in ((0, first_pairs), (2, last_pairs)):
                gates, ups = take(d_gate, pairs, start, size), take(d_up, pairs, start, size)

                def step(j, carry):
                    at = tile(j * columns, columns)
                    term = mm_nt(gates, wgate[at, :]) + mm_nt(ups, wup[at, :])
                    put(ns.part, pairs, start, size, term.astype(BF16), at)
                    return carry

                lax.fori_loop(0, width // columns, step, 0)
                middle.sums[h].cross(which, which + 1)

        def down_scope(wdown, product, stage):
            ns.wdown, ns.product, ns.stage = wdown, product, stage
            first_loads = loads((ns.product_in[layer], product))
            down_load = loads((ns.wdown_in[layer], wdown))
            chunks = [(start, pairs) for start in middle.starts for pairs in (first_pairs, last_pairs)]
            gateup_loads = [
                [
                    links.copy(
                        ns.gateup_in[layer].at[pl.ds(p * 2, 2), pl.ds(start, size)], stage.at[i % 2, 2 * j : 2 * j + 2]
                    )
                    for j, p in enumerate(pairs)
                ]
                for i, (start, pairs) in enumerate(chunks)
            ]
            for group in gateup_loads[:2]:
                for one in group:
                    one.start()
            wait(first_loads)
            compute_all(red_down, ns.joined, flat(product))
            wait(down_load)
            for i, (start, pairs) in enumerate(chunks):
                wait(gateup_loads[i])
                gate_up_back(ns, pairs, start, size, i % 2)
                if i < 2:
                    for one in gateup_loads[i + 2]:
                        one.start()
                if i == 1:
                    wait(weight_loads)
                    part_of(0)
                if i == 2:
                    middle.sums[0].send_y()
            finish_later()

        pl.run_scoped(
            down_scope,
            pltpu.VMEM((rows_all, ff), BF16),
            pltpu.VMEM((8, local, ff), BF16),
            pltpu.VMEM((2, 4, size, 2 * ff), BF16),
        )

        def rest_scope(b, mid, grad=None):
            b_load = loads((ns.mid_in[layer], mid), (ns.b_in[layer], b))
            if grad is None:
                grad = ns.out
            else:
                b_load += loads((ns.grad_in, grad))
            middle_rows = back_norm(mid, grad, gain_mlp, ns.d_mlp[layer], ns.grad_mid, True)
            part_of(1)
            middle.sums[0].send_z()
            middle.sums[1].send_y()
            wait(b_load)
            compute_all(red_gate, b, flat(d_gate))
            middle.sums[0].end(middle_rows)
            middle.spread[0].start()
            middle.sums[1].send_z()
            if started:
                pl.semaphore_wait(ns.credit, 3)
            pass_next()
            compute_all(red_up, b, flat(d_up), send=False)
            middle.sums[1].end(middle_rows)
            middle.spread[1].start()
            pass_next()

        pl.run_scoped(
            rest_scope,
            pltpu.VMEM((8, local, width), BF16),
            pltpu.VMEM((local, width), F32),
            *([] if started else [pltpu.VMEM((local, width), ns.grad_in.dtype)]),
        )

    pl.run_scoped(
        mlp_scope,
        pltpu.VMEM((rows_all, ff), BF16),
        pltpu.VMEM((rows_all, ff), BF16),
        pltpu.VMEM((8, local, ff), BF16),
        pltpu.VMEM((8, local, ff), BF16),
    )

    def attention_scope(
        cosine, sine, bias, hidden, wqkv, wo, a, q, k, v, raw, att, d_att, d_raw, d_keys, d_values
    ):
        ns.cosine, ns.sine, ns.bias, ns.hidden = cosine, sine, bias, hidden
        ns.q, ns.k, ns.v, ns.raw, ns.att = q, k, v, raw, att
        ns.d_att, ns.d_raw, ns.d_keys, ns.d_values = d_att, d_raw, d_keys, d_values
        o_loads = loads((ns.wo_in[layer], wo), (ns.att_in[layer], att))
        other_loads = loads(
            (ns.q_in[layer], q), (ns.k_in[layer], k), (ns.v_in[layer], v), (ns.raw_in[layer], raw),
            (ns.cosine_in, cosine), (ns.sine_in, sine), (ns.bias_in, bias), (ns.a_in[layer], a),
            (ns.wqkv_in[layer], wqkv), (ns.hidden_in[layer], hidden),
        )
        result_rows = back_norm(hidden, ns.grad_mid, gain_attn, ns.d_attn[layer], ns.out, not first)

        def d_attended(h):
            start = middle.starts[h]
            middle.spread[h].ready()
            middle.spread[h].drain()
            for pairs in (first_pairs, last_pairs):
                put(d_att, pairs, start, size, mm(take(ns.joined, pairs, start, size), wo[...]).astype(BF16))

        def part_of(h):
            start = end.starts[h]
            project_out(ns, d_raw, wqkv, first_pairs, start, size)
            end.sums[h].cross(0, 1)
            project_out(ns, d_raw, wqkv, last_pairs, start, size)
            end.sums[h].cross(2, 3)

        middle.spread[0].pass_on()
        middle.spread[1].pass_on()
        pass_next()
        wait(o_loads)
        middle.spread[0].pass_last()
        d_attended(0)
        pass_next()
        middle.spread[1].pass_last()
        d_attended(1)
        for q_part in ORDER:
            red_up.send(q_part)
        compute_all(red_o, ns.joined, flat(att))
        pass_next(2)
        wait(other_loads)
        attend_back(ns, 0)
        pass_next(2)
        attend_back(ns, 1)
        pass_next(2)
        part_of(0)
        end.sums[0].send_y()
        part_of(1)
        end.sums[1].send_y()
        compute_all(red_qkv, a, flat(d_raw))
        end.sums[0].send_z()
        end.sums[1].send_z()
        pass_next(2)
        end.sums[0].end(result_rows)
        if not first:
            end.spread[0].start()
        pass_next(4)
        end.sums[1].end(result_rows)
        if not first:
            end.spread[1].start()
        wait(kept)
        red_down.finish()

    pl.run_scoped(
        attention_scope,
        pltpu.VMEM(ns.cosine_in.shape, F32),
        pltpu.VMEM(ns.sine_in.shape, F32),
        pltpu.VMEM(ns.bias_in.shape, BF16),
        pltpu.VMEM(ns.hidden_in[layer].shape, F32),
        pltpu.VMEM((rows_all, qkv), BF16),
        pltpu.VMEM((rows_all, o), BF16),
        pltpu.VMEM((8, local, width), BF16),
        pltpu.VMEM(ns.q_in[layer].shape, BF16),
        pltpu.VMEM(ns.k_in[layer].shape, BF16),
        pltpu.VMEM(ns.v_in[layer].shape, BF16),
        pltpu.VMEM(ns.raw_in[layer].shape, F32),
        pltpu.VMEM(ns.att_in[layer].shape, BF16),
        pltpu.VMEM((8, local, o), BF16),
        pltpu.VMEM((8, local, qkv), BF16),
        pltpu.VMEM((group, HD), F32),
        pltpu.VMEM((group, HD), F32),
    )
    if not first:
        pass_next()
        end.spread[0].pass_on()
        end.spread[1].pass_on()
        pass_next(2)
        end.spread[0].pass_last()
        end.spread[1].pass_last()
        pass_next()
        red_gate.finish()
        for one in end.spread:
            one.ready()
            one.drain()
        env.going[0] = True


def backward(cotangent, kept, tables, gains, spread):
    rows, width = cotangent.shape
    cosine, sine, bias = tables
    layers = gains.shape[0]
    d_rows, ff = kept.save_wdown[0].shape
    o, qkv = kept.save_wo[0].shape[1], kept.save_wqkv[0].shape[1]
    part = d_rows // 4
    block = part // spread
    small = (8, width + 2 * HD)

    def far(arrays):
        return [(one, False) for one in arrays]

    ins = dict(
        grad_in=(cotangent, False), joined_in=(kept.save_grad, False),
        mid_in=far(kept.save_mid), hidden_in=far(kept.save_hidden), product_in=far(kept.save_product),
        gateup_in=far(kept.save_gateup), b_in=far(kept.save_b), a_in=far(kept.save_a),
        wdown_in=far(kept.save_wdown), wgate_in=far(kept.save_wgate), wup_in=far(kept.save_wup),
        wqkv_in=far(kept.save_wqkv), wo_in=far(kept.save_wo), q_in=far(kept.save_q), k_in=far(kept.save_k),
        v_in=far(kept.save_v), raw_in=far(kept.save_raw), att_in=far(kept.save_att),
        gains_attn=(gains[:, :width], True), gains_mlp=(gains[:, width : 2 * width], True),
        gains_q=(gains[:, 2 * width : 2 * width + HD], True), gains_k=(gains[:, 2 * width + HD :], True),
        cosine_in=(cosine, False), sine_in=(sine, False), bias_in=(bias, False),
    )
    sums = dict(g_q=(block, 2 * o), g_kv=(2, block, qkv - o), g_o=(block, 2 * o), g_mlp=(3, block, 2 * ff))

    def each(name):
        return ((layers, *sums[name]), BF16, False)

    outs = dict(
        input_grad=((rows, width), F32, False), gain_total=(small, F32, True),
        save_q=each("g_q"), save_kv=each("g_kv"), save_o=each("g_o"), save_mlp=each("g_mlp"),
    )
    scratch = exchange_scratch(rows, width)
    scratch.update({name: pltpu.VMEM(shape, BF16) for name, shape in sums.items()})
    side = spread - 1
    wide, thin = [pltpu.VMEM((1, width), F32)] * layers, [pltpu.VMEM((1, HD), F32)] * layers
    count = 88 + 22 * spread
    scratch.update(
        out=pltpu.VMEM((rows, width), F32), grad_mid=pltpu.VMEM((rows, width), F32),
        blocks=pltpu.VMEM((3, 4, part, ff), BF16),
        blocks_o=pltpu.VMEM((4, part, o), BF16), blocks_qkv=pltpu.VMEM((4, part, qkv), BF16),
        x_in=pltpu.VMEM((3, side, 4, block, ff), BF16),
        x_in_o=pltpu.VMEM((side, 4, block, o), BF16), x_in_qkv=pltpu.VMEM((side, 4, block, qkv), BF16),
        z_in_w=pltpu.VMEM((3, 3, block, ff), BF16),
        z_in_o=pltpu.VMEM((3, block, o), BF16), z_in_qkv=pltpu.VMEM((3, block, qkv), BF16),
        d_attn=wide, d_mlp=wide, d_q=thin, d_k=thin,
        terms=pltpu.VMEM((5, *small), F32), came=pltpu.VMEM((4, *small), F32),
        came_r=pltpu.VMEM((spread, *small), F32), credit=pltpu.SemaphoreType.REGULAR,
        local=pltpu.SemaphoreType.DMA((8 + 32 * layers,)),
        send=pltpu.SemaphoreType.DMA((count,)), recv=pltpu.SemaphoreType.DMA((count,)),
    )
    return call(partial(backward_kernel, layers, spread), ins, outs, scratch, 2, "backward")


def places(dp_size):
    spread = dp_size // 4
    me = lax.axis_index("dp")
    z = me // spread
    return spread, me, lax.rem(me, spread), lax.rem(z, 2), z // 2


def flip_lo(dp_size):
    spread = dp_size // 4
    return [(i, i + spread * (1 - 2 * ((i // spread) % 2))) for i in range(dp_size)]


def flip_hi(dp_size):
    spread = dp_size // 4
    return [(i, i + 2 * spread * (1 - 2 * (i // (2 * spread)))) for i in range(dp_size)]


def shift_r(dp_size, step):
    spread = dp_size // 4
    return [(i, (i // spread) * spread + (i % spread + step) % spread) for i in range(dp_size)]


def rope_tables(positions, head_size):
    half = head_size // 2
    frequency = jnp.power(THETA, -2.0 * jnp.arange(half, dtype=F32) / head_size)
    angle = positions.astype(F32)[:, None] * frequency[None, :]
    return (jnp.cos(angle)[:, None, :], jnp.sin(angle)[:, None, :])


def adamw(weight, first, second, grad, rate, decay):
    first_new = BETA_ONE * first + (1.0 - BETA_ONE) * grad
    second_new = BETA_TWO * second + (1.0 - BETA_TWO) * grad * grad
    first_hat = first_new / (1.0 - BETA_ONE**STEP)
    second_hat = second_new / (1.0 - BETA_TWO**STEP)
    weight_new = weight - rate * (first_hat / (jnp.sqrt(second_hat) + ADAM_EPS) + decay * weight)
    return (first_new, second_new, weight_new)


def body(
    tokens, cotangent, segment_ids, gains, gain_first, gain_second,
    query_weight, query_first, query_second,
    keyvalue_weight, keyvalue_first, keyvalue_second,
    output_weight, output_first, output_second,
    mlp_weight, mlp_first, mlp_second,
):
    dp_size = lax.axis_size("dp")
    spread, me, r, low, high = places(dp_size)
    layers = gains.shape[0]
    local_rows, width = tokens.shape
    group = segment_ids.shape[0]
    rows = 8 * local_rows
    index = jnp.arange(group, dtype=jnp.int32)
    other = lax.ppermute(segment_ids, "dp", flip_lo(dp_size))
    segments = jnp.stack([jnp.where(low == 0, segment_ids, other), jnp.where(low == 0, other, segment_ids)])
    positions = (index[None, :] - (segments - segments[:, :1])).reshape(rows)
    mask = (segments[:, :, None] == segments[:, None, :]) & (index[None, None, :] <= index[None, :, None])
    bias = jnp.where(mask, 0.0, -1e30).astype(BF16)
    cosine, sine = rope_tables(positions, HD)
    tables = (
        jnp.concatenate([cosine[:, 0], cosine[:, 0]], axis=1).reshape(8, local_rows, HD),
        jnp.concatenate([-sine[:, 0], sine[:, 0]], axis=1).reshape(8, local_rows, HD),
        bias,
    )
    masters = (query_weight, keyvalue_weight, output_weight, mlp_weight)

    kept = forward(tokens, cotangent, masters, tables, gains, spread)
    block_output = kept.out
    done = backward(cotangent, kept, tables, gains, spread)
    stacked = [one.astype(F32) for one in (done.save_q, done.save_kv, done.save_o, done.save_mlp)]
    sums = done.gain_total
    gain_total = jnp.stack(
        [
            jnp.concatenate([sums[2 * i, :width], sums[2 * i + 1, :width], sums[2 * i, width:]])
            for i in range(layers)
        ]
    )
    head_gain_grads = gain_total[:, 2 * width :]
    gain_new = adamw(gains, gain_first, gain_second, gain_total, GAIN_RATE, 0.0)
    query_new = adamw(query_weight, query_first, query_second, stacked[0], RATE, DECAY)
    keyvalue_new = adamw(keyvalue_weight, keyvalue_first, keyvalue_second, stacked[1], RATE, DECAY)
    output_new = adamw(output_weight, output_first, output_second, stacked[2], RATE * OUTPUT_FACTOR, DECAY)
    mlp_new = adamw(mlp_weight, mlp_first, mlp_second, stacked[3], RATE, DECAY)
    return (block_output, done.input_grad, *gain_new, head_gain_grads, *query_new, *keyvalue_new, *output_new, *mlp_new)


def solution(mesh):
    token = P(("dp", "tensor"), None)
    flat = P(None, "dp", "tensor")
    deep = P(None, None, "dp", "tensor")
    placed = (token, token, P("dp"), P(), P(), P(), *[flat] * 3, *[deep] * 3, *[flat] * 3, *[deep] * 3)
    outs = (token, token, P(), P(), P(), P(), *[flat] * 3, *[deep] * 3, *[flat] * 3, *[deep] * 3)
    return jax.shard_map(body, mesh=mesh, in_specs=placed, out_specs=outs, check_vma=False)
```
